32 devices in a mesh: members: 2 (over x), space: 16 (over z, y, core).
Axes of the slice: x: 2, y: 2, z: 4, core: 2. Of those that a mesh axis runs over, the one named last changes fastest.
Arguments:
- spectra: float32 [16384, 1296], P(('members', 'space')), parts along dimension 0, may hold values from 0.05 to 5
- wind_files: float32 [32, 2, 1024], P(('members', 'space')), parts along dimension 0, may hold values from -25 to 25
- current_files: float32 [32, 2, 1024], P(('members', 'space')), parts along dimension 0, may hold values from -1 to 1
- reader_turn: int32 [2], replicated, may hold values from 0 to 15
- cell_point: int32 [8192], P('space'), may hold values from 0 to 1023, as said below
- coupling: bfloat16 [1296, 1296], replicated, may hold values from -0.078125 to 0.078125
- send_list: int32 [16, 16, 64], P('space'), may hold values from 0 to 511, as said below
- send_count: int32 [16, 16], P('space'), may hold values from 0 to 64, as said below
- recv_list: int32 [16, 16, 64], P('space'), may hold values from 0 to 1023, as said below
- wet_mask: int32 [128, 128], P('space'), may hold values from 0 to 1, as said below
Outputs:
- new_spectra: float32 [16384, 1296], P(('members', 'space')), parts along dimension 0
The draws below stay inside these ranges and needn't reach their ends.
There are 2 independent parts, one for each index of `members`. The reference program is written for one: setup_inputs(seed, part) draws one part's arguments, and reference() takes and returns one part's arrays. A program takes and returns all parts, laid end to end along the dimension named above; an argument that names none is the same for every part. Nothing has to cross between parts.
Inputs may be any that keep to these rules, and one draw needn't show every extreme that they name: `send_count`: every entry is at most 64, and 64 is reached in every draw; each row sums to 512; column b sums to the number of wet cells of strip b. `send_list`: the live entries of row s name every local row of share s exactly once; entries past the count are 0. `recv_list`: the live entries for strip b name every wet cell of strip b exactly once (row-major within the strip's 8 x 128 cells), matched slot by slot to send_list; entries past the count are 0. `wet_mask`: equals 1 exactly on the cells that recv_list names. `cell_point`: the forcing point of the grid cell to which the row is sent.
All inputs are finite; a program needn't handle non-finite values.
Results may differ from the reference program's by a relative error of at most 0.0016.
Values sent between devices are 32-bit elements; how exact they have to be, the bound alone decides.
No kernel may reach another device: no remote copies, remote signals or barrier semaphores. Data moves between devices by JAX's collectives and lax.ppermute only.
A program may use at most 64 MiB of HBM per device.

```python
import math
import jax
import jax.numpy as jnp

DIRS = 36
FREQS = 36
SPEC = 1296
ROWS_DEV = 8
COLS = 128
COARSE = 4
WET_DEV = 512
CAP = 64
WET = 8192
GRID_ROWS = 128
FPTS = 1024
N_SPACE = 16


def layout_draw(key):
    sub_keys = jax.random.split(key, 8)
    half_cap = CAP // 2
    margin = max(CAP // 8, 1)
    pairs = N_SPACE // 2
    spread = jax.random.randint(sub_keys[0], (pairs,), 0, half_cap - margin + 1)
    spread = spread.at[jax.random.randint(sub_keys[1], (), 0, pairs)].set(half_cap - margin)
    block_level = jnp.stack([half_cap + spread, half_cap - spread], axis=1).reshape(N_SPACE)
    block_level = block_level[jax.random.permutation(sub_keys[2], N_SPACE)]
    jitter = jax.random.randint(sub_keys[3], (pairs,), 0, margin + 1)
    jitter = jitter.at[jax.random.randint(sub_keys[4], (), 0, pairs)].set(margin)
    offsets = jnp.stack([jitter, -jitter], axis=1).reshape(N_SPACE)
    offsets = offsets[jax.random.permutation(sub_keys[5], N_SPACE)]
    source_ids = jnp.arange(N_SPACE, dtype=jnp.int32)
    counts = block_level[None, :] + offsets[(source_ids[None, :] - source_ids[:, None]) % N_SPACE]
    counts = counts.astype(jnp.int32)
    grid_cells = ROWS_DEV * COLS
    row_perm = jax.vmap(lambda sub: jax.random.permutation(sub, WET_DEV))(jax.random.split(sub_keys[6], N_SPACE)).astype(jnp.int32)
    cell_perm = jax.vmap(lambda sub: jax.random.permutation(sub, grid_cells))(jax.random.split(sub_keys[7], N_SPACE)).astype(jnp.int32)
    send_start = jnp.cumsum(counts, axis=1) - counts
    recv_start = jnp.cumsum(counts, axis=0) - counts
    slot_ids = jnp.arange(CAP, dtype=jnp.int32)
    live = slot_ids[None, None, :] < counts[:, :, None]
    send_pos = jnp.clip(send_start[:, :, None] + slot_ids[None, None, :], 0, WET_DEV - 1)
    send_rows = jnp.where(live, row_perm[source_ids[:, None, None], send_pos], 0)
    recv_pos = jnp.clip(recv_start[:, :, None] + slot_ids[None, None, :], 0, grid_cells - 1)
    recv_cell = jnp.where(live, cell_perm[source_ids[None, :, None], recv_pos], 0)
    recv_rows = jnp.transpose(recv_cell, (1, 0, 2))
    wet_flags = (jnp.arange(grid_cells, dtype=jnp.int32)[None, :] < N_SPACE * block_level[:, None]).astype(jnp.int32)
    wet_cells = jnp.zeros((N_SPACE, grid_cells), jnp.int32).at[source_ids[:, None], cell_perm].set(wet_flags)
    wet_cells = wet_cells.reshape(N_SPACE * ROWS_DEV, COLS)
    global_row = source_ids[None, :, None] * ROWS_DEV + recv_cell // COLS
    global_col = recv_cell % COLS
    point_ids = global_row // COARSE * (COLS // COARSE) + global_col // COARSE
    flat_rows = (source_ids[:, None, None] * WET_DEV + send_rows).reshape(-1)
    points = jnp.zeros((N_SPACE * WET_DEV,), jnp.int32).at[flat_rows].add(jnp.where(live, point_ids, 0).reshape(-1))
    return (points, send_rows, counts, recv_rows, wet_cells)


def draw_cell_point(key, part):
    result = layout_draw(key)
    return result[0]


def draw_send_list(key, part):
    result = layout_draw(key)
    return result[1]


def draw_send_count(key, part):
    result = layout_draw(key)
    return result[2]


def draw_recv_list(key, part):
    result = layout_draw(key)
    return result[3]


def draw_wet_mask(key, part):
    result = layout_draw(key)
    return result[4]


def block_scale(key, dims, cuts, low, high):
    level, own = 1.0, jax.random.fold_in(key, 6)
    for dim, parts in cuts:
        draws = jnp.exp(jax.random.uniform(jax.random.fold_in(own, dim), (parts,), jnp.float32, low / len(cuts), high / len(cuts)))
        level = level * jnp.repeat(draws, dims[dim] // parts).reshape([-1 if axis == dim else 1 for axis in range(len(dims))])
    return level


def gaussian(rng, dims, width, most, pieces=(), held_as=jnp.bfloat16):
    entries = jax.random.normal(rng, dims, jnp.float32) * width
    if len(pieces) > 0:
        entries = block_scale(rng, dims, pieces, -0.22, 0.18) * entries
    return jnp.clip(entries, min=-most, max=most).astype(held_as)


def setup_inputs(seed: int = 0, part: int = 0) -> dict:
    arg_keys = jax.random.split(jax.random.key(seed), 11)
    part_splits = jax.random.split(jax.random.fold_in(arg_keys[10], part), 11)
    spectra = jnp.clip(jnp.exp(math.log(5.0) - 4.6051702 * jax.random.uniform(part_splits[0], (WET, SPEC), jnp.float32) ** block_scale(part_splits[0], (WET, SPEC), ((0, 16),), -0.2, 0.2)), 0.05, 5.0)
    wind_files = gaussian(part_splits[1], (N_SPACE, 2, FPTS), 8.0, 25.0, ((0, 16),), jnp.float32)
    current_files = gaussian(part_splits[2], (N_SPACE, 2, FPTS), 0.3, 1.0, ((0, 16),), jnp.float32)
    reader_turn = jax.random.randint(arg_keys[3], (2,), 0, N_SPACE).astype(jnp.int32)
    cell_point = draw_cell_point(jax.random.fold_in(arg_keys[10], 71), part)
    coupling = gaussian(arg_keys[5], (SPEC, SPEC), (4 * SPEC) ** -0.5, 0.078125)
    send_list = draw_send_list(jax.random.fold_in(arg_keys[10], 71), part)
    send_count = draw_send_count(jax.random.fold_in(arg_keys[10], 71), part)
    recv_list = draw_recv_list(jax.random.fold_in(arg_keys[10], 71), part)
    wet_mask = draw_wet_mask(jax.random.fold_in(arg_keys[10], 71), part)
    return dict(spectra=spectra, wind_files=wind_files, current_files=current_files, reader_turn=reader_turn, cell_point=cell_point, coupling=coupling, send_list=send_list, send_count=send_count, recv_list=recv_list, wet_mask=wet_mask)


gravity = 9.81
base_freq = 0.0418
freq_ratio = 1.1
freq_span = 35.0
input_coef = 1e-4
wind_gain = 1.12
dissip_coef = 5e-4
half_length = 300.0
courant_scale = 0.05


def spectral_tables():
    direction = (2.0 * math.pi / DIRS) * jnp.arange(DIRS, dtype=jnp.float32)
    exponent = jnp.arange(FREQS, dtype=jnp.float32) * (freq_span / (FREQS - 1))
    frequency = base_freq * freq_ratio ** exponent
    angular = 2.0 * math.pi * frequency
    phase_speed = gravity / angular
    return jnp.cos(direction), jnp.sin(direction), angular, phase_speed, 0.5 * phase_speed


def source_half(energy, wind_east, wind_north, coupling):
    cos_dir, sine_dir, angular, phase_speed, group_speed = spectral_tables()
    along_wind = wind_east[:, None] * cos_dir[None, :] + wind_north[:, None] * sine_dir[None, :]
    growth = input_coef * angular[None, None, :] * jnp.maximum(wind_gain * along_wind[:, :, None] / phase_speed[None, None, :] - 1.0, 0.0)
    growth = growth.reshape(energy.shape[0], -1)
    mean_square = jnp.mean(energy * energy, axis=1, keepdims=True)
    decay_rate = dissip_coef * jnp.tile(angular, DIRS)[None, :] * mean_square
    local_part = energy * (1.0 + half_length * growth) / (1.0 + half_length * decay_rate)
    return local_part + jnp.dot(local_part.astype(jnp.bfloat16), coupling, preferred_element_type=jnp.float32)


def advect(center, upwind_lo, upwind_hi, courant):
    ahead_part = jnp.maximum(courant, 0.0)
    behind = jnp.minimum(courant, 0.0)
    return center - ahead_part * (center - upwind_lo) - behind * (upwind_hi - center)


def sweep_cols(energy_grid, drift_east, wet_field):
    cos_dir, sine_dir, angular, phase_speed, group_speed = spectral_tables()
    wave_speed = (cos_dir[:, None] * group_speed[None, :]).reshape(-1)
    courant = (wave_speed[None, None, :] + drift_east[:, :, None]) * courant_scale
    zero_edge = jnp.zeros_like(energy_grid[:, :1])
    upwind_lo = jnp.concatenate([zero_edge, energy_grid[:, :-1]], axis=1)
    upwind_hi = jnp.concatenate([energy_grid[:, 1:], zero_edge], axis=1)
    return advect(energy_grid, upwind_lo, upwind_hi, courant) * wet_field[:, :, None]


def sweep_rows(energy_grid, row_above, row_below, drift_north, wet_field):
    cos_dir, sine_dir, angular, phase_speed, group_speed = spectral_tables()
    wave_speed = (sine_dir[:, None] * group_speed[None, :]).reshape(-1)
    courant = (wave_speed[None, None, :] + drift_north[:, :, None]) * courant_scale
    return advect(energy_grid, row_above, row_below, courant) * wet_field[:, :, None]


def forcing_points(row_start, row_count, col_count):
    rows_idx = row_start + jnp.arange(row_count, dtype=jnp.int32)
    cols_idx = jnp.arange(col_count, dtype=jnp.int32)
    return (rows_idx[:, None] // COARSE) * (col_count // COARSE) + cols_idx[None, :] // COARSE


def reference(spectra, wind_files, current_files, reader_turn, cell_point, coupling, send_list, send_count, recv_list, wet_mask):
    wind_mean = 0.5 * (wind_files[reader_turn[0]] + wind_files[reader_turn[1]])
    current_mean = 0.5 * (current_files[reader_turn[0]] + current_files[reader_turn[1]])
    cell_wind = jnp.take(wind_mean, cell_point, axis=1)
    first_half = source_half(spectra, cell_wind[0], cell_wind[1], coupling)
    slot_ids = jnp.arange(CAP, dtype=jnp.int32)
    weight = (slot_ids[None, None, :] < send_count[:, :, None]).astype(jnp.float32).reshape(-1, 1)
    source_rows = (jnp.arange(N_SPACE, dtype=jnp.int32)[:, None, None] * WET_DEV + send_list).reshape(-1)
    target_cells = (jnp.arange(N_SPACE, dtype=jnp.int32)[None, :, None] * (ROWS_DEV * COLS) + jnp.transpose(recv_list, (1, 0, 2))).reshape(-1)
    carried = first_half[source_rows] * weight
    energy_grid = jnp.zeros((GRID_ROWS * COLS, SPEC), jnp.float32).at[target_cells].add(carried)
    energy_grid = energy_grid.reshape(GRID_ROWS, COLS, SPEC)
    points = forcing_points(0, GRID_ROWS, COLS)
    drift = jnp.take(current_mean, points, axis=1)
    wet_field = wet_mask.astype(jnp.float32)
    swept_cols = sweep_cols(energy_grid, drift[0], wet_field)
    zero_row = jnp.zeros_like(swept_cols[:1])
    row_above = jnp.concatenate([zero_row, swept_cols[:-1]], axis=0)
    row_below = jnp.concatenate([swept_cols[1:], zero_row], axis=0)
    swept = sweep_rows(swept_cols, row_above, row_below, drift[1], wet_field).reshape(-1, SPEC)
    returned = swept[target_cells] * weight
    back_rows = jnp.zeros((WET, SPEC), jnp.float32).at[source_rows].add(returned)
    return source_half(back_rows, cell_wind[0], cell_wind[1], coupling)
```

```python
import functools
import math

import jax
import jax.numpy as jnp
import numpy as np
from jax import lax
from jax.experimental import pallas as pl
from jax.experimental.pallas import tpu as pltpu
from jax.sharding import PartitionSpec as P

DIRS = 36
FREQS = 36
COARSE = 4


gravity = 9.81
base_freq = 0.0418
freq_ratio = 1.1
freq_span = 35.0
input_coef = 0.0001
wind_gain = 1.12
dissip_coef = 0.0005
half_length = 300.0
courant_scale = 0.05


def from_root(array, axis, root):
    mine = lax.axis_index(axis) == root
    return lax.psum(jnp.where(mine, array, jnp.zeros_like(array)), axis)


def extended(array, sides, width):
    for axis, dim in sides:
        size, length = (lax.axis_size(axis), array.shape[dim])
        up = [(i, (i + 1) % size) for i in range(size - 1)]
        down = [(j, i) for i, j in up]
        last = lax.slice_in_dim(array, length - width, length, axis=dim)
        first = lax.slice_in_dim(array, 0, width, axis=dim)
        before = lax.ppermute(last, axis, up)
        after = lax.ppermute(first, axis, down)
        array = jnp.concatenate([before, array, after], axis=dim)
    return array


def spectral_tables():
    direction = 2.0 * math.pi / DIRS * jnp.arange(DIRS, dtype=jnp.float32)
    exponent = jnp.arange(FREQS, dtype=jnp.float32) * (freq_span / (FREQS - 1))
    frequency = base_freq * freq_ratio**exponent
    angular = 2.0 * math.pi * frequency
    phase_speed = gravity / angular
    return (jnp.cos(direction), jnp.sin(direction), angular, phase_speed, 0.5 * phase_speed)


def source_half(energy, wind_east, wind_north, coupling):
    cos_dir, sine_dir, angular, phase_speed, group_speed = spectral_tables()
    along_wind = wind_east[:, None] * cos_dir[None, :] + wind_north[:, None] * sine_dir[None, :]
    growth = (
        input_coef
        * angular[None, None, :]
        * jnp.maximum(wind_gain * along_wind[:, :, None] / phase_speed[None, None, :] - 1.0, 0.0)
    )
    growth = growth.reshape(energy.shape[0], -1)
    mean_square = jnp.mean(energy * energy, axis=1, keepdims=True)
    decay_rate = dissip_coef * jnp.tile(angular, DIRS)[None, :] * mean_square
    local_part = energy * (1.0 + half_length * growth) / (1.0 + half_length * decay_rate)
    return local_part + jnp.dot(
        local_part.astype(jnp.bfloat16), coupling, preferred_element_type=jnp.float32
    )


def advect(center, upwind_lo, upwind_hi, courant):
    ahead_part = jnp.maximum(courant, 0.0)
    behind = jnp.minimum(courant, 0.0)
    return center - ahead_part * (center - upwind_lo) - behind * (upwind_hi - center)


def sweep_cols(energy_grid, drift_east, wet_field):
    cos_dir, sine_dir, angular, phase_speed, group_speed = spectral_tables()
    wave_speed = (cos_dir[:, None] * group_speed[None, :]).reshape(-1)
    courant = (wave_speed[None, None, :] + drift_east[:, :, None]) * courant_scale
    zero_edge = jnp.zeros_like(energy_grid[:, :1])
    upwind_lo = jnp.concatenate([zero_edge, energy_grid[:, :-1]], axis=1)
    upwind_hi = jnp.concatenate([energy_grid[:, 1:], zero_edge], axis=1)
    return advect(energy_grid, upwind_lo, upwind_hi, courant) * wet_field[:, :, None]


def sweep_rows(energy_grid, row_above, row_below, drift_north, wet_field):
    cos_dir, sine_dir, angular, phase_speed, group_speed = spectral_tables()
    wave_speed = (sine_dir[:, None] * group_speed[None, :]).reshape(-1)
    courant = (wave_speed[None, None, :] + drift_north[:, :, None]) * courant_scale
    return advect(energy_grid, row_above, row_below, courant) * wet_field[:, :, None]


def forcing_points(row_start, row_count, col_count):
    rows_idx = row_start + jnp.arange(row_count, dtype=jnp.int32)
    cols_idx = jnp.arange(col_count, dtype=jnp.int32)
    return rows_idx[:, None] // COARSE * (col_count // COARSE) + cols_idx[None, :] // COARSE


def on_strips(
    spectra,
    wind_files,
    current_files,
    reader_turn,
    cell_point,
    coupling,
    send_list,
    send_count,
    recv_list,
    wet_mask,
):
    levels = []
    for time_level in range(2):
        levels.append(
            (
                from_root(wind_files[0], "space", reader_turn[time_level]),
                from_root(current_files[0], "space", reader_turn[time_level]),
            )
        )
    wind_mean = 0.5 * (levels[0][0] + levels[1][0])
    current_mean = 0.5 * (levels[0][1] + levels[1][1])
    cell_wind = jnp.take(wind_mean, cell_point, axis=1)
    first_half = source_half(spectra, cell_wind[0], cell_wind[1], coupling)
    send_rows = send_list[0]
    counts = send_count[0]
    places = recv_list[0]
    slot_count = send_rows.shape[1]
    spec_width = spectra.shape[1]
    live_slots = (jnp.arange(slot_count, dtype=jnp.int32)[None, :] < counts[:, None]).astype(
        jnp.float32
    )
    packed = first_half[send_rows] * live_slots[:, :, None]
    arrived = lax.all_to_all(packed, "space", split_axis=0, concat_axis=0, tiled=True)
    row_count = wet_mask.shape[0]
    col_count = wet_mask.shape[1]
    energy_grid = (
        jnp.zeros((row_count * col_count, spec_width), jnp.float32)
        .at[places.reshape(-1)]
        .add(arrived.reshape(-1, spec_width))
    )
    energy_grid = energy_grid.reshape(row_count, col_count, spec_width)
    points = forcing_points(lax.axis_index("space") * row_count, row_count, col_count)
    drift = jnp.take(current_mean, points, axis=1)
    wet_field = wet_mask.astype(jnp.float32)
    swept_cols = sweep_cols(energy_grid, drift[0], wet_field)
    padded = extended(swept_cols, (("space", 0),), 1)
    swept = sweep_rows(swept_cols, padded[:-2], padded[2:], drift[1], wet_field).reshape(
        -1, spec_width
    )
    outgoing = swept[places]
    flat_rows = send_rows.reshape(-1)
    empty_rows = jnp.zeros((spectra.shape[0], spec_width), jnp.float32)
    returned = lax.all_to_all(outgoing, "space", split_axis=0, concat_axis=0, tiled=True)
    back_rows = empty_rows.at[flat_rows].add(
        (returned * live_slots[:, :, None]).reshape(-1, spec_width)
    )
    result = source_half(back_rows, cell_wind[0], cell_wind[1], coupling)
    return result


LANES = 128
F32 = jnp.float32
VMEM_LIMIT = 56 * 1024 * 1024


def wave_tables():
    direction = 2.0 * np.pi / DIRS * np.arange(DIRS)
    frequency = base_freq * freq_ratio ** (np.arange(FREQS) * (freq_span / (FREQS - 1)))
    angular = 2.0 * np.pi * frequency
    phase = gravity / angular
    group = 0.5 * phase
    cos_dir, sin_dir = np.cos(direction)[:, None], np.sin(direction)[:, None]
    flat = lambda t: np.broadcast_to(t, (DIRS, FREQS)).reshape(-1)
    source = np.zeros((8, DIRS * FREQS), np.float32)
    source[0] = flat(wind_gain * cos_dir / phase)
    source[1] = flat(wind_gain * sin_dir / phase)
    source[2] = flat(half_length * input_coef * angular)
    source[3] = flat(half_length * dissip_coef * angular)
    east = flat(courant_scale * cos_dir * group).astype(np.float32)
    north = flat(courant_scale * sin_dir * group).astype(np.float32)
    return source, east, north


def pad_lanes(array, rows):
    flat = array.reshape(-1)
    return jnp.pad(flat, (0, rows * LANES - flat.shape[0])).reshape(rows, LANES)


def ceil_to(value, step):
    return -(-value // step) * step


def local_rows(energy, cp, winds, table_ref, spec):
    half = len(winds) // 2
    rows = energy.shape[0]
    lane = lax.broadcasted_iota(jnp.int32, (rows, LANES), 1)
    east = jnp.zeros((rows, LANES), F32)
    north = jnp.zeros((rows, LANES), F32)
    for q in range(half):
        hit = cp == lane + q * LANES
        east += jnp.where(hit, winds[q], 0.0)
        north += jnp.where(hit, winds[half + q], 0.0)
    east = jnp.sum(east, axis=1, keepdims=True)
    north = jnp.sum(north, axis=1, keepdims=True)
    mean_square = jnp.sum(energy * energy, axis=1, keepdims=True) * (1.0 / spec)
    along = east * table_ref[0:1, :] + north * table_ref[1:2, :]
    gain = 1.0 + table_ref[2:3, :] * jnp.maximum(along - 1.0, 0.0)
    loss = 1.0 + table_ref[3:4, :] * mean_square
    return energy * gain / loss


def local_all(energy_ref, cp_ref, wind_ref, table_ref, loc_ref, locb_ref, block=32):
    rows, spec = energy_ref.shape
    wind = jnp.sum(wind_ref[...], axis=0)
    winds = [wind[q : q + 1, :] for q in range(wind.shape[0])]

    @pl.loop(0, rows // block)
    def _(i):
        at = pl.ds(pl.multiple_of(i * block, block), block)
        local = local_rows(energy_ref[at, :], cp_ref[at, :], winds, table_ref, spec)
        loc_ref[at, :] = local
        locb_ref[at, :] = local.astype(jnp.bfloat16)


def first_kernel(energy_ref, cp_ref, wind_ref, table_ref, coup_ref, out_ref, loc_ref, locb_ref):
    rows, spec = energy_ref.shape
    tiles = rows // LANES
    local_all(energy_ref, cp_ref, wind_ref, table_ref, loc_ref, locb_ref)
    wide = 2 * LANES
    whole = spec // wide

    @pl.loop(0, whole)
    def _(q):
        cols = pl.ds(pl.multiple_of(q * wide, wide), wide)
        full = loc_ref[:, cols] + jnp.dot(
            locb_ref[...], coup_ref[:, cols], preferred_element_type=F32
        )
        turned = full.T
        start = pl.multiple_of(q * (wide * tiles), 8)
        for j in range(tiles):
            out_ref[pl.ds(start + j, wide, stride=tiles), :] = turned[:, j * LANES : (j + 1) * LANES]

    left = spec - whole * wide
    if left:
        cols = pl.ds(whole * wide, left)
        full = loc_ref[:, cols] + jnp.dot(
            locb_ref[...], coup_ref[:, cols], preferred_element_type=F32
        )
        turned = full.T
        for j in range(tiles):
            out_ref[pl.ds(whole * wide * tiles + j, left, stride=tiles), :] = turned[
                :, j * LANES : (j + 1) * LANES
            ]


def last_kernel(
    turned_ref, cp_ref, wind_ref, table_ref, coup_ref, out_ref, energy_ref, loc_ref, locb_ref
):
    rows, spec = energy_ref.shape
    tiles = rows // LANES
    whole = spec // LANES

    @pl.loop(0, whole)
    def _(q):
        start = pl.multiple_of(q * (LANES * tiles), 8)
        cols = pl.ds(pl.multiple_of(q * LANES, LANES), LANES)
        for j in range(tiles):
            piece = turned_ref[pl.ds(start + j, LANES, stride=tiles), :]
            energy_ref[j * LANES : (j + 1) * LANES, cols] = piece.T

    left = spec - whole * LANES
    if left:
        for j in range(tiles):
            piece = turned_ref[pl.ds(whole * LANES * tiles + j, left, stride=tiles), :]
            energy_ref[j * LANES : (j + 1) * LANES, whole * LANES :] = piece.T

    local_all(energy_ref, cp_ref, wind_ref, table_ref, loc_ref, locb_ref)
    wide = 2 * LANES
    whole = spec // wide

    @pl.loop(0, whole)
    def _(q):
        cols = pl.ds(pl.multiple_of(q * wide, wide), wide)
        out_ref[:, cols] = loc_ref[:, cols] + jnp.dot(
            locb_ref[...], coup_ref[:, cols], preferred_element_type=F32
        )

    left = spec - whole * wide
    if left:
        cols = pl.ds(whole * wide, left)
        out_ref[:, cols] = loc_ref[:, cols] + jnp.dot(
            locb_ref[...], coup_ref[:, cols], preferred_element_type=F32
        )


def upwind(center, before, after, courant):
    return center + jnp.abs(courant) * (jnp.where(courant > 0.0, before, after) - center)


def sweep_kernel(
    grid_rows, cols, depth, tiles,
    place_ref, came_ref, east_ref, north_ref, speed_ref, out_ref, cell_ref, one_ref, two_ref, piece_ref,
):
    pitch = cols + 8
    blocks = came_ref.shape[0] // (depth * tiles) * tiles
    flag = depth
    spare = lax.broadcasted_iota(jnp.int32, (LANES, LANES), 0) == flag
    piece_ref[...] = jnp.where(spare, 1.0, 0.0)

    @pl.loop(0, one_ref.shape[0] // LANES)
    def _(i):
        at = pl.ds(pl.multiple_of(i * LANES, LANES), LANES)
        one_ref[at, :] = jnp.zeros((LANES, LANES), F32)

    for edge in (0, grid_rows + 1):
        two_ref[edge * pitch : (edge + 1) * pitch, :] = jnp.zeros((pitch, LANES), F32)

    @pl.loop(0, blocks // tiles)
    def _(s):
        for j in range(tiles):
            start = s * (depth * tiles) + j
            piece_ref[0:depth, :] = came_ref[pl.ds(start, depth, stride=tiles), :]
            at = pl.ds(pl.multiple_of((s * tiles + j) * LANES, LANES), LANES)
            cell_ref[at, :] = piece_ref[...].T

    unroll = 32

    @pl.loop(0, blocks * LANES // unroll)
    def _(i):
        for t in range(unroll):
            row = i * unroll + t
            one_ref[pl.ds(place_ref[row], 1), :] = cell_ref[pl.ds(row, 1), :]

    @pl.loop(0, grid_rows // COARSE)
    def _(r4):
        point = pl.ds(pl.multiple_of(r4 * cols, cols), cols)
        courant = speed_ref[0:1, :] + east_ref[point, :]
        for dr in range(COARSE):
            base = pl.multiple_of((r4 * COARSE + dr + 1) * pitch + 8, 8)
            center = one_ref[pl.ds(base, cols), :]
            before = one_ref[pl.ds(base - 1, cols), :]
            after = one_ref[pl.ds(base + 1, cols), :]
            wet = jnp.broadcast_to(center[:, flag : flag + 1], center.shape)
            two_ref[pl.ds(base, cols), :] = upwind(center, before, after, courant) * wet

    @pl.loop(0, grid_rows // COARSE)
    def _(r4):
        point = pl.ds(pl.multiple_of(r4 * cols, cols), cols)
        courant = speed_ref[1:2, :] + north_ref[point, :]
        for dr in range(COARSE):
            base = pl.multiple_of((r4 * COARSE + dr + 1) * pitch + 8, 8)
            above = pl.multiple_of(base - pitch, 8)
            below = pl.multiple_of(base + pitch, 8)
            one_ref[pl.ds(base, cols), :] = upwind(
                two_ref[pl.ds(base, cols), :],
                two_ref[pl.ds(above, cols), :],
                two_ref[pl.ds(below, cols), :],
                courant,
            )

    @pl.loop(0, blocks * LANES // unroll)
    def _(i):
        for t in range(unroll):
            row = i * unroll + t
            cell_ref[pl.ds(row, 1), :] = one_ref[pl.ds(place_ref[row], 1), :]

    @pl.loop(0, blocks // tiles)
    def _(s):
        for j in range(tiles):
            start = s * (depth * tiles) + j
            at = pl.ds(pl.multiple_of((s * tiles + j) * LANES, LANES), LANES)
            turned = cell_ref[at, :].T
            out_ref[pl.ds(start, depth, stride=tiles), :] = turned[0:depth, :]


def in_vmem(count):
    return [pl.BlockSpec(memory_space=pltpu.VMEM)] * count


def on_spectrum(
    spectra,
    wind_files,
    current_files,
    reader_turn,
    cell_point,
    coupling,
    send_list,
    send_count,
    recv_list,
    wet_mask,
):
    shares = lax.axis_size("space")
    me = lax.axis_index("space")
    rows, spec = spectra.shape
    depth = spec // shares
    tiles = rows // LANES
    cap = send_list.shape[2]
    strip_rows, cols = wet_mask.shape
    grid_rows = strip_rows * shares
    points = wind_files.shape[2]
    pitch = cols + 8
    source, east_speed, north_speed = wave_tables()
    table = jnp.asarray(source)

    mine = 0.5 * (
        (reader_turn[0] == me).astype(F32) + (reader_turn[1] == me).astype(F32)
    )
    force_rows = 2 * points // LANES
    list_rows = -(-shares * cap // LANES)
    pack = jnp.concatenate(
        [
            mine * wind_files[0].reshape(force_rows, LANES),
            mine * current_files[0].reshape(force_rows, LANES),
            pad_lanes(send_list[0].astype(F32), list_rows),
            pad_lanes(recv_list[0].astype(F32), list_rows),
            pad_lanes(send_count[0].astype(F32), -(-shares // LANES)),
        ],
        axis=0,
    )
    pack = jnp.pad(pack, ((0, ceil_to(pack.shape[0], 8) - pack.shape[0]), (0, 0)))
    every = lax.all_gather(pack, "space")
    wind = every[:, :force_rows]
    current = jnp.sum(every[:, force_rows : 2 * force_rows], axis=0).reshape(2, points)
    at = 2 * force_rows
    sends = every[:, at : at + list_rows].reshape(shares, -1)[:, : shares * cap]
    at += list_rows
    lands = every[:, at : at + list_rows].reshape(shares, -1)[:, : shares * cap]
    at += list_rows
    counts = every[:, at:].reshape(shares, -1)[:, :shares]
    sends = sends.reshape(shares, shares, cap)
    lands = lands.reshape(shares, shares, cap).transpose(1, 0, 2)
    strip = jnp.arange(shares, dtype=F32)[None, :, None] * (strip_rows * cols)
    cell = (lands + strip).astype(jnp.int32)
    position = (cell // cols + 1) * pitch + 8 + cell % cols
    live = jnp.arange(cap, dtype=F32)[None, None, :] < counts[:, :, None]
    position = jnp.where(live, position, 0).reshape(shares, 1, shares * cap)
    names = jnp.where(live, sends, -1.0).reshape(shares, 1, shares * cap)
    own = jnp.arange(rows, dtype=F32)[None, :, None]
    place = jnp.sum(jnp.where(names == own, position, 0), axis=2).reshape(-1)

    drift = (courant_scale * current).reshape(2, grid_rows // COARSE, cols // COARSE)
    drift = jnp.repeat(drift, COARSE, axis=2).reshape(2, grid_rows // COARSE * cols, 1)
    drift = jnp.broadcast_to(drift, (2, grid_rows // COARSE * cols, LANES))
    speed = jnp.stack([jnp.asarray(east_speed), jnp.asarray(north_speed)])
    speed = jnp.pad(speed, ((0, 6), (0, LANES)))
    speed = lax.dynamic_slice(speed, (0, me * depth), (8, LANES))

    cp = cell_point.reshape(rows, 1)
    params = pltpu.CompilerParams(vmem_limit_bytes=VMEM_LIMIT)
    flops = 2 * rows * spec * spec
    turned = pl.pallas_call(
        first_kernel,
        out_shape=jax.ShapeDtypeStruct((spec * tiles, LANES), F32),
        in_specs=in_vmem(5),
        out_specs=pl.BlockSpec(memory_space=pltpu.VMEM),
        scratch_shapes=[pltpu.VMEM((rows, spec), F32), pltpu.VMEM((rows, spec), jnp.bfloat16)],
        compiler_params=params,
        cost_estimate=pl.CostEstimate(
            flops=flops, bytes_accessed=12 * rows * spec, transcendentals=0
        ),
        name="first_half",
    )(spectra, cp, wind, table, coupling)
    came = lax.all_to_all(
        turned.reshape(shares, depth, tiles, LANES), "space", 0, 0, tiled=True
    ).reshape(spec * tiles, LANES)
    grid_size = ceil_to((grid_rows + 2) * pitch + 8, LANES)
    swept = pl.pallas_call(
        functools.partial(sweep_kernel, grid_rows, cols, depth, tiles),
        out_shape=jax.ShapeDtypeStruct((spec * tiles, LANES), F32),
        in_specs=[pl.BlockSpec(memory_space=pltpu.SMEM)] + in_vmem(4),
        out_specs=pl.BlockSpec(memory_space=pltpu.VMEM),
        scratch_shapes=[
            pltpu.VMEM((shares * rows, LANES), F32),
            pltpu.VMEM((grid_size, LANES), F32),
            pltpu.VMEM((grid_size, LANES), F32),
            pltpu.VMEM((LANES, LANES), F32),
        ],
        compiler_params=params,
        cost_estimate=pl.CostEstimate(
            flops=20 * grid_size * LANES, bytes_accessed=8 * rows * spec, transcendentals=0
        ),
        name="sweeps",
    )(place, came, drift[0], drift[1], speed)
    back = lax.all_to_all(
        swept.reshape(shares, depth, tiles, LANES), "space", 0, 0, tiled=True
    ).reshape(spec * tiles, LANES)
    return pl.pallas_call(
        last_kernel,
        out_shape=jax.ShapeDtypeStruct((rows, spec), F32),
        in_specs=in_vmem(5),
        out_specs=pl.BlockSpec(memory_space=pltpu.VMEM),
        scratch_shapes=[
            pltpu.VMEM((rows, spec), F32),
            pltpu.VMEM((rows, spec), F32),
            pltpu.VMEM((rows, spec), jnp.bfloat16),
        ],
        compiler_params=params,
        cost_estimate=pl.CostEstimate(
            flops=flops, bytes_accessed=12 * rows * spec, transcendentals=0
        ),
        name="last_half",
    )(back, cp, wind, table, coupling)


def fits(shares, rows, spec, strip_rows, cols):
    if spec % shares or spec // shares >= LANES or rows % LANES or cols % LANES:
        return False
    cells = shares * strip_rows * cols
    held = LANES * 4 * (2 * (cells + cells // 8) + shares * rows + cells // 2)
    return held + 8 * rows * spec < VMEM_LIMIT


def on_device(*args):
    spectra, wet_mask = args[0], args[9]
    if fits(lax.axis_size("space"), *spectra.shape, *wet_mask.shape):
        return on_spectrum(*args)
    return on_strips(*args)


def solution(mesh):
    placed = (
        P(("members", "space"), None),
        P(("members", "space"), None, None),
        P(("members", "space"), None, None),
        P(),
        P("space"),
        P(),
        P("space", None, None),
        P("space", None),
        P("space", None, None),
        P("space", None),
    )
    return jax.shard_map(
        on_device,
        mesh=mesh,
        in_specs=placed,
        out_specs=P(("members", "space"), None),
        check_vma=False,
    )
```

```python
import functools
import math

import jax
import jax.numpy as jnp
import numpy as np
from jax import lax
from jax.experimental import pallas as pl
from jax.experimental.pallas import tpu as pltpu
from jax.sharding import PartitionSpec as P

DIRS = 36
FREQS = 36
COARSE = 4


gravity = 9.81
base_freq = 0.0418
freq_ratio = 1.1
freq_span = 35.0
input_coef = 0.0001
wind_gain = 1.12
dissip_coef = 0.0005
half_length = 300.0
courant_scale = 0.05


def from_root(array, axis, root):
    mine = lax.axis_index(axis) == root
    return lax.psum(jnp.where(mine, array, jnp.zeros_like(array)), axis)


def extended(array, sides, width):
    for axis, dim in sides:
        size, length = (lax.axis_size(axis), array.shape[dim])
        up = [(i, (i + 1) % size) for i in range(size - 1)]
        down = [(j, i) for i, j in up]
        last = lax.slice_in_dim(array, length - width, length, axis=dim)
        first = lax.slice_in_dim(array, 0, width, axis=dim)
        before = lax.ppermute(last, axis, up)
        after = lax.ppermute(first, axis, down)
        array = jnp.concatenate([before, array, after], axis=dim)
    return array


def spectral_tables():
    direction = 2.0 * math.pi / DIRS * jnp.arange(DIRS, dtype=jnp.float32)
    exponent = jnp.arange(FREQS, dtype=jnp.float32) * (freq_span / (FREQS - 1))
    frequency = base_freq * freq_ratio**exponent
    angular = 2.0 * math.pi * frequency
    phase_speed = gravity / angular
    return (jnp.cos(direction), jnp.sin(direction), angular, phase_speed, 0.5 * phase_speed)


def source_half(energy, wind_east, wind_north, coupling):
    cos_dir, sine_dir, angular, phase_speed, group_speed = spectral_tables()
    along_wind = wind_east[:, None] * cos_dir[None, :] + wind_north[:, None] * sine_dir[None, :]
    growth = (
        input_coef
        * angular[None, None, :]
        * jnp.maximum(wind_gain * along_wind[:, :, None] / phase_speed[None, None, :] - 1.0, 0.0)
    )
    growth = growth.reshape(energy.shape[0], -1)
    mean_square = jnp.mean(energy * energy, axis=1, keepdims=True)
    decay_rate = dissip_coef * jnp.tile(angular, DIRS)[None, :] * mean_square
    local_part = energy * (1.0 + half_length * growth) / (1.0 + half_length * decay_rate)
    return local_part + jnp.dot(
        local_part.astype(jnp.bfloat16), coupling, preferred_element_type=jnp.float32
    )


def advect(center, upwind_lo, upwind_hi, courant):
    ahead_part = jnp.maximum(courant, 0.0)
    behind = jnp.minimum(courant, 0.0)
    return center - ahead_part * (center - upwind_lo) - behind * (upwind_hi - center)


def sweep_cols(energy_grid, drift_east, wet_field):
    cos_dir, sine_dir, angular, phase_speed, group_speed = spectral_tables()
    wave_speed = (cos_dir[:, None] * group_speed[None, :]).reshape(-1)
    courant = (wave_speed[None, None, :] + drift_east[:, :, None]) * courant_scale
    zero_edge = jnp.zeros_like(energy_grid[:, :1])
    upwind_lo = jnp.concatenate([zero_edge, energy_grid[:, :-1]], axis=1)
    upwind_hi = jnp.concatenate([energy_grid[:, 1:], zero_edge], axis=1)
    return advect(energy_grid, upwind_lo, upwind_hi, courant) * wet_field[:, :, None]


def sweep_rows(energy_grid, row_above, row_below, drift_north, wet_field):
    cos_dir, sine_dir, angular, phase_speed, group_speed = spectral_tables()
    wave_speed = (sine_dir[:, None] * group_speed[None, :]).reshape(-1)
    courant = (wave_speed[None, None, :] + drift_north[:, :, None]) * courant_scale
    return advect(energy_grid, row_above, row_below, courant) * wet_field[:, :, None]


def forcing_points(row_start, row_count, col_count):
    rows_idx = row_start + jnp.arange(row_count, dtype=jnp.int32)
    cols_idx = jnp.arange(col_count, dtype=jnp.int32)
    return rows_idx[:, None] // COARSE * (col_count // COARSE) + cols_idx[None, :] // COARSE


def on_strips(
    spectra,
    wind_files,
    current_files,
    reader_turn,
    cell_point,
    coupling,
    send_list,
    send_count,
    recv_list,
    wet_mask,
):
    levels = []
    for time_level in range(2):
        levels.append(
            (
                from_root(wind_files[0], "space", reader_turn[time_level]),
                from_root(current_files[0], "space", reader_turn[time_level]),
            )
        )
    wind_mean = 0.5 * (levels[0][0] + levels[1][0])
    current_mean = 0.5 * (levels[0][1] + levels[1][1])
    cell_wind = jnp.take(wind_mean, cell_point, axis=1)
    first_half = source_half(spectra, cell_wind[0], cell_wind[1], coupling)
    send_rows = send_list[0]
    counts = send_count[0]
    places = recv_list[0]
    slot_count = send_rows.shape[1]
    spec_width = spectra.shape[1]
    live_slots = (jnp.arange(slot_count, dtype=jnp.int32)[None, :] < counts[:, None]).astype(
        jnp.float32
    )
    packed = first_half[send_rows] * live_slots[:, :, None]
    arrived = lax.all_to_all(packed, "space", split_axis=0, concat_axis=0, tiled=True)
    row_count = wet_mask.shape[0]
    col_count = wet_mask.shape[1]
    energy_grid = (
        jnp.zeros((row_count * col_count, spec_width), jnp.float32)
        .at[places.reshape(-1)]
        .add(arrived.reshape(-1, spec_width))
    )
    energy_grid = energy_grid.reshape(row_count, col_count, spec_width)
    points = forcing_points(lax.axis_index("space") * row_count, row_count, col_count)
    drift = jnp.take(current_mean, points, axis=1)
    wet_field = wet_mask.astype(jnp.float32)
    swept_cols = sweep_cols(energy_grid, drift[0], wet_field)
    padded = extended(swept_cols, (("space", 0),), 1)
    swept = sweep_rows(swept_cols, padded[:-2], padded[2:], drift[1], wet_field).reshape(
        -1, spec_width
    )
    outgoing = swept[places]
    flat_rows = send_rows.reshape(-1)
    empty_rows = jnp.zeros((spectra.shape[0], spec_width), jnp.float32)
    returned = lax.all_to_all(outgoing, "space", split_axis=0, concat_axis=0, tiled=True)
    back_rows = empty_rows.at[flat_rows].add(
        (returned * live_slots[:, :, None]).reshape(-1, spec_width)
    )
    result = source_half(back_rows, cell_wind[0], cell_wind[1], coupling)
    return result


LANES = 128
F32 = jnp.float32
BF16 = jnp.bfloat16
MIB = 1024 * 1024
GRID_VMEM = 56 * MIB
CHUNKS = 1


def wave_tables():
    direction = 2.0 * np.pi / DIRS * np.arange(DIRS)
    frequency = base_freq * freq_ratio ** (np.arange(FREQS) * (freq_span / (FREQS - 1)))
    angular = 2.0 * np.pi * frequency
    phase = gravity / angular
    group = 0.5 * phase
    cos_dir, sin_dir = np.cos(direction)[:, None], np.sin(direction)[:, None]
    flat = lambda t: np.broadcast_to(t, (DIRS, FREQS)).reshape(-1)
    source = np.zeros((DIRS * FREQS, 8), np.float32)
    source[:, 0] = flat(wind_gain * cos_dir / phase)
    source[:, 1] = flat(wind_gain * sin_dir / phase)
    source[:, 2] = flat(half_length * input_coef * angular)
    source[:, 3] = flat(half_length * dissip_coef * angular)
    east = flat(courant_scale * cos_dir * group).astype(np.float32)
    north = flat(courant_scale * sin_dir * group).astype(np.float32)
    return source, east, north


def pad_lanes(array, rows):
    flat = array.reshape(-1)
    return jnp.pad(flat, (0, rows * LANES - flat.shape[0])).reshape(rows, LANES)


def ceil_to(value, step):
    return -(-value // step) * step


def largest_step(size, step, most):
    return max(s for s in range(step, most + 1, step) if size % s == 0)


def cell_winds(wind_ref, cp_ref):
    wind = jnp.sum(wind_ref[...], axis=0)
    points, rows = wind.shape[1], cp_ref.shape[1]
    high = wind.astype(BF16).astype(F32)
    middle = (wind - high).astype(BF16).astype(F32)
    low = wind - high - middle
    parts = jnp.concatenate([high, middle, low, jnp.zeros((10, points), F32)], axis=0)
    point = lax.broadcasted_iota(jnp.int32, (points, rows), 0)
    hit = jnp.where(point == cp_ref[...], 1.0, 0.0).astype(BF16)
    picked = jnp.dot(parts.astype(BF16), hit, preferred_element_type=F32)
    both = picked[0:2] + picked[2:4] + picked[4:6]
    return both[0:1], both[1:2]


def half_step(load, spec, rows, wind_ref, cp_ref, table_ref, coup_ref, loc_ref, locb_ref, store):
    east, north = cell_winds(wind_ref, cp_ref)
    step = largest_step(spec, 16, 64)

    def squares(i, total):
        piece = load(pl.multiple_of(i * step, step), step)
        return total + jnp.sum((piece * piece).reshape(step // 8, 8, rows), axis=0)

    total = lax.fori_loop(0, spec // step, squares, jnp.zeros((8, rows), F32))
    mean_square = jnp.sum(total, axis=0, keepdims=True) * (1.0 / spec)

    @pl.loop(0, spec // step)
    def _(i):
        first = pl.multiple_of(i * step, step)
        at = pl.ds(first, step)
        table = table_ref[at, :]
        along = east * table[:, 0:1] + north * table[:, 1:2]
        gain = 1.0 + table[:, 2:3] * jnp.maximum(along - 1.0, 0.0)
        loss = 1.0 + table[:, 3:4] * mean_square
        local = load(first, step) * gain / loss
        loc_ref[at, :] = local
        locb_ref[at, :] = local.astype(BF16)

    tall = largest_step(spec, 16, 512)

    @pl.loop(0, spec // tall)
    def _(q):
        first = pl.multiple_of(q * tall, tall)
        at = pl.ds(first, tall)
        store(
            first,
            loc_ref[at, :]
            + jnp.dot(coup_ref[at, :], locb_ref[...], preferred_element_type=F32),
        )


def strided_load(ref, tiles):
    def load(first, count):
        start = pl.multiple_of(first * tiles, 8)
        return jnp.concatenate(
            [ref[pl.ds(start + j, count, stride=tiles), :] for j in range(tiles)], axis=1
        )

    return load


def strided_store(ref, tiles):
    def store(first, values):
        start = pl.multiple_of(first * tiles, 8)
        for j in range(tiles):
            ref[pl.ds(start + j, values.shape[0], stride=tiles), :] = values[
                :, j * LANES : (j + 1) * LANES
            ]

    return store


def first_kernel(energy_ref, cp_ref, wind_ref, table_ref, coup_ref, out_ref, loc_ref, locb_ref):
    spec, rows = energy_ref.shape
    half_step(
        lambda first, count: energy_ref[pl.ds(first, count), :],
        spec, rows, wind_ref, cp_ref, table_ref, coup_ref, loc_ref, locb_ref,
        strided_store(out_ref, rows // LANES),
    )


def last_kernel(came_ref, cp_ref, wind_ref, table_ref, coup_ref, out_ref, loc_ref, locb_ref):
    spec, rows = out_ref.shape

    def store(first, values):
        out_ref[pl.ds(first, values.shape[0]), :] = values

    half_step(
        strided_load(came_ref, rows // LANES),
        spec, rows, wind_ref, cp_ref, table_ref, coup_ref, loc_ref, locb_ref, store,
    )


def upwind(center, before, after, courant):
    return center + jnp.abs(courant) * (jnp.where(courant > 0.0, before, after) - center)


class Sweeps:
    def __init__(self, grid_rows, cols, depth, shares, rows, chunks):
        self.grid_rows, self.cols, self.depth, self.shares = grid_rows, cols, depth, shares
        self.rows = rows
        self.part = rows // chunks
        self.tiles = self.part // LANES
        self.pitch = cols + 8
        self.size = ceil_to((grid_rows + 2) * self.pitch + 8, LANES)

    def clear(self, grid_ref):
        @pl.loop(0, self.size // LANES)
        def _(i):
            at = pl.ds(pl.multiple_of(i * LANES, LANES), LANES)
            grid_ref[at, :] = jnp.zeros((LANES, LANES), F32)

    def turn_in(self, came_ref, cell_ref, piece_ref):
        depth, tiles = self.depth, self.tiles
        spare = lax.broadcasted_iota(jnp.int32, (LANES, LANES), 0) == depth
        piece_ref[...] = jnp.where(spare, 1.0, 0.0)

        @pl.loop(0, self.shares)
        def _(s):
            for j in range(tiles):
                start = s * (depth * tiles) + j
                piece_ref[0:depth, :] = came_ref[pl.ds(start, depth, stride=tiles), :]
                at = pl.ds(pl.multiple_of((s * tiles + j) * LANES, LANES), LANES)
                cell_ref[at, :] = piece_ref[...].T

    def turn_out(self, cell_ref, out_ref):
        depth, tiles = self.depth, self.tiles

        @pl.loop(0, self.shares)
        def _(s):
            for j in range(tiles):
                start = s * (depth * tiles) + j
                at = pl.ds(pl.multiple_of((s * tiles + j) * LANES, LANES), LANES)
                turned = cell_ref[at, :].T
                out_ref[pl.ds(start, depth, stride=tiles), :] = turned[0:depth, :]

    def each_row(self, chunk, place_ref, body, unroll=32):
        per = self.part // unroll

        @pl.loop(0, self.shares * per)
        def _(i):
            share, block = i // per, i % per
            first = share * self.rows + chunk * self.part + block * unroll
            for t in range(unroll):
                body(i * unroll + t, place_ref[first + t])

    def scatter(self, chunk, place_ref, cell_ref, grid_ref):
        def body(row, place):
            grid_ref[pl.ds(place, 1), :] = cell_ref[pl.ds(row, 1), :]

        self.each_row(chunk, place_ref, body)

    def gather(self, chunk, place_ref, cell_ref, grid_ref):
        def body(row, place):
            cell_ref[pl.ds(row, 1), :] = grid_ref[pl.ds(place, 1), :]

        self.each_row(chunk, place_ref, body)

    def sweep(self, drift_ref, speed_ref, one_ref, two_ref):
        grid_rows, cols, pitch, flag = self.grid_rows, self.cols, self.pitch, self.depth
        coarse_rows = grid_rows // COARSE
        for edge in (0, grid_rows + 1):
            two_ref[edge * pitch : (edge + 1) * pitch, :] = jnp.zeros((pitch, LANES), F32)
        lane = lax.broadcasted_iota(jnp.int32, (cols, drift_ref.shape[1]), 1)

        def courants(which, r4):
            hit = lane == which * coarse_rows + r4
            drift = jnp.sum(jnp.where(hit, drift_ref[...], 0.0), axis=1, keepdims=True)
            return speed_ref[which : which + 1, :] + drift

        @pl.loop(0, coarse_rows)
        def _(r4):
            courant = courants(0, r4)
            for dr in range(COARSE):
                base = pl.multiple_of((r4 * COARSE + dr + 1) * pitch + 8, 8)
                center = one_ref[pl.ds(base, cols), :]
                before = one_ref[pl.ds(base - 1, cols), :]
                after = one_ref[pl.ds(base + 1, cols), :]
                wet = jnp.broadcast_to(center[:, flag : flag + 1], center.shape)
                two_ref[pl.ds(base, cols), :] = upwind(center, before, after, courant) * wet

        @pl.loop(0, coarse_rows)
        def _(r4):
            courant = courants(1, r4)
            for dr in range(COARSE):
                base = pl.multiple_of((r4 * COARSE + dr + 1) * pitch + 8, 8)
                above = pl.multiple_of(base - pitch, 8)
                below = pl.multiple_of(base + pitch, 8)
                one_ref[pl.ds(base, cols), :] = upwind(
                    two_ref[pl.ds(base, cols), :],
                    two_ref[pl.ds(above, cols), :],
                    two_ref[pl.ds(below, cols), :],
                    courant,
                )


def sweep_kernel(
    sweeps, place_ref, came_ref, drift_ref, speed_ref, out_ref, cell_ref, one_ref, two_ref, piece_ref
):
    sweeps.clear(one_ref)
    sweeps.turn_in(came_ref, cell_ref, piece_ref)
    sweeps.scatter(0, place_ref, cell_ref, one_ref)
    sweeps.sweep(drift_ref, speed_ref, one_ref, two_ref)
    sweeps.gather(0, place_ref, cell_ref, one_ref)
    sweeps.turn_out(cell_ref, out_ref)


def in_vmem(count):
    return [pl.BlockSpec(memory_space=pltpu.VMEM)] * count


def on_spectrum(
    spectra,
    wind_files,
    current_files,
    reader_turn,
    cell_point,
    coupling,
    send_list,
    send_count,
    recv_list,
    wet_mask,
):
    shares = lax.axis_size("space")
    me = lax.axis_index("space")
    rows, spec = spectra.shape
    depth = spec // shares
    cap = send_list.shape[2]
    strip_rows, cols = wet_mask.shape
    grid_rows = strip_rows * shares
    points = wind_files.shape[2]
    sweeps = Sweeps(grid_rows, cols, depth, shares, rows, CHUNKS)
    part, tiles, pitch = sweeps.part, sweeps.tiles, sweeps.pitch
    source, east_speed, north_speed = wave_tables()
    table = jnp.asarray(source)

    mine = 0.5 * (
        (reader_turn[0] == me).astype(F32) + (reader_turn[1] == me).astype(F32)
    )
    wind = lax.all_to_all(
        jnp.broadcast_to(mine * wind_files, (shares, 2, points)), "space", 0, 0, tiled=True
    )

    force_rows = 2 * points // LANES
    list_rows = -(-shares * cap // LANES)
    pack = jnp.concatenate(
        [
            (mine * current_files[0]).reshape(force_rows, LANES),
            pad_lanes(send_list[0].astype(F32), list_rows),
            pad_lanes(recv_list[0].astype(F32), list_rows),
            pad_lanes(send_count[0].astype(F32), -(-shares // LANES)),
        ],
        axis=0,
    )
    pack = jnp.pad(pack, ((0, ceil_to(pack.shape[0], 8) - pack.shape[0]), (0, 0)))
    every = lax.all_gather(pack, "space")
    current = jnp.sum(every[:, :force_rows], axis=0).reshape(2, points)
    at = force_rows
    sends = every[:, at : at + list_rows].reshape(shares, -1)[:, : shares * cap]
    at += list_rows
    lands = every[:, at : at + list_rows].reshape(shares, -1)[:, : shares * cap]
    at += list_rows
    counts = every[:, at:].reshape(shares, -1)[:, :shares]
    sends = sends.reshape(shares, shares, cap)
    lands = lands.reshape(shares, shares, cap).transpose(1, 0, 2)
    strip = jnp.arange(shares, dtype=F32)[None, :, None] * (strip_rows * cols)
    cell = (lands + strip).astype(jnp.int32)
    position = (cell // cols + 1) * pitch + 8 + cell % cols
    live = jnp.arange(cap, dtype=F32)[None, None, :] < counts[:, :, None]
    position = jnp.where(live, position, 0).reshape(shares, 1, shares * cap)
    names = jnp.where(live, sends, -1.0).reshape(shares, 1, shares * cap)
    own = jnp.arange(rows, dtype=F32)[None, :, None]
    place = jnp.sum(jnp.where(names == own, position, 0), axis=2).reshape(-1)

    coarse_rows = grid_rows // COARSE
    drift = (courant_scale * current).reshape(2 * coarse_rows, cols // COARSE)
    drift = jnp.repeat(drift.T, COARSE, axis=0)
    speed = jnp.stack([jnp.asarray(east_speed), jnp.asarray(north_speed)])
    speed = jnp.pad(speed, ((0, 6), (0, LANES)))
    speed = lax.dynamic_slice(speed, (0, me * depth), (8, LANES))

    energy = spectra.T
    cp = cell_point.reshape(1, rows)
    coup = coupling.T
    h_params = pltpu.CompilerParams(vmem_limit_bytes=28 * MIB)
    h_cost = pl.CostEstimate(
        flops=2 * part * spec * spec, bytes_accessed=12 * part * spec, transcendentals=0
    )
    h_scratch = [pltpu.VMEM((spec, part), F32), pltpu.VMEM((spec, part), BF16)]
    turned = pl.pallas_call(
        first_kernel,
        out_shape=jax.ShapeDtypeStruct((spec * tiles, LANES), F32),
        in_specs=in_vmem(5),
        out_specs=pl.BlockSpec(memory_space=pltpu.VMEM),
        scratch_shapes=h_scratch,
        compiler_params=h_params,
        cost_estimate=h_cost,
        name="first_half",
    )(energy, cp, wind, table, coup)
    came = lax.all_to_all(
        turned.reshape(shares, depth, tiles, LANES), "space", 0, 0, tiled=True
    ).reshape(spec * tiles, LANES)
    swept = pl.pallas_call(
        functools.partial(sweep_kernel, sweeps),
        out_shape=jax.ShapeDtypeStruct((spec * tiles, LANES), F32),
        in_specs=[pl.BlockSpec(memory_space=pltpu.SMEM)] + in_vmem(3),
        out_specs=pl.BlockSpec(memory_space=pltpu.VMEM),
        scratch_shapes=[
            pltpu.VMEM((shares * part, LANES), F32),
            pltpu.VMEM((sweeps.size, LANES), F32),
            pltpu.VMEM((sweeps.size, LANES), F32),
            pltpu.VMEM((LANES, LANES), F32),
        ],
        compiler_params=pltpu.CompilerParams(vmem_limit_bytes=GRID_VMEM),
        cost_estimate=pl.CostEstimate(
            flops=20 * sweeps.size * LANES, bytes_accessed=8 * rows * spec, transcendentals=0
        ),
        name="sweeps",
    )(place, came, drift, speed)
    back = lax.all_to_all(
        swept.reshape(shares, depth, tiles, LANES), "space", 0, 0, tiled=True
    ).reshape(spec * tiles, LANES)
    result = pl.pallas_call(
        last_kernel,
        out_shape=jax.ShapeDtypeStruct((spec, rows), F32),
        in_specs=in_vmem(5),
        out_specs=pl.BlockSpec(memory_space=pltpu.VMEM),
        scratch_shapes=h_scratch,
        compiler_params=h_params,
        cost_estimate=h_cost,
        name="last_half",
    )(back, cp, wind, table, coup)
    return result.T


def fits(shares, rows, spec, strip_rows, cols):
    if spec % shares or spec // shares >= LANES or rows % (CHUNKS * LANES) or cols % LANES:
        return False
    cells = shares * strip_rows * cols
    held = LANES * 4 * (2 * (cells + cells // 8) + shares * rows)
    return held + 8 * rows * spec < GRID_VMEM


def on_device(*args):
    spectra, wet_mask = args[0], args[9]
    if fits(lax.axis_size("space"), *spectra.shape, *wet_mask.shape):
        return on_spectrum(*args)
    return on_strips(*args)


def solution(mesh):
    placed = (
        P(("members", "space"), None),
        P(("members", "space"), None, None),
        P(("members", "space"), None, None),
        P(),
        P("space"),
        P(),
        P("space", None, None),
        P("space", None),
        P("space", None, None),
        P("space", None),
    )
    return jax.shard_map(
        on_device,
        mesh=mesh,
        in_specs=placed,
        out_specs=P(("members", "space"), None),
        check_vma=False,
    )
```

```python
import functools
import math

import jax
import jax.numpy as jnp
import numpy as np
from jax import lax
from jax.experimental import pallas as pl
from jax.experimental.pallas import tpu as pltpu
from jax.sharding import PartitionSpec as P

DIRS = 36
FREQS = 36
COARSE = 4


gravity = 9.81
base_freq = 0.0418
freq_ratio = 1.1
freq_span = 35.0
input_coef = 0.0001
wind_gain = 1.12
dissip_coef = 0.0005
half_length = 300.0
courant_scale = 0.05


def from_root(array, axis, root):
    mine = lax.axis_index(axis) == root
    return lax.psum(jnp.where(mine, array, jnp.zeros_like(array)), axis)


def extended(array, sides, width):
    for axis, dim in sides:
        size, length = (lax.axis_size(axis), array.shape[dim])
        up = [(i, (i + 1) % size) for i in range(size - 1)]
        down = [(j, i) for i, j in up]
        last = lax.slice_in_dim(array, length - width, length, axis=dim)
        first = lax.slice_in_dim(array, 0, width, axis=dim)
        before = lax.ppermute(last, axis, up)
        after = lax.ppermute(first, axis, down)
        array = jnp.concatenate([before, array, after], axis=dim)
    return array


def spectral_tables():
    direction = 2.0 * math.pi / DIRS * jnp.arange(DIRS, dtype=jnp.float32)
    exponent = jnp.arange(FREQS, dtype=jnp.float32) * (freq_span / (FREQS - 1))
    frequency = base_freq * freq_ratio**exponent
    angular = 2.0 * math.pi * frequency
    phase_speed = gravity / angular
    return (jnp.cos(direction), jnp.sin(direction), angular, phase_speed, 0.5 * phase_speed)


def source_half(energy, wind_east, wind_north, coupling):
    cos_dir, sine_dir, angular, phase_speed, group_speed = spectral_tables()
    along_wind = wind_east[:, None] * cos_dir[None, :] + wind_north[:, None] * sine_dir[None, :]
    growth = (
        input_coef
        * angular[None, None, :]
        * jnp.maximum(wind_gain * along_wind[:, :, None] / phase_speed[None, None, :] - 1.0, 0.0)
    )
    growth = growth.reshape(energy.shape[0], -1)
    mean_square = jnp.mean(energy * energy, axis=1, keepdims=True)
    decay_rate = dissip_coef * jnp.tile(angular, DIRS)[None, :] * mean_square
    local_part = energy * (1.0 + half_length * growth) / (1.0 + half_length * decay_rate)
    return local_part + jnp.dot(
        local_part.astype(jnp.bfloat16), coupling, preferred_element_type=jnp.float32
    )


def advect(center, upwind_lo, upwind_hi, courant):
    ahead_part = jnp.maximum(courant, 0.0)
    behind = jnp.minimum(courant, 0.0)
    return center - ahead_part * (center - upwind_lo) - behind * (upwind_hi - center)


def sweep_cols(energy_grid, drift_east, wet_field):
    cos_dir, sine_dir, angular, phase_speed, group_speed = spectral_tables()
    wave_speed = (cos_dir[:, None] * group_speed[None, :]).reshape(-1)
    courant = (wave_speed[None, None, :] + drift_east[:, :, None]) * courant_scale
    zero_edge = jnp.zeros_like(energy_grid[:, :1])
    upwind_lo = jnp.concatenate([zero_edge, energy_grid[:, :-1]], axis=1)
    upwind_hi = jnp.concatenate([energy_grid[:, 1:], zero_edge], axis=1)
    return advect(energy_grid, upwind_lo, upwind_hi, courant) * wet_field[:, :, None]


def sweep_rows(energy_grid, row_above, row_below, drift_north, wet_field):
    cos_dir, sine_dir, angular, phase_speed, group_speed = spectral_tables()
    wave_speed = (sine_dir[:, None] * group_speed[None, :]).reshape(-1)
    courant = (wave_speed[None, None, :] + drift_north[:, :, None]) * courant_scale
    return advect(energy_grid, row_above, row_below, courant) * wet_field[:, :, None]


def forcing_points(row_start, row_count, col_count):
    rows_idx = row_start + jnp.arange(row_count, dtype=jnp.int32)
    cols_idx = jnp.arange(col_count, dtype=jnp.int32)
    return rows_idx[:, None] // COARSE * (col_count // COARSE) + cols_idx[None, :] // COARSE


def on_strips(
    spectra,
    wind_files,
    current_files,
    reader_turn,
    cell_point,
    coupling,
    send_list,
    send_count,
    recv_list,
    wet_mask,
):
    levels = []
    for time_level in range(2):
        levels.append(
            (
                from_root(wind_files[0], "space", reader_turn[time_level]),
                from_root(current_files[0], "space", reader_turn[time_level]),
            )
        )
    wind_mean = 0.5 * (levels[0][0] + levels[1][0])
    current_mean = 0.5 * (levels[0][1] + levels[1][1])
    cell_wind = jnp.take(wind_mean, cell_point, axis=1)
    first_half = source_half(spectra, cell_wind[0], cell_wind[1], coupling)
    send_rows = send_list[0]
    counts = send_count[0]
    places = recv_list[0]
    slot_count = send_rows.shape[1]
    spec_width = spectra.shape[1]
    live_slots = (jnp.arange(slot_count, dtype=jnp.int32)[None, :] < counts[:, None]).astype(
        jnp.float32
    )
    packed = first_half[send_rows] * live_slots[:, :, None]
    arrived = lax.all_to_all(packed, "space", split_axis=0, concat_axis=0, tiled=True)
    row_count = wet_mask.shape[0]
    col_count = wet_mask.shape[1]
    energy_grid = (
        jnp.zeros((row_count * col_count, spec_width), jnp.float32)
        .at[places.reshape(-1)]
        .add(arrived.reshape(-1, spec_width))
    )
    energy_grid = energy_grid.reshape(row_count, col_count, spec_width)
    points = forcing_points(lax.axis_index("space") * row_count, row_count, col_count)
    drift = jnp.take(current_mean, points, axis=1)
    wet_field = wet_mask.astype(jnp.float32)
    swept_cols = sweep_cols(energy_grid, drift[0], wet_field)
    padded = extended(swept_cols, (("space", 0),), 1)
    swept = sweep_rows(swept_cols, padded[:-2], padded[2:], drift[1], wet_field).reshape(
        -1, spec_width
    )
    outgoing = swept[places]
    flat_rows = send_rows.reshape(-1)
    empty_rows = jnp.zeros((spectra.shape[0], spec_width), jnp.float32)
    returned = lax.all_to_all(outgoing, "space", split_axis=0, concat_axis=0, tiled=True)
    back_rows = empty_rows.at[flat_rows].add(
        (returned * live_slots[:, :, None]).reshape(-1, spec_width)
    )
    result = source_half(back_rows, cell_wind[0], cell_wind[1], coupling)
    return result


LANES = 128
F32 = jnp.float32
BF16 = jnp.bfloat16
MIB = 1024 * 1024
GRID_VMEM = 44 * MIB
CHUNKS = 2


def wave_tables():
    direction = 2.0 * np.pi / DIRS * np.arange(DIRS)
    frequency = base_freq * freq_ratio ** (np.arange(FREQS) * (freq_span / (FREQS - 1)))
    angular = 2.0 * np.pi * frequency
    phase = gravity / angular
    group = 0.5 * phase
    cos_dir, sin_dir = np.cos(direction)[:, None], np.sin(direction)[:, None]
    flat = lambda t: np.broadcast_to(t, (DIRS, FREQS)).reshape(-1)
    source = np.zeros((DIRS * FREQS, 8), np.float32)
    source[:, 0] = flat(wind_gain * cos_dir / phase)
    source[:, 1] = flat(wind_gain * sin_dir / phase)
    source[:, 2] = flat(half_length * input_coef * angular)
    source[:, 3] = flat(half_length * dissip_coef * angular)
    east = flat(courant_scale * cos_dir * group).astype(np.float32)
    north = flat(courant_scale * sin_dir * group).astype(np.float32)
    return source, east, north


def ceil_to(value, step):
    return -(-value // step) * step


def largest_step(size, step, most):
    return max(s for s in range(step, most + 1, step) if size % s == 0)


class Plan:
    def __init__(self, shares, rows, spec, cap, strip_rows, cols, points):
        self.shares, self.rows, self.spec, self.cap = shares, rows, spec, cap
        self.cols, self.points = cols, points
        self.depth = spec // shares
        self.part = rows // CHUNKS
        self.tiles = self.part // LANES
        self.data = self.depth * self.tiles
        self.force = 2 * points // (LANES * shares)
        self.block = ceil_to(self.data + self.tiles + self.force, 8)
        self.strip = strip_rows * cols
        self.grid_rows = strip_rows * shares
        self.coarse_rows = self.grid_rows // COARSE
        self.pitch = cols + 8
        self.size = ceil_to((self.grid_rows + 2) * self.pitch + 8, LANES)

    def fits(self):
        if self.spec % self.shares or self.depth >= LANES or self.rows % (CHUNKS * LANES):
            return False
        if 2 * self.points % (LANES * self.shares) or self.cap > LANES or self.cols != LANES:
            return False
        if 2 * self.points // LANES > LANES:
            return False
        cells = 2 * self.size + 2 * self.coarse_rows * self.cols + self.shares * self.part
        held = LANES * 4 * (cells + self.shares * (self.block + self.data))
        return held + 4 * MIB < GRID_VMEM


def pack_kernel(plan, turn_ref, wind_ref, current_ref, recv_ref, out_ref):
    me = lax.axis_index("space")
    half = lambda at: jnp.where(turn_ref[at] == me, 0.5, 0.0)
    mine = half(0) + half(1)
    wind = mine * wind_ref[0]
    points, width, cap = plan.points, plan.force * LANES, plan.cap
    for s in range(plan.shares):
        out_ref[s, :, 0:points] = wind
        out_ref[s, :, points:] = jnp.zeros((2, out_ref.shape[2] - points), F32)
        out_ref[s, 0:1, points : points + cap] = recv_ref[0, s : s + 1, :].astype(F32)
        which, first = divmod(s * width, points)
        out_ref[s, 1:2, points : points + width] = (
            mine * current_ref[0, which : which + 1, first : first + width]
        )


def cell_winds(wind, cp):
    points, rows = wind.shape[1], cp.shape[1]
    high = wind.astype(BF16).astype(F32)
    middle = (wind - high).astype(BF16).astype(F32)
    low = wind - high - middle
    parts = jnp.concatenate([high, middle, low, jnp.zeros((10, points), F32)], axis=0)
    point = lax.broadcasted_iota(jnp.int32, (points, rows), 0)
    hit = jnp.where(point == cp, 1.0, 0.0).astype(BF16)
    picked = jnp.dot(parts.astype(BF16), hit, preferred_element_type=F32)
    both = picked[0:2] + picked[2:4] + picked[4:6]
    return both[0:1], both[1:2]


def half_step(plan, load, wind, cp, table_ref, coup_ref, loc_ref, locb_ref, store):
    spec, rows = plan.spec, plan.part
    east, north = cell_winds(wind, cp)
    step = largest_step(spec, 16, 64)

    def squares(i, total):
        piece = load(pl.multiple_of(i * step, step), step)
        return total + jnp.sum((piece * piece).reshape(step // 8, 8, rows), axis=0)

    total = lax.fori_loop(0, spec // step, squares, jnp.zeros((8, rows), F32))
    mean_square = jnp.sum(total, axis=0, keepdims=True) * (1.0 / spec)

    @pl.loop(0, spec // step)
    def _(i):
        first = pl.multiple_of(i * step, step)
        at = pl.ds(first, step)
        table = table_ref[at, :]
        along = east * table[:, 0:1] + north * table[:, 1:2]
        gain = 1.0 + table[:, 2:3] * jnp.maximum(along - 1.0, 0.0)
        loss = 1.0 + table[:, 3:4] * mean_square
        local = load(first, step) * gain / loss
        loc_ref[at, :] = local
        locb_ref[at, :] = local.astype(BF16)

    tall = largest_step(spec, 16, 512)
    for q in range(spec // tall):
        at = slice(q * tall, (q + 1) * tall)
        store(
            q * tall,
            loc_ref[at, :]
            + jnp.dot(coup_ref[at, :], locb_ref[...], preferred_element_type=F32),
        )


def first_kernel(
    plan, chunk,
    energy_ref, cp_ref, parcel_ref, names_ref, table_ref, coup_ref, out_ref, buf_ref, loc_ref, locb_ref,
):
    part, tiles, shares, points = plan.part, plan.tiles, plan.shares, plan.points
    lanes = slice(chunk * part, (chunk + 1) * part)

    def store(first, values):
        for j in range(tiles):
            buf_ref[pl.ds(first * tiles + j, values.shape[0], stride=tiles), :] = values[
                :, j * LANES : (j + 1) * LANES
            ]

    wind = jnp.sum(parcel_ref[:, :, 0:points], axis=0)
    half_step(
        plan, lambda first, count: energy_ref[pl.ds(first, count), lanes],
        wind, cp_ref[:, lanes], table_ref, coup_ref, loc_ref, locb_ref, store,
    )

    landing = jnp.concatenate(
        [parcel_ref[b, 0:1, points : points + LANES] for b in range(shares)], axis=0
    ).astype(jnp.int32)
    cell = landing + plan.strip * lax.broadcasted_iota(jnp.int32, (shares, LANES), 0)
    place = (cell + lax.div(cell, plan.cols) * (plan.pitch - plan.cols) + plan.pitch + 8).astype(F32)
    own = lax.broadcasted_iota(jnp.int32, (part, LANES), 0) + chunk * part
    found = jnp.zeros((part, LANES), F32)
    for b in range(shares):
        found += jnp.where(names_ref[b : b + 1, :] == own, place[b : b + 1, :], 0.0)
    found = jnp.broadcast_to(jnp.sum(found, axis=1, keepdims=True), (part, LANES))
    spare = [found[j * LANES : (j + 1) * LANES, :].T[0:1, :] for j in range(tiles)]
    if chunk == 0:
        width = plan.force * LANES
        current = jnp.sum(parcel_ref[:, :, points : points + width], axis=0)
        spare += [current[1:2, f * LANES : (f + 1) * LANES] for f in range(plan.force)]
    spare.append(jnp.zeros((plan.block - plan.data - len(spare), LANES), F32))
    spare = jnp.concatenate(spare, axis=0)
    for d in range(shares):
        out_ref[d * plan.block : (d + 1) * plan.block, :] = buf_ref[
            d * plan.data : d * plan.data + plan.block, :
        ]
        out_ref[d * plan.block + plan.data : (d + 1) * plan.block, :] = spare


def last_kernel(
    plan, chunk,
    came_ref, cp_ref, parcel_ref, table_ref, coup_ref, held_ref, out_ref, res_ref, loc_ref, locb_ref, sems,
):
    part, tiles = plan.part, plan.tiles
    lanes = slice(chunk * part, (chunk + 1) * part)
    copies = []

    def load(first, count):
        start = pl.multiple_of(first * tiles, 8)
        return jnp.concatenate(
            [came_ref[pl.ds(start + j, count, stride=tiles), :] for j in range(tiles)], axis=1
        )

    def store(first, values):
        at = slice(first, first + values.shape[0])
        res_ref[at, :] = values
        copies.append(
            pltpu.make_async_copy(res_ref.at[at, :], out_ref.at[at, lanes], sems.at[len(copies)])
        )
        copies[-1].start()

    wind = jnp.sum(parcel_ref[:, :, 0 : plan.points], axis=0)
    half_step(plan, load, wind, cp_ref[:, lanes], table_ref, coup_ref, loc_ref, locb_ref, store)
    for copy in copies:
        copy.wait()


def upwind(center, before, after, courant):
    return center + jnp.abs(courant) * (jnp.where(courant > 0.0, before, after) - center)


def clear(plan, grid_ref):
    @pl.loop(0, plan.size // LANES)
    def _(i):
        at = pl.ds(pl.multiple_of(i * LANES, LANES), LANES)
        grid_ref[at, :] = jnp.zeros((LANES, LANES), F32)


def turn_in(plan, came_ref, cell_ref, piece_ref):
    depth, tiles = plan.depth, plan.tiles
    flag = lax.broadcasted_iota(jnp.int32, (LANES, LANES), 0) == depth
    piece_ref[...] = jnp.where(flag, 1.0, 0.0)

    @pl.loop(0, plan.shares)
    def _(s):
        for j in range(tiles):
            piece_ref[0:depth, :] = came_ref[pl.ds(s * plan.block + j, depth, stride=tiles), :]
            at = pl.ds(pl.multiple_of((s * tiles + j) * LANES, LANES), LANES)
            cell_ref[at, :] = piece_ref[...].T


def turn_out(plan, cell_ref, out_ref):
    depth, tiles = plan.depth, plan.tiles

    @pl.loop(0, plan.shares)
    def _(s):
        for j in range(tiles):
            at = pl.ds(pl.multiple_of((s * tiles + j) * LANES, LANES), LANES)
            turned = cell_ref[at, :].T
            out_ref[pl.ds(s * plan.data + j, depth, stride=tiles), :] = turned[0:depth, :]


def places(plan, came_ref, spot_ref):
    for s in range(plan.shares):
        first = s * plan.block + plan.data
        spot_ref[s * plan.tiles : (s + 1) * plan.tiles, :] = came_ref[
            first : first + plan.tiles, :
        ].astype(jnp.int32)


def each_row(plan, spot_ref, body, unroll=32):
    per = LANES // unroll

    @pl.loop(0, plan.shares * plan.tiles * per)
    def _(i):
        block, first = i // per, (i % per) * unroll
        for t in range(unroll):
            body(i * unroll + t, spot_ref[block, first + t])


def scatter(plan, spot_ref, cell_ref, grid_ref):
    def body(row, place):
        grid_ref[pl.ds(place, 1), :] = cell_ref[pl.ds(row, 1), :]

    each_row(plan, spot_ref, body)


def gather(plan, spot_ref, cell_ref, grid_ref):
    def body(row, place):
        cell_ref[pl.ds(row, 1), :] = grid_ref[pl.ds(place, 1), :]

    each_row(plan, spot_ref, body)


def spread_drift(plan, came_ref, piece_ref, drift_ref):
    piece_ref[...] = jnp.zeros((LANES, LANES), F32)
    for s in range(plan.shares):
        first = s * plan.block + plan.data + plan.tiles
        piece_ref[s * plan.force : (s + 1) * plan.force, :] = came_ref[
            first : first + plan.force, :
        ]
    turned = (courant_scale * piece_ref[...]).T
    for q in range(plan.shares * plan.force):
        wide = jnp.broadcast_to(turned[:, q : q + 1], (LANES, LANES))
        for t in range(COARSE):
            drift_ref[pl.ds(q * LANES * COARSE + t, LANES, stride=COARSE), :] = wide


def sweep_columns(plan, drift_ref, speed_ref, one_ref, two_ref):
    cols, pitch, flag = plan.cols, plan.pitch, plan.depth

    @pl.loop(0, plan.coarse_rows)
    def _(r4):
        courant = speed_ref[0:1, :] + drift_ref[pl.ds(pl.multiple_of(r4 * cols, cols), cols), :]
        for dr in range(COARSE):
            base = pl.multiple_of((r4 * COARSE + dr + 1) * pitch + 8, 8)
            center = one_ref[pl.ds(base, cols), :]
            before = one_ref[pl.ds(base - 1, cols), :]
            after = one_ref[pl.ds(base + 1, cols), :]
            wet = jnp.broadcast_to(center[:, flag : flag + 1], center.shape)
            two_ref[pl.ds(base, cols), :] = upwind(center, before, after, courant) * wet


def sweep_rows_in_vmem(plan, drift_ref, speed_ref, one_ref, two_ref):
    cols, pitch = plan.cols, plan.pitch

    @pl.loop(0, plan.coarse_rows)
    def _(r4):
        point = pl.multiple_of((plan.coarse_rows + r4) * cols, cols)
        courant = speed_ref[1:2, :] + drift_ref[pl.ds(point, cols), :]
        for dr in range(COARSE):
            base = pl.multiple_of((r4 * COARSE + dr + 1) * pitch + 8, 8)
            above = pl.multiple_of(base - pitch, 8)
            below = pl.multiple_of(base + pitch, 8)
            one_ref[pl.ds(base, cols), :] = upwind(
                two_ref[pl.ds(base, cols), :],
                two_ref[pl.ds(above, cols), :],
                two_ref[pl.ds(below, cols), :],
                courant,
            )


def land_kernel(plan, came_ref, grid_ref, drift_ref, spot_ref, cell_ref, piece_ref, smem_ref, sem):
    places(plan, came_ref, spot_ref)
    copy = pltpu.make_async_copy(spot_ref, smem_ref, sem)
    copy.start()
    clear(plan, grid_ref)
    spread_drift(plan, came_ref, piece_ref, drift_ref)
    turn_in(plan, came_ref, cell_ref, piece_ref)
    copy.wait()
    scatter(plan, smem_ref, cell_ref, grid_ref)


def sweep_kernel(
    plan,
    came_ref, spot0_ref, speed_ref, grid_ref, drift_ref,
    out_ref, swept_ref, spot_ref,
    cell_ref, one_ref, two_ref, wide_ref, piece_ref, smem_ref, sems,
):
    get_grid = pltpu.make_async_copy(grid_ref, one_ref, sems.at[0])
    get_drift = pltpu.make_async_copy(drift_ref, wide_ref, sems.at[1])
    get_grid.start()
    get_drift.start()
    places(plan, came_ref, spot_ref)
    get_spot = pltpu.make_async_copy(spot_ref, smem_ref, sems.at[2])
    get_spot.start()
    for edge in (0, plan.grid_rows + 1):
        two_ref[edge * plan.pitch : (edge + 1) * plan.pitch, :] = jnp.zeros((plan.pitch, LANES), F32)
    turn_in(plan, came_ref, cell_ref, piece_ref)
    get_spot.wait()
    get_grid.wait()
    scatter(plan, smem_ref, cell_ref, one_ref)
    get_drift.wait()
    sweep_columns(plan, wide_ref, speed_ref, one_ref, two_ref)
    sweep_rows_in_vmem(plan, wide_ref, speed_ref, one_ref, two_ref)
    put_grid = pltpu.make_async_copy(one_ref, swept_ref, sems.at[0])
    put_grid.start()
    gather(plan, spot0_ref, cell_ref, one_ref)
    turn_out(plan, cell_ref, out_ref)
    put_grid.wait()


def take_kernel(plan, spot_ref, grid_ref, out_ref, cell_ref):
    gather(plan, spot_ref, cell_ref, grid_ref)
    turn_out(plan, cell_ref, out_ref)


VMEM = pl.BlockSpec(memory_space=pltpu.VMEM)
SMEM = pl.BlockSpec(memory_space=pltpu.SMEM)
ANY = pl.BlockSpec(memory_space=pl.ANY)


def on_spectrum(
    plan,
    spectra,
    wind_files,
    current_files,
    reader_turn,
    cell_point,
    coupling,
    send_list,
    send_count,
    recv_list,
):
    me = lax.axis_index("space")
    shares, rows, spec, points = plan.shares, plan.rows, plan.spec, plan.points
    part, tiles, size = plan.part, plan.tiles, plan.size
    source, east_speed, north_speed = wave_tables()
    table = jnp.asarray(source)
    block_rows, data_rows = shares * plan.block, shares * plan.data
    drift_rows = 2 * plan.coarse_rows * plan.cols

    def kernel(body, *, vmem, flops, traffic, **options):
        return pl.pallas_call(
            body,
            compiler_params=pltpu.CompilerParams(vmem_limit_bytes=vmem),
            cost_estimate=pl.CostEstimate(flops=flops, bytes_accessed=traffic, transcendentals=0),
            **options,
        )

    width = points + max(LANES, plan.force * LANES)
    parcel = kernel(
        functools.partial(pack_kernel, plan),
        vmem=8 * MIB, flops=0, traffic=4 * shares * 2 * width,
        out_shape=jax.ShapeDtypeStruct((shares, 2, width), F32),
        in_specs=[SMEM, VMEM, VMEM, VMEM],
        out_specs=VMEM,
        name="pack",
    )(reader_turn, wind_files, current_files, recv_list)
    parcel = lax.all_to_all(parcel, "space", 0, 0, tiled=True)

    slot = jnp.arange(plan.cap, dtype=jnp.int32)[None, :]
    names = jnp.where(slot < send_count[0][:, None], send_list[0], -1)
    names = jnp.pad(names, ((0, 0), (0, LANES - plan.cap)), constant_values=-1)
    speed = jnp.stack([jnp.asarray(east_speed), jnp.asarray(north_speed)])
    speed = jnp.pad(speed, ((0, 6), (0, LANES)))
    speed = lax.dynamic_slice(speed, (0, me * plan.depth), (8, LANES))

    energy = spectra.T
    cp = cell_point.reshape(1, rows)
    coup = coupling.T
    h_flops, h_traffic = 2 * part * spec * spec, 8 * part * spec
    h_scratch = [pltpu.VMEM((spec, part), F32), pltpu.VMEM((spec, part), BF16)]

    def first(chunk):
        block = kernel(
            functools.partial(first_kernel, plan, chunk),
            vmem=28 * MIB, flops=h_flops, traffic=h_traffic,
            out_shape=jax.ShapeDtypeStruct((block_rows, LANES), F32),
            in_specs=[VMEM] * 6,
            out_specs=VMEM,
            scratch_shapes=[pltpu.VMEM((data_rows + plan.block, LANES), F32)] + h_scratch,
            name=f"first_half_{chunk}",
        )(energy, cp, parcel, names, table, coup)
        block = block.reshape(shares, plan.block, LANES)
        return lax.all_to_all(block, "space", 0, 0, tiled=True).reshape(block_rows, LANES)

    def home(block):
        block = block.reshape(shares, plan.depth, tiles, LANES)
        return lax.all_to_all(block, "space", 0, 0, tiled=True).reshape(data_rows, LANES)

    cells = pltpu.VMEM((shares * part, LANES), F32)
    piece = pltpu.VMEM((LANES, LANES), F32)
    grid_shape = jax.ShapeDtypeStruct((size, LANES), F32)
    spot_shape = jax.ShapeDtypeStruct((shares * tiles, LANES), jnp.int32)
    smem = pltpu.SMEM((shares * tiles, LANES), jnp.int32)
    block_shape = jax.ShapeDtypeStruct((data_rows, LANES), F32)

    came = [first(chunk) for chunk in range(CHUNKS)]
    grid, drift, spot0 = kernel(
        functools.partial(land_kernel, plan),
        vmem=GRID_VMEM, flops=0, traffic=8 * size * LANES,
        out_shape=[grid_shape, jax.ShapeDtypeStruct((drift_rows, LANES), F32), spot_shape],
        in_specs=[VMEM],
        out_specs=[VMEM, VMEM, VMEM],
        scratch_shapes=[cells, piece, smem, pltpu.SemaphoreType.DMA],
        name="land",
    )(came[0])
    out0, swept, spot1 = kernel(
        functools.partial(sweep_kernel, plan),
        vmem=GRID_VMEM, flops=20 * size * LANES, traffic=16 * size * LANES,
        out_shape=[block_shape, grid_shape, spot_shape],
        in_specs=[VMEM, SMEM, VMEM, ANY, ANY],
        out_specs=[VMEM, ANY, VMEM],
        scratch_shapes=[
            cells,
            pltpu.VMEM((size, LANES), F32),
            pltpu.VMEM((size, LANES), F32),
            pltpu.VMEM((drift_rows, LANES), F32),
            piece,
            smem,
            pltpu.SemaphoreType.DMA((3,)),
        ],
        name="sweeps",
    )(came[1], spot0, speed, grid, drift)
    back0 = home(out0)
    out1 = kernel(
        functools.partial(take_kernel, plan),
        vmem=GRID_VMEM, flops=0, traffic=8 * size * LANES,
        out_shape=block_shape,
        in_specs=[SMEM, VMEM],
        out_specs=VMEM,
        scratch_shapes=[cells],
        name="take",
    )(spot1, swept)
    back1 = home(out1)

    result = jnp.zeros((8, LANES), F32)
    for chunk, back in enumerate((back0, back1)):
        result = kernel(
            functools.partial(last_kernel, plan, chunk),
            vmem=28 * MIB, flops=h_flops, traffic=h_traffic,
            out_shape=jax.ShapeDtypeStruct((spec, rows), F32),
            in_specs=[VMEM] * 5 + [ANY],
            out_specs=ANY,
            scratch_shapes=[pltpu.VMEM((spec, part), F32)] + h_scratch + [pltpu.SemaphoreType.DMA((8,))],
            input_output_aliases={5: 0} if chunk else {},
            name=f"last_half_{chunk}",
        )(back, cp, parcel, table, coup, result)
    return result.T


def on_device(*args):
    spectra, wind_files, send_list, wet_mask = args[0], args[1], args[6], args[9]
    plan = Plan(
        lax.axis_size("space"), *spectra.shape, send_list.shape[2], *wet_mask.shape, wind_files.shape[2]
    )
    if plan.fits():
        return on_spectrum(plan, *args[:9])
    return on_strips(*args)


def solution(mesh):
    placed = (
        P(("members", "space"), None),
        P(("members", "space"), None, None),
        P(("members", "space"), None, None),
        P(),
        P("space"),
        P(),
        P("space", None, None),
        P("space", None),
        P("space", None, None),
        P("space", None),
    )
    return jax.shard_map(
        on_device,
        mesh=mesh,
        in_specs=placed,
        out_specs=P(("members", "space"), None),
        check_vma=False,
    )
```

```python
import functools
import math

import jax
import jax.numpy as jnp
import numpy as np
from jax import lax
from jax.experimental import pallas as pl
from jax.experimental.pallas import tpu as pltpu
from jax.sharding import PartitionSpec as P

DIRS = 36
FREQS = 36
COARSE = 4


gravity = 9.81
base_freq = 0.0418
freq_ratio = 1.1
freq_span = 35.0
input_coef = 0.0001
wind_gain = 1.12
dissip_coef = 0.0005
half_length = 300.0
courant_scale = 0.05


def from_root(array, axis, root):
    mine = lax.axis_index(axis) == root
    return lax.psum(jnp.where(mine, array, jnp.zeros_like(array)), axis)


def extended(array, sides, width):
    for axis, dim in sides:
        size, length = (lax.axis_size(axis), array.shape[dim])
        up = [(i, (i + 1) % size) for i in range(size - 1)]
        down = [(j, i) for i, j in up]
        last = lax.slice_in_dim(array, length - width, length, axis=dim)
        first = lax.slice_in_dim(array, 0, width, axis=dim)
        before = lax.ppermute(last, axis, up)
        after = lax.ppermute(first, axis, down)
        array = jnp.concatenate([before, array, after], axis=dim)
    return array


def spectral_tables():
    direction = 2.0 * math.pi / DIRS * jnp.arange(DIRS, dtype=jnp.float32)
    exponent = jnp.arange(FREQS, dtype=jnp.float32) * (freq_span / (FREQS - 1))
    frequency = base_freq * freq_ratio**exponent
    angular = 2.0 * math.pi * frequency
    phase_speed = gravity / angular
    return (jnp.cos(direction), jnp.sin(direction), angular, phase_speed, 0.5 * phase_speed)


def source_half(energy, wind_east, wind_north, coupling):
    cos_dir, sine_dir, angular, phase_speed, group_speed = spectral_tables()
    along_wind = wind_east[:, None] * cos_dir[None, :] + wind_north[:, None] * sine_dir[None, :]
    growth = (
        input_coef
        * angular[None, None, :]
        * jnp.maximum(wind_gain * along_wind[:, :, None] / phase_speed[None, None, :] - 1.0, 0.0)
    )
    growth = growth.reshape(energy.shape[0], -1)
    mean_square = jnp.mean(energy * energy, axis=1, keepdims=True)
    decay_rate = dissip_coef * jnp.tile(angular, DIRS)[None, :] * mean_square
    local_part = energy * (1.0 + half_length * growth) / (1.0 + half_length * decay_rate)
    return local_part + jnp.dot(
        local_part.astype(jnp.bfloat16), coupling, preferred_element_type=jnp.float32
    )


def advect(center, upwind_lo, upwind_hi, courant):
    ahead_part = jnp.maximum(courant, 0.0)
    behind = jnp.minimum(courant, 0.0)
    return center - ahead_part * (center - upwind_lo) - behind * (upwind_hi - center)


def sweep_cols(energy_grid, drift_east, wet_field):
    cos_dir, sine_dir, angular, phase_speed, group_speed = spectral_tables()
    wave_speed = (cos_dir[:, None] * group_speed[None, :]).reshape(-1)
    courant = (wave_speed[None, None, :] + drift_east[:, :, None]) * courant_scale
    zero_edge = jnp.zeros_like(energy_grid[:, :1])
    upwind_lo = jnp.concatenate([zero_edge, energy_grid[:, :-1]], axis=1)
    upwind_hi = jnp.concatenate([energy_grid[:, 1:], zero_edge], axis=1)
    return advect(energy_grid, upwind_lo, upwind_hi, courant) * wet_field[:, :, None]


def sweep_rows(energy_grid, row_above, row_below, drift_north, wet_field):
    cos_dir, sine_dir, angular, phase_speed, group_speed = spectral_tables()
    wave_speed = (sine_dir[:, None] * group_speed[None, :]).reshape(-1)
    courant = (wave_speed[None, None, :] + drift_north[:, :, None]) * courant_scale
    return advect(energy_grid, row_above, row_below, courant) * wet_field[:, :, None]


def forcing_points(row_start, row_count, col_count):
    rows_idx = row_start + jnp.arange(row_count, dtype=jnp.int32)
    cols_idx = jnp.arange(col_count, dtype=jnp.int32)
    return rows_idx[:, None] // COARSE * (col_count // COARSE) + cols_idx[None, :] // COARSE


def on_strips(
    spectra,
    wind_files,
    current_files,
    reader_turn,
    cell_point,
    coupling,
    send_list,
    send_count,
    recv_list,
    wet_mask,
):
    levels = []
    for time_level in range(2):
        levels.append(
            (
                from_root(wind_files[0], "space", reader_turn[time_level]),
                from_root(current_files[0], "space", reader_turn[time_level]),
            )
        )
    wind_mean = 0.5 * (levels[0][0] + levels[1][0])
    current_mean = 0.5 * (levels[0][1] + levels[1][1])
    cell_wind = jnp.take(wind_mean, cell_point, axis=1)
    first_half = source_half(spectra, cell_wind[0], cell_wind[1], coupling)
    send_rows = send_list[0]
    counts = send_count[0]
    places = recv_list[0]
    slot_count = send_rows.shape[1]
    spec_width = spectra.shape[1]
    live_slots = (jnp.arange(slot_count, dtype=jnp.int32)[None, :] < counts[:, None]).astype(
        jnp.float32
    )
    packed = first_half[send_rows] * live_slots[:, :, None]
    arrived = lax.all_to_all(packed, "space", split_axis=0, concat_axis=0, tiled=True)
    row_count = wet_mask.shape[0]
    col_count = wet_mask.shape[1]
    energy_grid = (
        jnp.zeros((row_count * col_count, spec_width), jnp.float32)
        .at[places.reshape(-1)]
        .add(arrived.reshape(-1, spec_width))
    )
    energy_grid = energy_grid.reshape(row_count, col_count, spec_width)
    points = forcing_points(lax.axis_index("space") * row_count, row_count, col_count)
    drift = jnp.take(current_mean, points, axis=1)
    wet_field = wet_mask.astype(jnp.float32)
    swept_cols = sweep_cols(energy_grid, drift[0], wet_field)
    padded = extended(swept_cols, (("space", 0),), 1)
    swept = sweep_rows(swept_cols, padded[:-2], padded[2:], drift[1], wet_field).reshape(
        -1, spec_width
    )
    outgoing = swept[places]
    flat_rows = send_rows.reshape(-1)
    empty_rows = jnp.zeros((spectra.shape[0], spec_width), jnp.float32)
    returned = lax.all_to_all(outgoing, "space", split_axis=0, concat_axis=0, tiled=True)
    back_rows = empty_rows.at[flat_rows].add(
        (returned * live_slots[:, :, None]).reshape(-1, spec_width)
    )
    result = source_half(back_rows, cell_wind[0], cell_wind[1], coupling)
    return result


LANES = 128
F32 = jnp.float32
BF16 = jnp.bfloat16
MIB = 1024 * 1024
GRID_VMEM = 44 * MIB
WHOLE_VMEM = 60 * MIB
CHUNKS = 2


def wave_tables():
    direction = 2.0 * np.pi / DIRS * np.arange(DIRS)
    frequency = base_freq * freq_ratio ** (np.arange(FREQS) * (freq_span / (FREQS - 1)))
    angular = 2.0 * np.pi * frequency
    phase = gravity / angular
    group = 0.5 * phase
    cos_dir, sin_dir = np.cos(direction)[:, None], np.sin(direction)[:, None]
    flat = lambda t: np.broadcast_to(t, (DIRS, FREQS)).reshape(-1)
    source = np.zeros((DIRS * FREQS, 8), np.float32)
    source[:, 0] = flat(wind_gain * cos_dir / phase)
    source[:, 1] = flat(wind_gain * sin_dir / phase)
    source[:, 2] = flat(half_length * input_coef * angular)
    source[:, 3] = flat(half_length * dissip_coef * angular)
    east = flat(courant_scale * cos_dir * group).astype(np.float32)
    north = flat(courant_scale * sin_dir * group).astype(np.float32)
    return source, east, north


def ceil_to(value, step):
    return -(-value // step) * step


def largest_step(size, step, most):
    return max(s for s in range(step, most + 1, step) if size % s == 0)


class Plan:
    def __init__(self, shares, rows, spec, cap, strip_rows, cols, points):
        self.shares, self.rows, self.spec, self.cap = shares, rows, spec, cap
        self.cols, self.points = cols, points
        self.depth = spec // shares
        self.part = rows // CHUNKS
        self.tiles = self.part // LANES
        self.data = self.depth * self.tiles
        self.force = 2 * points // (LANES * shares)
        self.all_tiles = rows // LANES
        self.blocks = (
            ceil_to(self.data + self.all_tiles + self.force, 8), ceil_to(self.data, 8)
        )
        self.tall = ceil_to(self.depth + 1, 8)
        self.strip = strip_rows * cols
        self.grid_rows = strip_rows * shares
        self.coarse_rows = self.grid_rows // COARSE
        self.pitch = cols + 8
        self.size = ceil_to((self.grid_rows + 2) * self.pitch + 8, LANES)

    def fits(self):
        if self.spec % self.shares or self.depth >= LANES or self.rows % (CHUNKS * LANES):
            return False
        if 2 * self.points % (LANES * self.shares) or self.cap > LANES or self.cols != LANES:
            return False
        if 2 * self.points // LANES > LANES:
            return False
        cells = 2 * self.size + 2 * self.coarse_rows * self.cols + self.shares * self.part
        held = LANES * 4 * (cells + self.shares * (self.blocks[0] + self.data))
        return held + 4 * MIB < GRID_VMEM


def pack_kernel(plan, turn_ref, wind_ref, current_ref, recv_ref, out_ref):
    me = lax.axis_index("space")
    half = lambda at: jnp.where(turn_ref[at] == me, 0.5, 0.0)
    mine = half(0) + half(1)
    wind = mine * wind_ref[0]
    points, width, cap = plan.points, plan.force * LANES, plan.cap
    for s in range(plan.shares):
        out_ref[s, :, 0:points] = wind
        out_ref[s, :, points:] = jnp.zeros((2, out_ref.shape[2] - points), F32)
        out_ref[s, 0:1, points : points + cap] = recv_ref[0, s : s + 1, :].astype(F32)
        which, first = divmod(s * width, points)
        out_ref[s, 1:2, points : points + width] = (
            mine * current_ref[0, which : which + 1, first : first + width]
        )


def cell_winds(wind, cp):
    points, rows = wind.shape[1], cp.shape[1]
    high = wind.astype(BF16).astype(F32)
    middle = (wind - high).astype(BF16).astype(F32)
    low = wind - high - middle
    parts = jnp.concatenate([high, middle, low, jnp.zeros((10, points), F32)], axis=0)
    point = lax.broadcasted_iota(jnp.int32, (points, rows), 0)
    hit = jnp.where(point == cp, 1.0, 0.0).astype(BF16)
    picked = jnp.dot(parts.astype(BF16), hit, preferred_element_type=F32)
    both = picked[0:2] + picked[2:4] + picked[4:6]
    return both[0:1], both[1:2]


def half_step(plan, load, wind, cp, table_ref, coup_hbm, coup_ref, loc_ref, locb_ref, sem, store):
    spec, rows = plan.spec, plan.part
    fetch = pltpu.make_async_copy(coup_hbm, coup_ref, sem)
    fetch.start()
    east, north = cell_winds(wind, cp)
    step = largest_step(spec, 16, 64)

    def squares(i, total):
        piece = load(pl.multiple_of(i * step, step), step)
        return total + jnp.sum((piece * piece).reshape(step // 8, 8, rows), axis=0)

    total = lax.fori_loop(0, spec // step, squares, jnp.zeros((8, rows), F32))
    mean_square = jnp.sum(total, axis=0, keepdims=True) * (1.0 / spec)

    @pl.loop(0, spec // step)
    def _(i):
        first = pl.multiple_of(i * step, step)
        at = pl.ds(first, step)
        table = table_ref[at, :]
        along = east * table[:, 0:1] + north * table[:, 1:2]
        gain = 1.0 + table[:, 2:3] * jnp.maximum(along - 1.0, 0.0)
        loss = 1.0 + table[:, 3:4] * mean_square
        local = load(first, step) * gain / loss
        loc_ref[at, :] = local
        locb_ref[at, :] = local.astype(BF16)

    fetch.wait()
    tall = largest_step(spec, 16, 512)
    for q in range(spec // tall):
        at = slice(q * tall, (q + 1) * tall)
        store(
            q * tall,
            loc_ref[at, :]
            + jnp.dot(coup_ref[at, :], locb_ref[...], preferred_element_type=F32),
        )


def first_kernel(
    plan, chunk,
    energy_ref, cp_ref, parcel_ref, names_ref, table_ref, coup_hbm, out_ref,
    buf_ref, coup_ref, loc_ref, locb_ref, sem,
):
    part, tiles, shares, points = plan.part, plan.tiles, plan.shares, plan.points
    lanes = slice(chunk * part, (chunk + 1) * part)

    def store(first, values):
        for j in range(tiles):
            buf_ref[pl.ds(first * tiles + j, values.shape[0], stride=tiles), :] = values[
                :, j * LANES : (j + 1) * LANES
            ]

    wind = jnp.sum(parcel_ref[:, :, 0:points], axis=0)
    half_step(
        plan, lambda first, count: energy_ref[pl.ds(first, count), lanes],
        wind, cp_ref[:, lanes], table_ref, coup_hbm, coup_ref, loc_ref, locb_ref, sem, store,
    )

    block = plan.blocks[min(chunk, 1)]
    spare = []
    if chunk == 0:
        landing = jnp.concatenate(
            [parcel_ref[b, 0:1, points : points + LANES] for b in range(shares)], axis=0
        ).astype(jnp.int32)
        cell = landing + plan.strip * lax.broadcasted_iota(jnp.int32, (shares, LANES), 0)
        place = cell + lax.div(cell, plan.cols) * (plan.pitch - plan.cols) + plan.pitch + 8
        place = place.astype(F32)
        for j in range(plan.all_tiles):
            own = lax.broadcasted_iota(jnp.int32, (LANES, LANES), 0) + j * LANES
            found = jnp.zeros((LANES, LANES), F32)
            for b in range(shares):
                found += jnp.where(names_ref[b : b + 1, :] == own, place[b : b + 1, :], 0.0)
            found = jnp.broadcast_to(jnp.sum(found, axis=1, keepdims=True), (LANES, LANES))
            spare.append(found.T[0:1, :])
        width = plan.force * LANES
        current = jnp.sum(parcel_ref[:, :, points : points + width], axis=0)
        spare += [current[1:2, f * LANES : (f + 1) * LANES] for f in range(plan.force)]
    if block > plan.data + len(spare):
        spare.append(jnp.zeros((block - plan.data - len(spare), LANES), F32))
    for d in range(shares):
        out_ref[d * block : d * block + plan.data, :] = buf_ref[
            d * plan.data : (d + 1) * plan.data, :
        ]
        if spare:
            out_ref[d * block + plan.data : (d + 1) * block, :] = jnp.concatenate(spare, axis=0)


def last_kernel(
    plan, chunk,
    came_ref, cp_ref, parcel_ref, table_ref, coup_hbm, held_ref, out_ref,
    res_ref, sems, coup_ref, loc_ref, locb_ref, sem,
):
    part, tiles = plan.part, plan.tiles
    lanes = slice(chunk * part, (chunk + 1) * part)
    copies = []

    def load(first, count):
        start = pl.multiple_of(first * tiles, 8)
        return jnp.concatenate(
            [came_ref[pl.ds(start + j, count, stride=tiles), :] for j in range(tiles)], axis=1
        )

    def store(first, values):
        at = slice(first, first + values.shape[0])
        res_ref[at, :] = values
        copies.append(
            pltpu.make_async_copy(res_ref.at[at, :], out_ref.at[at, lanes], sems.at[len(copies)])
        )
        copies[-1].start()

    wind = jnp.sum(parcel_ref[:, :, 0 : plan.points], axis=0)
    half_step(
        plan, load, wind, cp_ref[:, lanes], table_ref, coup_hbm, coup_ref, loc_ref, locb_ref, sem, store
    )
    for copy in copies:
        copy.wait()


def upwind(center, before, after, courant):
    return center + jnp.abs(courant) * (jnp.where(courant > 0.0, before, after) - center)


def clear(plan, grid_ref):
    @pl.loop(0, plan.size // LANES)
    def _(i):
        at = pl.ds(pl.multiple_of(i * LANES, LANES), LANES)
        grid_ref[at, :] = jnp.zeros((LANES, LANES), F32)


def turn_in(plan, block, came_ref, cell_ref, piece_ref):
    depth, tiles, tall = plan.depth, plan.tiles, plan.tall
    flag = lax.broadcasted_iota(jnp.int32, (LANES, LANES), 0) == depth
    piece_ref[...] = jnp.where(flag, 1.0, 0.0)

    @pl.loop(0, plan.shares)
    def _(s):
        for j in range(tiles):
            piece_ref[0:depth, :] = came_ref[pl.ds(s * block + j, depth, stride=tiles), :]
            at = pl.ds(pl.multiple_of((s * tiles + j) * LANES, LANES), LANES)
            cell_ref[at, 0:tall] = piece_ref[0:tall, :].T


def turn_out(plan, cell_ref, out_ref):
    depth, tiles, tall = plan.depth, plan.tiles, plan.tall

    @pl.loop(0, plan.shares)
    def _(s):
        for j in range(tiles):
            at = pl.ds(pl.multiple_of((s * tiles + j) * LANES, LANES), LANES)
            turned = cell_ref[at, 0:tall].T
            out_ref[pl.ds(s * plan.data + j, depth, stride=tiles), :] = turned[0:depth, :]


def row_groups(plan, chunk, place_ref, body, groups=4):
    per = plan.part // (8 * groups)

    @pl.loop(0, plan.shares * per)
    def _(i):
        first = (i // per) * plan.rows + chunk * plan.part + (i % per) * (8 * groups)
        for g in range(groups):
            at = pl.ds(pl.multiple_of((i * groups + g) * 8, 8), 8)
            body(at, [place_ref[first + g * 8 + t] for t in range(8)])


def scatter(plan, chunk, place_ref, cell_ref, grid_ref):
    sub = lax.broadcasted_iota(jnp.int32, (8, LANES), 0)

    def body(at, spots):
        values = cell_ref[at, :]
        for t, spot in enumerate(spots):
            pltpu.store(grid_ref.at[pl.ds(spot - t, 8), :], values, mask=sub == t)

    row_groups(plan, chunk, place_ref, body)


def gather(plan, chunk, place_ref, cell_ref, grid_ref):
    sub = lax.broadcasted_iota(jnp.int32, (8, LANES), 0)

    def body(at, spots):
        values = grid_ref[pl.ds(spots[0], 8), :]
        for t, spot in enumerate(spots):
            if t:
                values = jnp.where(sub == t, grid_ref[pl.ds(spot - t, 8), :], values)
        cell_ref[at, :] = values

    row_groups(plan, chunk, place_ref, body)


def spread_drift(plan, came_ref, piece_ref, drift_ref):
    piece_ref[...] = jnp.zeros((LANES, LANES), F32)
    for s in range(plan.shares):
        first = s * plan.blocks[0] + plan.data + plan.all_tiles
        piece_ref[s * plan.force : (s + 1) * plan.force, :] = came_ref[
            first : first + plan.force, :
        ]
    turned = (courant_scale * piece_ref[...]).T
    for q in range(plan.shares * plan.force):
        wide = jnp.broadcast_to(turned[:, q : q + 1], (LANES, LANES))
        for t in range(COARSE):
            drift_ref[pl.ds(q * LANES * COARSE + t, LANES, stride=COARSE), :] = wide


def sweep(plan, drift_ref, speed_ref, one_ref, two_ref, wide=32):
    cols, pitch, flag, last = plan.cols, plan.pitch, plan.depth, plan.coarse_rows - 1

    for start in range(0, cols, wide):

        def courant(which, r4):
            point = pl.multiple_of((which * plan.coarse_rows + r4) * cols + start, 8)
            return speed_ref[which : which + 1, :] + drift_ref[pl.ds(point, wide), :]

        def at(row):
            return pl.multiple_of((row + 1) * pitch + 8 + start, 8)

        def along(row, speed):
            base = at(row)
            center = one_ref[pl.ds(base, wide), :]
            before = one_ref[pl.ds(base - 1, wide), :]
            after = one_ref[pl.ds(base + 1, wide), :]
            wet = jnp.broadcast_to(center[:, flag : flag + 1], center.shape)
            return upwind(center, before, after, speed) * wet

        def coarse(r4, held):
            above, here = held
            east, north = courant(0, r4), courant(1, r4)
            later = courant(0, jnp.minimum(r4 + 1, last))
            for dr in range(COARSE):
                row = r4 * COARSE + dr
                below = along(row + 1, east if dr < COARSE - 1 else later)
                two_ref[pl.ds(at(row), wide), :] = upwind(here, above, below, north)
                above, here = here, below
            return above, here

        lax.fori_loop(
            0, plan.coarse_rows, coarse, (jnp.zeros((wide, LANES), F32), along(0, courant(0, 0)))
        )


def land_kernel(plan, place_ref, came_ref, grid_ref, drift_ref, cell_ref, piece_ref):
    clear(plan, grid_ref)
    spread_drift(plan, came_ref, piece_ref, drift_ref)
    turn_in(plan, plan.blocks[0], came_ref, cell_ref, piece_ref)
    scatter(plan, 0, place_ref, cell_ref, grid_ref)


def sweep_kernel(
    plan,
    place_ref, came_ref, speed_ref, grid_ref, drift_ref, out_ref, swept_ref,
    cell_ref, one_ref, two_ref, wide_ref, piece_ref, sems,
):
    get_grid = pltpu.make_async_copy(grid_ref, one_ref, sems.at[0])
    get_drift = pltpu.make_async_copy(drift_ref, wide_ref, sems.at[1])
    get_grid.start()
    get_drift.start()
    turn_in(plan, plan.blocks[1], came_ref, cell_ref, piece_ref)
    get_grid.wait()
    scatter(plan, 1, place_ref, cell_ref, one_ref)
    get_drift.wait()
    sweep(plan, wide_ref, speed_ref, one_ref, two_ref)
    put_grid = pltpu.make_async_copy(two_ref, swept_ref, sems.at[2])
    put_grid.start()
    gather(plan, 0, place_ref, cell_ref, two_ref)
    turn_out(plan, cell_ref, out_ref)
    put_grid.wait()


def take_kernel(plan, place_ref, grid_ref, out_ref, cell_ref):
    gather(plan, 1, place_ref, cell_ref, grid_ref)
    turn_out(plan, cell_ref, out_ref)


VMEM = pl.BlockSpec(memory_space=pltpu.VMEM)
SMEM = pl.BlockSpec(memory_space=pltpu.SMEM)
ANY = pl.BlockSpec(memory_space=pl.ANY)


def on_spectrum(
    plan,
    spectra,
    wind_files,
    current_files,
    reader_turn,
    cell_point,
    coupling,
    send_list,
    send_count,
    recv_list,
):
    me = lax.axis_index("space")
    shares, rows, spec, points = plan.shares, plan.rows, plan.spec, plan.points
    part, tiles, size = plan.part, plan.tiles, plan.size
    source, east_speed, north_speed = wave_tables()
    table = jnp.asarray(source)
    data_rows = shares * plan.data
    drift_rows = 2 * plan.coarse_rows * plan.cols

    def kernel(body, *, vmem, flops, traffic, **options):
        return pl.pallas_call(
            body,
            compiler_params=pltpu.CompilerParams(vmem_limit_bytes=vmem),
            cost_estimate=pl.CostEstimate(flops=flops, bytes_accessed=traffic, transcendentals=0),
            **options,
        )

    width = points + max(LANES, plan.force * LANES)
    parcel = kernel(
        functools.partial(pack_kernel, plan),
        vmem=WHOLE_VMEM, flops=0, traffic=4 * shares * 2 * width,
        out_shape=jax.ShapeDtypeStruct((shares, 2, width), F32),
        in_specs=[SMEM, VMEM, VMEM, VMEM],
        out_specs=VMEM,
        name="pack",
    )(reader_turn, wind_files, current_files, recv_list)
    parcel = lax.all_to_all(parcel, "space", 0, 0, tiled=True)

    slot = jnp.arange(plan.cap, dtype=jnp.int32)[None, :]
    names = jnp.where(slot < send_count[0][:, None], send_list[0], -1)
    names = jnp.pad(names, ((0, 0), (0, LANES - plan.cap)), constant_values=-1)
    speed = jnp.stack([jnp.asarray(east_speed), jnp.asarray(north_speed)])
    speed = jnp.pad(speed, ((0, 6), (0, LANES)))
    speed = lax.dynamic_slice(speed, (0, me * plan.depth), (8, LANES))

    energy = spectra.T
    cp = cell_point.reshape(1, rows)
    coup = coupling.T
    h_flops, h_traffic = 2 * part * spec * spec, 8 * part * spec
    h_scratch = [
        pltpu.VMEM((spec, spec), BF16),
        pltpu.VMEM((spec, part), F32),
        pltpu.VMEM((spec, part), BF16),
        pltpu.SemaphoreType.DMA,
    ]

    def first(chunk):
        rows_sent = plan.blocks[min(chunk, 1)]
        block = kernel(
            functools.partial(first_kernel, plan, chunk),
            vmem=WHOLE_VMEM, flops=h_flops, traffic=h_traffic,
            out_shape=jax.ShapeDtypeStruct((shares * rows_sent, LANES), F32),
            in_specs=[VMEM] * 5 + [ANY],
            out_specs=VMEM,
            scratch_shapes=[pltpu.VMEM((data_rows, LANES), F32)] + h_scratch,
            name=f"first_half_{chunk}",
        )(energy, cp, parcel, names, table, coup)
        block = block.reshape(shares, rows_sent, LANES)
        return lax.all_to_all(block, "space", 0, 0, tiled=True).reshape(-1, LANES)

    def home(block):
        block = block.reshape(shares, plan.depth, tiles, LANES)
        return lax.all_to_all(block, "space", 0, 0, tiled=True).reshape(data_rows, LANES)

    cells = pltpu.VMEM((shares * part, LANES), F32)
    piece = pltpu.VMEM((LANES, LANES), F32)
    grid_shape = jax.ShapeDtypeStruct((size, LANES), F32)
    block_shape = jax.ShapeDtypeStruct((data_rows, LANES), F32)

    came = [first(chunk) for chunk in range(CHUNKS)]
    place = came[0].reshape(shares, plan.blocks[0], LANES)[:, plan.data : plan.data + plan.all_tiles]
    place = place.astype(jnp.int32).reshape(-1)
    grid, drift = kernel(
        functools.partial(land_kernel, plan),
        vmem=WHOLE_VMEM, flops=0, traffic=8 * size * LANES,
        out_shape=[grid_shape, jax.ShapeDtypeStruct((drift_rows, LANES), F32)],
        in_specs=[SMEM, VMEM],
        out_specs=[VMEM, VMEM],
        scratch_shapes=[cells, piece],
        name="land",
    )(place, came[0])
    out0, swept = kernel(
        functools.partial(sweep_kernel, plan),
        vmem=WHOLE_VMEM, flops=20 * size * LANES, traffic=16 * size * LANES,
        out_shape=[block_shape, grid_shape],
        in_specs=[SMEM, VMEM, VMEM, ANY, ANY],
        out_specs=[VMEM, ANY],
        scratch_shapes=[
            cells,
            pltpu.VMEM((size, LANES), F32),
            pltpu.VMEM((size, LANES), F32),
            pltpu.VMEM((drift_rows, LANES), F32),
            piece,
            pltpu.SemaphoreType.DMA((3,)),
        ],
        name="sweeps",
    )(place, came[1], speed, grid, drift)
    back0 = home(out0)
    out1 = kernel(
        functools.partial(take_kernel, plan),
        vmem=WHOLE_VMEM, flops=0, traffic=8 * size * LANES,
        out_shape=block_shape,
        in_specs=[SMEM, VMEM],
        out_specs=VMEM,
        scratch_shapes=[cells],
        name="take",
    )(place, swept)
    back1 = home(out1)

    result = jnp.zeros((8, LANES), F32)
    for chunk, back in enumerate((back0, back1)):
        result = kernel(
            functools.partial(last_kernel, plan, chunk),
            vmem=WHOLE_VMEM, flops=h_flops, traffic=h_traffic,
            out_shape=jax.ShapeDtypeStruct((spec, rows), F32),
            in_specs=[VMEM] * 4 + [ANY] * 2,
            out_specs=ANY,
            scratch_shapes=[pltpu.VMEM((spec, part), F32), pltpu.SemaphoreType.DMA((8,))] + h_scratch,
            input_output_aliases={5: 0} if chunk else {},
            name=f"last_half_{chunk}",
        )(back, cp, parcel, table, coup, result)
    return result.T


def on_device(*args):
    spectra, wind_files, send_list, wet_mask = args[0], args[1], args[6], args[9]
    plan = Plan(
        lax.axis_size("space"), *spectra.shape, send_list.shape[2], *wet_mask.shape, wind_files.shape[2]
    )
    if plan.fits():
        return on_spectrum(plan, *args[:9])
    return on_strips(*args)


def solution(mesh):
    placed = (
        P(("members", "space"), None),
        P(("members", "space"), None, None),
        P(("members", "space"), None, None),
        P(),
        P("space"),
        P(),
        P("space", None, None),
        P("space", None),
        P("space", None, None),
        P("space", None),
    )
    return jax.shard_map(
        on_device,
        mesh=mesh,
        in_specs=placed,
        out_specs=P(("members", "space"), None),
        check_vma=False,
    )
```

```python
import functools
import math

import jax
import jax.numpy as jnp
import numpy as np
from jax import lax
from jax.experimental import pallas as pl
from jax.experimental.pallas import tpu as pltpu
from jax.sharding import PartitionSpec as P

DIRS = 36
FREQS = 36
COARSE = 4


gravity = 9.81
base_freq = 0.0418
freq_ratio = 1.1
freq_span = 35.0
input_coef = 0.0001
wind_gain = 1.12
dissip_coef = 0.0005
half_length = 300.0
courant_scale = 0.05


def from_root(array, axis, root):
    mine = lax.axis_index(axis) == root
    return lax.psum(jnp.where(mine, array, jnp.zeros_like(array)), axis)


def extended(array, sides, width):
    for axis, dim in sides:
        size, length = (lax.axis_size(axis), array.shape[dim])
        up = [(i, (i + 1) % size) for i in range(size - 1)]
        down = [(j, i) for i, j in up]
        last = lax.slice_in_dim(array, length - width, length, axis=dim)
        first = lax.slice_in_dim(array, 0, width, axis=dim)
        before = lax.ppermute(last, axis, up)
        after = lax.ppermute(first, axis, down)
        array = jnp.concatenate([before, array, after], axis=dim)
    return array


def spectral_tables():
    direction = 2.0 * math.pi / DIRS * jnp.arange(DIRS, dtype=jnp.float32)
    exponent = jnp.arange(FREQS, dtype=jnp.float32) * (freq_span / (FREQS - 1))
    frequency = base_freq * freq_ratio**exponent
    angular = 2.0 * math.pi * frequency
    phase_speed = gravity / angular
    return (jnp.cos(direction), jnp.sin(direction), angular, phase_speed, 0.5 * phase_speed)


def source_half(energy, wind_east, wind_north, coupling):
    cos_dir, sine_dir, angular, phase_speed, group_speed = spectral_tables()
    along_wind = wind_east[:, None] * cos_dir[None, :] + wind_north[:, None] * sine_dir[None, :]
    growth = (
        input_coef
        * angular[None, None, :]
        * jnp.maximum(wind_gain * along_wind[:, :, None] / phase_speed[None, None, :] - 1.0, 0.0)
    )
    growth = growth.reshape(energy.shape[0], -1)
    mean_square = jnp.mean(energy * energy, axis=1, keepdims=True)
    decay_rate = dissip_coef * jnp.tile(angular, DIRS)[None, :] * mean_square
    local_part = energy * (1.0 + half_length * growth) / (1.0 + half_length * decay_rate)
    return local_part + jnp.dot(
        local_part.astype(jnp.bfloat16), coupling, preferred_element_type=jnp.float32
    )


def advect(center, upwind_lo, upwind_hi, courant):
    ahead_part = jnp.maximum(courant, 0.0)
    behind = jnp.minimum(courant, 0.0)
    return center - ahead_part * (center - upwind_lo) - behind * (upwind_hi - center)


def sweep_cols(energy_grid, drift_east, wet_field):
    cos_dir, sine_dir, angular, phase_speed, group_speed = spectral_tables()
    wave_speed = (cos_dir[:, None] * group_speed[None, :]).reshape(-1)
    courant = (wave_speed[None, None, :] + drift_east[:, :, None]) * courant_scale
    zero_edge = jnp.zeros_like(energy_grid[:, :1])
    upwind_lo = jnp.concatenate([zero_edge, energy_grid[:, :-1]], axis=1)
    upwind_hi = jnp.concatenate([energy_grid[:, 1:], zero_edge], axis=1)
    return advect(energy_grid, upwind_lo, upwind_hi, courant) * wet_field[:, :, None]


def sweep_rows(energy_grid, row_above, row_below, drift_north, wet_field):
    cos_dir, sine_dir, angular, phase_speed, group_speed = spectral_tables()
    wave_speed = (sine_dir[:, None] * group_speed[None, :]).reshape(-1)
    courant = (wave_speed[None, None, :] + drift_north[:, :, None]) * courant_scale
    return advect(energy_grid, row_above, row_below, courant) * wet_field[:, :, None]


def forcing_points(row_start, row_count, col_count):
    rows_idx = row_start + jnp.arange(row_count, dtype=jnp.int32)
    cols_idx = jnp.arange(col_count, dtype=jnp.int32)
    return rows_idx[:, None] // COARSE * (col_count // COARSE) + cols_idx[None, :] // COARSE


def on_strips(
    spectra,
    wind_files,
    current_files,
    reader_turn,
    cell_point,
    coupling,
    send_list,
    send_count,
    recv_list,
    wet_mask,
):
    levels = []
    for time_level in range(2):
        levels.append(
            (
                from_root(wind_files[0], "space", reader_turn[time_level]),
                from_root(current_files[0], "space", reader_turn[time_level]),
            )
        )
    wind_mean = 0.5 * (levels[0][0] + levels[1][0])
    current_mean = 0.5 * (levels[0][1] + levels[1][1])
    cell_wind = jnp.take(wind_mean, cell_point, axis=1)
    first_half = source_half(spectra, cell_wind[0], cell_wind[1], coupling)
    send_rows = send_list[0]
    counts = send_count[0]
    places = recv_list[0]
    slot_count = send_rows.shape[1]
    spec_width = spectra.shape[1]
    live_slots = (jnp.arange(slot_count, dtype=jnp.int32)[None, :] < counts[:, None]).astype(
        jnp.float32
    )
    packed = first_half[send_rows] * live_slots[:, :, None]
    arrived = lax.all_to_all(packed, "space", split_axis=0, concat_axis=0, tiled=True)
    row_count = wet_mask.shape[0]
    col_count = wet_mask.shape[1]
    energy_grid = (
        jnp.zeros((row_count * col_count, spec_width), jnp.float32)
        .at[places.reshape(-1)]
        .add(arrived.reshape(-1, spec_width))
    )
    energy_grid = energy_grid.reshape(row_count, col_count, spec_width)
    points = forcing_points(lax.axis_index("space") * row_count, row_count, col_count)
    drift = jnp.take(current_mean, points, axis=1)
    wet_field = wet_mask.astype(jnp.float32)
    swept_cols = sweep_cols(energy_grid, drift[0], wet_field)
    padded = extended(swept_cols, (("space", 0),), 1)
    swept = sweep_rows(swept_cols, padded[:-2], padded[2:], drift[1], wet_field).reshape(
        -1, spec_width
    )
    outgoing = swept[places]
    flat_rows = send_rows.reshape(-1)
    empty_rows = jnp.zeros((spectra.shape[0], spec_width), jnp.float32)
    returned = lax.all_to_all(outgoing, "space", split_axis=0, concat_axis=0, tiled=True)
    back_rows = empty_rows.at[flat_rows].add(
        (returned * live_slots[:, :, None]).reshape(-1, spec_width)
    )
    result = source_half(back_rows, cell_wind[0], cell_wind[1], coupling)
    return result


LANES = 128
SUBS = 8
F32 = jnp.float32
BF16 = jnp.bfloat16
MIB = 1024 * 1024
WHOLE_VMEM = 60 * MIB
DRY = 1e30
PARTS = 4


def wave_tables():
    direction = 2.0 * np.pi / DIRS * np.arange(DIRS)
    frequency = base_freq * freq_ratio ** (np.arange(FREQS) * (freq_span / (FREQS - 1)))
    angular = 2.0 * np.pi * frequency
    phase = gravity / angular
    group = 0.5 * phase
    cos_dir, sin_dir = np.cos(direction)[:, None], np.sin(direction)[:, None]
    flat = lambda t: np.broadcast_to(t, (DIRS, FREQS)).reshape(-1)
    source = np.zeros((DIRS * FREQS, 8), np.float32)
    source[:, 0] = flat(wind_gain * cos_dir / phase)
    source[:, 1] = flat(wind_gain * sin_dir / phase)
    source[:, 2] = flat(half_length * input_coef * angular)
    source[:, 3] = flat(half_length * dissip_coef * angular)
    east = flat(courant_scale * cos_dir * group).astype(np.float32)
    north = flat(courant_scale * sin_dir * group).astype(np.float32)
    return source, east, north


def ceil_to(value, step):
    return -(-value // step) * step


def largest_step(size, step, most):
    return max(s for s in range(step, most + 1, step) if size % s == 0)


class Plan:
    def __init__(self, shares, rows, spec, cap, strip_rows, cols, points):
        self.shares, self.rows, self.spec, self.cap = shares, rows, spec, cap
        self.cols, self.points = cols, points
        self.depth = spec // shares
        self.tiles = rows // LANES
        self.data = self.depth * self.tiles
        self.force = 2 * points // (LANES * shares)
        self.block = ceil_to(self.data + self.tiles + self.force, SUBS)
        self.tall = ceil_to(self.depth, SUBS)
        self.strip = strip_rows * cols
        self.grid_rows = strip_rows * shares
        self.coarse_rows = self.grid_rows // COARSE
        self.vregs = cols // SUBS
        self.size = (self.grid_rows + 2) * cols

    def fits(self):
        if self.spec % self.shares or self.depth > LANES or self.rows % (2 * LANES):
            return False
        if 2 * self.points % (LANES * self.shares) or self.points % LANES or self.cap > LANES:
            return False
        if 2 * self.points // LANES > LANES or self.cols != LANES or self.shares % PARTS:
            return False
        held = 2 * self.size + 2 * self.points + self.shares * (self.block + self.data)
        return 4 * LANES * held + 4 * MIB < 32 * MIB


def pack_kernel(plan, turn_ref, wind_ref, current_ref, recv_ref, out_ref):
    me = lax.axis_index("space")
    half = lambda at: jnp.where(turn_ref[at] == me, 0.5, 0.0)
    mine = half(0) + half(1)
    wind = mine * wind_ref[0]
    points, width, cap = plan.points, plan.force * LANES, plan.cap
    for s in range(plan.shares):
        out_ref[s, :, 0:points] = wind
        out_ref[s, :, points:] = jnp.zeros((2, out_ref.shape[2] - points), F32)
        out_ref[s, 0:1, points : points + cap] = recv_ref[0, s : s + 1, :].astype(F32)
        which, first = divmod(s * width, points)
        out_ref[s, 1:2, points : points + width] = (
            mine * current_ref[0, which : which + 1, first : first + width]
        )


def cell_winds(wind, cp):
    points, rows = wind.shape[1], cp.shape[1]
    high = wind.astype(BF16).astype(F32)
    middle = (wind - high).astype(BF16).astype(F32)
    low = wind - high - middle
    parts = jnp.concatenate([high, middle, low, jnp.zeros((10, points), F32)], axis=0)
    point = lax.broadcasted_iota(jnp.int32, (points, rows), 0)
    hit = jnp.where(point == cp, 1.0, 0.0).astype(BF16)
    picked = jnp.dot(parts.astype(BF16), hit, preferred_element_type=F32)
    both = picked[0:2] + picked[2:4] + picked[4:6]
    return both[0:1], both[1:2]


def half_step(
    plan, energy_hbm, energy_ref, load, parcel_ref, cp_ref, table_ref, coup_hbm, coup_ref,
    loc_ref, locb_ref, sems, store,
):
    spec, rows = plan.spec, plan.rows
    tall = largest_step(spec, 16, 512)
    thirds = spec // tall
    tall_rows = energy_ref.shape[0] // thirds
    arrive = [
        pltpu.make_async_copy(
            energy_hbm.at[pl.ds(q * tall_rows, tall_rows), :],
            energy_ref.at[pl.ds(q * tall_rows, tall_rows), :],
            sems.at[q],
        )
        for q in range(thirds)
    ]
    fetch = pltpu.make_async_copy(coup_hbm, coup_ref, sems.at[thirds])
    for copy in arrive:
        copy.start()
    fetch.start()
    east, north = cell_winds(jnp.sum(parcel_ref[:, :, 0 : plan.points], axis=0), cp_ref[...])
    step = largest_step(tall, 16, 64)

    def squares(i, total):
        piece = load(pl.multiple_of(i * step, step), step)
        return total + jnp.sum((piece * piece).reshape(step // SUBS, SUBS, rows), axis=0)

    total = jnp.zeros((SUBS, rows), F32)
    for q in range(thirds):
        arrive[q].wait()
        total = lax.fori_loop(q * tall // step, (q + 1) * tall // step, squares, total)
    mean_square = jnp.sum(total, axis=0, keepdims=True) * (1.0 / spec)

    @pl.loop(0, spec // step)
    def _(i):
        first = pl.multiple_of(i * step, step)
        at = pl.ds(first, step)
        table = table_ref[at, :]
        along = east * table[:, 0:1] + north * table[:, 1:2]
        gain = 1.0 + table[:, 2:3] * jnp.maximum(along - 1.0, 0.0)
        loss = 1.0 + table[:, 3:4] * mean_square
        local = load(first, step) * gain / loss
        loc_ref[at, :] = local
        locb_ref[at, :] = local.astype(BF16)

    fetch.wait()
    for q in range(thirds):
        at = slice(q * tall, (q + 1) * tall)
        store(
            q * tall,
            loc_ref[at, :]
            + jnp.dot(coup_ref[at, :], locb_ref[...], preferred_element_type=F32),
        )


def own_places(plan, parcel_ref, names_ref):
    points, cols, vregs = plan.points, plan.cols, plan.vregs
    landing = jnp.concatenate(
        [parcel_ref[b, 0:1, points : points + LANES] for b in range(plan.shares)], axis=0
    ).astype(jnp.int32)
    cell = landing + plan.strip * lax.broadcasted_iota(jnp.int32, (plan.shares, LANES), 0)
    column = lax.rem(cell, cols)
    place = cell - column + cols + lax.rem(column, vregs) * SUBS + lax.div(column, vregs)
    place = place.astype(F32)
    rows = []
    for j in range(plan.tiles):
        own = lax.broadcasted_iota(jnp.int32, (LANES, LANES), 0) + j * LANES
        found = jnp.zeros((LANES, LANES), F32)
        for b in range(plan.shares):
            found += jnp.where(names_ref[b : b + 1, :] == own, place[b : b + 1, :], 0.0)
        found = jnp.broadcast_to(jnp.sum(found, axis=1, keepdims=True), (LANES, LANES))
        rows.append(found.T[0:1, :])
    return rows


def first_kernel(
    plan,
    cp_ref, parcel_ref, names_ref, table_ref, energy_hbm, coup_hbm, out_hbm,
    out_ref, buf_ref, out_sems, energy_ref, coup_ref, loc_ref, locb_ref, sems,
):
    tiles, shares, points, block, data = plan.tiles, plan.shares, plan.points, plan.block, plan.data
    width = plan.force * LANES
    current = jnp.sum(parcel_ref[:, :, points : points + width], axis=0)
    spare = own_places(plan, parcel_ref, names_ref)
    spare += [current[1:2, f * LANES : (f + 1) * LANES] for f in range(plan.force)]
    if block > data + len(spare):
        spare.append(jnp.zeros((block - data - len(spare), LANES), F32))
    for d in range(shares):
        out_ref[d * block + data : (d + 1) * block, :] = jnp.concatenate(spare, axis=0)
    sent, copies = [0], []

    def store(first, values):
        for j in range(tiles):
            buf_ref[pl.ds(first * tiles + j, values.shape[0], stride=tiles), :] = values[
                :, j * LANES : (j + 1) * LANES
            ]
        upto = (first + values.shape[0]) // plan.depth
        for d in range(sent[0], upto):
            out_ref[d * block : d * block + data, :] = buf_ref[d * data : (d + 1) * data, :]
        at = slice(sent[0] * block, upto * block)
        copies.append(
            pltpu.make_async_copy(out_ref.at[at, :], out_hbm.at[at, :], out_sems.at[len(copies)])
        )
        copies[-1].start()
        sent[0] = upto

    half_step(
        plan, energy_hbm, energy_ref, lambda first, count: energy_ref[pl.ds(first, count), :],
        parcel_ref, cp_ref, table_ref, coup_hbm, coup_ref, loc_ref, locb_ref, sems, store,
    )
    for copy in copies:
        copy.wait()


def last_kernel(
    plan,
    cp_ref, parcel_ref, table_ref, came_hbm, coup_hbm, out_hbm,
    res_ref, out_sems, came_ref, coup_ref, loc_ref, locb_ref, sems,
):
    tiles = plan.tiles
    copies = []

    def load(first, count):
        start = pl.multiple_of(first * tiles, SUBS)
        return jnp.concatenate(
            [came_ref[pl.ds(start + j, count, stride=tiles), :] for j in range(tiles)], axis=1
        )

    def store(first, values):
        at = slice(first, first + values.shape[0])
        res_ref[at, :] = values
        copies.append(
            pltpu.make_async_copy(res_ref.at[at, :], out_hbm.at[at, :], out_sems.at[len(copies)])
        )
        copies[-1].start()

    half_step(
        plan, came_hbm, came_ref, load,
        parcel_ref, cp_ref, table_ref, coup_hbm, coup_ref, loc_ref, locb_ref, sems, store,
    )
    for copy in copies:
        copy.wait()


def scatter(plan, place_ref, came_ref, grid_ref, piece_refs, arrived):
    depth, tiles, tall, block = plan.depth, plan.tiles, plan.tall, plan.block
    blocks = plan.shares * tiles
    sub = lax.broadcasted_iota(jnp.int32, (SUBS, LANES), 0)

    def turn(i, piece_ref):
        s, j = i // tiles, i % tiles
        values = came_ref[pl.ds(s * block + j, depth, stride=tiles), :]
        if tall > depth:
            values = jnp.concatenate([values, jnp.zeros((tall - depth, LANES), F32)], axis=0)
        piece_ref[:, 0:tall] = values.T

    def put(i, piece_ref):
        for g in range(LANES // SUBS):
            values = piece_ref[g * SUBS : (g + 1) * SUBS, :]
            for t in range(SUBS):
                spot = place_ref[i * LANES + g * SUBS + t]
                pltpu.store(grid_ref.at[pl.ds(spot - t, SUBS), :], values, mask=sub == t)

    even_ref, odd_ref = piece_refs
    arrived(0)
    turn(0, even_ref)
    per = blocks // (2 * PARTS)

    @pl.loop(0, PARTS)
    def _(part):
        @pl.loop(0, per)
        def _(i):
            at = (part * per + i) * 2
            turn(at + 1, odd_ref)
            put(at, even_ref)

            @pl.when(jnp.logical_and(i == per - 1, part < PARTS - 1))
            def _():
                arrived(part + 1)

            turn(jnp.minimum(at + 2, blocks - 1), even_ref)
            put(at + 1, odd_ref)


def gather(plan, place_ref, out_ref, grid_ref, piece_refs, finished):
    depth, tiles, tall = plan.depth, plan.tiles, plan.tall
    blocks = plan.shares * tiles
    sub = lax.broadcasted_iota(jnp.int32, (SUBS, LANES), 0)

    def turn(i, piece_ref):
        s, j = i // tiles, i % tiles
        turned = piece_ref[:, 0:tall].T
        out_ref[pl.ds(s * plan.data + j, depth, stride=tiles), :] = turned[0:depth, :]

    def get(i, piece_ref):
        for g in range(LANES // SUBS):
            first = i * LANES + g * SUBS
            values = grid_ref[pl.ds(place_ref[first], SUBS), :]
            for t in range(1, SUBS):
                shifted = grid_ref[pl.ds(place_ref[first + t] - t, SUBS), :]
                values = jnp.where(sub == t, shifted, values)
            piece_ref[g * SUBS : (g + 1) * SUBS, :] = values

    even_ref, odd_ref = piece_refs
    get(0, even_ref)
    per = blocks // (2 * PARTS)

    @pl.loop(0, PARTS)
    def _(part):
        @pl.loop(0, per)
        def _(i):
            at = (part * per + i) * 2
            get(at + 1, odd_ref)
            turn(at, even_ref)
            get(jnp.minimum(at + 2, blocks - 1), even_ref)
            turn(at + 1, odd_ref)

        finished(part)


def spread_drift(plan, came_ref, piece_ref, wide_ref, drift_ref):
    piece_ref[...] = jnp.zeros((LANES, LANES), F32)
    for s in range(plan.shares):
        first = s * plan.block + plan.data + plan.tiles
        piece_ref[s * plan.force : (s + 1) * plan.force, :] = came_ref[
            first : first + plan.force, :
        ]
    turned = (courant_scale * piece_ref[...]).T
    groups = plan.vregs // COARSE
    for q in range(plan.shares * plan.force):
        wide_ref[...] = jnp.broadcast_to(turned[:, q : q + 1], (LANES, LANES))
        for a in range(LANES // (groups * SUBS)):
            for m in range(groups):
                to = q * LANES + (a * groups + m) * SUBS
                drift_ref[to : to + SUBS, :] = wide_ref[
                    pl.ds(a * groups * SUBS + m, SUBS, stride=groups), :
                ]


def sweep(plan, drift_ref, speed_ref, one_ref, two_ref):
    cols, last = plan.cols, plan.coarse_rows - 1
    groups = plan.vregs // COARSE
    sub = lax.broadcasted_iota(jnp.int32, (SUBS, LANES), 0)
    speeds = [jnp.broadcast_to(speed_ref[d : d + 1, :], (SUBS, LANES)) for d in range(2)]

    for m in range(groups):

        def courant(which, r4):
            at = pl.multiple_of(((which * plan.coarse_rows + r4) * groups + m) * SUBS, SUBS)
            value = speeds[which] + drift_ref[pl.ds(at, SUBS), :]
            return value > 0.0, jnp.abs(value)

        def at(row, q):
            return pl.ds(pl.multiple_of((row + 1) * cols + q * SUBS, SUBS), SUBS)

        def along(row, speed):
            ahead, size = speed
            base = pl.multiple_of((row + 1) * cols, SUBS)
            first, count = m * COARSE, COARSE
            line = [one_ref[at(row, q), :] for q in range(first, first + count)]
            if first:
                before = one_ref[at(row, first - 1), :]
            else:
                before = one_ref[pl.ds(base + cols - SUBS - 1, SUBS), :]
                before = jnp.where(sub == 0, DRY, before)
            if first + count < plan.vregs:
                after = one_ref[at(row, first + count), :]
            else:
                after = jnp.where(sub == SUBS - 1, DRY, one_ref[pl.ds(base + 1, SUBS), :])
            line = [before] + line + [after]
            swept = []
            for q in range(1, count + 1):
                pick = jnp.where(ahead, line[q - 1], line[q + 1])
                pick = jnp.where(pick < DRY, pick, 0.0)
                moved = line[q] + size * (pick - line[q])
                swept.append(jnp.where(line[q] < DRY, moved, 0.0))
            return swept

        def coarse(r4, held):
            above, here = held
            east = courant(0, r4)
            ahead, size = courant(1, r4)
            later = courant(0, jnp.minimum(r4 + 1, last))
            for dr in range(COARSE):
                row = r4 * COARSE + dr
                below = along(row + 1, east if dr < COARSE - 1 else later)
                for q in range(COARSE):
                    pick = jnp.where(ahead, above[q], below[q])
                    two_ref[at(row, m * COARSE + q), :] = here[q] + size * (pick - here[q])
                above, here = here, below
            return above, here

        zero = [jnp.zeros((SUBS, LANES), F32)] * COARSE
        lax.fori_loop(0, plan.coarse_rows, coarse, (zero, along(0, courant(0, 0))))


def middle_kernel(
    plan,
    place_ref, speed_ref, came_hbm, out_hbm,
    came_ref, out_ref, one_ref, two_ref, drift_ref, even_ref, odd_ref, in_sems, out_sems,
):
    shares, block, data = plan.shares, plan.block, plan.data
    part_in, part_out = shares // PARTS * block, shares // PARTS * data

    def copy_in(part):
        at = pl.ds(pl.multiple_of(part * part_in, SUBS), part_in)
        return pltpu.make_async_copy(came_hbm.at[at, :], came_ref.at[at, :], in_sems.at[part])

    def copy_out(part):
        at = pl.ds(pl.multiple_of(part * part_out, SUBS), part_out)
        return pltpu.make_async_copy(out_ref.at[at, :], out_hbm.at[at, :], out_sems.at[part])

    for part in range(PARTS):
        copy_in(part).start()

    @pl.loop(0, plan.size // LANES)
    def _(i):
        at = pl.ds(pl.multiple_of(i * LANES, LANES), LANES)
        one_ref[at, :] = jnp.full((LANES, LANES), DRY, F32)

    pieces = (even_ref, odd_ref)
    scatter(plan, place_ref, came_ref, one_ref, pieces, lambda part: copy_in(part).wait())
    spread_drift(plan, came_ref, even_ref, odd_ref, drift_ref)
    me = lax.axis_index("space")
    sweep(plan, drift_ref, speed_ref.at[me], one_ref, two_ref)
    gather(plan, place_ref, out_ref, two_ref, pieces, lambda part: copy_out(part).start())
    for part in range(PARTS):
        copy_out(part).wait()


VMEM = pl.BlockSpec(memory_space=pltpu.VMEM)
SMEM = pl.BlockSpec(memory_space=pltpu.SMEM)
ANY = pl.BlockSpec(memory_space=pl.ANY)


def on_spectrum(
    plan,
    spectra,
    wind_files,
    current_files,
    reader_turn,
    cell_point,
    coupling,
    send_list,
    send_count,
    recv_list,
):
    shares, rows, spec, points = plan.shares, plan.rows, plan.spec, plan.points
    tiles, depth, size, data_rows = plan.tiles, plan.depth, plan.size, plan.shares * plan.data
    source, east_speed, north_speed = wave_tables()
    table = jnp.asarray(source)
    speed = np.zeros((shares, SUBS, LANES), np.float32)
    speed[:, 0, :depth] = east_speed.reshape(shares, depth)
    speed[:, 1, :depth] = north_speed.reshape(shares, depth)

    def kernel(body, *, flops, traffic, vmem=WHOLE_VMEM, **options):
        return pl.pallas_call(
            body,
            compiler_params=pltpu.CompilerParams(vmem_limit_bytes=vmem),
            cost_estimate=pl.CostEstimate(flops=flops, bytes_accessed=traffic, transcendentals=0),
            **options,
        )

    width = points + max(LANES, plan.force * LANES)
    parcel = kernel(
        functools.partial(pack_kernel, plan),
        flops=0, traffic=4 * shares * 2 * width,
        out_shape=jax.ShapeDtypeStruct((shares, 2, width), F32),
        in_specs=[SMEM, VMEM, VMEM, VMEM],
        out_specs=VMEM,
        name="pack",
    )(reader_turn, wind_files, current_files, recv_list)
    parcel = lax.all_to_all(parcel, "space", 0, 0, tiled=True)

    slot = jnp.arange(plan.cap, dtype=jnp.int32)[None, :]
    names = jnp.where(slot < send_count[0][:, None], send_list[0], -1)
    names = jnp.pad(names, ((0, 0), (0, LANES - plan.cap)), constant_values=-1)

    cp = cell_point.reshape(1, rows)
    coup = coupling.T
    h_cost = dict(flops=2 * rows * spec * spec, traffic=12 * rows * spec)
    h_scratch = [
        pltpu.VMEM((spec, spec), BF16),
        pltpu.VMEM((spec, rows), F32),
        pltpu.VMEM((spec, rows), BF16),
        pltpu.SemaphoreType.DMA((8,)),
    ]
    sent = kernel(
        functools.partial(first_kernel, plan),
        **h_cost,
        out_shape=jax.ShapeDtypeStruct((shares * plan.block, LANES), F32),
        in_specs=[VMEM] * 4 + [ANY] * 2,
        out_specs=ANY,
        scratch_shapes=[
            pltpu.VMEM((shares * plan.block, LANES), F32),
            pltpu.VMEM((data_rows, LANES), F32),
            pltpu.SemaphoreType.DMA((8,)),
            pltpu.VMEM((spec, rows), F32),
        ]
        + h_scratch,
        name="first_half",
    )(cp, parcel, names, table, spectra.T, coup)
    came = lax.all_to_all(
        sent.reshape(shares, plan.block, LANES), "space", 0, 0, tiled=True
    )
    place = came[:, plan.data : plan.data + tiles].astype(jnp.int32).reshape(-1)
    swept = kernel(
        functools.partial(middle_kernel, plan),
        flops=24 * size * LANES, traffic=8 * rows * spec, vmem=32 * MIB,
        out_shape=jax.ShapeDtypeStruct((data_rows, LANES), F32),
        in_specs=[SMEM, VMEM, ANY],
        out_specs=ANY,
        scratch_shapes=[
            pltpu.VMEM((shares * plan.block, LANES), F32),
            pltpu.VMEM((data_rows, LANES), F32),
            pltpu.VMEM((size, LANES), F32),
            pltpu.VMEM((size, LANES), F32),
            pltpu.VMEM((2 * points, LANES), F32),
            pltpu.VMEM((LANES, LANES), F32),
            pltpu.VMEM((LANES, LANES), F32),
            pltpu.SemaphoreType.DMA((PARTS,)),
            pltpu.SemaphoreType.DMA((PARTS,)),
        ],
        name="sweeps",
    )(place, jnp.asarray(speed), came.reshape(-1, LANES))
    back = lax.all_to_all(
        swept.reshape(shares, depth, tiles, LANES), "space", 0, 0, tiled=True
    )
    result = kernel(
        functools.partial(last_kernel, plan),
        vmem=24 * MIB, **h_cost,
        out_shape=jax.ShapeDtypeStruct((spec, rows), F32),
        in_specs=[VMEM] * 3 + [ANY] * 2,
        out_specs=ANY,
        scratch_shapes=[
            pltpu.VMEM((spec, rows), F32),
            pltpu.SemaphoreType.DMA((8,)),
            pltpu.VMEM((data_rows, LANES), F32),
        ]
        + h_scratch,
        name="last_half",
    )(cp, parcel, table, back.reshape(data_rows, LANES), coup)
    return result.T


def on_device(*args):
    spectra, wind_files, send_list, wet_mask = args[0], args[1], args[6], args[9]
    plan = Plan(
        lax.axis_size("space"), *spectra.shape, send_list.shape[2], *wet_mask.shape, wind_files.shape[2]
    )
    if plan.fits():
        return on_spectrum(plan, *args[:9])
    return on_strips(*args)


def solution(mesh):
    placed = (
        P(("members", "space"), None),
        P(("members", "space"), None, None),
        P(("members", "space"), None, None),
        P(),
        P("space"),
        P(),
        P("space", None, None),
        P("space", None),
        P("space", None, None),
        P("space", None),
    )
    return jax.shard_map(
        on_device,
        mesh=mesh,
        in_specs=placed,
        out_specs=P(("members", "space"), None),
        check_vma=False,
    )
```

```python
import functools
import math

import jax
import jax.numpy as jnp
import numpy as np
from jax import lax
from jax.experimental import pallas as pl
from jax.experimental.pallas import tpu as pltpu
from jax.sharding import PartitionSpec as P

DIRS = 36
FREQS = 36
COARSE = 4


gravity = 9.81
base_freq = 0.0418
freq_ratio = 1.1
freq_span = 35.0
input_coef = 0.0001
wind_gain = 1.12
dissip_coef = 0.0005
half_length = 300.0
courant_scale = 0.05


def from_root(array, axis, root):
    mine = lax.axis_index(axis) == root
    return lax.psum(jnp.where(mine, array, jnp.zeros_like(array)), axis)


def extended(array, sides, width):
    for axis, dim in sides:
        size, length = (lax.axis_size(axis), array.shape[dim])
        up = [(i, (i + 1) % size) for i in range(size - 1)]
        down = [(j, i) for i, j in up]
        last = lax.slice_in_dim(array, length - width, length, axis=dim)
        first = lax.slice_in_dim(array, 0, width, axis=dim)
        before = lax.ppermute(last, axis, up)
        after = lax.ppermute(first, axis, down)
        array = jnp.concatenate([before, array, after], axis=dim)
    return array


def spectral_tables():
    direction = 2.0 * math.pi / DIRS * jnp.arange(DIRS, dtype=jnp.float32)
    exponent = jnp.arange(FREQS, dtype=jnp.float32) * (freq_span / (FREQS - 1))
    frequency = base_freq * freq_ratio**exponent
    angular = 2.0 * math.pi * frequency
    phase_speed = gravity / angular
    return (jnp.cos(direction), jnp.sin(direction), angular, phase_speed, 0.5 * phase_speed)


def source_half(energy, wind_east, wind_north, coupling):
    cos_dir, sine_dir, angular, phase_speed, group_speed = spectral_tables()
    along_wind = wind_east[:, None] * cos_dir[None, :] + wind_north[:, None] * sine_dir[None, :]
    growth = (
        input_coef
        * angular[None, None, :]
        * jnp.maximum(wind_gain * along_wind[:, :, None] / phase_speed[None, None, :] - 1.0, 0.0)
    )
    growth = growth.reshape(energy.shape[0], -1)
    mean_square = jnp.mean(energy * energy, axis=1, keepdims=True)
    decay_rate = dissip_coef * jnp.tile(angular, DIRS)[None, :] * mean_square
    local_part = energy * (1.0 + half_length * growth) / (1.0 + half_length * decay_rate)
    return local_part + jnp.dot(
        local_part.astype(jnp.bfloat16), coupling, preferred_element_type=jnp.float32
    )


def advect(center, upwind_lo, upwind_hi, courant):
    ahead_part = jnp.maximum(courant, 0.0)
    behind = jnp.minimum(courant, 0.0)
    return center - ahead_part * (center - upwind_lo) - behind * (upwind_hi - center)


def sweep_cols(energy_grid, drift_east, wet_field):
    cos_dir, sine_dir, angular, phase_speed, group_speed = spectral_tables()
    wave_speed = (cos_dir[:, None] * group_speed[None, :]).reshape(-1)
    courant = (wave_speed[None, None, :] + drift_east[:, :, None]) * courant_scale
    zero_edge = jnp.zeros_like(energy_grid[:, :1])
    upwind_lo = jnp.concatenate([zero_edge, energy_grid[:, :-1]], axis=1)
    upwind_hi = jnp.concatenate([energy_grid[:, 1:], zero_edge], axis=1)
    return advect(energy_grid, upwind_lo, upwind_hi, courant) * wet_field[:, :, None]


def sweep_rows(energy_grid, row_above, row_below, drift_north, wet_field):
    cos_dir, sine_dir, angular, phase_speed, group_speed = spectral_tables()
    wave_speed = (sine_dir[:, None] * group_speed[None, :]).reshape(-1)
    courant = (wave_speed[None, None, :] + drift_north[:, :, None]) * courant_scale
    return advect(energy_grid, row_above, row_below, courant) * wet_field[:, :, None]


def forcing_points(row_start, row_count, col_count):
    rows_idx = row_start + jnp.arange(row_count, dtype=jnp.int32)
    cols_idx = jnp.arange(col_count, dtype=jnp.int32)
    return rows_idx[:, None] // COARSE * (col_count // COARSE) + cols_idx[None, :] // COARSE


def on_strips(
    spectra,
    wind_files,
    current_files,
    reader_turn,
    cell_point,
    coupling,
    send_list,
    send_count,
    recv_list,
    wet_mask,
):
    levels = []
    for time_level in range(2):
        levels.append(
            (
                from_root(wind_files[0], "space", reader_turn[time_level]),
                from_root(current_files[0], "space", reader_turn[time_level]),
            )
        )
    wind_mean = 0.5 * (levels[0][0] + levels[1][0])
    current_mean = 0.5 * (levels[0][1] + levels[1][1])
    cell_wind = jnp.take(wind_mean, cell_point, axis=1)
    first_half = source_half(spectra, cell_wind[0], cell_wind[1], coupling)
    send_rows = send_list[0]
    counts = send_count[0]
    places = recv_list[0]
    slot_count = send_rows.shape[1]
    spec_width = spectra.shape[1]
    live_slots = (jnp.arange(slot_count, dtype=jnp.int32)[None, :] < counts[:, None]).astype(
        jnp.float32
    )
    packed = first_half[send_rows] * live_slots[:, :, None]
    arrived = lax.all_to_all(packed, "space", split_axis=0, concat_axis=0, tiled=True)
    row_count = wet_mask.shape[0]
    col_count = wet_mask.shape[1]
    energy_grid = (
        jnp.zeros((row_count * col_count, spec_width), jnp.float32)
        .at[places.reshape(-1)]
        .add(arrived.reshape(-1, spec_width))
    )
    energy_grid = energy_grid.reshape(row_count, col_count, spec_width)
    points = forcing_points(lax.axis_index("space") * row_count, row_count, col_count)
    drift = jnp.take(current_mean, points, axis=1)
    wet_field = wet_mask.astype(jnp.float32)
    swept_cols = sweep_cols(energy_grid, drift[0], wet_field)
    padded = extended(swept_cols, (("space", 0),), 1)
    swept = sweep_rows(swept_cols, padded[:-2], padded[2:], drift[1], wet_field).reshape(
        -1, spec_width
    )
    outgoing = swept[places]
    flat_rows = send_rows.reshape(-1)
    empty_rows = jnp.zeros((spectra.shape[0], spec_width), jnp.float32)
    returned = lax.all_to_all(outgoing, "space", split_axis=0, concat_axis=0, tiled=True)
    back_rows = empty_rows.at[flat_rows].add(
        (returned * live_slots[:, :, None]).reshape(-1, spec_width)
    )
    result = source_half(back_rows, cell_wind[0], cell_wind[1], coupling)
    return result


LANES = 128
SUBS = 8
F32 = jnp.float32
BF16 = jnp.bfloat16
MIB = 1024 * 1024
WHOLE_VMEM = 60 * MIB
DRY = 1e30
PARTS = 4
PERIOD = 4 * FREQS


def wave_tables():
    direction = 2.0 * np.pi / DIRS * np.arange(DIRS)
    frequency = base_freq * freq_ratio ** (np.arange(FREQS) * (freq_span / (FREQS - 1)))
    angular = 2.0 * np.pi * frequency
    phase = gravity / angular
    group = 0.5 * phase
    cos_dir, sin_dir = np.cos(direction)[:, None], np.sin(direction)[:, None]
    flat = lambda t: np.broadcast_to(t, (DIRS, FREQS)).reshape(-1)
    growth = half_length * input_coef * angular
    source = np.zeros((DIRS * FREQS, 8), np.float32)
    source[:, 0] = flat(growth * wind_gain * cos_dir / phase)
    source[:, 1] = flat(growth * wind_gain * sin_dir / phase)
    source[:, 2] = flat(1.0 - growth)
    source[:, 3] = flat(half_length * dissip_coef * angular)
    east = flat(courant_scale * cos_dir * group).astype(np.float32)
    north = flat(courant_scale * sin_dir * group).astype(np.float32)
    return source, east, north


def ceil_to(value, step):
    return -(-value // step) * step


def largest_step(size, step, most):
    return max(s for s in range(step, most + 1, step) if size % s == 0)


class Plan:
    def __init__(self, shares, rows, spec, cap, strip_rows, cols, points):
        self.shares, self.rows, self.spec, self.cap = shares, rows, spec, cap
        self.cols, self.points = cols, points
        self.depth = spec // shares
        self.tiles = rows // LANES
        self.data = self.depth * self.tiles
        self.force = 2 * points // (LANES * shares)
        self.block = ceil_to(self.data + self.tiles + self.force, SUBS)
        self.tall = ceil_to(self.depth, SUBS)
        self.strip = strip_rows * cols
        self.grid_rows = strip_rows * shares
        self.coarse_rows = self.grid_rows // COARSE
        self.vregs = cols // SUBS
        self.size = (self.grid_rows + 2) * cols
        self.tall_step = largest_step(spec, PERIOD, 512)
        self.thirds = spec // self.tall_step

    def fits(self):
        if self.spec % self.shares or self.depth > LANES or self.rows % (2 * LANES):
            return False
        if 2 * self.points % (LANES * self.shares) or self.points % LANES or self.cap > LANES:
            return False
        if 2 * self.points // LANES > LANES or self.cols != LANES or self.shares % PARTS:
            return False
        held = 2 * self.size + 2 * self.points + self.shares * (self.block + self.data)
        return 4 * LANES * held + 4 * MIB < 32 * MIB


def pack_kernel(plan, turn_ref, wind_ref, current_ref, recv_ref, out_ref):
    me = lax.axis_index("space")
    half = lambda at: jnp.where(turn_ref[at] == me, 0.5, 0.0)
    mine = half(0) + half(1)
    wind = mine * wind_ref[0]
    points, width, cap = plan.points, plan.force * LANES, plan.cap
    for s in range(plan.shares):
        out_ref[s, :, 0:points] = wind
        out_ref[s, :, points:] = jnp.zeros((2, out_ref.shape[2] - points), F32)
        out_ref[s, 0:1, points : points + cap] = recv_ref[0, s : s + 1, :].astype(F32)
        which, first = divmod(s * width, points)
        out_ref[s, 1:2, points : points + width] = (
            mine * current_ref[0, which : which + 1, first : first + width]
        )


def cell_winds(wind, cp):
    points, rows = wind.shape[1], cp.shape[1]
    high = wind.astype(BF16).astype(F32)
    middle = (wind - high).astype(BF16).astype(F32)
    low = wind - high - middle
    parts = jnp.concatenate([high, middle, low, jnp.zeros((10, points), F32)], axis=0)
    point = lax.broadcasted_iota(jnp.int32, (points, rows), 0)
    hit = jnp.where(point == cp, 1.0, 0.0).astype(BF16)
    picked = jnp.dot(parts.astype(BF16), hit, preferred_element_type=F32)
    both = picked[0:2] + picked[2:4] + picked[4:6]
    return both[0:1], both[1:2]


def fetch(source, target, sems, parts):
    size = target.shape[0] // parts
    copies = [
        pltpu.make_async_copy(
            source.at[pl.ds(q * size, size), :], target.at[pl.ds(q * size, size), :], sems.at[q]
        )
        for q in range(parts)
    ]
    for copy in copies:
        copy.start()
    return copies


def unit_loss(plan, load, arrive, table_ref, unit_ref):
    tall = plan.spec // len(arrive)

    def squares(i, total):
        piece = load(pl.multiple_of(i * 48, 48), 48)
        return total + jnp.sum((piece * piece).reshape(48 // SUBS, SUBS, plan.rows), axis=0)

    total = jnp.zeros((SUBS, plan.rows), F32)
    for q, copy in enumerate(arrive):
        copy.wait()
        total = lax.fori_loop(q * tall // 48, (q + 1) * tall // 48, squares, total)
    mean_square = jnp.sum(total, axis=0, keepdims=True) * (1.0 / plan.spec)
    unit_ref[...] = 1.0 / (1.0 + table_ref[0:PERIOD, 3:4] * mean_square)


def growth_step(first, east, north, table_ref):
    table = table_ref[pl.ds(first, PERIOD), :]
    return jnp.maximum(east * table[:, 0:1] + north * table[:, 1:2] + table[:, 2:3], 1.0)


def coupled(plan, coup_ref, loc_ref, locb_ref, store):
    for q in range(plan.thirds):
        at = slice(q * plan.tall_step, (q + 1) * plan.tall_step)
        store(
            q * plan.tall_step,
            loc_ref[at, :]
            + jnp.dot(coup_ref[at, :], locb_ref[...], preferred_element_type=F32),
        )


def ready_kernel(
    plan, table_ref, coup_hbm, energy_hbm, turned_hbm, base_hbm,
    coup_ref, turned_ref, energy_ref, unit_ref, sems, coup_sem, out_sems,
):
    spec = plan.spec
    get = pltpu.make_async_copy(coup_hbm, coup_ref, coup_sem)
    get.start()
    arrive = fetch(energy_hbm, energy_ref, sems, plan.thirds)
    unit_loss(plan, lambda first, count: energy_ref[pl.ds(first, count), :], arrive, table_ref, unit_ref)

    @pl.loop(0, spec // PERIOD)
    def _(i):
        at = pl.ds(pl.multiple_of(i * PERIOD, PERIOD), PERIOD)
        energy_ref[at, :] = energy_ref[at, :] * unit_ref[...]

    put_base = pltpu.make_async_copy(energy_ref, base_hbm, out_sems.at[0])
    put_base.start()
    get.wait()
    for first in range(0, spec, LANES):
        at = slice(first, min(first + LANES, spec))
        turned_ref[at, :] = coup_ref[:, at].T
    put_turned = pltpu.make_async_copy(turned_ref, turned_hbm, out_sems.at[1])
    put_turned.start()
    put_base.wait()
    put_turned.wait()


def own_places(plan, parcel_ref, send_ref, count_ref):
    points, cols, vregs, cap = plan.points, plan.cols, plan.vregs, plan.cap
    landing = jnp.concatenate(
        [parcel_ref[b, 0:1, points : points + cap] for b in range(plan.shares)], axis=0
    ).astype(jnp.int32)
    cell = landing + plan.strip * lax.broadcasted_iota(jnp.int32, (plan.shares, cap), 0)
    column = lax.rem(cell, cols)
    place = cell - column + cols + lax.rem(column, vregs) * SUBS + lax.div(column, vregs)
    place = place.astype(F32)
    slot = lax.broadcasted_iota(jnp.int32, (1, cap), 1)
    names = [
        jnp.where(slot < count_ref[0, b], send_ref[0, b : b + 1, :], -1) for b in range(plan.shares)
    ]
    rows = []
    for j in range(plan.tiles):
        own = lax.broadcasted_iota(jnp.int32, (LANES, cap), 0) + j * LANES
        found = jnp.zeros((LANES, cap), F32)
        for b in range(plan.shares):
            found += jnp.where(names[b] == own, place[b : b + 1, :], 0.0)
        found = jnp.broadcast_to(jnp.sum(found, axis=1, keepdims=True), (LANES, LANES))
        rows.append(found.T[0:1, :])
    return rows


def first_kernel(
    plan,
    count_ref, cp_ref, parcel_ref, send_ref, table_ref, base_hbm, coup_hbm, winds_ref, out_hbm,
    out_ref, buf_ref, base_ref, coup_ref, locb_ref, sems, coup_sem, out_sems,
):
    tiles, shares, points, block, data = plan.tiles, plan.shares, plan.points, plan.block, plan.data
    arrive = fetch(base_hbm, base_ref, sems, plan.thirds)
    get = pltpu.make_async_copy(coup_hbm, coup_ref, coup_sem)
    get.start()
    width = plan.force * LANES
    current = jnp.sum(parcel_ref[:, :, points : points + width], axis=0)
    spare = own_places(plan, parcel_ref, send_ref, count_ref)
    spare += [current[1:2, f * LANES : (f + 1) * LANES] for f in range(plan.force)]
    if block > data + len(spare):
        spare.append(jnp.zeros((block - data - len(spare), LANES), F32))
    for d in range(shares):
        out_ref[d * block + data : (d + 1) * block, :] = jnp.concatenate(spare, axis=0)
    east, north = cell_winds(jnp.sum(parcel_ref[:, :, 0:points], axis=0), cp_ref[...])
    winds_ref[0:1, :] = east
    winds_ref[1:2, :] = north
    per = plan.tall_step // PERIOD
    for q in range(plan.thirds):
        arrive[q].wait()

        @pl.loop(q * per, (q + 1) * per)
        def _(i):
            first = pl.multiple_of(i * PERIOD, PERIOD)
            at = pl.ds(first, PERIOD)
            local = base_ref[at, :] * growth_step(first, east, north, table_ref)
            base_ref[at, :] = local
            locb_ref[at, :] = local.astype(BF16)

    get.wait()
    sent, copies = [0], []

    def store(first, values):
        for j in range(tiles):
            buf_ref[pl.ds(first * tiles + j, values.shape[0], stride=tiles), :] = values[
                :, j * LANES : (j + 1) * LANES
            ]
        upto = (first + values.shape[0]) // plan.depth
        for d in range(sent[0], upto):
            out_ref[d * block : d * block + data, :] = buf_ref[d * data : (d + 1) * data, :]
        at = slice(sent[0] * block, upto * block)
        copies.append(
            pltpu.make_async_copy(out_ref.at[at, :], out_hbm.at[at, :], out_sems.at[len(copies)])
        )
        copies[-1].start()
        sent[0] = upto

    coupled(plan, coup_ref, base_ref, locb_ref, store)
    for copy in copies:
        copy.wait()


def last_kernel(
    plan,
    winds_ref, table_ref, came_hbm, coup_hbm, out_hbm,
    came_ref, coup_ref, loc_ref, locb_ref, unit_ref, sems, coup_sem, out_sems,
):
    tiles = plan.tiles
    copies = []
    arrive = fetch(came_hbm, came_ref, sems, plan.thirds)
    get = pltpu.make_async_copy(coup_hbm, coup_ref, coup_sem)
    get.start()

    def load(first, count):
        start = pl.multiple_of(first * tiles, SUBS)
        return jnp.concatenate(
            [came_ref[pl.ds(start + j, count, stride=tiles), :] for j in range(tiles)], axis=1
        )

    unit_loss(plan, load, arrive, table_ref, unit_ref)
    east, north = winds_ref[0:1, :], winds_ref[1:2, :]

    @pl.loop(0, plan.spec // PERIOD)
    def _(i):
        first = pl.multiple_of(i * PERIOD, PERIOD)
        at = pl.ds(first, PERIOD)
        local = load(first, PERIOD) * unit_ref[...] * growth_step(first, east, north, table_ref)
        loc_ref[at, :] = local
        locb_ref[at, :] = local.astype(BF16)

    def store(first, values):
        at = slice(first, first + values.shape[0])
        loc_ref[at, :] = values
        copies.append(
            pltpu.make_async_copy(loc_ref.at[at, :], out_hbm.at[at, :], out_sems.at[len(copies)])
        )
        copies[-1].start()

    get.wait()
    coupled(plan, coup_ref, loc_ref, locb_ref, store)
    for copy in copies:
        copy.wait()


def scatter(plan, place_ref, came_ref, grid_ref, piece_refs, arrived):
    depth, tiles, tall, block = plan.depth, plan.tiles, plan.tall, plan.block
    blocks = plan.shares * tiles
    sub = lax.broadcasted_iota(jnp.int32, (SUBS, LANES), 0)

    def turn(i, piece_ref):
        s, j = i // tiles, i % tiles
        values = came_ref[pl.ds(s * block + j, depth, stride=tiles), :]
        if tall > depth:
            values = jnp.concatenate([values, jnp.zeros((tall - depth, LANES), F32)], axis=0)
        piece_ref[:, 0:tall] = values.T

    def put(i, piece_ref):
        for g in range(LANES // SUBS):
            values = piece_ref[g * SUBS : (g + 1) * SUBS, :]
            for t in range(SUBS):
                spot = place_ref[i * LANES + g * SUBS + t]
                pltpu.store(grid_ref.at[pl.ds(spot - t, SUBS), :], values, mask=sub == t)

    even_ref, odd_ref = piece_refs
    arrived(0)
    turn(0, even_ref)
    per = blocks // (2 * PARTS)

    @pl.loop(0, PARTS)
    def _(part):
        @pl.loop(0, per)
        def _(i):
            at = (part * per + i) * 2
            turn(at + 1, odd_ref)
            put(at, even_ref)

            @pl.when(jnp.logical_and(i == per - 1, part < PARTS - 1))
            def _():
                arrived(part + 1)

            turn(jnp.minimum(at + 2, blocks - 1), even_ref)
            put(at + 1, odd_ref)


def gather(plan, place_ref, out_ref, grid_ref, piece_refs, finished):
    depth, tiles, tall = plan.depth, plan.tiles, plan.tall
    blocks = plan.shares * tiles
    sub = lax.broadcasted_iota(jnp.int32, (SUBS, LANES), 0)

    def turn(i, piece_ref):
        s, j = i // tiles, i % tiles
        turned = piece_ref[:, 0:tall].T
        out_ref[pl.ds(s * plan.data + j, depth, stride=tiles), :] = turned[0:depth, :]

    def get(i, piece_ref):
        for g in range(LANES // SUBS):
            first = i * LANES + g * SUBS
            values = grid_ref[pl.ds(place_ref[first], SUBS), :]
            for t in range(1, SUBS):
                shifted = grid_ref[pl.ds(place_ref[first + t] - t, SUBS), :]
                values = jnp.where(sub == t, shifted, values)
            piece_ref[g * SUBS : (g + 1) * SUBS, :] = values

    even_ref, odd_ref = piece_refs
    get(0, even_ref)
    per = blocks // (2 * PARTS)

    @pl.loop(0, PARTS)
    def _(part):
        @pl.loop(0, per)
        def _(i):
            at = (part * per + i) * 2
            get(at + 1, odd_ref)
            turn(at, even_ref)
            get(jnp.minimum(at + 2, blocks - 1), even_ref)
            turn(at + 1, odd_ref)

        finished(part)


def spread_drift(plan, came_ref, piece_ref, wide_ref, drift_ref):
    piece_ref[...] = jnp.zeros((LANES, LANES), F32)
    for s in range(plan.shares):
        first = s * plan.block + plan.data + plan.tiles
        piece_ref[s * plan.force : (s + 1) * plan.force, :] = came_ref[
            first : first + plan.force, :
        ]
    turned = (courant_scale * piece_ref[...]).T
    groups = plan.vregs // COARSE
    for q in range(plan.shares * plan.force):
        wide_ref[...] = jnp.broadcast_to(turned[:, q : q + 1], (LANES, LANES))
        for a in range(LANES // (groups * SUBS)):
            for m in range(groups):
                to = q * LANES + (a * groups + m) * SUBS
                drift_ref[to : to + SUBS, :] = wide_ref[
                    pl.ds(a * groups * SUBS + m, SUBS, stride=groups), :
                ]


def sweep(plan, drift_ref, speed_ref, one_ref, two_ref):
    cols, last = plan.cols, plan.coarse_rows - 1
    groups = plan.vregs // COARSE
    sub = lax.broadcasted_iota(jnp.int32, (SUBS, LANES), 0)
    speeds = [jnp.broadcast_to(speed_ref[d : d + 1, :], (SUBS, LANES)) for d in range(2)]

    for m in range(groups):

        def courant(which, r4):
            at = pl.multiple_of(((which * plan.coarse_rows + r4) * groups + m) * SUBS, SUBS)
            value = speeds[which] + drift_ref[pl.ds(at, SUBS), :]
            return value > 0.0, jnp.abs(value)

        def at(row, q):
            return pl.ds(pl.multiple_of((row + 1) * cols + q * SUBS, SUBS), SUBS)

        def along(row, speed):
            ahead, size = speed
            base = pl.multiple_of((row + 1) * cols, SUBS)
            first, count = m * COARSE, COARSE
            line = [one_ref[at(row, q), :] for q in range(first, first + count)]
            if first:
                before = one_ref[at(row, first - 1), :]
            else:
                before = one_ref[pl.ds(base + cols - SUBS - 1, SUBS), :]
                before = jnp.where(sub == 0, DRY, before)
            if first + count < plan.vregs:
                after = one_ref[at(row, first + count), :]
            else:
                after = jnp.where(sub == SUBS - 1, DRY, one_ref[pl.ds(base + 1, SUBS), :])
            line = [before] + line + [after]
            swept = []
            for q in range(1, count + 1):
                pick = jnp.where(ahead, line[q - 1], line[q + 1])
                pick = jnp.where(pick < DRY, pick, 0.0)
                moved = line[q] + size * (pick - line[q])
                swept.append(jnp.where(line[q] < DRY, moved, 0.0))
            return swept

        def coarse(r4, held):
            above, here = held
            east = courant(0, r4)
            ahead, size = courant(1, r4)
            later = courant(0, jnp.minimum(r4 + 1, last))
            for dr in range(COARSE):
                row = r4 * COARSE + dr
                below = along(row + 1, east if dr < COARSE - 1 else later)
                for q in range(COARSE):
                    pick = jnp.where(ahead, above[q], below[q])
                    two_ref[at(row, m * COARSE + q), :] = here[q] + size * (pick - here[q])
                above, here = here, below
            return above, here

        zero = [jnp.zeros((SUBS, LANES), F32)] * COARSE
        lax.fori_loop(0, plan.coarse_rows, coarse, (zero, along(0, courant(0, 0))))


def middle_kernel(
    plan,
    place_ref, speed_ref, came_hbm, out_hbm,
    came_ref, out_ref, one_ref, two_ref, drift_ref, even_ref, odd_ref, in_sems, out_sems,
):
    shares, block, data = plan.shares, plan.block, plan.data
    part_in, part_out = shares // PARTS * block, shares // PARTS * data

    def copy_in(part):
        at = pl.ds(pl.multiple_of(part * part_in, SUBS), part_in)
        return pltpu.make_async_copy(came_hbm.at[at, :], came_ref.at[at, :], in_sems.at[part])

    def copy_out(part):
        at = pl.ds(pl.multiple_of(part * part_out, SUBS), part_out)
        return pltpu.make_async_copy(out_ref.at[at, :], out_hbm.at[at, :], out_sems.at[part])

    for part in range(PARTS):
        copy_in(part).start()

    @pl.loop(0, plan.size // LANES)
    def _(i):
        at = pl.ds(pl.multiple_of(i * LANES, LANES), LANES)
        one_ref[at, :] = jnp.full((LANES, LANES), DRY, F32)

    pieces = (even_ref, odd_ref)
    scatter(plan, place_ref, came_ref, one_ref, pieces, lambda part: copy_in(part).wait())
    spread_drift(plan, came_ref, even_ref, odd_ref, drift_ref)
    me = lax.axis_index("space")
    sweep(plan, drift_ref, speed_ref.at[me], one_ref, two_ref)
    gather(plan, place_ref, out_ref, two_ref, pieces, lambda part: copy_out(part).start())
    for part in range(PARTS):
        copy_out(part).wait()


VMEM = pl.BlockSpec(memory_space=pltpu.VMEM)
SMEM = pl.BlockSpec(memory_space=pltpu.SMEM)
ANY = pl.BlockSpec(memory_space=pl.ANY)


def on_spectrum(
    plan,
    spectra,
    wind_files,
    current_files,
    reader_turn,
    cell_point,
    coupling,
    send_list,
    send_count,
    recv_list,
):
    shares, rows, spec, points = plan.shares, plan.rows, plan.spec, plan.points
    tiles, depth, size, data_rows = plan.tiles, plan.depth, plan.size, plan.shares * plan.data
    source, east_speed, north_speed = wave_tables()
    table = jnp.asarray(source)
    speed = np.zeros((shares, SUBS, LANES), np.float32)
    speed[:, 0, :depth] = east_speed.reshape(shares, depth)
    speed[:, 1, :depth] = north_speed.reshape(shares, depth)

    def kernel(body, *, flops, traffic, vmem=WHOLE_VMEM, **options):
        return pl.pallas_call(
            body,
            compiler_params=pltpu.CompilerParams(vmem_limit_bytes=vmem),
            cost_estimate=pl.CostEstimate(flops=flops, bytes_accessed=traffic, transcendentals=0),
            **options,
        )

    width = points + max(LANES, plan.force * LANES)
    parcel = kernel(
        functools.partial(pack_kernel, plan),
        flops=0, traffic=4 * shares * 2 * width,
        out_shape=jax.ShapeDtypeStruct((shares, 2, width), F32),
        in_specs=[SMEM, VMEM, VMEM, VMEM],
        out_specs=VMEM,
        name="pack",
    )(reader_turn, wind_files, current_files, recv_list)
    parcel = lax.all_to_all(parcel, "space", 0, 0, tiled=True)

    cp = cell_point.reshape(1, rows)
    h_cost = dict(flops=2 * rows * spec * spec, traffic=12 * rows * spec)
    whole = pltpu.VMEM((spec, rows), F32)
    rounded = pltpu.VMEM((spec, rows), BF16)
    square = pltpu.VMEM((spec, spec), BF16)
    unit = pltpu.VMEM((PERIOD, rows), F32)
    dma = pltpu.SemaphoreType.DMA
    coup, base = kernel(
        functools.partial(ready_kernel, plan),
        flops=0, traffic=12 * rows * spec,
        out_shape=[
            jax.ShapeDtypeStruct((spec, spec), BF16), jax.ShapeDtypeStruct((spec, rows), F32)
        ],
        in_specs=[VMEM, ANY, ANY],
        out_specs=[ANY, ANY],
        scratch_shapes=[square, square, whole, unit, dma((plan.thirds,)), dma, dma((2,))],
        name="ready",
    )(table, coupling, spectra.T)
    winds, sent = kernel(
        functools.partial(first_kernel, plan),
        **h_cost,
        out_shape=[
            jax.ShapeDtypeStruct((SUBS, rows), F32),
            jax.ShapeDtypeStruct((shares * plan.block, LANES), F32),
        ],
        in_specs=[SMEM] + [VMEM] * 4 + [ANY] * 2,
        out_specs=[VMEM, ANY],
        scratch_shapes=[
            pltpu.VMEM((shares * plan.block, LANES), F32),
            pltpu.VMEM((data_rows, LANES), F32),
            whole, square, rounded, dma((plan.thirds,)), dma, dma((plan.thirds,)),
        ],
        name="first_half",
    )(send_count, cp, parcel, send_list, table, base, coup)
    came = lax.all_to_all(
        sent.reshape(shares, plan.block, LANES), "space", 0, 0, tiled=True
    )
    place = came[:, plan.data : plan.data + tiles].astype(jnp.int32).reshape(-1)
    swept = kernel(
        functools.partial(middle_kernel, plan),
        flops=24 * size * LANES, traffic=8 * rows * spec, vmem=32 * MIB,
        out_shape=jax.ShapeDtypeStruct((data_rows, LANES), F32),
        in_specs=[SMEM, VMEM, ANY],
        out_specs=ANY,
        scratch_shapes=[
            pltpu.VMEM((shares * plan.block, LANES), F32),
            pltpu.VMEM((data_rows, LANES), F32),
            pltpu.VMEM((size, LANES), F32),
            pltpu.VMEM((size, LANES), F32),
            pltpu.VMEM((2 * points, LANES), F32),
            pltpu.VMEM((LANES, LANES), F32),
            pltpu.VMEM((LANES, LANES), F32),
            pltpu.SemaphoreType.DMA((PARTS,)),
            pltpu.SemaphoreType.DMA((PARTS,)),
        ],
        name="sweeps",
    )(place, jnp.asarray(speed), came.reshape(-1, LANES))
    back = lax.all_to_all(
        swept.reshape(shares, depth, tiles, LANES), "space", 0, 0, tiled=True
    )
    result = kernel(
        functools.partial(last_kernel, plan),
        vmem=24 * MIB, **h_cost,
        out_shape=jax.ShapeDtypeStruct((spec, rows), F32),
        in_specs=[VMEM] * 2 + [ANY] * 2,
        out_specs=ANY,
        scratch_shapes=[
            pltpu.VMEM((data_rows, LANES), F32),
            square, whole, rounded, unit, dma((plan.thirds,)), dma, dma((plan.thirds,)),
        ],
        name="last_half",
    )(winds, table, back.reshape(data_rows, LANES), coup)
    return result.T


def on_device(*args):
    spectra, wind_files, send_list, wet_mask = args[0], args[1], args[6], args[9]
    plan = Plan(
        lax.axis_size("space"), *spectra.shape, send_list.shape[2], *wet_mask.shape, wind_files.shape[2]
    )
    if plan.fits():
        return on_spectrum(plan, *args[:9])
    return on_strips(*args)


def solution(mesh):
    placed = (
        P(("members", "space"), None),
        P(("members", "space"), None, None),
        P(("members", "space"), None, None),
        P(),
        P("space"),
        P(),
        P("space", None, None),
        P("space", None),
        P("space", None, None),
        P("space", None),
    )
    return jax.shard_map(
        on_device,
        mesh=mesh,
        in_specs=placed,
        out_specs=P(("members", "space"), None),
        check_vma=False,
    )
```

```python
import functools
import math

import jax
import jax.numpy as jnp
import numpy as np
from jax import lax
from jax.experimental import pallas as pl
from jax.experimental.pallas import tpu as pltpu
from jax.sharding import PartitionSpec as P

DIRS = 36
FREQS = 36
COARSE = 4


gravity = 9.81
base_freq = 0.0418
freq_ratio = 1.1
freq_span = 35.0
input_coef = 0.0001
wind_gain = 1.12
dissip_coef = 0.0005
half_length = 300.0
courant_scale = 0.05


def from_root(array, axis, root):
    mine = lax.axis_index(axis) == root
    return lax.psum(jnp.where(mine, array, jnp.zeros_like(array)), axis)


def extended(array, sides, width):
    for axis, dim in sides:
        size, length = (lax.axis_size(axis), array.shape[dim])
        up = [(i, (i + 1) % size) for i in range(size - 1)]
        down = [(j, i) for i, j in up]
        last = lax.slice_in_dim(array, length - width, length, axis=dim)
        first = lax.slice_in_dim(array, 0, width, axis=dim)
        before = lax.ppermute(last, axis, up)
        after = lax.ppermute(first, axis, down)
        array = jnp.concatenate([before, array, after], axis=dim)
    return array


def spectral_tables():
    direction = 2.0 * math.pi / DIRS * jnp.arange(DIRS, dtype=jnp.float32)
    exponent = jnp.arange(FREQS, dtype=jnp.float32) * (freq_span / (FREQS - 1))
    frequency = base_freq * freq_ratio**exponent
    angular = 2.0 * math.pi * frequency
    phase_speed = gravity / angular
    return (jnp.cos(direction), jnp.sin(direction), angular, phase_speed, 0.5 * phase_speed)


def source_half(energy, wind_east, wind_north, coupling):
    cos_dir, sine_dir, angular, phase_speed, group_speed = spectral_tables()
    along_wind = wind_east[:, None] * cos_dir[None, :] + wind_north[:, None] * sine_dir[None, :]
    growth = (
        input_coef
        * angular[None, None, :]
        * jnp.maximum(wind_gain * along_wind[:, :, None] / phase_speed[None, None, :] - 1.0, 0.0)
    )
    growth = growth.reshape(energy.shape[0], -1)
    mean_square = jnp.mean(energy * energy, axis=1, keepdims=True)
    decay_rate = dissip_coef * jnp.tile(angular, DIRS)[None, :] * mean_square
    local_part = energy * (1.0 + half_length * growth) / (1.0 + half_length * decay_rate)
    return local_part + jnp.dot(
        local_part.astype(jnp.bfloat16), coupling, preferred_element_type=jnp.float32
    )


def advect(center, upwind_lo, upwind_hi, courant):
    ahead_part = jnp.maximum(courant, 0.0)
    behind = jnp.minimum(courant, 0.0)
    return center - ahead_part * (center - upwind_lo) - behind * (upwind_hi - center)


def sweep_cols(energy_grid, drift_east, wet_field):
    cos_dir, sine_dir, angular, phase_speed, group_speed = spectral_tables()
    wave_speed = (cos_dir[:, None] * group_speed[None, :]).reshape(-1)
    courant = (wave_speed[None, None, :] + drift_east[:, :, None]) * courant_scale
    zero_edge = jnp.zeros_like(energy_grid[:, :1])
    upwind_lo = jnp.concatenate([zero_edge, energy_grid[:, :-1]], axis=1)
    upwind_hi = jnp.concatenate([energy_grid[:, 1:], zero_edge], axis=1)
    return advect(energy_grid, upwind_lo, upwind_hi, courant) * wet_field[:, :, None]


def sweep_rows(energy_grid, row_above, row_below, drift_north, wet_field):
    cos_dir, sine_dir, angular, phase_speed, group_speed = spectral_tables()
    wave_speed = (sine_dir[:, None] * group_speed[None, :]).reshape(-1)
    courant = (wave_speed[None, None, :] + drift_north[:, :, None]) * courant_scale
    return advect(energy_grid, row_above, row_below, courant) * wet_field[:, :, None]


def forcing_points(row_start, row_count, col_count):
    rows_idx = row_start + jnp.arange(row_count, dtype=jnp.int32)
    cols_idx = jnp.arange(col_count, dtype=jnp.int32)
    return rows_idx[:, None] // COARSE * (col_count // COARSE) + cols_idx[None, :] // COARSE


def on_strips(
    spectra,
    wind_files,
    current_files,
    reader_turn,
    cell_point,
    coupling,
    send_list,
    send_count,
    recv_list,
    wet_mask,
):
    levels = []
    for time_level in range(2):
        levels.append(
            (
                from_root(wind_files[0], "space", reader_turn[time_level]),
                from_root(current_files[0], "space", reader_turn[time_level]),
            )
        )
    wind_mean = 0.5 * (levels[0][0] + levels[1][0])
    current_mean = 0.5 * (levels[0][1] + levels[1][1])
    cell_wind = jnp.take(wind_mean, cell_point, axis=1)
    first_half = source_half(spectra, cell_wind[0], cell_wind[1], coupling)
    send_rows = send_list[0]
    counts = send_count[0]
    places = recv_list[0]
    slot_count = send_rows.shape[1]
    spec_width = spectra.shape[1]
    live_slots = (jnp.arange(slot_count, dtype=jnp.int32)[None, :] < counts[:, None]).astype(
        jnp.float32
    )
    packed = first_half[send_rows] * live_slots[:, :, None]
    arrived = lax.all_to_all(packed, "space", split_axis=0, concat_axis=0, tiled=True)
    row_count = wet_mask.shape[0]
    col_count = wet_mask.shape[1]
    energy_grid = (
        jnp.zeros((row_count * col_count, spec_width), jnp.float32)
        .at[places.reshape(-1)]
        .add(arrived.reshape(-1, spec_width))
    )
    energy_grid = energy_grid.reshape(row_count, col_count, spec_width)
    points = forcing_points(lax.axis_index("space") * row_count, row_count, col_count)
    drift = jnp.take(current_mean, points, axis=1)
    wet_field = wet_mask.astype(jnp.float32)
    swept_cols = sweep_cols(energy_grid, drift[0], wet_field)
    padded = extended(swept_cols, (("space", 0),), 1)
    swept = sweep_rows(swept_cols, padded[:-2], padded[2:], drift[1], wet_field).reshape(
        -1, spec_width
    )
    outgoing = swept[places]
    flat_rows = send_rows.reshape(-1)
    empty_rows = jnp.zeros((spectra.shape[0], spec_width), jnp.float32)
    returned = lax.all_to_all(outgoing, "space", split_axis=0, concat_axis=0, tiled=True)
    back_rows = empty_rows.at[flat_rows].add(
        (returned * live_slots[:, :, None]).reshape(-1, spec_width)
    )
    result = source_half(back_rows, cell_wind[0], cell_wind[1], coupling)
    return result


LANES = 128
SUBS = 8
F32 = jnp.float32
BF16 = jnp.bfloat16
MIB = 1024 * 1024
WHOLE_VMEM = 60 * MIB
DRY = 1e30
PARTS = 4
PERIOD = 4 * FREQS


def wave_tables():
    direction = 2.0 * np.pi / DIRS * np.arange(DIRS)
    frequency = base_freq * freq_ratio ** (np.arange(FREQS) * (freq_span / (FREQS - 1)))
    angular = 2.0 * np.pi * frequency
    phase = gravity / angular
    group = 0.5 * phase
    cos_dir, sin_dir = np.cos(direction)[:, None], np.sin(direction)[:, None]
    flat = lambda t: np.broadcast_to(t, (DIRS, FREQS)).reshape(-1)
    growth = half_length * input_coef * angular
    source = np.zeros((DIRS * FREQS, 8), np.float32)
    source[:, 0] = flat(growth * wind_gain * cos_dir / phase)
    source[:, 1] = flat(growth * wind_gain * sin_dir / phase)
    source[:, 2] = flat(1.0 - growth)
    source[:, 3] = flat(half_length * dissip_coef * angular)
    east = flat(courant_scale * cos_dir * group).astype(np.float32)
    north = flat(courant_scale * sin_dir * group).astype(np.float32)
    return source, east, north


def ceil_to(value, step):
    return -(-value // step) * step


def largest_step(size, step, most):
    return max(s for s in range(step, most + 1, step) if size % s == 0)


class Plan:
    def __init__(self, shares, rows, spec, cap, strip_rows, cols, points):
        self.shares, self.rows, self.spec, self.cap = shares, rows, spec, cap
        self.cols, self.points = cols, points
        self.depth = spec // shares
        self.tiles = rows // LANES
        self.data = self.depth * self.tiles
        self.force = 2 * points // (LANES * shares)
        self.block = ceil_to(self.data + self.tiles + self.force, SUBS)
        self.tall = ceil_to(self.depth, SUBS)
        self.strip = strip_rows * cols
        self.grid_rows = strip_rows * shares
        self.coarse_rows = self.grid_rows // COARSE
        self.vregs = cols // SUBS
        self.size = (self.grid_rows + 2) * cols
        self.tall_step = largest_step(spec, PERIOD, 512)
        self.thirds = spec // self.tall_step

    def fits(self):
        if self.spec % self.shares or self.depth > LANES or self.rows % (2 * LANES):
            return False
        if 2 * self.points % (LANES * self.shares) or self.points % LANES or self.cap > LANES:
            return False
        if 2 * self.points // LANES > LANES or self.cols != LANES or self.shares % PARTS:
            return False
        held = 2 * self.size + 2 * self.points + self.shares * (self.block + self.data)
        return 4 * LANES * held + 4 * MIB < 32 * MIB


def pack_kernel(plan, turn_ref, wind_ref, current_ref, recv_ref, out_ref):
    me = lax.axis_index("space")
    half = lambda at: jnp.where(turn_ref[at] == me, 0.5, 0.0)
    mine = half(0) + half(1)
    wind = mine * wind_ref[0]
    points, width, cap = plan.points, plan.force * LANES, plan.cap
    for s in range(plan.shares):
        out_ref[s, :, 0:points] = wind
        out_ref[s, :, points:] = jnp.zeros((2, out_ref.shape[2] - points), F32)
        out_ref[s, 0:1, points : points + cap] = recv_ref[0, s : s + 1, :].astype(F32)
        which, first = divmod(s * width, points)
        out_ref[s, 1:2, points : points + width] = (
            mine * current_ref[0, which : which + 1, first : first + width]
        )


def cell_winds(wind, cp):
    points, rows = wind.shape[1], cp.shape[1]
    high = wind.astype(BF16).astype(F32)
    middle = (wind - high).astype(BF16).astype(F32)
    low = wind - high - middle
    parts = jnp.concatenate([high, middle, low, jnp.zeros((10, points), F32)], axis=0)
    point = lax.broadcasted_iota(jnp.int32, (points, rows), 0)
    hit = jnp.where(point == cp, 1.0, 0.0).astype(BF16)
    picked = jnp.dot(parts.astype(BF16), hit, preferred_element_type=F32)
    both = picked[0:2] + picked[2:4] + picked[4:6]
    return both[0:1], both[1:2]


def fetch(source, target, sems, parts):
    size = target.shape[0] // parts
    copies = [
        pltpu.make_async_copy(
            source.at[pl.ds(q * size, size), :], target.at[pl.ds(q * size, size), :], sems.at[q]
        )
        for q in range(parts)
    ]
    for copy in copies:
        copy.start()
    return copies


def unit_loss(plan, load, arrive, table_ref, unit_ref):
    tall = plan.spec // len(arrive)

    def squares(i, total):
        piece = load(pl.multiple_of(i * 48, 48), 48)
        return total + jnp.sum((piece * piece).reshape(48 // SUBS, SUBS, plan.rows), axis=0)

    total = jnp.zeros((SUBS, plan.rows), F32)
    for q, copy in enumerate(arrive):
        copy.wait()
        total = lax.fori_loop(q * tall // 48, (q + 1) * tall // 48, squares, total)
    mean_square = jnp.sum(total, axis=0, keepdims=True) * (1.0 / plan.spec)
    unit_ref[...] = 1.0 / (1.0 + table_ref[0:PERIOD, 3:4] * mean_square)


def growth_step(first, east, north, table_ref):
    table = table_ref[pl.ds(first, PERIOD), :]
    return jnp.maximum(east * table[:, 0:1] + north * table[:, 1:2] + table[:, 2:3], 1.0)


def coupled(plan, coup_ref, loc_ref, locb_ref, store):
    for q in range(plan.thirds):
        at = slice(q * plan.tall_step, (q + 1) * plan.tall_step)
        store(
            q * plan.tall_step,
            loc_ref[at, :]
            + jnp.dot(coup_ref[at, :], locb_ref[...], preferred_element_type=F32),
        )


def ready_kernel(
    plan, table_ref, coup_hbm, energy_hbm, turned_hbm, base_hbm,
    coup_ref, turned_ref, energy_ref, unit_ref, sems, coup_sem, out_sems,
):
    spec = plan.spec
    get = pltpu.make_async_copy(coup_hbm, coup_ref, coup_sem)
    get.start()
    arrive = fetch(energy_hbm, energy_ref, sems, plan.thirds)
    unit_loss(plan, lambda first, count: energy_ref[pl.ds(first, count), :], arrive, table_ref, unit_ref)

    @pl.loop(0, spec // PERIOD)
    def _(i):
        at = pl.ds(pl.multiple_of(i * PERIOD, PERIOD), PERIOD)
        energy_ref[at, :] = energy_ref[at, :] * unit_ref[...]

    put_base = pltpu.make_async_copy(energy_ref, base_hbm, out_sems.at[0])
    put_base.start()
    get.wait()
    for first in range(0, spec, LANES):
        at = slice(first, min(first + LANES, spec))
        turned_ref[at, :] = coup_ref[:, at].T
    put_turned = pltpu.make_async_copy(turned_ref, turned_hbm, out_sems.at[1])
    put_turned.start()
    put_base.wait()
    put_turned.wait()


def own_places(plan, parcel_ref, send_ref, count_ref):
    points, cols, vregs, cap = plan.points, plan.cols, plan.vregs, plan.cap
    landing = jnp.concatenate(
        [parcel_ref[b, 0:1, points : points + cap] for b in range(plan.shares)], axis=0
    ).astype(jnp.int32)
    cell = landing + plan.strip * lax.broadcasted_iota(jnp.int32, (plan.shares, cap), 0)
    column = lax.rem(cell, cols)
    place = cell - column + cols + lax.rem(column, vregs) * SUBS + lax.div(column, vregs)
    place = place.astype(F32)
    slot = lax.broadcasted_iota(jnp.int32, (1, cap), 1)
    names = [
        jnp.where(slot < count_ref[0, b], send_ref[0, b : b + 1, :], -1) for b in range(plan.shares)
    ]
    rows = []
    for j in range(plan.tiles):
        own = lax.broadcasted_iota(jnp.int32, (LANES, cap), 0) + j * LANES
        found = jnp.zeros((LANES, cap), F32)
        for b in range(plan.shares):
            found += jnp.where(names[b] == own, place[b : b + 1, :], 0.0)
        found = jnp.broadcast_to(jnp.sum(found, axis=1, keepdims=True), (LANES, LANES))
        rows.append(found.T[0:1, :])
    return rows


def first_kernel(
    plan,
    count_ref, cp_ref, parcel_ref, send_ref, table_ref, base_hbm, coup_hbm, winds_ref, out_hbm,
    out_ref, buf_ref, base_ref, coup_ref, locb_ref, sems, coup_sem, out_sems,
):
    tiles, shares, points, block, data = plan.tiles, plan.shares, plan.points, plan.block, plan.data
    arrive = fetch(base_hbm, base_ref, sems, plan.thirds)
    get = pltpu.make_async_copy(coup_hbm, coup_ref, coup_sem)
    get.start()
    width = plan.force * LANES
    current = jnp.sum(parcel_ref[:, :, points : points + width], axis=0)
    spare = own_places(plan, parcel_ref, send_ref, count_ref)
    spare += [current[1:2, f * LANES : (f + 1) * LANES] for f in range(plan.force)]
    if block > data + len(spare):
        spare.append(jnp.zeros((block - data - len(spare), LANES), F32))
    for d in range(shares):
        out_ref[d * block + data : (d + 1) * block, :] = jnp.concatenate(spare, axis=0)
    east, north = cell_winds(jnp.sum(parcel_ref[:, :, 0:points], axis=0), cp_ref[...])
    winds_ref[0:1, :] = east
    winds_ref[1:2, :] = north
    per = plan.tall_step // PERIOD
    for q in range(plan.thirds):
        arrive[q].wait()

        @pl.loop(q * per, (q + 1) * per)
        def _(i):
            first = pl.multiple_of(i * PERIOD, PERIOD)
            at = pl.ds(first, PERIOD)
            local = base_ref[at, :] * growth_step(first, east, north, table_ref)
            base_ref[at, :] = local
            locb_ref[at, :] = local.astype(BF16)

    get.wait()
    sent, copies = [0], []

    def store(first, values):
        for j in range(tiles):
            buf_ref[pl.ds(first * tiles + j, values.shape[0], stride=tiles), :] = values[
                :, j * LANES : (j + 1) * LANES
            ]
        upto = (first + values.shape[0]) // plan.depth
        for d in range(sent[0], upto):
            out_ref[d * block : d * block + data, :] = buf_ref[d * data : (d + 1) * data, :]
        at = slice(sent[0] * block, upto * block)
        copies.append(
            pltpu.make_async_copy(out_ref.at[at, :], out_hbm.at[at, :], out_sems.at[len(copies)])
        )
        copies[-1].start()
        sent[0] = upto

    coupled(plan, coup_ref, base_ref, locb_ref, store)
    for copy in copies:
        copy.wait()


def last_kernel(
    plan,
    winds_ref, table_ref, came_hbm, coup_hbm, out_hbm,
    came_ref, coup_ref, loc_ref, locb_ref, unit_ref, sems, coup_sem, out_sems,
):
    tiles = plan.tiles
    copies = []
    arrive = fetch(came_hbm, came_ref, sems, plan.thirds)
    get = pltpu.make_async_copy(coup_hbm, coup_ref, coup_sem)
    get.start()

    def load(first, count):
        start = pl.multiple_of(first * tiles, SUBS)
        return jnp.concatenate(
            [came_ref[pl.ds(start + j, count, stride=tiles), :] for j in range(tiles)], axis=1
        )

    unit_loss(plan, load, arrive, table_ref, unit_ref)
    east, north = winds_ref[0:1, :], winds_ref[1:2, :]

    @pl.loop(0, plan.spec // PERIOD)
    def _(i):
        first = pl.multiple_of(i * PERIOD, PERIOD)
        at = pl.ds(first, PERIOD)
        local = load(first, PERIOD) * unit_ref[...] * growth_step(first, east, north, table_ref)
        loc_ref[at, :] = local
        locb_ref[at, :] = local.astype(BF16)

    def store(first, values):
        at = slice(first, first + values.shape[0])
        loc_ref[at, :] = values
        copies.append(
            pltpu.make_async_copy(loc_ref.at[at, :], out_hbm.at[at, :], out_sems.at[len(copies)])
        )
        copies[-1].start()

    get.wait()
    coupled(plan, coup_ref, loc_ref, locb_ref, store)
    for copy in copies:
        copy.wait()


def scatter(plan, place_ref, came_ref, grid_ref, piece_ref, arrived):
    depth, tiles, tall, block = plan.depth, plan.tiles, plan.tall, plan.block
    blocks = plan.shares * tiles

    def turn(i):
        s, j = i // tiles, i % tiles
        values = came_ref[pl.ds(s * block + j, depth, stride=tiles), :]
        if tall > depth:
            values = jnp.concatenate([values, jnp.zeros((tall - depth, LANES), F32)], axis=0)
        to = pl.ds(pl.multiple_of(i % 2 * LANES, LANES), LANES)
        piece_ref[to, 0:tall] = values.T

    def put(i):
        base = i % 2 * LANES
        for t in range(LANES):
            spot = place_ref[i * LANES + t]
            grid_ref[pl.ds(spot, 1), :] = piece_ref[pl.ds(base + t, 1), :]

    arrived(0)
    turn(0)
    per = blocks // PARTS

    @pl.loop(0, blocks)
    def _(i):
        @pl.when(jnp.logical_and(i % per == per - 1, i < blocks - 1))
        def _():
            arrived(i // per + 1)

        put(i)
        turn(jnp.minimum(i + 1, blocks - 1))


def gather(plan, place_ref, out_ref, grid_ref, piece_ref, finished):
    depth, tiles, tall = plan.depth, plan.tiles, plan.tall
    blocks = plan.shares * tiles

    def turn(i):
        s, j = i // tiles, i % tiles
        at = pl.ds(pl.multiple_of(i % 2 * LANES, LANES), LANES)
        turned = piece_ref[at, 0:tall].T
        out_ref[pl.ds(s * plan.data + j, depth, stride=tiles), :] = turned[0:depth, :]

    def get(i, row):
        base = i % 2 * LANES
        for t in range(LANES):
            spot = place_ref[row * LANES + t]
            piece_ref[pl.ds(base + t, 1), :] = grid_ref[pl.ds(spot, 1), :]

    get(0, 0)
    per = blocks // PARTS

    @pl.loop(0, blocks)
    def _(i):
        turn(i)
        get(i + 1, jnp.minimum(i + 1, blocks - 1))

        @pl.when(i % per == per - 1)
        def _():
            finished(i // per)


def spread_drift(plan, came_ref, piece_ref, drift_ref):
    held, turned = piece_ref.at[0:LANES], piece_ref.at[LANES : 2 * LANES]
    held[...] = jnp.zeros((LANES, LANES), F32)
    for s in range(plan.shares):
        first = s * plan.block + plan.data + plan.tiles
        held[s * plan.force : (s + 1) * plan.force, :] = came_ref[first : first + plan.force, :]
    turned[...] = (courant_scale * held[...]).T
    groups = plan.vregs // COARSE
    ordered = jnp.concatenate(
        [
            turned[pl.ds(a * groups * SUBS + m, SUBS, stride=groups), :]
            for a in range(LANES // (groups * SUBS))
            for m in range(groups)
        ],
        axis=0,
    )
    for q in range(plan.shares * plan.force):
        drift_ref[q * LANES : (q + 1) * LANES, :] = jnp.broadcast_to(
            ordered[:, q : q + 1], (LANES, LANES)
        )


def sweep(plan, drift_ref, speed_ref, one_ref, two_ref):
    cols, last = plan.cols, plan.coarse_rows - 1
    groups = plan.vregs // COARSE
    sub = lax.broadcasted_iota(jnp.int32, (SUBS, LANES), 0)
    speeds = [jnp.broadcast_to(speed_ref[d : d + 1, :], (SUBS, LANES)) for d in range(2)]

    for m in range(groups):

        def courant(which, r4):
            at = pl.multiple_of(((which * plan.coarse_rows + r4) * groups + m) * SUBS, SUBS)
            value = speeds[which] + drift_ref[pl.ds(at, SUBS), :]
            return value > 0.0, jnp.abs(value)

        def at(row, q):
            return pl.ds(pl.multiple_of((row + 1) * cols + q * SUBS, SUBS), SUBS)

        def along(row, speed):
            ahead, size = speed
            base = pl.multiple_of((row + 1) * cols, SUBS)
            first, count = m * COARSE, COARSE
            line = [one_ref[at(row, q), :] for q in range(first, first + count)]
            if first:
                before = one_ref[at(row, first - 1), :]
            else:
                before = one_ref[pl.ds(base + cols - SUBS - 1, SUBS), :]
                before = jnp.where(sub == 0, DRY, before)
            if first + count < plan.vregs:
                after = one_ref[at(row, first + count), :]
            else:
                after = jnp.where(sub == SUBS - 1, DRY, one_ref[pl.ds(base + 1, SUBS), :])
            line = [before] + line + [after]
            swept = []
            for q in range(1, count + 1):
                pick = jnp.where(ahead, line[q - 1], line[q + 1])
                pick = jnp.where(pick < DRY, pick, 0.0)
                moved = line[q] + size * (pick - line[q])
                swept.append(jnp.where(line[q] < DRY, moved, 0.0))
            return swept

        def coarse(r4, held):
            above, here = held
            east = courant(0, r4)
            ahead, size = courant(1, r4)
            later = courant(0, jnp.minimum(r4 + 1, last))
            for dr in range(COARSE):
                row = r4 * COARSE + dr
                below = along(row + 1, east if dr < COARSE - 1 else later)
                for q in range(COARSE):
                    pick = jnp.where(ahead, above[q], below[q])
                    two_ref[at(row, m * COARSE + q), :] = here[q] + size * (pick - here[q])
                above, here = here, below
            return above, here

        zero = [jnp.zeros((SUBS, LANES), F32)] * COARSE
        lax.fori_loop(0, plan.coarse_rows, coarse, (zero, along(0, courant(0, 0))), unroll=2)


def middle_kernel(
    plan,
    place_ref, speed_ref, came_hbm, out_hbm,
    came_ref, out_ref, one_ref, two_ref, drift_ref, piece_ref, in_sems, out_sems,
):
    shares, block, data = plan.shares, plan.block, plan.data
    part_in, part_out = shares // PARTS * block, shares // PARTS * data

    def copy_in(part):
        at = pl.ds(pl.multiple_of(part * part_in, SUBS), part_in)
        return pltpu.make_async_copy(came_hbm.at[at, :], came_ref.at[at, :], in_sems.at[part])

    def copy_out(part):
        at = pl.ds(pl.multiple_of(part * part_out, SUBS), part_out)
        return pltpu.make_async_copy(out_ref.at[at, :], out_hbm.at[at, :], out_sems.at[part])

    for part in range(PARTS):
        copy_in(part).start()

    @pl.loop(0, plan.size // LANES)
    def _(i):
        at = pl.ds(pl.multiple_of(i * LANES, LANES), LANES)
        one_ref[at, :] = jnp.full((LANES, LANES), DRY, F32)

    scatter(plan, place_ref, came_ref, one_ref, piece_ref, lambda part: copy_in(part).wait())
    spread_drift(plan, came_ref, piece_ref, drift_ref)
    me = lax.axis_index("space")
    sweep(plan, drift_ref, speed_ref.at[me], one_ref, two_ref)
    gather(plan, place_ref, out_ref, two_ref, piece_ref, lambda part: copy_out(part).start())
    for part in range(PARTS):
        copy_out(part).wait()


VMEM = pl.BlockSpec(memory_space=pltpu.VMEM)
SMEM = pl.BlockSpec(memory_space=pltpu.SMEM)
ANY = pl.BlockSpec(memory_space=pl.ANY)


def on_spectrum(
    plan,
    spectra,
    wind_files,
    current_files,
    reader_turn,
    cell_point,
    coupling,
    send_list,
    send_count,
    recv_list,
):
    shares, rows, spec, points = plan.shares, plan.rows, plan.spec, plan.points
    tiles, depth, size, data_rows = plan.tiles, plan.depth, plan.size, plan.shares * plan.data
    source, east_speed, north_speed = wave_tables()
    table = jnp.asarray(source)
    speed = np.zeros((shares, SUBS, LANES), np.float32)
    speed[:, 0, :depth] = east_speed.reshape(shares, depth)
    speed[:, 1, :depth] = north_speed.reshape(shares, depth)

    def kernel(body, *, flops, traffic, vmem=WHOLE_VMEM, **options):
        return pl.pallas_call(
            body,
            compiler_params=pltpu.CompilerParams(vmem_limit_bytes=vmem),
            cost_estimate=pl.CostEstimate(flops=flops, bytes_accessed=traffic, transcendentals=0),
            **options,
        )

    width = points + max(LANES, plan.force * LANES)
    parcel = kernel(
        functools.partial(pack_kernel, plan),
        flops=0, traffic=4 * shares * 2 * width,
        out_shape=jax.ShapeDtypeStruct((shares, 2, width), F32),
        in_specs=[SMEM, VMEM, VMEM, VMEM],
        out_specs=VMEM,
        name="pack",
    )(reader_turn, wind_files, current_files, recv_list)
    parcel = lax.all_to_all(parcel, "space", 0, 0, tiled=True)

    cp = cell_point.reshape(1, rows)
    h_cost = dict(flops=2 * rows * spec * spec, traffic=12 * rows * spec)
    whole = pltpu.VMEM((spec, rows), F32)
    rounded = pltpu.VMEM((spec, rows), BF16)
    square = pltpu.VMEM((spec, spec), BF16)
    unit = pltpu.VMEM((PERIOD, rows), F32)
    dma = pltpu.SemaphoreType.DMA
    coup, base = kernel(
        functools.partial(ready_kernel, plan),
        flops=0, traffic=12 * rows * spec,
        out_shape=[
            jax.ShapeDtypeStruct((spec, spec), BF16), jax.ShapeDtypeStruct((spec, rows), F32)
        ],
        in_specs=[VMEM, ANY, ANY],
        out_specs=[ANY, ANY],
        scratch_shapes=[square, square, whole, unit, dma((plan.thirds,)), dma, dma((2,))],
        name="ready",
    )(table, coupling, spectra.T)
    winds, sent = kernel(
        functools.partial(first_kernel, plan),
        **h_cost,
        out_shape=[
            jax.ShapeDtypeStruct((SUBS, rows), F32),
            jax.ShapeDtypeStruct((shares * plan.block, LANES), F32),
        ],
        in_specs=[SMEM] + [VMEM] * 4 + [ANY] * 2,
        out_specs=[VMEM, ANY],
        scratch_shapes=[
            pltpu.VMEM((shares * plan.block, LANES), F32),
            pltpu.VMEM((data_rows, LANES), F32),
            whole, square, rounded, dma((plan.thirds,)), dma, dma((plan.thirds,)),
        ],
        name="first_half",
    )(send_count, cp, parcel, send_list, table, base, coup)
    came = lax.all_to_all(
        sent.reshape(shares, plan.block, LANES), "space", 0, 0, tiled=True
    )
    place = came[:, plan.data : plan.data + tiles].astype(jnp.int32).reshape(-1)
    swept = kernel(
        functools.partial(middle_kernel, plan),
        flops=24 * size * LANES, traffic=8 * rows * spec, vmem=32 * MIB,
        out_shape=jax.ShapeDtypeStruct((data_rows, LANES), F32),
        in_specs=[SMEM, VMEM, ANY],
        out_specs=ANY,
        scratch_shapes=[
            pltpu.VMEM((shares * plan.block, LANES), F32),
            pltpu.VMEM((data_rows, LANES), F32),
            pltpu.VMEM((size, LANES), F32),
            pltpu.VMEM((size, LANES), F32),
            pltpu.VMEM((2 * points, LANES), F32),
            pltpu.VMEM((2 * LANES, LANES), F32),
            pltpu.SemaphoreType.DMA((PARTS,)),
            pltpu.SemaphoreType.DMA((PARTS,)),
        ],
        name="sweeps",
    )(place, jnp.asarray(speed), came.reshape(-1, LANES))
    back = lax.all_to_all(
        swept.reshape(shares, depth, tiles, LANES), "space", 0, 0, tiled=True
    )
    result = kernel(
        functools.partial(last_kernel, plan),
        vmem=24 * MIB, **h_cost,
        out_shape=jax.ShapeDtypeStruct((spec, rows), F32),
        in_specs=[VMEM] * 2 + [ANY] * 2,
        out_specs=ANY,
        scratch_shapes=[
            pltpu.VMEM((data_rows, LANES), F32),
            square, whole, rounded, unit, dma((plan.thirds,)), dma, dma((plan.thirds,)),
        ],
        name="last_half",
    )(winds, table, back.reshape(data_rows, LANES), coup)
    return result.T


def on_device(*args):
    spectra, wind_files, send_list, wet_mask = args[0], args[1], args[6], args[9]
    plan = Plan(
        lax.axis_size("space"), *spectra.shape, send_list.shape[2], *wet_mask.shape, wind_files.shape[2]
    )
    if plan.fits():
        return on_spectrum(plan, *args[:9])
    return on_strips(*args)


def solution(mesh):
    placed = (
        P(("members", "space"), None),
        P(("members", "space"), None, None),
        P(("members", "space"), None, None),
        P(),
        P("space"),
        P(),
        P("space", None, None),
        P("space", None),
        P("space", None, None),
        P("space", None),
    )
    return jax.shard_map(
        on_device,
        mesh=mesh,
        in_specs=placed,
        out_specs=P(("members", "space"), None),
        check_vma=False,
    )
```

```python
import functools
import math

import jax
import jax.numpy as jnp
import numpy as np
from jax import lax
from jax.experimental import pallas as pl
from jax.experimental.pallas import tpu as pltpu
from jax.sharding import PartitionSpec as P

DIRS = 36
FREQS = 36
COARSE = 4


gravity = 9.81
base_freq = 0.0418
freq_ratio = 1.1
freq_span = 35.0
input_coef = 0.0001
wind_gain = 1.12
dissip_coef = 0.0005
half_length = 300.0
courant_scale = 0.05


def from_root(array, axis, root):
    mine = lax.axis_index(axis) == root
    return lax.psum(jnp.where(mine, array, jnp.zeros_like(array)), axis)


def extended(array, sides, width):
    for axis, dim in sides:
        size, length = (lax.axis_size(axis), array.shape[dim])
        up = [(i, (i + 1) % size) for i in range(size - 1)]
        down = [(j, i) for i, j in up]
        last = lax.slice_in_dim(array, length - width, length, axis=dim)
        first = lax.slice_in_dim(array, 0, width, axis=dim)
        before = lax.ppermute(last, axis, up)
        after = lax.ppermute(first, axis, down)
        array = jnp.concatenate([before, array, after], axis=dim)
    return array


def spectral_tables():
    direction = 2.0 * math.pi / DIRS * jnp.arange(DIRS, dtype=jnp.float32)
    exponent = jnp.arange(FREQS, dtype=jnp.float32) * (freq_span / (FREQS - 1))
    frequency = base_freq * freq_ratio**exponent
    angular = 2.0 * math.pi * frequency
    phase_speed = gravity / angular
    return (jnp.cos(direction), jnp.sin(direction), angular, phase_speed, 0.5 * phase_speed)


def source_half(energy, wind_east, wind_north, coupling):
    cos_dir, sine_dir, angular, phase_speed, group_speed = spectral_tables()
    along_wind = wind_east[:, None] * cos_dir[None, :] + wind_north[:, None] * sine_dir[None, :]
    growth = (
        input_coef
        * angular[None, None, :]
        * jnp.maximum(wind_gain * along_wind[:, :, None] / phase_speed[None, None, :] - 1.0, 0.0)
    )
    growth = growth.reshape(energy.shape[0], -1)
    mean_square = jnp.mean(energy * energy, axis=1, keepdims=True)
    decay_rate = dissip_coef * jnp.tile(angular, DIRS)[None, :] * mean_square
    local_part = energy * (1.0 + half_length * growth) / (1.0 + half_length * decay_rate)
    return local_part + jnp.dot(
        local_part.astype(jnp.bfloat16), coupling, preferred_element_type=jnp.float32
    )


def advect(center, upwind_lo, upwind_hi, courant):
    ahead_part = jnp.maximum(courant, 0.0)
    behind = jnp.minimum(courant, 0.0)
    return center - ahead_part * (center - upwind_lo) - behind * (upwind_hi - center)


def sweep_cols(energy_grid, drift_east, wet_field):
    cos_dir, sine_dir, angular, phase_speed, group_speed = spectral_tables()
    wave_speed = (cos_dir[:, None] * group_speed[None, :]).reshape(-1)
    courant = (wave_speed[None, None, :] + drift_east[:, :, None]) * courant_scale
    zero_edge = jnp.zeros_like(energy_grid[:, :1])
    upwind_lo = jnp.concatenate([zero_edge, energy_grid[:, :-1]], axis=1)
    upwind_hi = jnp.concatenate([energy_grid[:, 1:], zero_edge], axis=1)
    return advect(energy_grid, upwind_lo, upwind_hi, courant) * wet_field[:, :, None]


def sweep_rows(energy_grid, row_above, row_below, drift_north, wet_field):
    cos_dir, sine_dir, angular, phase_speed, group_speed = spectral_tables()
    wave_speed = (sine_dir[:, None] * group_speed[None, :]).reshape(-1)
    courant = (wave_speed[None, None, :] + drift_north[:, :, None]) * courant_scale
    return advect(energy_grid, row_above, row_below, courant) * wet_field[:, :, None]


def forcing_points(row_start, row_count, col_count):
    rows_idx = row_start + jnp.arange(row_count, dtype=jnp.int32)
    cols_idx = jnp.arange(col_count, dtype=jnp.int32)
    return rows_idx[:, None] // COARSE * (col_count // COARSE) + cols_idx[None, :] // COARSE


def on_strips(
    spectra,
    wind_files,
    current_files,
    reader_turn,
    cell_point,
    coupling,
    send_list,
    send_count,
    recv_list,
    wet_mask,
):
    levels = []
    for time_level in range(2):
        levels.append(
            (
                from_root(wind_files[0], "space", reader_turn[time_level]),
                from_root(current_files[0], "space", reader_turn[time_level]),
            )
        )
    wind_mean = 0.5 * (levels[0][0] + levels[1][0])
    current_mean = 0.5 * (levels[0][1] + levels[1][1])
    cell_wind = jnp.take(wind_mean, cell_point, axis=1)
    first_half = source_half(spectra, cell_wind[0], cell_wind[1], coupling)
    send_rows = send_list[0]
    counts = send_count[0]
    places = recv_list[0]
    slot_count = send_rows.shape[1]
    spec_width = spectra.shape[1]
    live_slots = (jnp.arange(slot_count, dtype=jnp.int32)[None, :] < counts[:, None]).astype(
        jnp.float32
    )
    packed = first_half[send_rows] * live_slots[:, :, None]
    arrived = lax.all_to_all(packed, "space", split_axis=0, concat_axis=0, tiled=True)
    row_count = wet_mask.shape[0]
    col_count = wet_mask.shape[1]
    energy_grid = (
        jnp.zeros((row_count * col_count, spec_width), jnp.float32)
        .at[places.reshape(-1)]
        .add(arrived.reshape(-1, spec_width))
    )
    energy_grid = energy_grid.reshape(row_count, col_count, spec_width)
    points = forcing_points(lax.axis_index("space") * row_count, row_count, col_count)
    drift = jnp.take(current_mean, points, axis=1)
    wet_field = wet_mask.astype(jnp.float32)
    swept_cols = sweep_cols(energy_grid, drift[0], wet_field)
    padded = extended(swept_cols, (("space", 0),), 1)
    swept = sweep_rows(swept_cols, padded[:-2], padded[2:], drift[1], wet_field).reshape(
        -1, spec_width
    )
    outgoing = swept[places]
    flat_rows = send_rows.reshape(-1)
    empty_rows = jnp.zeros((spectra.shape[0], spec_width), jnp.float32)
    returned = lax.all_to_all(outgoing, "space", split_axis=0, concat_axis=0, tiled=True)
    back_rows = empty_rows.at[flat_rows].add(
        (returned * live_slots[:, :, None]).reshape(-1, spec_width)
    )
    result = source_half(back_rows, cell_wind[0], cell_wind[1], coupling)
    return result


LANES = 128
SUBS = 8
F32 = jnp.float32
BF16 = jnp.bfloat16
MIB = 1024 * 1024
WHOLE_VMEM = 60 * MIB
DRY = 1e30
PARTS = 4
PERIOD = 4 * FREQS


def wave_tables():
    direction = 2.0 * np.pi / DIRS * np.arange(DIRS)
    frequency = base_freq * freq_ratio ** (np.arange(FREQS) * (freq_span / (FREQS - 1)))
    angular = 2.0 * np.pi * frequency
    phase = gravity / angular
    group = 0.5 * phase
    cos_dir, sin_dir = np.cos(direction)[:, None], np.sin(direction)[:, None]
    flat = lambda t: np.broadcast_to(t, (DIRS, FREQS)).reshape(-1)
    growth = half_length * input_coef * angular
    source = np.zeros((DIRS * FREQS, 8), np.float32)
    source[:, 0] = flat(growth * wind_gain * cos_dir / phase)
    source[:, 1] = flat(growth * wind_gain * sin_dir / phase)
    source[:, 2] = flat(1.0 - growth)
    source[:, 3] = flat(half_length * dissip_coef * angular)
    east = flat(courant_scale * cos_dir * group).astype(np.float32)
    north = flat(courant_scale * sin_dir * group).astype(np.float32)
    return source, east, north


def ceil_to(value, step):
    return -(-value // step) * step


def largest_step(size, step, most):
    return max(s for s in range(step, most + 1, step) if size % s == 0)


class Plan:
    def __init__(self, shares, rows, spec, cap, strip_rows, cols, points):
        self.shares, self.rows, self.spec, self.cap = shares, rows, spec, cap
        self.cols, self.points = cols, points
        self.depth = spec // shares
        self.tiles = rows // LANES
        self.data = self.depth * self.tiles
        self.force = 2 * points // (LANES * shares)
        self.block = ceil_to(self.data + self.tiles + self.force, SUBS)
        self.tall = ceil_to(self.depth, SUBS)
        self.strip = strip_rows * cols
        self.grid_rows = strip_rows * shares
        self.coarse_rows = self.grid_rows // COARSE
        self.vregs = cols // SUBS
        self.size = (self.grid_rows + 2) * cols
        self.tall_step = largest_step(spec, PERIOD, 512)
        self.thirds = spec // self.tall_step

    def fits(self):
        if self.spec % self.shares or self.depth > LANES or self.rows % (2 * LANES):
            return False
        if 2 * self.points % (LANES * self.shares) or self.points % LANES or self.cap > LANES:
            return False
        if 2 * self.points // LANES > LANES or self.cols != LANES or self.shares % PARTS:
            return False
        held = 2 * self.size + 2 * self.points + self.shares * (self.block + self.data)
        return 4 * LANES * held + 4 * MIB < 32 * MIB


def pack_kernel(plan, turn_ref, wind_ref, current_ref, recv_ref, out_ref):
    me = lax.axis_index("space")
    half = lambda at: jnp.where(turn_ref[at] == me, 0.5, 0.0)
    mine = half(0) + half(1)
    wind = mine * wind_ref[0]
    points, width, cap = plan.points, plan.force * LANES, plan.cap
    for s in range(plan.shares):
        out_ref[s, :, 0:points] = wind
        out_ref[s, :, points:] = jnp.zeros((2, out_ref.shape[2] - points), F32)
        out_ref[s, 0:1, points : points + cap] = recv_ref[0, s : s + 1, :].astype(F32)
        which, first = divmod(s * width, points)
        out_ref[s, 1:2, points : points + width] = (
            mine * current_ref[0, which : which + 1, first : first + width]
        )


def cell_winds(wind, cp):
    points, rows = wind.shape[1], cp.shape[1]
    high = wind.astype(BF16).astype(F32)
    middle = (wind - high).astype(BF16).astype(F32)
    low = wind - high - middle
    parts = jnp.concatenate([high, middle, low, jnp.zeros((10, points), F32)], axis=0)
    point = lax.broadcasted_iota(jnp.int32, (points, rows), 0)
    hit = jnp.where(point == cp, 1.0, 0.0).astype(BF16)
    picked = jnp.dot(parts.astype(BF16), hit, preferred_element_type=F32)
    both = picked[0:2] + picked[2:4] + picked[4:6]
    return both[0:1], both[1:2]


def fetch(source, target, sems, parts):
    size = target.shape[0] // parts
    copies = [
        pltpu.make_async_copy(
            source.at[pl.ds(q * size, size), :], target.at[pl.ds(q * size, size), :], sems.at[q]
        )
        for q in range(parts)
    ]
    for copy in copies:
        copy.start()
    return copies


def unit_loss(plan, load, arrive, table_ref, unit_ref):
    tall = plan.spec // len(arrive)

    def squares(i, total):
        piece = load(pl.multiple_of(i * 48, 48), 48)
        return total + jnp.sum((piece * piece).reshape(48 // SUBS, SUBS, plan.rows), axis=0)

    total = jnp.zeros((SUBS, plan.rows), F32)
    for q, copy in enumerate(arrive):
        copy.wait()
        total = lax.fori_loop(q * tall // 48, (q + 1) * tall // 48, squares, total)
    mean_square = jnp.sum(total, axis=0, keepdims=True) * (1.0 / plan.spec)
    unit_ref[...] = 1.0 / (1.0 + table_ref[0:PERIOD, 3:4] * mean_square)


def growth_step(first, east, north, table_ref):
    table = table_ref[pl.ds(first, PERIOD), :]
    return jnp.maximum(east * table[:, 0:1] + north * table[:, 1:2] + table[:, 2:3], 1.0)


def coupled(plan, coup_ref, loc_ref, locb_ref, store):
    for q in range(plan.thirds):
        at = slice(q * plan.tall_step, (q + 1) * plan.tall_step)
        store(
            q * plan.tall_step,
            loc_ref[at, :]
            + jnp.dot(coup_ref[at, :], locb_ref[...], preferred_element_type=F32),
        )


def ready_kernel(
    plan, table_ref, coup_hbm, energy_hbm, turned_ref, base_ref,
    coup_ref, energy_ref, unit_ref, sems, coup_sem,
):
    spec = plan.spec
    get = pltpu.make_async_copy(coup_hbm, coup_ref, coup_sem)
    get.start()
    arrive = fetch(energy_hbm, energy_ref, sems, plan.thirds)
    unit_loss(plan, lambda first, count: energy_ref[pl.ds(first, count), :], arrive, table_ref, unit_ref)

    @pl.loop(0, spec // PERIOD)
    def _(i):
        at = pl.ds(pl.multiple_of(i * PERIOD, PERIOD), PERIOD)
        base_ref[at, :] = energy_ref[at, :] * unit_ref[...]

    get.wait()
    for first in range(0, spec, LANES):
        at = slice(first, min(first + LANES, spec))
        turned_ref[at, :] = coup_ref[:, at].T


def own_places(plan, parcel_ref, send_ref, count_ref):
    points, cols, vregs, cap = plan.points, plan.cols, plan.vregs, plan.cap
    landing = jnp.concatenate(
        [parcel_ref[b, 0:1, points : points + cap] for b in range(plan.shares)], axis=0
    ).astype(jnp.int32)
    cell = landing + plan.strip * lax.broadcasted_iota(jnp.int32, (plan.shares, cap), 0)
    column = lax.rem(cell, cols)
    place = cell - column + cols + lax.rem(column, vregs) * SUBS + lax.div(column, vregs)
    place = place.astype(F32)
    slot = lax.broadcasted_iota(jnp.int32, (1, cap), 1)
    names = [
        jnp.where(slot < count_ref[0, b], send_ref[0, b : b + 1, :], -1) for b in range(plan.shares)
    ]
    rows = []
    for j in range(plan.tiles):
        own = lax.broadcasted_iota(jnp.int32, (LANES, cap), 0) + j * LANES
        found = jnp.zeros((LANES, cap), F32)
        for b in range(plan.shares):
            found += jnp.where(names[b] == own, place[b : b + 1, :], 0.0)
        found = jnp.broadcast_to(jnp.sum(found, axis=1, keepdims=True), (LANES, LANES)).T
        shift = lax.rem(lax.broadcasted_iota(jnp.int32, (1, LANES), 1), SUBS).astype(F32)
        rows.append(found[0:1, :] - shift)
    return rows


def first_kernel(
    plan,
    count_ref, cp_ref, parcel_ref, send_ref, table_ref, base_ref, coup_ref, winds_ref, out_hbm,
    out_ref, buf_ref, loc_ref, locb_ref, out_sems,
):
    tiles, shares, points, block, data = plan.tiles, plan.shares, plan.points, plan.block, plan.data
    width = plan.force * LANES
    current = jnp.sum(parcel_ref[:, :, points : points + width], axis=0)
    spare = own_places(plan, parcel_ref, send_ref, count_ref)
    spare += [current[1:2, f * LANES : (f + 1) * LANES] for f in range(plan.force)]
    if block > data + len(spare):
        spare.append(jnp.zeros((block - data - len(spare), LANES), F32))
    for d in range(shares):
        out_ref[d * block + data : (d + 1) * block, :] = jnp.concatenate(spare, axis=0)
    east, north = cell_winds(jnp.sum(parcel_ref[:, :, 0:points], axis=0), cp_ref[...])
    winds_ref[0:1, :] = east
    winds_ref[1:2, :] = north

    @pl.loop(0, plan.spec // PERIOD)
    def _(i):
        first = pl.multiple_of(i * PERIOD, PERIOD)
        at = pl.ds(first, PERIOD)
        local = base_ref[at, :] * growth_step(first, east, north, table_ref)
        loc_ref[at, :] = local
        locb_ref[at, :] = local.astype(BF16)

    sent, copies = [0], []

    def store(first, values):
        for j in range(tiles):
            buf_ref[pl.ds(first * tiles + j, values.shape[0], stride=tiles), :] = values[
                :, j * LANES : (j + 1) * LANES
            ]
        upto = (first + values.shape[0]) // plan.depth
        for d in range(sent[0], upto):
            out_ref[d * block : d * block + data, :] = buf_ref[d * data : (d + 1) * data, :]
        at = slice(sent[0] * block, upto * block)
        copies.append(
            pltpu.make_async_copy(out_ref.at[at, :], out_hbm.at[at, :], out_sems.at[len(copies)])
        )
        copies[-1].start()
        sent[0] = upto

    coupled(plan, coup_ref, loc_ref, locb_ref, store)
    for copy in copies:
        copy.wait()


def last_kernel(
    plan,
    winds_ref, table_ref, came_hbm, coup_hbm, out_hbm,
    came_ref, coup_ref, loc_ref, locb_ref, unit_ref, sems, coup_sem, out_sems,
):
    tiles = plan.tiles
    copies = []
    arrive = fetch(came_hbm, came_ref, sems, plan.thirds)
    get = pltpu.make_async_copy(coup_hbm, coup_ref, coup_sem)
    get.start()

    def load(first, count):
        start = pl.multiple_of(first * tiles, SUBS)
        return jnp.concatenate(
            [came_ref[pl.ds(start + j, count, stride=tiles), :] for j in range(tiles)], axis=1
        )

    unit_loss(plan, load, arrive, table_ref, unit_ref)
    east, north = winds_ref[0:1, :], winds_ref[1:2, :]

    @pl.loop(0, plan.spec // PERIOD)
    def _(i):
        first = pl.multiple_of(i * PERIOD, PERIOD)
        at = pl.ds(first, PERIOD)
        local = load(first, PERIOD) * unit_ref[...] * growth_step(first, east, north, table_ref)
        loc_ref[at, :] = local
        locb_ref[at, :] = local.astype(BF16)

    def store(first, values):
        at = slice(first, first + values.shape[0])
        loc_ref[at, :] = values
        copies.append(
            pltpu.make_async_copy(loc_ref.at[at, :], out_hbm.at[at, :], out_sems.at[len(copies)])
        )
        copies[-1].start()

    get.wait()
    coupled(plan, coup_ref, loc_ref, locb_ref, store)
    for copy in copies:
        copy.wait()


def scatter(plan, place_ref, came_ref, grid_ref, piece_refs, arrived):
    depth, tiles, tall, block = plan.depth, plan.tiles, plan.tall, plan.block
    blocks = plan.shares * tiles
    sub = lax.broadcasted_iota(jnp.int32, (SUBS, LANES), 0)

    def turn(i, piece_ref):
        s, j = i // tiles, i % tiles
        values = came_ref[pl.ds(s * block + j, depth, stride=tiles), :]
        if tall > depth:
            values = jnp.concatenate([values, jnp.zeros((tall - depth, LANES), F32)], axis=0)
        piece_ref[:, 0:tall] = values.T

    def put(i, piece_ref):
        for g in range(LANES // SUBS):
            values = piece_ref[g * SUBS : (g + 1) * SUBS, :]
            for t in range(SUBS):
                spot = place_ref[i * LANES + g * SUBS + t]
                pltpu.store(grid_ref.at[pl.ds(spot, SUBS), :], values, mask=sub == t)

    even_ref, odd_ref = piece_refs
    arrived(0)
    turn(0, even_ref)
    per = blocks // (2 * PARTS)

    @pl.loop(0, PARTS)
    def _(part):
        @pl.loop(0, per)
        def _(i):
            at = (part * per + i) * 2
            turn(at + 1, odd_ref)
            put(at, even_ref)

            @pl.when(jnp.logical_and(i == per - 1, part < PARTS - 1))
            def _():
                arrived(part + 1)

            turn(jnp.minimum(at + 2, blocks - 1), even_ref)
            put(at + 1, odd_ref)


def gather(plan, place_ref, out_ref, grid_ref, piece_refs, finished):
    depth, tiles, tall = plan.depth, plan.tiles, plan.tall
    blocks = plan.shares * tiles
    sub = lax.broadcasted_iota(jnp.int32, (SUBS, LANES), 0)

    def turn(i, piece_ref):
        s, j = i // tiles, i % tiles
        turned = piece_ref[:, 0:tall].T
        out_ref[pl.ds(s * plan.data + j, depth, stride=tiles), :] = turned[0:depth, :]

    def get(i, piece_ref):
        for g in range(LANES // SUBS):
            first = i * LANES + g * SUBS
            values = grid_ref[pl.ds(place_ref[first], SUBS), :]
            for t in range(1, SUBS):
                shifted = grid_ref[pl.ds(place_ref[first + t], SUBS), :]
                values = jnp.where(sub == t, shifted, values)
            piece_ref[g * SUBS : (g + 1) * SUBS, :] = values

    even_ref, odd_ref = piece_refs
    get(0, even_ref)
    per = blocks // (2 * PARTS)

    @pl.loop(0, PARTS)
    def _(part):
        @pl.loop(0, per)
        def _(i):
            at = (part * per + i) * 2
            get(at + 1, odd_ref)
            turn(at, even_ref)
            get(jnp.minimum(at + 2, blocks - 1), even_ref)
            turn(at + 1, odd_ref)

        finished(part)


def spread_drift(plan, came_ref, held, turned, drift_ref):
    held[...] = jnp.zeros((LANES, LANES), F32)
    for s in range(plan.shares):
        first = s * plan.block + plan.data + plan.tiles
        held[s * plan.force : (s + 1) * plan.force, :] = came_ref[first : first + plan.force, :]
    turned[...] = (courant_scale * held[...]).T
    groups = plan.vregs // COARSE
    ordered = jnp.concatenate(
        [
            turned[pl.ds(a * groups * SUBS + m, SUBS, stride=groups), :]
            for a in range(LANES // (groups * SUBS))
            for m in range(groups)
        ],
        axis=0,
    )
    for q in range(plan.shares * plan.force):
        drift_ref[q * LANES : (q + 1) * LANES, :] = jnp.broadcast_to(
            ordered[:, q : q + 1], (LANES, LANES)
        )


def sweep(plan, drift_ref, speed_ref, one_ref, two_ref):
    cols, last = plan.cols, plan.coarse_rows - 1
    groups = plan.vregs // COARSE
    sub = lax.broadcasted_iota(jnp.int32, (SUBS, LANES), 0)
    speeds = [jnp.broadcast_to(speed_ref[d : d + 1, :], (SUBS, LANES)) for d in range(2)]

    for m in range(groups):

        def courant(which, r4):
            at = pl.multiple_of(((which * plan.coarse_rows + r4) * groups + m) * SUBS, SUBS)
            value = speeds[which] + drift_ref[pl.ds(at, SUBS), :]
            return value > 0.0, jnp.abs(value)

        def at(row, q):
            return pl.ds(pl.multiple_of((row + 1) * cols + q * SUBS, SUBS), SUBS)

        def along(row, speed):
            ahead, size = speed
            base = pl.multiple_of((row + 1) * cols, SUBS)
            first, count = m * COARSE, COARSE
            line = [one_ref[at(row, q), :] for q in range(first, first + count)]
            if first:
                before = one_ref[at(row, first - 1), :]
            else:
                before = one_ref[pl.ds(base + cols - SUBS - 1, SUBS), :]
                before = jnp.where(sub == 0, DRY, before)
            if first + count < plan.vregs:
                after = one_ref[at(row, first + count), :]
            else:
                after = jnp.where(sub == SUBS - 1, DRY, one_ref[pl.ds(base + 1, SUBS), :])
            line = [before] + line + [after]
            swept = []
            for q in range(1, count + 1):
                pick = jnp.where(ahead, line[q - 1], line[q + 1])
                pick = jnp.where(pick < DRY, pick, 0.0)
                moved = line[q] + size * (pick - line[q])
                swept.append(jnp.where(line[q] < DRY, moved, 0.0))
            return swept

        def coarse(r4, held):
            above, here = held
            east = courant(0, r4)
            ahead, size = courant(1, r4)
            later = courant(0, jnp.minimum(r4 + 1, last))
            for dr in range(COARSE):
                row = r4 * COARSE + dr
                below = along(row + 1, east if dr < COARSE - 1 else later)
                for q in range(COARSE):
                    pick = jnp.where(ahead, above[q], below[q])
                    two_ref[at(row, m * COARSE + q), :] = here[q] + size * (pick - here[q])
                above, here = here, below
            return above, here

        zero = [jnp.zeros((SUBS, LANES), F32)] * COARSE
        lax.fori_loop(0, plan.coarse_rows, coarse, (zero, along(0, courant(0, 0))), unroll=2)


def middle_kernel(
    plan,
    place_ref, speed_ref, came_hbm, out_hbm,
    came_ref, out_ref, one_ref, two_ref, drift_ref, even_ref, odd_ref, in_sems, out_sems,
):
    shares, block, data = plan.shares, plan.block, plan.data
    part_in, part_out = shares // PARTS * block, shares // PARTS * data

    def copy_in(part):
        at = pl.ds(pl.multiple_of(part * part_in, SUBS), part_in)
        return pltpu.make_async_copy(came_hbm.at[at, :], came_ref.at[at, :], in_sems.at[part])

    def copy_out(part):
        at = pl.ds(pl.multiple_of(part * part_out, SUBS), part_out)
        return pltpu.make_async_copy(out_ref.at[at, :], out_hbm.at[at, :], out_sems.at[part])

    for part in range(PARTS):
        copy_in(part).start()

    @pl.loop(0, plan.size // LANES)
    def _(i):
        at = pl.ds(pl.multiple_of(i * LANES, LANES), LANES)
        one_ref[at, :] = jnp.full((LANES, LANES), DRY, F32)

    scatter(plan, place_ref, came_ref, one_ref, (even_ref, odd_ref), lambda part: copy_in(part).wait())
    spread_drift(plan, came_ref, even_ref, odd_ref, drift_ref)
    me = lax.axis_index("space")
    sweep(plan, drift_ref, speed_ref.at[me], one_ref, two_ref)
    gather(plan, place_ref, out_ref, two_ref, (even_ref, odd_ref), lambda part: copy_out(part).start())
    for part in range(PARTS):
        copy_out(part).wait()


VMEM = pl.BlockSpec(memory_space=pltpu.VMEM)
SMEM = pl.BlockSpec(memory_space=pltpu.SMEM)
ANY = pl.BlockSpec(memory_space=pl.ANY)


def on_spectrum(
    plan,
    spectra,
    wind_files,
    current_files,
    reader_turn,
    cell_point,
    coupling,
    send_list,
    send_count,
    recv_list,
):
    shares, rows, spec, points = plan.shares, plan.rows, plan.spec, plan.points
    tiles, depth, size, data_rows = plan.tiles, plan.depth, plan.size, plan.shares * plan.data
    source, east_speed, north_speed = wave_tables()
    table = jnp.asarray(source)
    speed = np.zeros((shares, SUBS, LANES), np.float32)
    speed[:, 0, :depth] = east_speed.reshape(shares, depth)
    speed[:, 1, :depth] = north_speed.reshape(shares, depth)

    def kernel(body, *, flops, traffic, vmem=WHOLE_VMEM, **options):
        return pl.pallas_call(
            body,
            compiler_params=pltpu.CompilerParams(vmem_limit_bytes=vmem),
            cost_estimate=pl.CostEstimate(flops=flops, bytes_accessed=traffic, transcendentals=0),
            **options,
        )

    width = points + max(LANES, plan.force * LANES)
    parcel = kernel(
        functools.partial(pack_kernel, plan),
        flops=0, traffic=4 * shares * 2 * width,
        out_shape=jax.ShapeDtypeStruct((shares, 2, width), F32),
        in_specs=[SMEM, VMEM, VMEM, VMEM],
        out_specs=VMEM,
        name="pack",
    )(reader_turn, wind_files, current_files, recv_list)
    parcel = lax.all_to_all(parcel, "space", 0, 0, tiled=True)

    cp = cell_point.reshape(1, rows)
    h_cost = dict(flops=2 * rows * spec * spec, traffic=12 * rows * spec)
    whole = pltpu.VMEM((spec, rows), F32)
    rounded = pltpu.VMEM((spec, rows), BF16)
    square = pltpu.VMEM((spec, spec), BF16)
    unit = pltpu.VMEM((PERIOD, rows), F32)
    dma = pltpu.SemaphoreType.DMA
    coup, base = kernel(
        functools.partial(ready_kernel, plan),
        flops=0, traffic=12 * rows * spec, vmem=20 * MIB,
        out_shape=[
            jax.ShapeDtypeStruct((spec, spec), BF16), jax.ShapeDtypeStruct((spec, rows), F32)
        ],
        in_specs=[VMEM, ANY, ANY],
        out_specs=[VMEM, VMEM],
        scratch_shapes=[square, whole, unit, dma((plan.thirds,)), dma],
        name="ready",
    )(table, coupling, spectra.T)
    winds, sent = kernel(
        functools.partial(first_kernel, plan),
        vmem=24 * MIB, **h_cost,
        out_shape=[
            jax.ShapeDtypeStruct((SUBS, rows), F32),
            jax.ShapeDtypeStruct((shares * plan.block, LANES), F32),
        ],
        in_specs=[SMEM] + [VMEM] * 6,
        out_specs=[VMEM, ANY],
        scratch_shapes=[
            pltpu.VMEM((shares * plan.block, LANES), F32),
            pltpu.VMEM((data_rows, LANES), F32),
            whole, rounded, dma((plan.thirds,)),
        ],
        name="first_half",
    )(send_count, cp, parcel, send_list, table, base, coup)
    came = lax.all_to_all(
        sent.reshape(shares, plan.block, LANES), "space", 0, 0, tiled=True
    )
    place = came[:, plan.data : plan.data + tiles].astype(jnp.int32).reshape(-1)
    swept = kernel(
        functools.partial(middle_kernel, plan),
        flops=24 * size * LANES, traffic=8 * rows * spec, vmem=32 * MIB,
        out_shape=jax.ShapeDtypeStruct((data_rows, LANES), F32),
        in_specs=[SMEM, VMEM, ANY],
        out_specs=ANY,
        scratch_shapes=[
            pltpu.VMEM((shares * plan.block, LANES), F32),
            pltpu.VMEM((data_rows, LANES), F32),
            pltpu.VMEM((size, LANES), F32),
            pltpu.VMEM((size, LANES), F32),
            pltpu.VMEM((2 * points, LANES), F32),
            pltpu.VMEM((LANES, LANES), F32),
            pltpu.VMEM((LANES, LANES), F32),
            pltpu.SemaphoreType.DMA((PARTS,)),
            pltpu.SemaphoreType.DMA((PARTS,)),
        ],
        name="sweeps",
    )(place, jnp.asarray(speed), came.reshape(-1, LANES))
    back = lax.all_to_all(
        swept.reshape(shares, depth, tiles, LANES), "space", 0, 0, tiled=True
    )
    result = kernel(
        functools.partial(last_kernel, plan),
        vmem=24 * MIB, **h_cost,
        out_shape=jax.ShapeDtypeStruct((spec, rows), F32),
        in_specs=[VMEM] * 2 + [ANY] * 2,
        out_specs=ANY,
        scratch_shapes=[
            pltpu.VMEM((data_rows, LANES), F32),
            square, whole, rounded, unit, dma((plan.thirds,)), dma, dma((plan.thirds,)),
        ],
        name="last_half",
    )(winds, table, back.reshape(data_rows, LANES), coup)
    return result.T


def on_device(*args):
    spectra, wind_files, send_list, wet_mask = args[0], args[1], args[6], args[9]
    plan = Plan(
        lax.axis_size("space"), *spectra.shape, send_list.shape[2], *wet_mask.shape, wind_files.shape[2]
    )
    if plan.fits():
        return on_spectrum(plan, *args[:9])
    return on_strips(*args)


def solution(mesh):
    placed = (
        P(("members", "space"), None),
        P(("members", "space"), None, None),
        P(("members", "space"), None, None),
        P(),
        P("space"),
        P(),
        P("space", None, None),
        P("space", None),
        P("space", None, None),
        P("space", None),
    )
    return jax.shard_map(
        on_device,
        mesh=mesh,
        in_specs=placed,
        out_specs=P(("members", "space"), None),
        check_vma=False,
    )
```

```python
import functools
import math

import jax
import jax.numpy as jnp
import numpy as np
from jax import lax
from jax.experimental import pallas as pl
from jax.experimental.pallas import tpu as pltpu
from jax.sharding import PartitionSpec as P

DIRS = 36
FREQS = 36
COARSE = 4


gravity = 9.81
base_freq = 0.0418
freq_ratio = 1.1
freq_span = 35.0
input_coef = 0.0001
wind_gain = 1.12
dissip_coef = 0.0005
half_length = 300.0
courant_scale = 0.05


def from_root(array, axis, root):
    mine = lax.axis_index(axis) == root
    return lax.psum(jnp.where(mine, array, jnp.zeros_like(array)), axis)


def extended(array, sides, width):
    for axis, dim in sides:
        size, length = (lax.axis_size(axis), array.shape[dim])
        up = [(i, (i + 1) % size) for i in range(size - 1)]
        down = [(j, i) for i, j in up]
        last = lax.slice_in_dim(array, length - width, length, axis=dim)
        first = lax.slice_in_dim(array, 0, width, axis=dim)
        before = lax.ppermute(last, axis, up)
        after = lax.ppermute(first, axis, down)
        array = jnp.concatenate([before, array, after], axis=dim)
    return array


def spectral_tables():
    direction = 2.0 * math.pi / DIRS * jnp.arange(DIRS, dtype=jnp.float32)
    exponent = jnp.arange(FREQS, dtype=jnp.float32) * (freq_span / (FREQS - 1))
    frequency = base_freq * freq_ratio**exponent
    angular = 2.0 * math.pi * frequency
    phase_speed = gravity / angular
    return (jnp.cos(direction), jnp.sin(direction), angular, phase_speed, 0.5 * phase_speed)


def source_half(energy, wind_east, wind_north, coupling):
    cos_dir, sine_dir, angular, phase_speed, group_speed = spectral_tables()
    along_wind = wind_east[:, None] * cos_dir[None, :] + wind_north[:, None] * sine_dir[None, :]
    growth = (
        input_coef
        * angular[None, None, :]
        * jnp.maximum(wind_gain * along_wind[:, :, None] / phase_speed[None, None, :] - 1.0, 0.0)
    )
    growth = growth.reshape(energy.shape[0], -1)
    mean_square = jnp.mean(energy * energy, axis=1, keepdims=True)
    decay_rate = dissip_coef * jnp.tile(angular, DIRS)[None, :] * mean_square
    local_part = energy * (1.0 + half_length * growth) / (1.0 + half_length * decay_rate)
    return local_part + jnp.dot(
        local_part.astype(jnp.bfloat16), coupling, preferred_element_type=jnp.float32
    )


def advect(center, upwind_lo, upwind_hi, courant):
    ahead_part = jnp.maximum(courant, 0.0)
    behind = jnp.minimum(courant, 0.0)
    return center - ahead_part * (center - upwind_lo) - behind * (upwind_hi - center)


def sweep_cols(energy_grid, drift_east, wet_field):
    cos_dir, sine_dir, angular, phase_speed, group_speed = spectral_tables()
    wave_speed = (cos_dir[:, None] * group_speed[None, :]).reshape(-1)
    courant = (wave_speed[None, None, :] + drift_east[:, :, None]) * courant_scale
    zero_edge = jnp.zeros_like(energy_grid[:, :1])
    upwind_lo = jnp.concatenate([zero_edge, energy_grid[:, :-1]], axis=1)
    upwind_hi = jnp.concatenate([energy_grid[:, 1:], zero_edge], axis=1)
    return advect(energy_grid, upwind_lo, upwind_hi, courant) * wet_field[:, :, None]


def sweep_rows(energy_grid, row_above, row_below, drift_north, wet_field):
    cos_dir, sine_dir, angular, phase_speed, group_speed = spectral_tables()
    wave_speed = (sine_dir[:, None] * group_speed[None, :]).reshape(-1)
    courant = (wave_speed[None, None, :] + drift_north[:, :, None]) * courant_scale
    return advect(energy_grid, row_above, row_below, courant) * wet_field[:, :, None]


def forcing_points(row_start, row_count, col_count):
    rows_idx = row_start + jnp.arange(row_count, dtype=jnp.int32)
    cols_idx = jnp.arange(col_count, dtype=jnp.int32)
    return rows_idx[:, None] // COARSE * (col_count // COARSE) + cols_idx[None, :] // COARSE


def on_strips(
    spectra,
    wind_files,
    current_files,
    reader_turn,
    cell_point,
    coupling,
    send_list,
    send_count,
    recv_list,
    wet_mask,
):
    levels = []
    for time_level in range(2):
        levels.append(
            (
                from_root(wind_files[0], "space", reader_turn[time_level]),
                from_root(current_files[0], "space", reader_turn[time_level]),
            )
        )
    wind_mean = 0.5 * (levels[0][0] + levels[1][0])
    current_mean = 0.5 * (levels[0][1] + levels[1][1])
    cell_wind = jnp.take(wind_mean, cell_point, axis=1)
    first_half = source_half(spectra, cell_wind[0], cell_wind[1], coupling)
    send_rows = send_list[0]
    counts = send_count[0]
    places = recv_list[0]
    slot_count = send_rows.shape[1]
    spec_width = spectra.shape[1]
    live_slots = (jnp.arange(slot_count, dtype=jnp.int32)[None, :] < counts[:, None]).astype(
        jnp.float32
    )
    packed = first_half[send_rows] * live_slots[:, :, None]
    arrived = lax.all_to_all(packed, "space", split_axis=0, concat_axis=0, tiled=True)
    row_count = wet_mask.shape[0]
    col_count = wet_mask.shape[1]
    energy_grid = (
        jnp.zeros((row_count * col_count, spec_width), jnp.float32)
        .at[places.reshape(-1)]
        .add(arrived.reshape(-1, spec_width))
    )
    energy_grid = energy_grid.reshape(row_count, col_count, spec_width)
    points = forcing_points(lax.axis_index("space") * row_count, row_count, col_count)
    drift = jnp.take(current_mean, points, axis=1)
    wet_field = wet_mask.astype(jnp.float32)
    swept_cols = sweep_cols(energy_grid, drift[0], wet_field)
    padded = extended(swept_cols, (("space", 0),), 1)
    swept = sweep_rows(swept_cols, padded[:-2], padded[2:], drift[1], wet_field).reshape(
        -1, spec_width
    )
    outgoing = swept[places]
    flat_rows = send_rows.reshape(-1)
    empty_rows = jnp.zeros((spectra.shape[0], spec_width), jnp.float32)
    returned = lax.all_to_all(outgoing, "space", split_axis=0, concat_axis=0, tiled=True)
    back_rows = empty_rows.at[flat_rows].add(
        (returned * live_slots[:, :, None]).reshape(-1, spec_width)
    )
    result = source_half(back_rows, cell_wind[0], cell_wind[1], coupling)
    return result


LANES = 128
SUBS = 8
F32 = jnp.float32
BF16 = jnp.bfloat16
MIB = 1024 * 1024
WHOLE_VMEM = 60 * MIB
DRY = 1e30
PARTS = 4
PERIOD = 4 * FREQS


def wave_tables():
    direction = 2.0 * np.pi / DIRS * np.arange(DIRS)
    frequency = base_freq * freq_ratio ** (np.arange(FREQS) * (freq_span / (FREQS - 1)))
    angular = 2.0 * np.pi * frequency
    phase = gravity / angular
    group = 0.5 * phase
    cos_dir, sin_dir = np.cos(direction)[:, None], np.sin(direction)[:, None]
    flat = lambda t: np.broadcast_to(t, (DIRS, FREQS)).reshape(-1)
    growth = half_length * input_coef * angular
    source = np.zeros((DIRS * FREQS, 8), np.float32)
    source[:, 0] = flat(growth * wind_gain * cos_dir / phase)
    source[:, 1] = flat(growth * wind_gain * sin_dir / phase)
    source[:, 2] = flat(1.0 - growth)
    source[:, 3] = flat(half_length * dissip_coef * angular)
    east = flat(courant_scale * cos_dir * group).astype(np.float32)
    north = flat(courant_scale * sin_dir * group).astype(np.float32)
    return source, east, north


def ceil_to(value, step):
    return -(-value // step) * step


def largest_step(size, step, most):
    return max(s for s in range(step, most + 1, step) if size % s == 0)


class Plan:
    def __init__(self, shares, rows, spec, cap, strip_rows, cols, points):
        self.shares, self.rows, self.spec, self.cap = shares, rows, spec, cap
        self.cols, self.points = cols, points
        self.depth = spec // shares
        self.tiles = rows // LANES
        self.data = self.depth * self.tiles
        self.force = 2 * points // (LANES * shares)
        self.block = ceil_to(self.data + self.tiles + self.force, SUBS)
        self.strip = strip_rows * cols
        self.grid_rows = strip_rows * shares
        self.coarse_rows = self.grid_rows // COARSE
        self.vregs = cols // SUBS
        self.size = (self.grid_rows + 2) * cols
        self.tall_step = largest_step(spec, PERIOD, 512)
        self.thirds = spec // self.tall_step

    def fits(self):
        if self.spec % self.shares or self.depth > LANES or self.rows % (2 * LANES):
            return False
        if 2 * self.points % (LANES * self.shares) or self.points % LANES or self.cap > LANES:
            return False
        if 2 * self.points // LANES > LANES or self.cols != LANES or self.shares % PARTS:
            return False
        held = 2 * self.size + 2 * self.points + self.shares * (self.block + self.data)
        return 4 * LANES * held + 4 * MIB < 32 * MIB


def pack_kernel(plan, turn_ref, wind_ref, current_ref, recv_ref, out_ref):
    me = lax.axis_index("space")
    half = lambda at: jnp.where(turn_ref[at] == me, 0.5, 0.0)
    mine = half(0) + half(1)
    wind = mine * wind_ref[0]
    points, width, cap = plan.points, plan.force * LANES, plan.cap
    for s in range(plan.shares):
        out_ref[s, :, 0:points] = wind
        out_ref[s, :, points:] = jnp.zeros((2, out_ref.shape[2] - points), F32)
        out_ref[s, 0:1, points : points + cap] = recv_ref[0, s : s + 1, :].astype(F32)
        which, first = divmod(s * width, points)
        out_ref[s, 1:2, points : points + width] = (
            mine * current_ref[0, which : which + 1, first : first + width]
        )


def cell_winds(wind, cp):
    points, rows = wind.shape[1], cp.shape[1]
    high = wind.astype(BF16).astype(F32)
    middle = (wind - high).astype(BF16).astype(F32)
    low = wind - high - middle
    parts = jnp.concatenate([high, middle, low, jnp.zeros((10, points), F32)], axis=0)
    point = lax.broadcasted_iota(jnp.int32, (points, rows), 0)
    hit = jnp.where(point == cp, 1.0, 0.0).astype(BF16)
    picked = jnp.dot(parts.astype(BF16), hit, preferred_element_type=F32)
    both = picked[0:2] + picked[2:4] + picked[4:6]
    return both[0:1], both[1:2]


def fetch(source, target, sems, parts):
    size = target.shape[0] // parts
    copies = [
        pltpu.make_async_copy(
            source.at[pl.ds(q * size, size), :], target.at[pl.ds(q * size, size), :], sems.at[q]
        )
        for q in range(parts)
    ]
    for copy in copies:
        copy.start()
    return copies


def unit_loss(plan, load, arrive, table_ref, unit_ref):
    tall = plan.spec // len(arrive)

    def squares(i, total):
        piece = load(pl.multiple_of(i * 48, 48), 48)
        return total + jnp.sum((piece * piece).reshape(48 // SUBS, SUBS, plan.rows), axis=0)

    total = jnp.zeros((SUBS, plan.rows), F32)
    for q, copy in enumerate(arrive):
        copy.wait()
        total = lax.fori_loop(q * tall // 48, (q + 1) * tall // 48, squares, total)
    mean_square = jnp.sum(total, axis=0, keepdims=True) * (1.0 / plan.spec)
    unit_ref[...] = 1.0 / (1.0 + table_ref[0:PERIOD, 3:4] * mean_square)


def growth_step(first, east, north, table_ref):
    table = table_ref[pl.ds(first, PERIOD), :]
    return jnp.maximum(east * table[:, 0:1] + north * table[:, 1:2] + table[:, 2:3], 1.0)


def coupled(plan, coup_ref, loc_ref, locb_ref, store):
    for q in range(plan.thirds):
        at = slice(q * plan.tall_step, (q + 1) * plan.tall_step)
        store(
            q * plan.tall_step,
            loc_ref[at, :]
            + jnp.dot(coup_ref[at, :], locb_ref[...], preferred_element_type=F32),
        )


def ready_kernel(
    plan, table_ref, coup_hbm, energy_hbm, unit_ref, turned_hbm,
    coup_ref, turned_ref, energy_ref, sems, coup_sem, out_sems,
):
    spec = plan.spec
    arrive = fetch(energy_hbm, energy_ref, sems, plan.thirds)
    get = pltpu.make_async_copy(coup_hbm, coup_ref, coup_sem)
    get.start()
    unit_loss(plan, lambda first, count: energy_ref[pl.ds(first, count), :], arrive, table_ref, unit_ref)
    get.wait()
    copies, wide = [], 3 * LANES
    for first in range(0, spec, LANES):
        at = slice(first, min(first + LANES, spec))
        turned_ref[at, :] = coup_ref[:, at].T
        if at.stop % wide == 0 or at.stop == spec:
            done = slice((at.stop - 1) // wide * wide, at.stop)
            copies.append(
                pltpu.make_async_copy(
                    turned_ref.at[done, :], turned_hbm.at[done, :], out_sems.at[len(copies)]
                )
            )
            copies[-1].start()
    for copy in copies:
        copy.wait()


def own_places(plan, parcel_ref, send_ref, count_ref):
    points, cols, vregs, cap = plan.points, plan.cols, plan.vregs, plan.cap
    landing = jnp.concatenate(
        [parcel_ref[b, 0:1, points : points + cap] for b in range(plan.shares)], axis=0
    ).astype(jnp.int32)
    cell = landing + plan.strip * lax.broadcasted_iota(jnp.int32, (plan.shares, cap), 0)
    column = lax.rem(cell, cols)
    place = cell - column + cols + lax.rem(column, vregs) * SUBS + lax.div(column, vregs)
    place = place.astype(F32)
    slot = lax.broadcasted_iota(jnp.int32, (1, cap), 1)
    names = [
        jnp.where(slot < count_ref[0, b], send_ref[0, b : b + 1, :], -1) for b in range(plan.shares)
    ]
    rows = []
    for j in range(plan.tiles):
        own = lax.broadcasted_iota(jnp.int32, (LANES, cap), 0) + j * LANES
        found = jnp.zeros((LANES, cap), F32)
        for b in range(plan.shares):
            found += jnp.where(names[b] == own, place[b : b + 1, :], 0.0)
        found = jnp.broadcast_to(jnp.sum(found, axis=1, keepdims=True), (LANES, LANES)).T
        shift = lax.rem(lax.broadcasted_iota(jnp.int32, (1, LANES), 1), SUBS).astype(F32)
        rows.append(found[0:1, :] - shift)
    return rows


def first_kernel(
    plan,
    count_ref, cp_ref, parcel_ref, send_ref, table_ref, unit_ref, energy_hbm, coup_hbm, winds_ref, out_hbm,
    out_ref, buf_ref, loc_ref, coup_ref, locb_ref, sems, coup_sem, out_sems,
):
    tiles, shares, points, block, data = plan.tiles, plan.shares, plan.points, plan.block, plan.data
    arrive = fetch(energy_hbm, loc_ref, sems, plan.thirds)
    get = pltpu.make_async_copy(coup_hbm, coup_ref, coup_sem)
    get.start()
    width = plan.force * LANES
    current = jnp.sum(parcel_ref[:, :, points : points + width], axis=0)
    spare = own_places(plan, parcel_ref, send_ref, count_ref)
    spare += [current[1:2, f * LANES : (f + 1) * LANES] for f in range(plan.force)]
    if block > data + len(spare):
        spare.append(jnp.zeros((block - data - len(spare), LANES), F32))
    for d in range(shares):
        out_ref[d * block + data : (d + 1) * block, :] = jnp.concatenate(spare, axis=0)
    east, north = cell_winds(jnp.sum(parcel_ref[:, :, 0:points], axis=0), cp_ref[...])
    winds_ref[0:1, :] = east
    winds_ref[1:2, :] = north
    per = plan.tall_step // PERIOD
    for q in range(plan.thirds):
        arrive[q].wait()

        @pl.loop(q * per, (q + 1) * per)
        def _(i):
            first = pl.multiple_of(i * PERIOD, PERIOD)
            at = pl.ds(first, PERIOD)
            local = loc_ref[at, :] * unit_ref[...] * growth_step(first, east, north, table_ref)
            loc_ref[at, :] = local
            locb_ref[at, :] = local.astype(BF16)

    get.wait()
    sent, copies = [0], []

    def store(first, values):
        for j in range(tiles):
            buf_ref[pl.ds(first * tiles + j, values.shape[0], stride=tiles), :] = values[
                :, j * LANES : (j + 1) * LANES
            ]
        upto = (first + values.shape[0]) // plan.depth
        for d in range(sent[0], upto):
            out_ref[d * block : d * block + data, :] = buf_ref[d * data : (d + 1) * data, :]
        at = slice(sent[0] * block, upto * block)
        copies.append(
            pltpu.make_async_copy(out_ref.at[at, :], out_hbm.at[at, :], out_sems.at[len(copies)])
        )
        copies[-1].start()
        sent[0] = upto

    coupled(plan, coup_ref, loc_ref, locb_ref, store)
    for copy in copies:
        copy.wait()


def last_kernel(
    plan,
    winds_ref, table_ref, came_hbm, coup_hbm, out_hbm,
    came_ref, coup_ref, loc_ref, locb_ref, unit_ref, sems, coup_sem, out_sems,
):
    tiles = plan.tiles
    copies = []
    arrive = fetch(came_hbm, came_ref, sems, plan.thirds)
    get = pltpu.make_async_copy(coup_hbm, coup_ref, coup_sem)
    get.start()

    def load(first, count):
        start = pl.multiple_of(first * tiles, SUBS)
        return jnp.concatenate(
            [came_ref[pl.ds(start + j, count, stride=tiles), :] for j in range(tiles)], axis=1
        )

    unit_loss(plan, load, arrive, table_ref, unit_ref)
    east, north = winds_ref[0:1, :], winds_ref[1:2, :]

    @pl.loop(0, plan.spec // PERIOD)
    def _(i):
        first = pl.multiple_of(i * PERIOD, PERIOD)
        at = pl.ds(first, PERIOD)
        local = load(first, PERIOD) * unit_ref[...] * growth_step(first, east, north, table_ref)
        loc_ref[at, :] = local
        locb_ref[at, :] = local.astype(BF16)

    def store(first, values):
        at = slice(first, first + values.shape[0])
        loc_ref[at, :] = values
        copies.append(
            pltpu.make_async_copy(loc_ref.at[at, :], out_hbm.at[at, :], out_sems.at[len(copies)])
        )
        copies[-1].start()

    get.wait()
    coupled(plan, coup_ref, loc_ref, locb_ref, store)
    for copy in copies:
        copy.wait()


def turned_block(values, one_ref):
    high = values.astype(BF16)
    low = (values - high.astype(F32)).astype(BF16)
    return lax.dot_general(
        one_ref[...],
        jnp.concatenate([high, low], axis=1),
        (((1,), (1,)), ((), ())),
        preferred_element_type=F32,
    )


def scatter(plan, place_ref, came_ref, grid_ref, piece_refs, eye_ref, arrived):
    depth, tiles, block = plan.depth, plan.tiles, plan.block
    blocks = plan.shares * tiles
    sub = lax.broadcasted_iota(jnp.int32, (SUBS, LANES), 0)

    def turn(i, piece_ref):
        s, j = i // tiles, i % tiles
        values = came_ref[pl.ds(s * block + j, depth, stride=tiles), :]
        if LANES > depth:
            values = jnp.concatenate([values, jnp.zeros((LANES - depth, LANES), F32)], axis=0)
        piece_ref[...] = turned_block(values, eye_ref)

    def put(i, piece_ref):
        for g in range(LANES // SUBS):
            values = piece_ref[g * SUBS : (g + 1) * SUBS, :]
            for t in range(SUBS):
                spot = place_ref[i * LANES + g * SUBS + t]
                pltpu.store(grid_ref.at[pl.ds(spot, SUBS), :], values, mask=sub == t)

    even_ref, odd_ref = piece_refs
    arrived(0)
    turn(0, even_ref)
    per = blocks // (2 * PARTS)

    @pl.loop(0, PARTS)
    def _(part):
        @pl.loop(0, per)
        def _(i):
            at = (part * per + i) * 2
            turn(at + 1, odd_ref)
            put(at, even_ref)

            @pl.when(jnp.logical_and(i == per - 1, part < PARTS - 1))
            def _():
                arrived(part + 1)

            turn(jnp.minimum(at + 2, blocks - 1), even_ref)
            put(at + 1, odd_ref)


def gather(plan, place_ref, out_ref, grid_ref, piece_refs, eye_ref, finished):
    depth, tiles = plan.depth, plan.tiles
    blocks = plan.shares * tiles
    sub = lax.broadcasted_iota(jnp.int32, (SUBS, LANES), 0)

    def turn(i, piece_ref):
        s, j = i // tiles, i % tiles
        turned = turned_block(piece_ref[...], eye_ref)
        out_ref[pl.ds(s * plan.data + j, depth, stride=tiles), :] = turned[0:depth, :]

    def get(i, piece_ref):
        for g in range(LANES // SUBS):
            first = i * LANES + g * SUBS
            values = grid_ref[pl.ds(place_ref[first], SUBS), :]
            for t in range(1, SUBS):
                shifted = grid_ref[pl.ds(place_ref[first + t], SUBS), :]
                values = jnp.where(sub == t, shifted, values)
            piece_ref[g * SUBS : (g + 1) * SUBS, :] = values

    even_ref, odd_ref = piece_refs
    get(0, even_ref)
    per = blocks // (2 * PARTS)

    @pl.loop(0, PARTS)
    def _(part):
        @pl.loop(0, per)
        def _(i):
            at = (part * per + i) * 2
            get(at + 1, odd_ref)
            turn(at, even_ref)
            get(jnp.minimum(at + 2, blocks - 1), even_ref)
            turn(at + 1, odd_ref)

        finished(part)


def spread_drift(plan, came_ref, held, turned, drift_ref):
    held[...] = jnp.zeros((LANES, LANES), F32)
    for s in range(plan.shares):
        first = s * plan.block + plan.data + plan.tiles
        held[s * plan.force : (s + 1) * plan.force, :] = came_ref[first : first + plan.force, :]
    turned[...] = (courant_scale * held[...]).T
    groups = plan.vregs // COARSE
    ordered = jnp.concatenate(
        [
            turned[pl.ds(a * groups * SUBS + m, SUBS, stride=groups), :]
            for a in range(LANES // (groups * SUBS))
            for m in range(groups)
        ],
        axis=0,
    )
    for q in range(plan.shares * plan.force):
        drift_ref[q * LANES : (q + 1) * LANES, :] = jnp.broadcast_to(
            ordered[:, q : q + 1], (LANES, LANES)
        )


def sweep(plan, drift_ref, speed_ref, one_ref, two_ref):
    cols, last = plan.cols, plan.coarse_rows - 1
    groups = plan.vregs // COARSE
    sub = lax.broadcasted_iota(jnp.int32, (SUBS, LANES), 0)
    speeds = [jnp.broadcast_to(speed_ref[d : d + 1, :], (SUBS, LANES)) for d in range(2)]

    for m in range(groups):

        def courant(which, r4):
            at = pl.multiple_of(((which * plan.coarse_rows + r4) * groups + m) * SUBS, SUBS)
            value = speeds[which] + drift_ref[pl.ds(at, SUBS), :]
            return value > 0.0, jnp.abs(value)

        def at(row, q):
            return pl.ds(pl.multiple_of((row + 1) * cols + q * SUBS, SUBS), SUBS)

        def along(row, speed):
            ahead, size = speed
            base = pl.multiple_of((row + 1) * cols, SUBS)
            first, count = m * COARSE, COARSE
            line = [one_ref[at(row, q), :] for q in range(first, first + count)]
            if first:
                before = one_ref[at(row, first - 1), :]
            else:
                before = one_ref[pl.ds(base + cols - SUBS - 1, SUBS), :]
                before = jnp.where(sub == 0, DRY, before)
            if first + count < plan.vregs:
                after = one_ref[at(row, first + count), :]
            else:
                after = jnp.where(sub == SUBS - 1, DRY, one_ref[pl.ds(base + 1, SUBS), :])
            line = [before] + line + [after]
            swept = []
            for q in range(1, count + 1):
                pick = jnp.where(ahead, line[q - 1], line[q + 1])
                pick = jnp.where(pick < DRY, pick, 0.0)
                moved = line[q] + size * (pick - line[q])
                swept.append(jnp.where(line[q] < DRY, moved, 0.0))
            return swept

        def coarse(r4, held):
            above, here = held
            east = courant(0, r4)
            ahead, size = courant(1, r4)
            later = courant(0, jnp.minimum(r4 + 1, last))
            for dr in range(COARSE):
                row = r4 * COARSE + dr
                below = along(row + 1, east if dr < COARSE - 1 else later)
                for q in range(COARSE):
                    pick = jnp.where(ahead, above[q], below[q])
                    two_ref[at(row, m * COARSE + q), :] = here[q] + size * (pick - here[q])
                above, here = here, below
            return above, here

        zero = [jnp.zeros((SUBS, LANES), F32)] * COARSE
        lax.fori_loop(0, plan.coarse_rows, coarse, (zero, along(0, courant(0, 0))), unroll=2)


def middle_kernel(
    plan,
    place_ref, speed_ref, came_hbm, out_hbm,
    came_ref, out_ref, one_ref, two_ref, drift_ref, even_ref, odd_ref, eye_ref, in_sems, out_sems,
):
    shares, block, data = plan.shares, plan.block, plan.data
    part_in, part_out = shares // PARTS * block, shares // PARTS * data

    def copy_in(part):
        at = pl.ds(pl.multiple_of(part * part_in, SUBS), part_in)
        return pltpu.make_async_copy(came_hbm.at[at, :], came_ref.at[at, :], in_sems.at[part])

    def copy_out(part):
        at = pl.ds(pl.multiple_of(part * part_out, SUBS), part_out)
        return pltpu.make_async_copy(out_ref.at[at, :], out_hbm.at[at, :], out_sems.at[part])

    for part in range(PARTS):
        copy_in(part).start()

    row = lax.broadcasted_iota(jnp.int32, (LANES, LANES), 0)
    lane = lax.broadcasted_iota(jnp.int32, (LANES, LANES), 1)
    eye = jnp.where(row == lane, 1.0, 0.0).astype(BF16)
    eye_ref[:, 0:LANES] = eye
    eye_ref[:, LANES : 2 * LANES] = eye

    @pl.loop(0, plan.size // LANES)
    def _(i):
        at = pl.ds(pl.multiple_of(i * LANES, LANES), LANES)
        one_ref[at, :] = jnp.full((LANES, LANES), DRY, F32)

    scatter(plan, place_ref, came_ref, one_ref, (even_ref, odd_ref), eye_ref, lambda part: copy_in(part).wait())
    spread_drift(plan, came_ref, even_ref, odd_ref, drift_ref)
    me = lax.axis_index("space")
    sweep(plan, drift_ref, speed_ref.at[me], one_ref, two_ref)
    gather(plan, place_ref, out_ref, two_ref, (even_ref, odd_ref), eye_ref, lambda part: copy_out(part).start())
    for part in range(PARTS):
        copy_out(part).wait()


VMEM = pl.BlockSpec(memory_space=pltpu.VMEM)
SMEM = pl.BlockSpec(memory_space=pltpu.SMEM)
ANY = pl.BlockSpec(memory_space=pl.ANY)


def on_spectrum(
    plan,
    spectra,
    wind_files,
    current_files,
    reader_turn,
    cell_point,
    coupling,
    send_list,
    send_count,
    recv_list,
):
    shares, rows, spec, points = plan.shares, plan.rows, plan.spec, plan.points
    tiles, depth, size, data_rows = plan.tiles, plan.depth, plan.size, plan.shares * plan.data
    source, east_speed, north_speed = wave_tables()
    table = jnp.asarray(source)
    speed = np.zeros((shares, SUBS, LANES), np.float32)
    speed[:, 0, :depth] = east_speed.reshape(shares, depth)
    speed[:, 1, :depth] = north_speed.reshape(shares, depth)

    def kernel(body, *, flops, traffic, vmem=WHOLE_VMEM, **options):
        return pl.pallas_call(
            body,
            compiler_params=pltpu.CompilerParams(vmem_limit_bytes=vmem),
            cost_estimate=pl.CostEstimate(flops=flops, bytes_accessed=traffic, transcendentals=0),
            **options,
        )

    width = points + max(LANES, plan.force * LANES)
    parcel = kernel(
        functools.partial(pack_kernel, plan),
        flops=0, traffic=4 * shares * 2 * width,
        out_shape=jax.ShapeDtypeStruct((shares, 2, width), F32),
        in_specs=[SMEM, VMEM, VMEM, VMEM],
        out_specs=VMEM,
        name="pack",
    )(reader_turn, wind_files, current_files, recv_list)
    parcel = lax.all_to_all(parcel, "space", 0, 0, tiled=True)

    cp = cell_point.reshape(1, rows)
    h_cost = dict(flops=2 * rows * spec * spec, traffic=12 * rows * spec)
    whole = pltpu.VMEM((spec, rows), F32)
    rounded = pltpu.VMEM((spec, rows), BF16)
    square = pltpu.VMEM((spec, spec), BF16)
    unit = pltpu.VMEM((PERIOD, rows), F32)
    dma = pltpu.SemaphoreType.DMA
    unit_loss_held, coup = kernel(
        functools.partial(ready_kernel, plan),
        flops=0, traffic=12 * rows * spec,
        out_shape=[
            jax.ShapeDtypeStruct((PERIOD, rows), F32), jax.ShapeDtypeStruct((spec, spec), BF16)
        ],
        in_specs=[VMEM, ANY, ANY],
        out_specs=[VMEM, ANY],
        scratch_shapes=[square, square, whole, dma((plan.thirds,)), dma, dma((8,))],
        name="ready",
    )(table, coupling, spectra.T)
    winds, sent = kernel(
        functools.partial(first_kernel, plan),
        **h_cost,
        out_shape=[
            jax.ShapeDtypeStruct((SUBS, rows), F32),
            jax.ShapeDtypeStruct((shares * plan.block, LANES), F32),
        ],
        in_specs=[SMEM] + [VMEM] * 5 + [ANY] * 2,
        out_specs=[VMEM, ANY],
        scratch_shapes=[
            pltpu.VMEM((shares * plan.block, LANES), F32),
            pltpu.VMEM((data_rows, LANES), F32),
            whole, square, rounded, dma((plan.thirds,)), dma, dma((plan.thirds,)),
        ],
        name="first_half",
    )(send_count, cp, parcel, send_list, table, unit_loss_held, spectra.T, coup)
    came = lax.all_to_all(
        sent.reshape(shares, plan.block, LANES), "space", 0, 0, tiled=True
    )
    place = came[:, plan.data : plan.data + tiles].astype(jnp.int32).reshape(-1)
    swept = kernel(
        functools.partial(middle_kernel, plan),
        flops=24 * size * LANES, traffic=8 * rows * spec, vmem=32 * MIB,
        out_shape=jax.ShapeDtypeStruct((data_rows, LANES), F32),
        in_specs=[SMEM, VMEM, ANY],
        out_specs=ANY,
        scratch_shapes=[
            pltpu.VMEM((shares * plan.block, LANES), F32),
            pltpu.VMEM((data_rows, LANES), F32),
            pltpu.VMEM((size, LANES), F32),
            pltpu.VMEM((size, LANES), F32),
            pltpu.VMEM((2 * points, LANES), F32),
            pltpu.VMEM((LANES, LANES), F32),
            pltpu.VMEM((LANES, LANES), F32),
            pltpu.VMEM((LANES, 2 * LANES), BF16),
            pltpu.SemaphoreType.DMA((PARTS,)),
            pltpu.SemaphoreType.DMA((PARTS,)),
        ],
        name="sweeps",
    )(place, jnp.asarray(speed), came.reshape(-1, LANES))
    back = lax.all_to_all(
        swept.reshape(shares, depth, tiles, LANES), "space", 0, 0, tiled=True
    )
    result = kernel(
        functools.partial(last_kernel, plan),
        vmem=24 * MIB, **h_cost,
        out_shape=jax.ShapeDtypeStruct((spec, rows), F32),
        in_specs=[VMEM] * 2 + [ANY] * 2,
        out_specs=ANY,
        scratch_shapes=[
            pltpu.VMEM((data_rows, LANES), F32),
            square, whole, rounded, unit, dma((plan.thirds,)), dma, dma((plan.thirds,)),
        ],
        name="last_half",
    )(winds, table, back.reshape(data_rows, LANES), coup)
    return result.T


def on_device(*args):
    spectra, wind_files, send_list, wet_mask = args[0], args[1], args[6], args[9]
    plan = Plan(
        lax.axis_size("space"), *spectra.shape, send_list.shape[2], *wet_mask.shape, wind_files.shape[2]
    )
    if plan.fits():
        return on_spectrum(plan, *args[:9])
    return on_strips(*args)


def solution(mesh):
    placed = (
        P(("members", "space"), None),
        P(("members", "space"), None, None),
        P(("members", "space"), None, None),
        P(),
        P("space"),
        P(),
        P("space", None, None),
        P("space", None),
        P("space", None, None),
        P("space", None),
    )
    return jax.shard_map(
        on_device,
        mesh=mesh,
        in_specs=placed,
        out_specs=P(("members", "space"), None),
        check_vma=False,
    )
```

```python
import functools
import math

import jax
import jax.numpy as jnp
import numpy as np
from jax import lax
from jax.experimental import pallas as pl
from jax.experimental.pallas import tpu as pltpu
from jax.sharding import PartitionSpec as P

DIRS = 36
FREQS = 36
COARSE = 4


gravity = 9.81
base_freq = 0.0418
freq_ratio = 1.1
freq_span = 35.0
input_coef = 0.0001
wind_gain = 1.12
dissip_coef = 0.0005
half_length = 300.0
courant_scale = 0.05


def from_root(array, axis, root):
    mine = lax.axis_index(axis) == root
    return lax.psum(jnp.where(mine, array, jnp.zeros_like(array)), axis)


def extended(array, sides, width):
    for axis, dim in sides:
        size, length = (lax.axis_size(axis), array.shape[dim])
        up = [(i, (i + 1) % size) for i in range(size - 1)]
        down = [(j, i) for i, j in up]
        last = lax.slice_in_dim(array, length - width, length, axis=dim)
        first = lax.slice_in_dim(array, 0, width, axis=dim)
        before = lax.ppermute(last, axis, up)
        after = lax.ppermute(first, axis, down)
        array = jnp.concatenate([before, array, after], axis=dim)
    return array


def spectral_tables():
    direction = 2.0 * math.pi / DIRS * jnp.arange(DIRS, dtype=jnp.float32)
    exponent = jnp.arange(FREQS, dtype=jnp.float32) * (freq_span / (FREQS - 1))
    frequency = base_freq * freq_ratio**exponent
    angular = 2.0 * math.pi * frequency
    phase_speed = gravity / angular
    return (jnp.cos(direction), jnp.sin(direction), angular, phase_speed, 0.5 * phase_speed)


def source_half(energy, wind_east, wind_north, coupling):
    cos_dir, sine_dir, angular, phase_speed, group_speed = spectral_tables()
    along_wind = wind_east[:, None] * cos_dir[None, :] + wind_north[:, None] * sine_dir[None, :]
    growth = (
        input_coef
        * angular[None, None, :]
        * jnp.maximum(wind_gain * along_wind[:, :, None] / phase_speed[None, None, :] - 1.0, 0.0)
    )
    growth = growth.reshape(energy.shape[0], -1)
    mean_square = jnp.mean(energy * energy, axis=1, keepdims=True)
    decay_rate = dissip_coef * jnp.tile(angular, DIRS)[None, :] * mean_square
    local_part = energy * (1.0 + half_length * growth) / (1.0 + half_length * decay_rate)
    return local_part + jnp.dot(
        local_part.astype(jnp.bfloat16), coupling, preferred_element_type=jnp.float32
    )


def advect(center, upwind_lo, upwind_hi, courant):
    ahead_part = jnp.maximum(courant, 0.0)
    behind = jnp.minimum(courant, 0.0)
    return center - ahead_part * (center - upwind_lo) - behind * (upwind_hi - center)


def sweep_cols(energy_grid, drift_east, wet_field):
    cos_dir, sine_dir, angular, phase_speed, group_speed = spectral_tables()
    wave_speed = (cos_dir[:, None] * group_speed[None, :]).reshape(-1)
    courant = (wave_speed[None, None, :] + drift_east[:, :, None]) * courant_scale
    zero_edge = jnp.zeros_like(energy_grid[:, :1])
    upwind_lo = jnp.concatenate([zero_edge, energy_grid[:, :-1]], axis=1)
    upwind_hi = jnp.concatenate([energy_grid[:, 1:], zero_edge], axis=1)
    return advect(energy_grid, upwind_lo, upwind_hi, courant) * wet_field[:, :, None]


def sweep_rows(energy_grid, row_above, row_below, drift_north, wet_field):
    cos_dir, sine_dir, angular, phase_speed, group_speed = spectral_tables()
    wave_speed = (sine_dir[:, None] * group_speed[None, :]).reshape(-1)
    courant = (wave_speed[None, None, :] + drift_north[:, :, None]) * courant_scale
    return advect(energy_grid, row_above, row_below, courant) * wet_field[:, :, None]


def forcing_points(row_start, row_count, col_count):
    rows_idx = row_start + jnp.arange(row_count, dtype=jnp.int32)
    cols_idx = jnp.arange(col_count, dtype=jnp.int32)
    return rows_idx[:, None] // COARSE * (col_count // COARSE) + cols_idx[None, :] // COARSE


def on_strips(
    spectra,
    wind_files,
    current_files,
    reader_turn,
    cell_point,
    coupling,
    send_list,
    send_count,
    recv_list,
    wet_mask,
):
    levels = []
    for time_level in range(2):
        levels.append(
            (
                from_root(wind_files[0], "space", reader_turn[time_level]),
                from_root(current_files[0], "space", reader_turn[time_level]),
            )
        )
    wind_mean = 0.5 * (levels[0][0] + levels[1][0])
    current_mean = 0.5 * (levels[0][1] + levels[1][1])
    cell_wind = jnp.take(wind_mean, cell_point, axis=1)
    first_half = source_half(spectra, cell_wind[0], cell_wind[1], coupling)
    send_rows = send_list[0]
    counts = send_count[0]
    places = recv_list[0]
    slot_count = send_rows.shape[1]
    spec_width = spectra.shape[1]
    live_slots = (jnp.arange(slot_count, dtype=jnp.int32)[None, :] < counts[:, None]).astype(
        jnp.float32
    )
    packed = first_half[send_rows] * live_slots[:, :, None]
    arrived = lax.all_to_all(packed, "space", split_axis=0, concat_axis=0, tiled=True)
    row_count = wet_mask.shape[0]
    col_count = wet_mask.shape[1]
    energy_grid = (
        jnp.zeros((row_count * col_count, spec_width), jnp.float32)
        .at[places.reshape(-1)]
        .add(arrived.reshape(-1, spec_width))
    )
    energy_grid = energy_grid.reshape(row_count, col_count, spec_width)
    points = forcing_points(lax.axis_index("space") * row_count, row_count, col_count)
    drift = jnp.take(current_mean, points, axis=1)
    wet_field = wet_mask.astype(jnp.float32)
    swept_cols = sweep_cols(energy_grid, drift[0], wet_field)
    padded = extended(swept_cols, (("space", 0),), 1)
    swept = sweep_rows(swept_cols, padded[:-2], padded[2:], drift[1], wet_field).reshape(
        -1, spec_width
    )
    outgoing = swept[places]
    flat_rows = send_rows.reshape(-1)
    empty_rows = jnp.zeros((spectra.shape[0], spec_width), jnp.float32)
    returned = lax.all_to_all(outgoing, "space", split_axis=0, concat_axis=0, tiled=True)
    back_rows = empty_rows.at[flat_rows].add(
        (returned * live_slots[:, :, None]).reshape(-1, spec_width)
    )
    result = source_half(back_rows, cell_wind[0], cell_wind[1], coupling)
    return result


LANES = 128
SUBS = 8
F32 = jnp.float32
BF16 = jnp.bfloat16
MIB = 1024 * 1024
WHOLE_VMEM = 60 * MIB
DRY = 1e30
PARTS = 4
PERIOD = 4 * FREQS


def wave_tables():
    direction = 2.0 * np.pi / DIRS * np.arange(DIRS)
    frequency = base_freq * freq_ratio ** (np.arange(FREQS) * (freq_span / (FREQS - 1)))
    angular = 2.0 * np.pi * frequency
    phase = gravity / angular
    group = 0.5 * phase
    cos_dir, sin_dir = np.cos(direction)[:, None], np.sin(direction)[:, None]
    flat = lambda t: np.broadcast_to(t, (DIRS, FREQS)).reshape(-1)
    growth = half_length * input_coef * angular
    source = np.zeros((DIRS * FREQS, 8), np.float32)
    source[:, 0] = flat(growth * wind_gain * cos_dir / phase)
    source[:, 1] = flat(growth * wind_gain * sin_dir / phase)
    source[:, 2] = flat(1.0 - growth)
    source[:, 3] = flat(half_length * dissip_coef * angular)
    east = flat(courant_scale * cos_dir * group).astype(np.float32)
    north = flat(courant_scale * sin_dir * group).astype(np.float32)
    return source, east, north


def ceil_to(value, step):
    return -(-value // step) * step


def largest_step(size, step, most):
    return max(s for s in range(step, most + 1, step) if size % s == 0)


class Plan:
    def __init__(self, shares, rows, spec, cap, strip_rows, cols, points):
        self.shares, self.rows, self.spec, self.cap = shares, rows, spec, cap
        self.cols, self.points = cols, points
        self.depth = spec // shares
        self.tiles = rows // LANES
        self.data = self.depth * self.tiles
        self.force = 2 * points // (LANES * shares)
        self.block = ceil_to(self.data + self.tiles + self.force, SUBS)
        self.tall = ceil_to(self.depth, SUBS)
        self.strip = strip_rows * cols
        self.grid_rows = strip_rows * shares
        self.coarse_rows = self.grid_rows // COARSE
        self.vregs = cols // SUBS
        self.size = (self.grid_rows + 2) * cols
        self.tall_step = largest_step(spec, PERIOD, 512)
        self.thirds = spec // self.tall_step

    def fits(self):
        if self.spec % self.shares or self.depth > LANES or self.rows % (2 * LANES):
            return False
        if 2 * self.points % (LANES * self.shares) or self.points % LANES or self.cap > LANES:
            return False
        if 2 * self.points // LANES > LANES or self.cols != LANES or self.shares % PARTS:
            return False
        held = 2 * self.size + 2 * self.points + self.shares * (self.block + self.data)
        return 4 * LANES * held + 4 * MIB < 32 * MIB


def pack_kernel(plan, turn_ref, wind_ref, current_ref, recv_ref, out_ref):
    me = lax.axis_index("space")
    half = lambda at: jnp.where(turn_ref[at] == me, 0.5, 0.0)
    mine = half(0) + half(1)
    wind = mine * wind_ref[0]
    points, width, cap = plan.points, plan.force * LANES, plan.cap
    for s in range(plan.shares):
        out_ref[s, :, 0:points] = wind
        out_ref[s, :, points:] = jnp.zeros((2, out_ref.shape[2] - points), F32)
        out_ref[s, 0:1, points : points + cap] = recv_ref[0, s : s + 1, :].astype(F32)
        which, first = divmod(s * width, points)
        out_ref[s, 1:2, points : points + width] = (
            mine * current_ref[0, which : which + 1, first : first + width]
        )


def cell_winds(wind, cp):
    points, rows = wind.shape[1], cp.shape[1]
    high = wind.astype(BF16).astype(F32)
    middle = (wind - high).astype(BF16).astype(F32)
    low = wind - high - middle
    parts = jnp.concatenate([high, middle, low, jnp.zeros((10, points), F32)], axis=0)
    point = lax.broadcasted_iota(jnp.int32, (points, rows), 0)
    hit = jnp.where(point == cp, 1.0, 0.0).astype(BF16)
    picked = jnp.dot(parts.astype(BF16), hit, preferred_element_type=F32)
    both = picked[0:2] + picked[2:4] + picked[4:6]
    return both[0:1], both[1:2]


def fetch(source, target, sems, parts):
    size = target.shape[0] // parts
    copies = [
        pltpu.make_async_copy(
            source.at[pl.ds(q * size, size), :], target.at[pl.ds(q * size, size), :], sems.at[q]
        )
        for q in range(parts)
    ]
    for copy in copies:
        copy.start()
    return copies


def unit_loss(plan, load, arrive, table_ref, unit_ref):
    tall = plan.spec // len(arrive)

    def squares(i, total):
        piece = load(pl.multiple_of(i * 48, 48), 48)
        return total + jnp.sum((piece * piece).reshape(48 // SUBS, SUBS, plan.rows), axis=0)

    total = jnp.zeros((SUBS, plan.rows), F32)
    for q, copy in enumerate(arrive):
        copy.wait()
        total = lax.fori_loop(q * tall // 48, (q + 1) * tall // 48, squares, total)
    mean_square = jnp.sum(total, axis=0, keepdims=True) * (1.0 / plan.spec)
    unit_ref[...] = 1.0 / (1.0 + table_ref[0:PERIOD, 3:4] * mean_square)


def growth_step(first, east, north, table_ref):
    table = table_ref[pl.ds(first, PERIOD), :]
    return jnp.maximum(east * table[:, 0:1] + north * table[:, 1:2] + table[:, 2:3], 1.0)


def coupled(plan, coup_ref, loc_ref, locb_ref, store):
    for q in range(plan.thirds):
        at = slice(q * plan.tall_step, (q + 1) * plan.tall_step)
        store(
            q * plan.tall_step,
            loc_ref[at, :]
            + jnp.dot(coup_ref[at, :], locb_ref[...], preferred_element_type=F32),
        )


def ready_kernel(
    plan, table_ref, coup_hbm, energy_hbm, unit_ref, turned_hbm,
    coup_ref, turned_ref, energy_ref, sems, coup_sem, out_sems,
):
    spec = plan.spec
    arrive = fetch(energy_hbm, energy_ref, sems, plan.thirds)
    get = pltpu.make_async_copy(coup_hbm, coup_ref, coup_sem)
    get.start()
    unit_loss(plan, lambda first, count: energy_ref[pl.ds(first, count), :], arrive, table_ref, unit_ref)
    get.wait()
    copies, wide = [], 3 * LANES
    for first in range(0, spec, LANES):
        at = slice(first, min(first + LANES, spec))
        turned_ref[at, :] = coup_ref[:, at].T
        if at.stop % wide == 0 or at.stop == spec:
            done = slice((at.stop - 1) // wide * wide, at.stop)
            copies.append(
                pltpu.make_async_copy(
                    turned_ref.at[done, :], turned_hbm.at[done, :], out_sems.at[len(copies)]
                )
            )
            copies[-1].start()
    for copy in copies:
        copy.wait()


def own_places(plan, parcel_ref, send_ref, count_ref):
    points, cols, vregs, cap = plan.points, plan.cols, plan.vregs, plan.cap
    landing = jnp.concatenate(
        [parcel_ref[b, 0:1, points : points + cap] for b in range(plan.shares)], axis=0
    ).astype(jnp.int32)
    cell = landing + plan.strip * lax.broadcasted_iota(jnp.int32, (plan.shares, cap), 0)
    column = lax.rem(cell, cols)
    place = cell - column + cols + lax.rem(column, vregs) * SUBS + lax.div(column, vregs)
    place = place.astype(F32)
    slot = lax.broadcasted_iota(jnp.int32, (1, cap), 1)
    names = [
        jnp.where(slot < count_ref[0, b], send_ref[0, b : b + 1, :], -1) for b in range(plan.shares)
    ]
    rows = []
    for j in range(plan.tiles):
        own = lax.broadcasted_iota(jnp.int32, (LANES, cap), 0) + j * LANES
        found = jnp.zeros((LANES, cap), F32)
        for b in range(plan.shares):
            found += jnp.where(names[b] == own, place[b : b + 1, :], 0.0)
        found = jnp.broadcast_to(jnp.sum(found, axis=1, keepdims=True), (LANES, LANES)).T
        shift = lax.rem(lax.broadcasted_iota(jnp.int32, (1, LANES), 1), SUBS).astype(F32)
        rows.append(found[0:1, :] - shift)
    return rows


def first_kernel(
    plan,
    count_ref, cp_ref, parcel_ref, send_ref, table_ref, unit_ref, energy_hbm, coup_hbm, winds_ref, out_hbm,
    out_ref, buf_ref, loc_ref, coup_ref, locb_ref, sems, coup_sem, out_sems,
):
    tiles, shares, points, block, data = plan.tiles, plan.shares, plan.points, plan.block, plan.data
    arrive = fetch(energy_hbm, loc_ref, sems, plan.thirds)
    get = pltpu.make_async_copy(coup_hbm, coup_ref, coup_sem)
    get.start()
    width = plan.force * LANES
    current = jnp.sum(parcel_ref[:, :, points : points + width], axis=0)
    spare = own_places(plan, parcel_ref, send_ref, count_ref)
    spare += [current[1:2, f * LANES : (f + 1) * LANES] for f in range(plan.force)]
    if block > data + len(spare):
        spare.append(jnp.zeros((block - data - len(spare), LANES), F32))
    for d in range(shares):
        out_ref[d * block + data : (d + 1) * block, :] = jnp.concatenate(spare, axis=0)
    east, north = cell_winds(jnp.sum(parcel_ref[:, :, 0:points], axis=0), cp_ref[...])
    winds_ref[0:1, :] = east
    winds_ref[1:2, :] = north
    per = plan.tall_step // PERIOD
    for q in range(plan.thirds):
        arrive[q].wait()

        @pl.loop(q * per, (q + 1) * per)
        def _(i):
            first = pl.multiple_of(i * PERIOD, PERIOD)
            at = pl.ds(first, PERIOD)
            local = loc_ref[at, :] * unit_ref[...] * growth_step(first, east, north, table_ref)
            loc_ref[at, :] = local
            locb_ref[at, :] = local.astype(BF16)

    get.wait()
    sent, copies = [0], []

    def store(first, values):
        for j in range(tiles):
            buf_ref[pl.ds(first * tiles + j, values.shape[0], stride=tiles), :] = values[
                :, j * LANES : (j + 1) * LANES
            ]
        upto = (first + values.shape[0]) // plan.depth
        for d in range(sent[0], upto):
            out_ref[d * block : d * block + data, :] = buf_ref[d * data : (d + 1) * data, :]
        at = slice(sent[0] * block, upto * block)
        copies.append(
            pltpu.make_async_copy(out_ref.at[at, :], out_hbm.at[at, :], out_sems.at[len(copies)])
        )
        copies[-1].start()
        sent[0] = upto

    coupled(plan, coup_ref, loc_ref, locb_ref, store)
    for copy in copies:
        copy.wait()


def last_kernel(
    plan,
    winds_ref, table_ref, came_hbm, coup_hbm, out_hbm,
    came_ref, coup_ref, loc_ref, locb_ref, unit_ref, sems, coup_sem, out_sems,
):
    tiles = plan.tiles
    copies = []
    arrive = fetch(came_hbm, came_ref, sems, plan.thirds)
    get = pltpu.make_async_copy(coup_hbm, coup_ref, coup_sem)
    get.start()

    def load(first, count):
        start = pl.multiple_of(first * tiles, SUBS)
        return jnp.concatenate(
            [came_ref[pl.ds(start + j, count, stride=tiles), :] for j in range(tiles)], axis=1
        )

    unit_loss(plan, load, arrive, table_ref, unit_ref)
    east, north = winds_ref[0:1, :], winds_ref[1:2, :]

    @pl.loop(0, plan.spec // PERIOD)
    def _(i):
        first = pl.multiple_of(i * PERIOD, PERIOD)
        at = pl.ds(first, PERIOD)
        local = load(first, PERIOD) * unit_ref[...] * growth_step(first, east, north, table_ref)
        loc_ref[at, :] = local
        locb_ref[at, :] = local.astype(BF16)

    def store(first, values):
        at = slice(first, first + values.shape[0])
        loc_ref[at, :] = values
        copies.append(
            pltpu.make_async_copy(loc_ref.at[at, :], out_hbm.at[at, :], out_sems.at[len(copies)])
        )
        copies[-1].start()

    get.wait()
    coupled(plan, coup_ref, loc_ref, locb_ref, store)
    for copy in copies:
        copy.wait()


def scatter(plan, place_ref, came_ref, grid_ref, cell_ref, arrived):
    depth, tiles, tall = plan.depth, plan.tiles, plan.tall
    sub = lax.broadcasted_iota(jnp.int32, (SUBS, LANES), 0)
    fill = [jnp.zeros((tall - depth, LANES), F32)] if tall > depth else []
    per = plan.shares // PARTS

    @pl.loop(0, plan.shares)
    def _(s):
        @pl.when(s % per == 0)
        def _():
            arrived(s // per)

        blocks = [
            came_ref[pl.ds(s * plan.block + j, depth, stride=tiles), :] for j in range(tiles)
        ]
        turned = [jnp.concatenate([block] + fill, axis=0).T for block in blocks]
        for j in range(tiles):
            cell_ref[j * LANES : (j + 1) * LANES, 0:tall] = turned[j]

        @pl.loop(0, tiles)
        def _(j):
            first = s * plan.rows + j * LANES
            for g in range(LANES // SUBS):
                at = pl.ds(pl.multiple_of(j * LANES + g * SUBS, SUBS), SUBS)
                values = cell_ref[at, :]
                for t in range(SUBS):
                    spot = place_ref[first + g * SUBS + t]
                    pltpu.store(grid_ref.at[pl.ds(spot, SUBS), :], values, mask=sub == t)


def gather(plan, place_ref, out_ref, grid_ref, cell_ref, finished):
    depth, tiles, tall = plan.depth, plan.tiles, plan.tall
    sub = lax.broadcasted_iota(jnp.int32, (SUBS, LANES), 0)
    per = plan.shares // PARTS

    @pl.loop(0, plan.shares)
    def _(s):
        @pl.loop(0, tiles)
        def _(j):
            first = s * plan.rows + j * LANES
            for g in range(LANES // SUBS):
                values = grid_ref[pl.ds(place_ref[first + g * SUBS], SUBS), :]
                for t in range(1, SUBS):
                    shifted = grid_ref[pl.ds(place_ref[first + g * SUBS + t], SUBS), :]
                    values = jnp.where(sub == t, shifted, values)
                cell_ref[pl.ds(pl.multiple_of(j * LANES + g * SUBS, SUBS), SUBS), :] = values

        turned = [cell_ref[j * LANES : (j + 1) * LANES, 0:tall].T for j in range(tiles)]
        for j in range(tiles):
            out_ref[pl.ds(s * plan.data + j, depth, stride=tiles), :] = turned[j][0:depth, :]

        @pl.when(s % per == per - 1)
        def _():
            finished(s // per)


def spread_drift(plan, came_ref, held, turned, drift_ref):
    held[...] = jnp.zeros((LANES, LANES), F32)
    for s in range(plan.shares):
        first = s * plan.block + plan.data + plan.tiles
        held[s * plan.force : (s + 1) * plan.force, :] = came_ref[first : first + plan.force, :]
    turned[...] = (courant_scale * held[...]).T
    groups = plan.vregs // COARSE
    ordered = jnp.concatenate(
        [
            turned[pl.ds(a * groups * SUBS + m, SUBS, stride=groups), :]
            for a in range(LANES // (groups * SUBS))
            for m in range(groups)
        ],
        axis=0,
    )
    for q in range(plan.shares * plan.force):
        drift_ref[q * LANES : (q + 1) * LANES, :] = jnp.broadcast_to(
            ordered[:, q : q + 1], (LANES, LANES)
        )


def sweep(plan, drift_ref, speed_ref, one_ref, two_ref):
    cols, last = plan.cols, plan.coarse_rows - 1
    groups = plan.vregs // COARSE
    sub = lax.broadcasted_iota(jnp.int32, (SUBS, LANES), 0)
    speeds = [jnp.broadcast_to(speed_ref[d : d + 1, :], (SUBS, LANES)) for d in range(2)]

    for m in range(groups):

        def courant(which, r4):
            at = pl.multiple_of(((which * plan.coarse_rows + r4) * groups + m) * SUBS, SUBS)
            value = speeds[which] + drift_ref[pl.ds(at, SUBS), :]
            return value > 0.0, jnp.abs(value)

        def at(row, q):
            return pl.ds(pl.multiple_of((row + 1) * cols + q * SUBS, SUBS), SUBS)

        def along(row, speed):
            ahead, size = speed
            base = pl.multiple_of((row + 1) * cols, SUBS)
            first, count = m * COARSE, COARSE
            line = [one_ref[at(row, q), :] for q in range(first, first + count)]
            if first:
                before = one_ref[at(row, first - 1), :]
            else:
                before = one_ref[pl.ds(base + cols - SUBS - 1, SUBS), :]
                before = jnp.where(sub == 0, DRY, before)
            if first + count < plan.vregs:
                after = one_ref[at(row, first + count), :]
            else:
                after = jnp.where(sub == SUBS - 1, DRY, one_ref[pl.ds(base + 1, SUBS), :])
            line = [before] + line + [after]
            swept = []
            for q in range(1, count + 1):
                pick = jnp.where(ahead, line[q - 1], line[q + 1])
                pick = jnp.where(pick < DRY, pick, 0.0)
                moved = line[q] + size * (pick - line[q])
                swept.append(jnp.where(line[q] < DRY, moved, 0.0))
            return swept

        def coarse(r4, held):
            above, here = held
            east = courant(0, r4)
            ahead, size = courant(1, r4)
            later = courant(0, jnp.minimum(r4 + 1, last))
            for dr in range(COARSE):
                row = r4 * COARSE + dr
                below = along(row + 1, east if dr < COARSE - 1 else later)
                for q in range(COARSE):
                    pick = jnp.where(ahead, above[q], below[q])
                    two_ref[at(row, m * COARSE + q), :] = here[q] + size * (pick - here[q])
                above, here = here, below
            return above, here

        zero = [jnp.zeros((SUBS, LANES), F32)] * COARSE
        lax.fori_loop(0, plan.coarse_rows, coarse, (zero, along(0, courant(0, 0))), unroll=2)


def middle_kernel(
    plan,
    place_ref, speed_ref, came_hbm, out_hbm,
    came_ref, out_ref, one_ref, two_ref, drift_ref, cell_ref, in_sems, out_sems,
):
    shares, block, data = plan.shares, plan.block, plan.data
    part_in, part_out = shares // PARTS * block, shares // PARTS * data

    def copy_in(part):
        at = pl.ds(pl.multiple_of(part * part_in, SUBS), part_in)
        return pltpu.make_async_copy(came_hbm.at[at, :], came_ref.at[at, :], in_sems.at[part])

    def copy_out(part):
        at = pl.ds(pl.multiple_of(part * part_out, SUBS), part_out)
        return pltpu.make_async_copy(out_ref.at[at, :], out_hbm.at[at, :], out_sems.at[part])

    for part in range(PARTS):
        copy_in(part).start()

    @pl.loop(0, plan.size // LANES)
    def _(i):
        at = pl.ds(pl.multiple_of(i * LANES, LANES), LANES)
        one_ref[at, :] = jnp.full((LANES, LANES), DRY, F32)

    scatter(plan, place_ref, came_ref, one_ref, cell_ref, lambda part: copy_in(part).wait())
    spread_drift(plan, came_ref, cell_ref.at[0:LANES], cell_ref.at[LANES : 2 * LANES], drift_ref)
    me = lax.axis_index("space")
    sweep(plan, drift_ref, speed_ref.at[me], one_ref, two_ref)
    gather(plan, place_ref, out_ref, two_ref, cell_ref, lambda part: copy_out(part).start())
    for part in range(PARTS):
        copy_out(part).wait()


VMEM = pl.BlockSpec(memory_space=pltpu.VMEM)
SMEM = pl.BlockSpec(memory_space=pltpu.SMEM)
ANY = pl.BlockSpec(memory_space=pl.ANY)


def on_spectrum(
    plan,
    spectra,
    wind_files,
    current_files,
    reader_turn,
    cell_point,
    coupling,
    send_list,
    send_count,
    recv_list,
):
    shares, rows, spec, points = plan.shares, plan.rows, plan.spec, plan.points
    tiles, depth, size, data_rows = plan.tiles, plan.depth, plan.size, plan.shares * plan.data
    source, east_speed, north_speed = wave_tables()
    table = jnp.asarray(source)
    speed = np.zeros((shares, SUBS, LANES), np.float32)
    speed[:, 0, :depth] = east_speed.reshape(shares, depth)
    speed[:, 1, :depth] = north_speed.reshape(shares, depth)

    def kernel(body, *, flops, traffic, vmem=WHOLE_VMEM, **options):
        return pl.pallas_call(
            body,
            compiler_params=pltpu.CompilerParams(vmem_limit_bytes=vmem),
            cost_estimate=pl.CostEstimate(flops=flops, bytes_accessed=traffic, transcendentals=0),
            **options,
        )

    width = points + max(LANES, plan.force * LANES)
    parcel = kernel(
        functools.partial(pack_kernel, plan),
        flops=0, traffic=4 * shares * 2 * width,
        out_shape=jax.ShapeDtypeStruct((shares, 2, width), F32),
        in_specs=[SMEM, VMEM, VMEM, VMEM],
        out_specs=VMEM,
        name="pack",
    )(reader_turn, wind_files, current_files, recv_list)
    parcel = lax.all_to_all(parcel, "space", 0, 0, tiled=True)

    cp = cell_point.reshape(1, rows)
    h_cost = dict(flops=2 * rows * spec * spec, traffic=12 * rows * spec)
    whole = pltpu.VMEM((spec, rows), F32)
    rounded = pltpu.VMEM((spec, rows), BF16)
    square = pltpu.VMEM((spec, spec), BF16)
    unit = pltpu.VMEM((PERIOD, rows), F32)
    dma = pltpu.SemaphoreType.DMA
    unit_loss_held, coup = kernel(
        functools.partial(ready_kernel, plan),
        flops=0, traffic=12 * rows * spec,
        out_shape=[
            jax.ShapeDtypeStruct((PERIOD, rows), F32), jax.ShapeDtypeStruct((spec, spec), BF16)
        ],
        in_specs=[VMEM, ANY, ANY],
        out_specs=[VMEM, ANY],
        scratch_shapes=[square, square, whole, dma((plan.thirds,)), dma, dma((8,))],
        name="ready",
    )(table, coupling, spectra.T)
    winds, sent = kernel(
        functools.partial(first_kernel, plan),
        **h_cost,
        out_shape=[
            jax.ShapeDtypeStruct((SUBS, rows), F32),
            jax.ShapeDtypeStruct((shares * plan.block, LANES), F32),
        ],
        in_specs=[SMEM] + [VMEM] * 5 + [ANY] * 2,
        out_specs=[VMEM, ANY],
        scratch_shapes=[
            pltpu.VMEM((shares * plan.block, LANES), F32),
            pltpu.VMEM((data_rows, LANES), F32),
            whole, square, rounded, dma((plan.thirds,)), dma, dma((plan.thirds,)),
        ],
        name="first_half",
    )(send_count, cp, parcel, send_list, table, unit_loss_held, spectra.T, coup)
    came = lax.all_to_all(
        sent.reshape(shares, plan.block, LANES), "space", 0, 0, tiled=True
    )
    place = came[:, plan.data : plan.data + tiles].astype(jnp.int32).reshape(-1)
    swept = kernel(
        functools.partial(middle_kernel, plan),
        flops=24 * size * LANES, traffic=8 * rows * spec, vmem=32 * MIB,
        out_shape=jax.ShapeDtypeStruct((data_rows, LANES), F32),
        in_specs=[SMEM, VMEM, ANY],
        out_specs=ANY,
        scratch_shapes=[
            pltpu.VMEM((shares * plan.block, LANES), F32),
            pltpu.VMEM((data_rows, LANES), F32),
            pltpu.VMEM((size, LANES), F32),
            pltpu.VMEM((size, LANES), F32),
            pltpu.VMEM((2 * points, LANES), F32),
            pltpu.VMEM((rows, LANES), F32),
            pltpu.SemaphoreType.DMA((PARTS,)),
            pltpu.SemaphoreType.DMA((PARTS,)),
        ],
        name="sweeps",
    )(place, jnp.asarray(speed), came.reshape(-1, LANES))
    back = lax.all_to_all(
        swept.reshape(shares, depth, tiles, LANES), "space", 0, 0, tiled=True
    )
    result = kernel(
        functools.partial(last_kernel, plan),
        vmem=24 * MIB, **h_cost,
        out_shape=jax.ShapeDtypeStruct((spec, rows), F32),
        in_specs=[VMEM] * 2 + [ANY] * 2,
        out_specs=ANY,
        scratch_shapes=[
            pltpu.VMEM((data_rows, LANES), F32),
            square, whole, rounded, unit, dma((plan.thirds,)), dma, dma((plan.thirds,)),
        ],
        name="last_half",
    )(winds, table, back.reshape(data_rows, LANES), coup)
    return result.T


def on_device(*args):
    spectra, wind_files, send_list, wet_mask = args[0], args[1], args[6], args[9]
    plan = Plan(
        lax.axis_size("space"), *spectra.shape, send_list.shape[2], *wet_mask.shape, wind_files.shape[2]
    )
    if plan.fits():
        return on_spectrum(plan, *args[:9])
    return on_strips(*args)


def solution(mesh):
    placed = (
        P(("members", "space"), None),
        P(("members", "space"), None, None),
        P(("members", "space"), None, None),
        P(),
        P("space"),
        P(),
        P("space", None, None),
        P("space", None),
        P("space", None, None),
        P("space", None),
    )
    return jax.shard_map(
        on_device,
        mesh=mesh,
        in_specs=placed,
        out_specs=P(("members", "space"), None),
        check_vma=False,
    )
```

```python
import functools
import math

import jax
import jax.numpy as jnp
import numpy as np
from jax import lax
from jax.experimental import pallas as pl
from jax.experimental.pallas import tpu as pltpu
from jax.sharding import PartitionSpec as P

DIRS = 36
FREQS = 36
COARSE = 4


gravity = 9.81
base_freq = 0.0418
freq_ratio = 1.1
freq_span = 35.0
input_coef = 0.0001
wind_gain = 1.12
dissip_coef = 0.0005
half_length = 300.0
courant_scale = 0.05


def from_root(array, axis, root):
    mine = lax.axis_index(axis) == root
    return lax.psum(jnp.where(mine, array, jnp.zeros_like(array)), axis)


def extended(array, sides, width):
    for axis, dim in sides:
        size, length = (lax.axis_size(axis), array.shape[dim])
        up = [(i, (i + 1) % size) for i in range(size - 1)]
        down = [(j, i) for i, j in up]
        last = lax.slice_in_dim(array, length - width, length, axis=dim)
        first = lax.slice_in_dim(array, 0, width, axis=dim)
        before = lax.ppermute(last, axis, up)
        after = lax.ppermute(first, axis, down)
        array = jnp.concatenate([before, array, after], axis=dim)
    return array


def spectral_tables():
    direction = 2.0 * math.pi / DIRS * jnp.arange(DIRS, dtype=jnp.float32)
    exponent = jnp.arange(FREQS, dtype=jnp.float32) * (freq_span / (FREQS - 1))
    frequency = base_freq * freq_ratio**exponent
    angular = 2.0 * math.pi * frequency
    phase_speed = gravity / angular
    return (jnp.cos(direction), jnp.sin(direction), angular, phase_speed, 0.5 * phase_speed)


def source_half(energy, wind_east, wind_north, coupling):
    cos_dir, sine_dir, angular, phase_speed, group_speed = spectral_tables()
    along_wind = wind_east[:, None] * cos_dir[None, :] + wind_north[:, None] * sine_dir[None, :]
    growth = (
        input_coef
        * angular[None, None, :]
        * jnp.maximum(wind_gain * along_wind[:, :, None] / phase_speed[None, None, :] - 1.0, 0.0)
    )
    growth = growth.reshape(energy.shape[0], -1)
    mean_square = jnp.mean(energy * energy, axis=1, keepdims=True)
    decay_rate = dissip_coef * jnp.tile(angular, DIRS)[None, :] * mean_square
    local_part = energy * (1.0 + half_length * growth) / (1.0 + half_length * decay_rate)
    return local_part + jnp.dot(
        local_part.astype(jnp.bfloat16), coupling, preferred_element_type=jnp.float32
    )


def advect(center, upwind_lo, upwind_hi, courant):
    ahead_part = jnp.maximum(courant, 0.0)
    behind = jnp.minimum(courant, 0.0)
    return center - ahead_part * (center - upwind_lo) - behind * (upwind_hi - center)


def sweep_cols(energy_grid, drift_east, wet_field):
    cos_dir, sine_dir, angular, phase_speed, group_speed = spectral_tables()
    wave_speed = (cos_dir[:, None] * group_speed[None, :]).reshape(-1)
    courant = (wave_speed[None, None, :] + drift_east[:, :, None]) * courant_scale
    zero_edge = jnp.zeros_like(energy_grid[:, :1])
    upwind_lo = jnp.concatenate([zero_edge, energy_grid[:, :-1]], axis=1)
    upwind_hi = jnp.concatenate([energy_grid[:, 1:], zero_edge], axis=1)
    return advect(energy_grid, upwind_lo, upwind_hi, courant) * wet_field[:, :, None]


def sweep_rows(energy_grid, row_above, row_below, drift_north, wet_field):
    cos_dir, sine_dir, angular, phase_speed, group_speed = spectral_tables()
    wave_speed = (sine_dir[:, None] * group_speed[None, :]).reshape(-1)
    courant = (wave_speed[None, None, :] + drift_north[:, :, None]) * courant_scale
    return advect(energy_grid, row_above, row_below, courant) * wet_field[:, :, None]


def forcing_points(row_start, row_count, col_count):
    rows_idx = row_start + jnp.arange(row_count, dtype=jnp.int32)
    cols_idx = jnp.arange(col_count, dtype=jnp.int32)
    return rows_idx[:, None] // COARSE * (col_count // COARSE) + cols_idx[None, :] // COARSE


def on_strips(
    spectra,
    wind_files,
    current_files,
    reader_turn,
    cell_point,
    coupling,
    send_list,
    send_count,
    recv_list,
    wet_mask,
):
    levels = []
    for time_level in range(2):
        levels.append(
            (
                from_root(wind_files[0], "space", reader_turn[time_level]),
                from_root(current_files[0], "space", reader_turn[time_level]),
            )
        )
    wind_mean = 0.5 * (levels[0][0] + levels[1][0])
    current_mean = 0.5 * (levels[0][1] + levels[1][1])
    cell_wind = jnp.take(wind_mean, cell_point, axis=1)
    first_half = source_half(spectra, cell_wind[0], cell_wind[1], coupling)
    send_rows = send_list[0]
    counts = send_count[0]
    places = recv_list[0]
    slot_count = send_rows.shape[1]
    spec_width = spectra.shape[1]
    live_slots = (jnp.arange(slot_count, dtype=jnp.int32)[None, :] < counts[:, None]).astype(
        jnp.float32
    )
    packed = first_half[send_rows] * live_slots[:, :, None]
    arrived = lax.all_to_all(packed, "space", split_axis=0, concat_axis=0, tiled=True)
    row_count = wet_mask.shape[0]
    col_count = wet_mask.shape[1]
    energy_grid = (
        jnp.zeros((row_count * col_count, spec_width), jnp.float32)
        .at[places.reshape(-1)]
        .add(arrived.reshape(-1, spec_width))
    )
    energy_grid = energy_grid.reshape(row_count, col_count, spec_width)
    points = forcing_points(lax.axis_index("space") * row_count, row_count, col_count)
    drift = jnp.take(current_mean, points, axis=1)
    wet_field = wet_mask.astype(jnp.float32)
    swept_cols = sweep_cols(energy_grid, drift[0], wet_field)
    padded = extended(swept_cols, (("space", 0),), 1)
    swept = sweep_rows(swept_cols, padded[:-2], padded[2:], drift[1], wet_field).reshape(
        -1, spec_width
    )
    outgoing = swept[places]
    flat_rows = send_rows.reshape(-1)
    empty_rows = jnp.zeros((spectra.shape[0], spec_width), jnp.float32)
    returned = lax.all_to_all(outgoing, "space", split_axis=0, concat_axis=0, tiled=True)
    back_rows = empty_rows.at[flat_rows].add(
        (returned * live_slots[:, :, None]).reshape(-1, spec_width)
    )
    result = source_half(back_rows, cell_wind[0], cell_wind[1], coupling)
    return result


LANES = 128
SUBS = 8
F32 = jnp.float32
BF16 = jnp.bfloat16
MIB = 1024 * 1024
WHOLE_VMEM = 60 * MIB
DRY = 1e30
PARTS = 2
PERIOD = 4 * FREQS


def wave_tables():
    direction = 2.0 * np.pi / DIRS * np.arange(DIRS)
    frequency = base_freq * freq_ratio ** (np.arange(FREQS) * (freq_span / (FREQS - 1)))
    angular = 2.0 * np.pi * frequency
    phase = gravity / angular
    group = 0.5 * phase
    cos_dir, sin_dir = np.cos(direction)[:, None], np.sin(direction)[:, None]
    flat = lambda t: np.broadcast_to(t, (DIRS, FREQS)).reshape(-1)
    growth = half_length * input_coef * angular
    source = np.zeros((DIRS * FREQS, 8), np.float32)
    source[:, 0] = flat(growth * wind_gain * cos_dir / phase)
    source[:, 1] = flat(growth * wind_gain * sin_dir / phase)
    source[:, 2] = flat(1.0 - growth)
    source[:, 3] = flat(half_length * dissip_coef * angular)
    east = flat(courant_scale * cos_dir * group).astype(np.float32)
    north = flat(courant_scale * sin_dir * group).astype(np.float32)
    return source, east, north


def ceil_to(value, step):
    return -(-value // step) * step


def largest_step(size, step, most):
    return max(s for s in range(step, most + 1, step) if size % s == 0)


class Plan:
    def __init__(self, shares, rows, spec, cap, strip_rows, cols, points):
        self.shares, self.rows, self.spec, self.cap = shares, rows, spec, cap
        self.cols, self.points = cols, points
        self.depth = spec // shares
        self.tiles = rows // LANES
        self.data = self.depth * self.tiles
        self.force = 2 * points // (LANES * shares)
        self.block = self.data + self.tiles + self.force
        self.tall = ceil_to(self.depth, SUBS)
        self.strip = strip_rows * cols
        self.grid_rows = strip_rows * shares
        self.coarse_rows = self.grid_rows // COARSE
        self.vregs = cols // SUBS
        self.size = (self.grid_rows + 2) * cols
        self.tall_step = largest_step(spec, PERIOD, 512)
        self.thirds = spec // self.tall_step

    def fits(self):
        if self.spec % self.shares or self.depth > LANES or self.rows % (2 * LANES):
            return False
        if 2 * self.points % (LANES * self.shares) or self.points % LANES or self.cap > LANES:
            return False
        if self.shares // PARTS * self.block % SUBS or self.shares // PARTS * self.data % SUBS:
            return False
        if 2 * self.points // LANES > LANES or self.cols != LANES or self.shares % PARTS:
            return False
        held = 2 * self.size + 2 * self.points + self.shares * (self.block + self.data)
        return 4 * LANES * held + 4 * MIB < 32 * MIB


def pack_kernel(plan, turn_ref, wind_ref, current_ref, recv_ref, out_ref):
    me = lax.axis_index("space")
    half = lambda at: jnp.where(turn_ref[at] == me, 0.5, 0.0)
    mine = half(0) + half(1)
    wind = mine * wind_ref[0]
    points, width, cap = plan.points, plan.force * LANES, plan.cap
    for s in range(plan.shares):
        out_ref[s, :, 0:points] = wind
        out_ref[s, :, points:] = jnp.zeros((2, out_ref.shape[2] - points), F32)
        out_ref[s, 0:1, points : points + cap] = recv_ref[0, s : s + 1, :].astype(F32)
        which, first = divmod(s * width, points)
        out_ref[s, 1:2, points : points + width] = (
            mine * current_ref[0, which : which + 1, first : first + width]
        )


def cell_winds(wind, cp):
    points, rows = wind.shape[1], cp.shape[1]
    high = wind.astype(BF16).astype(F32)
    middle = (wind - high).astype(BF16).astype(F32)
    low = wind - high - middle
    parts = jnp.concatenate([high, middle, low, jnp.zeros((10, points), F32)], axis=0)
    point = lax.broadcasted_iota(jnp.int32, (points, rows), 0)
    hit = jnp.where(point == cp, 1.0, 0.0).astype(BF16)
    picked = jnp.dot(parts.astype(BF16), hit, preferred_element_type=F32)
    both = picked[0:2] + picked[2:4] + picked[4:6]
    return both[0:1], both[1:2]


def fetch(source, target, sems, parts):
    size = target.shape[0] // parts
    copies = [
        pltpu.make_async_copy(
            source.at[pl.ds(q * size, size), :], target.at[pl.ds(q * size, size), :], sems.at[q]
        )
        for q in range(parts)
    ]
    for copy in copies:
        copy.start()
    return copies


def unit_loss(plan, load, arrive, table_ref, unit_ref):
    tall = plan.spec // len(arrive)

    def squares(i, total):
        piece = load(pl.multiple_of(i * 48, 48), 48)
        return total + jnp.sum((piece * piece).reshape(48 // SUBS, SUBS, plan.rows), axis=0)

    total = jnp.zeros((SUBS, plan.rows), F32)
    for q, copy in enumerate(arrive):
        copy.wait()
        total = lax.fori_loop(q * tall // 48, (q + 1) * tall // 48, squares, total)
    mean_square = jnp.sum(total, axis=0, keepdims=True) * (1.0 / plan.spec)
    unit_ref[...] = 1.0 / (1.0 + table_ref[0:PERIOD, 3:4] * mean_square)


def growth_step(first, east, north, table_ref):
    table = table_ref[pl.ds(first, PERIOD), :]
    return jnp.maximum(east * table[:, 0:1] + north * table[:, 1:2] + table[:, 2:3], 1.0)


def coupled(plan, coup_ref, loc_ref, locb_ref, store):
    for q in range(plan.thirds):
        at = slice(q * plan.tall_step, (q + 1) * plan.tall_step)
        store(
            q * plan.tall_step,
            loc_ref[at, :]
            + jnp.dot(coup_ref[at, :], locb_ref[...], preferred_element_type=F32),
        )


def ready_kernel(
    plan, table_ref, coup_hbm, energy_hbm, unit_ref, turned_hbm,
    coup_ref, turned_ref, energy_ref, sems, coup_sem, out_sems,
):
    spec = plan.spec
    arrive = fetch(energy_hbm, energy_ref, sems, plan.thirds)
    get = pltpu.make_async_copy(coup_hbm, coup_ref, coup_sem)
    get.start()
    unit_loss(plan, lambda first, count: energy_ref[pl.ds(first, count), :], arrive, table_ref, unit_ref)
    get.wait()
    copies, wide = [], 3 * LANES
    for first in range(0, spec, LANES):
        at = slice(first, min(first + LANES, spec))
        turned_ref[at, :] = coup_ref[:, at].T
        if at.stop % wide == 0 or at.stop == spec:
            done = slice((at.stop - 1) // wide * wide, at.stop)
            copies.append(
                pltpu.make_async_copy(
                    turned_ref.at[done, :], turned_hbm.at[done, :], out_sems.at[len(copies)]
                )
            )
            copies[-1].start()
    for copy in copies:
        copy.wait()


def own_places(plan, parcel_ref, send_ref, count_ref):
    points, cols, vregs, cap = plan.points, plan.cols, plan.vregs, plan.cap
    landing = jnp.concatenate(
        [parcel_ref[b, 0:1, points : points + cap] for b in range(plan.shares)], axis=0
    ).astype(jnp.int32)
    cell = landing + plan.strip * lax.broadcasted_iota(jnp.int32, (plan.shares, cap), 0)
    column = lax.rem(cell, cols)
    place = cell - column + cols + lax.rem(column, vregs) * SUBS + lax.div(column, vregs)
    place = place.astype(F32)
    slot = lax.broadcasted_iota(jnp.int32, (1, cap), 1)
    names = [
        jnp.where(slot < count_ref[0, b], send_ref[0, b : b + 1, :], -1) for b in range(plan.shares)
    ]
    rows = []
    for j in range(plan.tiles):
        own = lax.broadcasted_iota(jnp.int32, (LANES, cap), 0) + j * LANES
        found = jnp.zeros((LANES, cap), F32)
        for b in range(plan.shares):
            found += jnp.where(names[b] == own, place[b : b + 1, :], 0.0)
        found = jnp.broadcast_to(jnp.sum(found, axis=1, keepdims=True), (LANES, LANES)).T
        shift = lax.rem(lax.broadcasted_iota(jnp.int32, (1, LANES), 1), SUBS).astype(F32)
        rows.append(found[0:1, :] - shift)
    return rows


def first_kernel(
    plan,
    count_ref, cp_ref, parcel_ref, send_ref, table_ref, unit_ref, energy_hbm, coup_hbm, winds_ref, out_hbm,
    out_ref, buf_ref, loc_ref, coup_ref, locb_ref, sems, coup_sem, out_sems,
):
    tiles, shares, points, block, data = plan.tiles, plan.shares, plan.points, plan.block, plan.data
    arrive = fetch(energy_hbm, loc_ref, sems, plan.thirds)
    get = pltpu.make_async_copy(coup_hbm, coup_ref, coup_sem)
    get.start()
    width = plan.force * LANES
    current = jnp.sum(parcel_ref[:, :, points : points + width], axis=0)
    spare = own_places(plan, parcel_ref, send_ref, count_ref)
    spare += [current[1:2, f * LANES : (f + 1) * LANES] for f in range(plan.force)]
    for d in range(shares):
        out_ref[d * block + data : (d + 1) * block, :] = jnp.concatenate(spare, axis=0)
    east, north = cell_winds(jnp.sum(parcel_ref[:, :, 0:points], axis=0), cp_ref[...])
    winds_ref[0:1, :] = east
    winds_ref[1:2, :] = north
    per = plan.tall_step // PERIOD
    for q in range(plan.thirds):
        arrive[q].wait()

        @pl.loop(q * per, (q + 1) * per)
        def _(i):
            first = pl.multiple_of(i * PERIOD, PERIOD)
            at = pl.ds(first, PERIOD)
            local = loc_ref[at, :] * unit_ref[...] * growth_step(first, east, north, table_ref)
            loc_ref[at, :] = local
            locb_ref[at, :] = local.astype(BF16)

    get.wait()
    sent, copies = [0], []

    def store(first, values):
        for j in range(tiles):
            buf_ref[pl.ds(first * tiles + j, values.shape[0], stride=tiles), :] = values[
                :, j * LANES : (j + 1) * LANES
            ]
        upto = (first + values.shape[0]) // plan.depth
        for d in range(sent[0], upto):
            out_ref[d * block : d * block + data, :] = buf_ref[d * data : (d + 1) * data, :]
        at = slice(sent[0] * block // SUBS * SUBS, upto * block // SUBS * SUBS)
        copies.append(
            pltpu.make_async_copy(out_ref.at[at, :], out_hbm.at[at, :], out_sems.at[len(copies)])
        )
        copies[-1].start()
        sent[0] = upto

    coupled(plan, coup_ref, loc_ref, locb_ref, store)
    for copy in copies:
        copy.wait()


def last_kernel(
    plan,
    winds_ref, table_ref, came_hbm, coup_hbm, out_hbm,
    came_ref, coup_ref, loc_ref, locb_ref, unit_ref, sems, coup_sem, out_sems,
):
    tiles = plan.tiles
    copies = []
    arrive = fetch(came_hbm, came_ref, sems, plan.thirds)
    get = pltpu.make_async_copy(coup_hbm, coup_ref, coup_sem)
    get.start()

    def load(first, count):
        start = pl.multiple_of(first * tiles, SUBS)
        return jnp.concatenate(
            [came_ref[pl.ds(start + j, count, stride=tiles), :] for j in range(tiles)], axis=1
        )

    unit_loss(plan, load, arrive, table_ref, unit_ref)
    east, north = winds_ref[0:1, :], winds_ref[1:2, :]

    @pl.loop(0, plan.spec // PERIOD)
    def _(i):
        first = pl.multiple_of(i * PERIOD, PERIOD)
        at = pl.ds(first, PERIOD)
        local = load(first, PERIOD) * unit_ref[...] * growth_step(first, east, north, table_ref)
        loc_ref[at, :] = local
        locb_ref[at, :] = local.astype(BF16)

    def store(first, values):
        at = slice(first, first + values.shape[0])
        loc_ref[at, :] = values
        copies.append(
            pltpu.make_async_copy(loc_ref.at[at, :], out_hbm.at[at, :], out_sems.at[len(copies)])
        )
        copies[-1].start()

    get.wait()
    coupled(plan, coup_ref, loc_ref, locb_ref, store)
    for copy in copies:
        copy.wait()


def scatter(plan, place_ref, came_ref, grid_ref, cell_ref, arrived):
    depth, tiles, tall = plan.depth, plan.tiles, plan.tall
    sub = lax.broadcasted_iota(jnp.int32, (SUBS, LANES), 0)
    fill = [jnp.zeros((tall - depth, LANES), F32)] if tall > depth else []
    per = plan.shares // PARTS

    @pl.loop(0, plan.shares)
    def _(s):
        @pl.when(s % per == 0)
        def _():
            arrived(s // per)

        blocks = [
            came_ref[pl.ds(s * plan.block + j, depth, stride=tiles), :] for j in range(tiles)
        ]
        turned = [jnp.concatenate([block] + fill, axis=0).T for block in blocks]
        for j in range(tiles):
            cell_ref[j * LANES : (j + 1) * LANES, 0:tall] = turned[j]

        @pl.loop(0, tiles)
        def _(j):
            first = s * plan.rows + j * LANES
            for g in range(LANES // SUBS):
                at = pl.ds(pl.multiple_of(j * LANES + g * SUBS, SUBS), SUBS)
                values = cell_ref[at, :]
                for t in range(SUBS):
                    spot = place_ref[first + g * SUBS + t]
                    pltpu.store(grid_ref.at[pl.ds(spot, SUBS), :], values, mask=sub == t)


def gather(plan, place_ref, out_ref, grid_ref, cell_ref, finished):
    depth, tiles, tall = plan.depth, plan.tiles, plan.tall
    sub = lax.broadcasted_iota(jnp.int32, (SUBS, LANES), 0)
    per = plan.shares // PARTS

    @pl.loop(0, plan.shares)
    def _(s):
        @pl.loop(0, tiles)
        def _(j):
            first = s * plan.rows + j * LANES
            for g in range(LANES // SUBS):
                values = grid_ref[pl.ds(place_ref[first + g * SUBS], SUBS), :]
                for t in range(1, SUBS):
                    shifted = grid_ref[pl.ds(place_ref[first + g * SUBS + t], SUBS), :]
                    values = jnp.where(sub == t, shifted, values)
                cell_ref[pl.ds(pl.multiple_of(j * LANES + g * SUBS, SUBS), SUBS), :] = values

        turned = [cell_ref[j * LANES : (j + 1) * LANES, 0:tall].T for j in range(tiles)]
        for j in range(tiles):
            out_ref[pl.ds(s * plan.data + j, depth, stride=tiles), :] = turned[j][0:depth, :]

        @pl.when(s % per == per - 1)
        def _():
            finished(s // per)


def spread_drift(plan, came_ref, held, turned, drift_ref):
    held[...] = jnp.zeros((LANES, LANES), F32)
    for s in range(plan.shares):
        first = s * plan.block + plan.data + plan.tiles
        held[s * plan.force : (s + 1) * plan.force, :] = came_ref[first : first + plan.force, :]
    turned[...] = (courant_scale * held[...]).T
    groups = plan.vregs // COARSE
    ordered = jnp.concatenate(
        [
            turned[pl.ds(a * groups * SUBS + m, SUBS, stride=groups), :]
            for a in range(LANES // (groups * SUBS))
            for m in range(groups)
        ],
        axis=0,
    )
    for q in range(plan.shares * plan.force):
        drift_ref[q * LANES : (q + 1) * LANES, :] = jnp.broadcast_to(
            ordered[:, q : q + 1], (LANES, LANES)
        )


def sweep(plan, drift_ref, speed_ref, one_ref, two_ref):
    cols, last = plan.cols, plan.coarse_rows - 1
    groups = plan.vregs // COARSE
    sub = lax.broadcasted_iota(jnp.int32, (SUBS, LANES), 0)
    speeds = [jnp.broadcast_to(speed_ref[d : d + 1, :], (SUBS, LANES)) for d in range(2)]

    for m in range(groups):

        def courant(which, r4):
            at = pl.multiple_of(((which * plan.coarse_rows + r4) * groups + m) * SUBS, SUBS)
            value = speeds[which] + drift_ref[pl.ds(at, SUBS), :]
            return value > 0.0, jnp.abs(value)

        def at(row, q):
            return pl.ds(pl.multiple_of((row + 1) * cols + q * SUBS, SUBS), SUBS)

        def along(row, speed):
            ahead, size = speed
            base = pl.multiple_of((row + 1) * cols, SUBS)
            first, count = m * COARSE, COARSE
            line = [one_ref[at(row, q), :] for q in range(first, first + count)]
            if first:
                before = one_ref[at(row, first - 1), :]
            else:
                before = one_ref[pl.ds(base + cols - SUBS - 1, SUBS), :]
                before = jnp.where(sub == 0, DRY, before)
            if first + count < plan.vregs:
                after = one_ref[at(row, first + count), :]
            else:
                after = jnp.where(sub == SUBS - 1, DRY, one_ref[pl.ds(base + 1, SUBS), :])
            line = [before] + line + [after]
            swept = []
            for q in range(1, count + 1):
                pick = jnp.where(ahead, line[q - 1], line[q + 1])
                pick = jnp.where(pick < DRY, pick, 0.0)
                moved = line[q] + size * (pick - line[q])
                swept.append(jnp.where(line[q] < DRY, moved, 0.0))
            return swept

        def coarse(r4, held):
            above, here = held
            east = courant(0, r4)
            ahead, size = courant(1, r4)
            later = courant(0, jnp.minimum(r4 + 1, last))
            for dr in range(COARSE):
                row = r4 * COARSE + dr
                below = along(row + 1, east if dr < COARSE - 1 else later)
                for q in range(COARSE):
                    pick = jnp.where(ahead, above[q], below[q])
                    two_ref[at(row, m * COARSE + q), :] = here[q] + size * (pick - here[q])
                above, here = here, below
            return above, here

        zero = [jnp.zeros((SUBS, LANES), F32)] * COARSE
        lax.fori_loop(0, plan.coarse_rows, coarse, (zero, along(0, courant(0, 0))), unroll=2)


def middle_kernel(
    plan,
    place_ref, speed_ref, came_hbm, out_hbm,
    came_ref, out_ref, one_ref, two_ref, drift_ref, cell_ref, in_sems, out_sems,
):
    shares, block, data = plan.shares, plan.block, plan.data
    part_in, part_out = shares // PARTS * block, shares // PARTS * data

    def copy_in(part):
        at = pl.ds(pl.multiple_of(part * part_in, SUBS), part_in)
        return pltpu.make_async_copy(came_hbm.at[at, :], came_ref.at[at, :], in_sems.at[part])

    def copy_out(part):
        at = pl.ds(pl.multiple_of(part * part_out, SUBS), part_out)
        return pltpu.make_async_copy(out_ref.at[at, :], out_hbm.at[at, :], out_sems.at[part])

    for part in range(PARTS):
        copy_in(part).start()

    @pl.loop(0, plan.size // LANES)
    def _(i):
        at = pl.ds(pl.multiple_of(i * LANES, LANES), LANES)
        one_ref[at, :] = jnp.full((LANES, LANES), DRY, F32)

    scatter(plan, place_ref, came_ref, one_ref, cell_ref, lambda part: copy_in(part).wait())
    spread_drift(plan, came_ref, cell_ref.at[0:LANES], cell_ref.at[LANES : 2 * LANES], drift_ref)
    me = lax.axis_index("space")
    sweep(plan, drift_ref, speed_ref.at[me], one_ref, two_ref)
    gather(plan, place_ref, out_ref, two_ref, cell_ref, lambda part: copy_out(part).start())
    for part in range(PARTS):
        copy_out(part).wait()


VMEM = pl.BlockSpec(memory_space=pltpu.VMEM)
SMEM = pl.BlockSpec(memory_space=pltpu.SMEM)
ANY = pl.BlockSpec(memory_space=pl.ANY)


def on_spectrum(
    plan,
    spectra,
    wind_files,
    current_files,
    reader_turn,
    cell_point,
    coupling,
    send_list,
    send_count,
    recv_list,
):
    shares, rows, spec, points = plan.shares, plan.rows, plan.spec, plan.points
    tiles, depth, size, data_rows = plan.tiles, plan.depth, plan.size, plan.shares * plan.data
    source, east_speed, north_speed = wave_tables()
    table = jnp.asarray(source)
    speed = np.zeros((shares, SUBS, LANES), np.float32)
    speed[:, 0, :depth] = east_speed.reshape(shares, depth)
    speed[:, 1, :depth] = north_speed.reshape(shares, depth)

    def kernel(body, *, flops, traffic, vmem=WHOLE_VMEM, **options):
        return pl.pallas_call(
            body,
            compiler_params=pltpu.CompilerParams(vmem_limit_bytes=vmem),
            cost_estimate=pl.CostEstimate(flops=flops, bytes_accessed=traffic, transcendentals=0),
            **options,
        )

    width = points + max(LANES, plan.force * LANES)
    parcel = kernel(
        functools.partial(pack_kernel, plan),
        flops=0, traffic=4 * shares * 2 * width,
        out_shape=jax.ShapeDtypeStruct((shares, 2, width), F32),
        in_specs=[SMEM, VMEM, VMEM, VMEM],
        out_specs=VMEM,
        name="pack",
    )(reader_turn, wind_files, current_files, recv_list)
    parcel = lax.all_to_all(parcel, "space", 0, 0, tiled=True)

    cp = cell_point.reshape(1, rows)
    h_cost = dict(flops=2 * rows * spec * spec, traffic=12 * rows * spec)
    whole = pltpu.VMEM((spec, rows), F32)
    rounded = pltpu.VMEM((spec, rows), BF16)
    square = pltpu.VMEM((spec, spec), BF16)
    unit = pltpu.VMEM((PERIOD, rows), F32)
    dma = pltpu.SemaphoreType.DMA
    unit_loss_held, coup = kernel(
        functools.partial(ready_kernel, plan),
        flops=0, traffic=12 * rows * spec,
        out_shape=[
            jax.ShapeDtypeStruct((PERIOD, rows), F32), jax.ShapeDtypeStruct((spec, spec), BF16)
        ],
        in_specs=[VMEM, ANY, ANY],
        out_specs=[VMEM, ANY],
        scratch_shapes=[square, square, whole, dma((plan.thirds,)), dma, dma((8,))],
        name="ready",
    )(table, coupling, spectra.T)
    winds, sent = kernel(
        functools.partial(first_kernel, plan),
        **h_cost,
        out_shape=[
            jax.ShapeDtypeStruct((SUBS, rows), F32),
            jax.ShapeDtypeStruct((shares * plan.block, LANES), F32),
        ],
        in_specs=[SMEM] + [VMEM] * 5 + [ANY] * 2,
        out_specs=[VMEM, ANY],
        scratch_shapes=[
            pltpu.VMEM((shares * plan.block, LANES), F32),
            pltpu.VMEM((data_rows, LANES), F32),
            whole, square, rounded, dma((plan.thirds,)), dma, dma((plan.thirds,)),
        ],
        name="first_half",
    )(send_count, cp, parcel, send_list, table, unit_loss_held, spectra.T, coup)
    came = lax.all_to_all(
        sent.reshape(shares, plan.block, 1, LANES), "space", 0, 0, tiled=True
    )
    place = came[:, plan.data : plan.data + tiles].astype(jnp.int32).reshape(-1)
    swept = kernel(
        functools.partial(middle_kernel, plan),
        flops=24 * size * LANES, traffic=8 * rows * spec, vmem=32 * MIB,
        out_shape=jax.ShapeDtypeStruct((data_rows, LANES), F32),
        in_specs=[SMEM, VMEM, ANY],
        out_specs=ANY,
        scratch_shapes=[
            pltpu.VMEM((shares * plan.block, LANES), F32),
            pltpu.VMEM((data_rows, LANES), F32),
            pltpu.VMEM((size, LANES), F32),
            pltpu.VMEM((size, LANES), F32),
            pltpu.VMEM((2 * points, LANES), F32),
            pltpu.VMEM((rows, LANES), F32),
            pltpu.SemaphoreType.DMA((PARTS,)),
            pltpu.SemaphoreType.DMA((PARTS,)),
        ],
        name="sweeps",
    )(place, jnp.asarray(speed), came.reshape(-1, LANES))
    back = lax.all_to_all(
        swept.reshape(shares, depth, tiles, LANES), "space", 0, 0, tiled=True
    )
    result = kernel(
        functools.partial(last_kernel, plan),
        vmem=24 * MIB, **h_cost,
        out_shape=jax.ShapeDtypeStruct((spec, rows), F32),
        in_specs=[VMEM] * 2 + [ANY] * 2,
        out_specs=ANY,
        scratch_shapes=[
            pltpu.VMEM((data_rows, LANES), F32),
            square, whole, rounded, unit, dma((plan.thirds,)), dma, dma((plan.thirds,)),
        ],
        name="last_half",
    )(winds, table, back.reshape(data_rows, LANES), coup)
    return result.T


def on_device(*args):
    spectra, wind_files, send_list, wet_mask = args[0], args[1], args[6], args[9]
    plan = Plan(
        lax.axis_size("space"), *spectra.shape, send_list.shape[2], *wet_mask.shape, wind_files.shape[2]
    )
    if plan.fits():
        return on_spectrum(plan, *args[:9])
    return on_strips(*args)


def solution(mesh):
    placed = (
        P(("members", "space"), None),
        P(("members", "space"), None, None),
        P(("members", "space"), None, None),
        P(),
        P("space"),
        P(),
        P("space", None, None),
        P("space", None),
        P("space", None, None),
        P("space", None),
    )
    return jax.shard_map(
        on_device,
        mesh=mesh,
        in_specs=placed,
        out_specs=P(("members", "space"), None),
        check_vma=False,
    )
```

```python
import functools
import math

import jax
import jax.numpy as jnp
import numpy as np
from jax import lax
from jax.experimental import pallas as pl
from jax.experimental.pallas import tpu as pltpu
from jax.sharding import PartitionSpec as P

DIRS = 36
FREQS = 36
COARSE = 4


gravity = 9.81
base_freq = 0.0418
freq_ratio = 1.1
freq_span = 35.0
input_coef = 0.0001
wind_gain = 1.12
dissip_coef = 0.0005
half_length = 300.0
courant_scale = 0.05


def from_root(array, axis, root):
    mine = lax.axis_index(axis) == root
    return lax.psum(jnp.where(mine, array, jnp.zeros_like(array)), axis)


def extended(array, sides, width):
    for axis, dim in sides:
        size, length = (lax.axis_size(axis), array.shape[dim])
        up = [(i, (i + 1) % size) for i in range(size - 1)]
        down = [(j, i) for i, j in up]
        last = lax.slice_in_dim(array, length - width, length, axis=dim)
        first = lax.slice_in_dim(array, 0, width, axis=dim)
        before = lax.ppermute(last, axis, up)
        after = lax.ppermute(first, axis, down)
        array = jnp.concatenate([before, array, after], axis=dim)
    return array


def spectral_tables():
    direction = 2.0 * math.pi / DIRS * jnp.arange(DIRS, dtype=jnp.float32)
    exponent = jnp.arange(FREQS, dtype=jnp.float32) * (freq_span / (FREQS - 1))
    frequency = base_freq * freq_ratio**exponent
    angular = 2.0 * math.pi * frequency
    phase_speed = gravity / angular
    return (jnp.cos(direction), jnp.sin(direction), angular, phase_speed, 0.5 * phase_speed)


def source_half(energy, wind_east, wind_north, coupling):
    cos_dir, sine_dir, angular, phase_speed, group_speed = spectral_tables()
    along_wind = wind_east[:, None] * cos_dir[None, :] + wind_north[:, None] * sine_dir[None, :]
    growth = (
        input_coef
        * angular[None, None, :]
        * jnp.maximum(wind_gain * along_wind[:, :, None] / phase_speed[None, None, :] - 1.0, 0.0)
    )
    growth = growth.reshape(energy.shape[0], -1)
    mean_square = jnp.mean(energy * energy, axis=1, keepdims=True)
    decay_rate = dissip_coef * jnp.tile(angular, DIRS)[None, :] * mean_square
    local_part = energy * (1.0 + half_length * growth) / (1.0 + half_length * decay_rate)
    return local_part + jnp.dot(
        local_part.astype(jnp.bfloat16), coupling, preferred_element_type=jnp.float32
    )


def advect(center, upwind_lo, upwind_hi, courant):
    ahead_part = jnp.maximum(courant, 0.0)
    behind = jnp.minimum(courant, 0.0)
    return center - ahead_part * (center - upwind_lo) - behind * (upwind_hi - center)


def sweep_cols(energy_grid, drift_east, wet_field):
    cos_dir, sine_dir, angular, phase_speed, group_speed = spectral_tables()
    wave_speed = (cos_dir[:, None] * group_speed[None, :]).reshape(-1)
    courant = (wave_speed[None, None, :] + drift_east[:, :, None]) * courant_scale
    zero_edge = jnp.zeros_like(energy_grid[:, :1])
    upwind_lo = jnp.concatenate([zero_edge, energy_grid[:, :-1]], axis=1)
    upwind_hi = jnp.concatenate([energy_grid[:, 1:], zero_edge], axis=1)
    return advect(energy_grid, upwind_lo, upwind_hi, courant) * wet_field[:, :, None]


def sweep_rows(energy_grid, row_above, row_below, drift_north, wet_field):
    cos_dir, sine_dir, angular, phase_speed, group_speed = spectral_tables()
    wave_speed = (sine_dir[:, None] * group_speed[None, :]).reshape(-1)
    courant = (wave_speed[None, None, :] + drift_north[:, :, None]) * courant_scale
    return advect(energy_grid, row_above, row_below, courant) * wet_field[:, :, None]


def forcing_points(row_start, row_count, col_count):
    rows_idx = row_start + jnp.arange(row_count, dtype=jnp.int32)
    cols_idx = jnp.arange(col_count, dtype=jnp.int32)
    return rows_idx[:, None] // COARSE * (col_count // COARSE) + cols_idx[None, :] // COARSE


def on_strips(
    spectra,
    wind_files,
    current_files,
    reader_turn,
    cell_point,
    coupling,
    send_list,
    send_count,
    recv_list,
    wet_mask,
):
    levels = []
    for time_level in range(2):
        levels.append(
            (
                from_root(wind_files[0], "space", reader_turn[time_level]),
                from_root(current_files[0], "space", reader_turn[time_level]),
            )
        )
    wind_mean = 0.5 * (levels[0][0] + levels[1][0])
    current_mean = 0.5 * (levels[0][1] + levels[1][1])
    cell_wind = jnp.take(wind_mean, cell_point, axis=1)
    first_half = source_half(spectra, cell_wind[0], cell_wind[1], coupling)
    send_rows = send_list[0]
    counts = send_count[0]
    places = recv_list[0]
    slot_count = send_rows.shape[1]
    spec_width = spectra.shape[1]
    live_slots = (jnp.arange(slot_count, dtype=jnp.int32)[None, :] < counts[:, None]).astype(
        jnp.float32
    )
    packed = first_half[send_rows] * live_slots[:, :, None]
    arrived = lax.all_to_all(packed, "space", split_axis=0, concat_axis=0, tiled=True)
    row_count = wet_mask.shape[0]
    col_count = wet_mask.shape[1]
    energy_grid = (
        jnp.zeros((row_count * col_count, spec_width), jnp.float32)
        .at[places.reshape(-1)]
        .add(arrived.reshape(-1, spec_width))
    )
    energy_grid = energy_grid.reshape(row_count, col_count, spec_width)
    points = forcing_points(lax.axis_index("space") * row_count, row_count, col_count)
    drift = jnp.take(current_mean, points, axis=1)
    wet_field = wet_mask.astype(jnp.float32)
    swept_cols = sweep_cols(energy_grid, drift[0], wet_field)
    padded = extended(swept_cols, (("space", 0),), 1)
    swept = sweep_rows(swept_cols, padded[:-2], padded[2:], drift[1], wet_field).reshape(
        -1, spec_width
    )
    outgoing = swept[places]
    flat_rows = send_rows.reshape(-1)
    empty_rows = jnp.zeros((spectra.shape[0], spec_width), jnp.float32)
    returned = lax.all_to_all(outgoing, "space", split_axis=0, concat_axis=0, tiled=True)
    back_rows = empty_rows.at[flat_rows].add(
        (returned * live_slots[:, :, None]).reshape(-1, spec_width)
    )
    result = source_half(back_rows, cell_wind[0], cell_wind[1], coupling)
    return result


LANES = 128
SUBS = 8
F32 = jnp.float32
BF16 = jnp.bfloat16
MIB = 1024 * 1024
WHOLE_VMEM = 60 * MIB
DRY = 1e30
PERIOD = 4 * FREQS


def wave_tables():
    direction = 2.0 * np.pi / DIRS * np.arange(DIRS)
    frequency = base_freq * freq_ratio ** (np.arange(FREQS) * (freq_span / (FREQS - 1)))
    angular = 2.0 * np.pi * frequency
    phase = gravity / angular
    group = 0.5 * phase
    cos_dir, sin_dir = np.cos(direction)[:, None], np.sin(direction)[:, None]
    flat = lambda t: np.broadcast_to(t, (DIRS, FREQS)).reshape(-1)
    growth = half_length * input_coef * angular
    source = np.zeros((DIRS * FREQS, 8), np.float32)
    source[:, 0] = flat(growth * wind_gain * cos_dir / phase)
    source[:, 1] = flat(growth * wind_gain * sin_dir / phase)
    source[:, 2] = flat(1.0 - growth)
    source[:, 3] = flat(half_length * dissip_coef * angular)
    east = flat(courant_scale * cos_dir * group).astype(np.float32)
    north = flat(courant_scale * sin_dir * group).astype(np.float32)
    return source, east, north


def ceil_to(value, step):
    return -(-value // step) * step


def largest_step(size, step, most):
    return max(s for s in range(step, most + 1, step) if size % s == 0)


class Plan:
    def __init__(self, shares, rows, spec, cap, strip_rows, cols, points):
        self.shares, self.rows, self.spec, self.cap = shares, rows, spec, cap
        self.cols, self.points = cols, points
        self.depth = spec // shares
        self.tiles = rows // LANES
        self.data = self.depth * self.tiles
        self.force = 2 * points // (LANES * shares)
        self.block = self.data + self.tiles + self.force
        self.tall = ceil_to(self.depth, SUBS)
        self.strip = strip_rows * cols
        self.grid_rows = strip_rows * shares
        self.coarse_rows = self.grid_rows // COARSE
        self.vregs = cols // SUBS
        self.size = (self.grid_rows + 2) * cols
        self.tall_step = largest_step(spec, PERIOD, 512)
        self.thirds = spec // self.tall_step

    def fits(self):
        if self.spec % self.shares or self.depth > LANES or self.rows % (2 * LANES):
            return False
        if 2 * self.points % (LANES * self.shares) or self.points % LANES or self.cap > LANES:
            return False
        if self.shares * self.block % SUBS or self.shares * self.data % SUBS:
            return False
        if 2 * self.points // LANES > LANES or self.cols != LANES:
            return False
        held = 2 * self.size + 2 * self.points + self.shares * (self.block + self.data)
        return 4 * LANES * held + 4 * MIB < 32 * MIB


def pack_kernel(plan, turn_ref, wind_ref, current_ref, recv_ref, out_ref):
    me = lax.axis_index("space")
    half = lambda at: jnp.where(turn_ref[at] == me, 0.5, 0.0)
    mine = half(0) + half(1)
    wind = mine * wind_ref[0]
    points, width, cap = plan.points, plan.force * LANES, plan.cap
    for s in range(plan.shares):
        out_ref[s, :, 0:points] = wind
        out_ref[s, :, points:] = jnp.zeros((2, out_ref.shape[2] - points), F32)
        out_ref[s, 0:1, points : points + cap] = recv_ref[0, s : s + 1, :].astype(F32)
        which, first = divmod(s * width, points)
        out_ref[s, 1:2, points : points + width] = (
            mine * current_ref[0, which : which + 1, first : first + width]
        )


def cell_winds(wind, cp):
    points, rows = wind.shape[1], cp.shape[1]
    high = wind.astype(BF16).astype(F32)
    middle = (wind - high).astype(BF16).astype(F32)
    low = wind - high - middle
    parts = jnp.concatenate([high, middle, low, jnp.zeros((10, points), F32)], axis=0)
    point = lax.broadcasted_iota(jnp.int32, (points, rows), 0)
    hit = jnp.where(point == cp, 1.0, 0.0).astype(BF16)
    picked = jnp.dot(parts.astype(BF16), hit, preferred_element_type=F32)
    both = picked[0:2] + picked[2:4] + picked[4:6]
    return both[0:1], both[1:2]


def fetch(source, target, sems, parts):
    size = target.shape[0] // parts
    copies = [
        pltpu.make_async_copy(
            source.at[pl.ds(q * size, size), :], target.at[pl.ds(q * size, size), :], sems.at[q]
        )
        for q in range(parts)
    ]
    for copy in copies:
        copy.start()
    return copies


def unit_loss(plan, load, arrive, table_ref, unit_ref):
    tall = plan.spec // len(arrive)

    def squares(i, total):
        piece = load(pl.multiple_of(i * 48, 48), 48)
        return total + jnp.sum((piece * piece).reshape(48 // SUBS, SUBS, plan.rows), axis=0)

    total = jnp.zeros((SUBS, plan.rows), F32)
    for q, copy in enumerate(arrive):
        copy.wait()
        total = lax.fori_loop(q * tall // 48, (q + 1) * tall // 48, squares, total)
    mean_square = jnp.sum(total, axis=0, keepdims=True) * (1.0 / plan.spec)
    unit_ref[...] = 1.0 / (1.0 + table_ref[0:PERIOD, 3:4] * mean_square)


def growth_step(first, east, north, table_ref):
    table = table_ref[pl.ds(first, PERIOD), :]
    return jnp.maximum(east * table[:, 0:1] + north * table[:, 1:2] + table[:, 2:3], 1.0)


def coupled(plan, coup_ref, loc_ref, locb_ref, store):
    for q in range(plan.thirds):
        at = slice(q * plan.tall_step, (q + 1) * plan.tall_step)
        store(
            q * plan.tall_step,
            loc_ref[at, :]
            + jnp.dot(coup_ref[at, :], locb_ref[...], preferred_element_type=F32),
        )


def ready_kernel(
    plan, table_ref, coup_hbm, energy_hbm, unit_ref, turned_hbm,
    coup_ref, turned_ref, energy_ref, sems, coup_sem, out_sems,
):
    spec = plan.spec
    arrive = fetch(energy_hbm, energy_ref, sems, plan.thirds)
    get = pltpu.make_async_copy(coup_hbm, coup_ref, coup_sem)
    get.start()
    unit_loss(plan, lambda first, count: energy_ref[pl.ds(first, count), :], arrive, table_ref, unit_ref)
    get.wait()
    copies, wide = [], 3 * LANES
    for first in range(0, spec, LANES):
        at = slice(first, min(first + LANES, spec))
        turned_ref[at, :] = coup_ref[:, at].T
        if at.stop % wide == 0 or at.stop == spec:
            done = slice((at.stop - 1) // wide * wide, at.stop)
            copies.append(
                pltpu.make_async_copy(
                    turned_ref.at[done, :], turned_hbm.at[done, :], out_sems.at[len(copies)]
                )
            )
            copies[-1].start()
    for copy in copies:
        copy.wait()


def own_places(plan, parcel_ref, send_ref, count_ref):
    points, cols, vregs, cap = plan.points, plan.cols, plan.vregs, plan.cap
    landing = jnp.concatenate(
        [parcel_ref[b, 0:1, points : points + cap] for b in range(plan.shares)], axis=0
    ).astype(jnp.int32)
    cell = landing + plan.strip * lax.broadcasted_iota(jnp.int32, (plan.shares, cap), 0)
    column = lax.rem(cell, cols)
    place = cell - column + cols + lax.rem(column, vregs) * SUBS + lax.div(column, vregs)
    place = place.astype(F32)
    slot = lax.broadcasted_iota(jnp.int32, (1, cap), 1)
    names = [
        jnp.where(slot < count_ref[0, b], send_ref[0, b : b + 1, :], -1) for b in range(plan.shares)
    ]
    rows = []
    for j in range(plan.tiles):
        own = lax.broadcasted_iota(jnp.int32, (LANES, cap), 0) + j * LANES
        found = jnp.zeros((LANES, cap), F32)
        for b in range(plan.shares):
            found += jnp.where(names[b] == own, place[b : b + 1, :], 0.0)
        found = jnp.broadcast_to(jnp.sum(found, axis=1, keepdims=True), (LANES, LANES)).T
        shift = lax.rem(lax.broadcasted_iota(jnp.int32, (1, LANES), 1), SUBS).astype(F32)
        rows.append(found[0:1, :] - shift)
    return rows


def first_kernel(
    plan,
    count_ref, cp_ref, parcel_ref, send_ref, table_ref, unit_ref, energy_hbm, coup_hbm, winds_ref, out_hbm,
    out_ref, buf_ref, loc_ref, coup_ref, locb_ref, sems, coup_sem, out_sems,
):
    tiles, shares, points, block, data = plan.tiles, plan.shares, plan.points, plan.block, plan.data
    arrive = fetch(energy_hbm, loc_ref, sems, plan.thirds)
    get = pltpu.make_async_copy(coup_hbm, coup_ref, coup_sem)
    get.start()
    width = plan.force * LANES
    current = jnp.sum(parcel_ref[:, :, points : points + width], axis=0)
    spare = own_places(plan, parcel_ref, send_ref, count_ref)
    spare += [current[1:2, f * LANES : (f + 1) * LANES] for f in range(plan.force)]
    for d in range(shares):
        out_ref[d * block + data : (d + 1) * block, :] = jnp.concatenate(spare, axis=0)
    east, north = cell_winds(jnp.sum(parcel_ref[:, :, 0:points], axis=0), cp_ref[...])
    winds_ref[0:1, :] = east
    winds_ref[1:2, :] = north
    per = plan.tall_step // PERIOD
    for q in range(plan.thirds):
        arrive[q].wait()

        @pl.loop(q * per, (q + 1) * per)
        def _(i):
            first = pl.multiple_of(i * PERIOD, PERIOD)
            at = pl.ds(first, PERIOD)
            local = loc_ref[at, :] * unit_ref[...] * growth_step(first, east, north, table_ref)
            loc_ref[at, :] = local
            locb_ref[at, :] = local.astype(BF16)

    get.wait()
    sent, copies = [0], []

    def store(first, values):
        for j in range(tiles):
            buf_ref[pl.ds(first * tiles + j, values.shape[0], stride=tiles), :] = values[
                :, j * LANES : (j + 1) * LANES
            ]
        upto = (first + values.shape[0]) // plan.depth
        for d in range(sent[0], upto):
            out_ref[d * block : d * block + data, :] = buf_ref[d * data : (d + 1) * data, :]
        at = slice(sent[0] * block // SUBS * SUBS, upto * block // SUBS * SUBS)
        copies.append(
            pltpu.make_async_copy(out_ref.at[at, :], out_hbm.at[at, :], out_sems.at[len(copies)])
        )
        copies[-1].start()
        sent[0] = upto

    coupled(plan, coup_ref, loc_ref, locb_ref, store)
    for copy in copies:
        copy.wait()


def last_kernel(
    plan,
    winds_ref, table_ref, came_hbm, coup_hbm, out_hbm,
    came_ref, coup_ref, loc_ref, locb_ref, unit_ref, sems, coup_sem, out_sems,
):
    tiles = plan.tiles
    copies = []
    arrive = fetch(came_hbm, came_ref, sems, plan.thirds)
    get = pltpu.make_async_copy(coup_hbm, coup_ref, coup_sem)
    get.start()

    def load(first, count):
        start = pl.multiple_of(first * tiles, SUBS)
        return jnp.concatenate(
            [came_ref[pl.ds(start + j, count, stride=tiles), :] for j in range(tiles)], axis=1
        )

    unit_loss(plan, load, arrive, table_ref, unit_ref)
    east, north = winds_ref[0:1, :], winds_ref[1:2, :]

    @pl.loop(0, plan.spec // PERIOD)
    def _(i):
        first = pl.multiple_of(i * PERIOD, PERIOD)
        at = pl.ds(first, PERIOD)
        local = load(first, PERIOD) * unit_ref[...] * growth_step(first, east, north, table_ref)
        loc_ref[at, :] = local
        locb_ref[at, :] = local.astype(BF16)

    def store(first, values):
        at = slice(first, first + values.shape[0])
        loc_ref[at, :] = values
        copies.append(
            pltpu.make_async_copy(loc_ref.at[at, :], out_hbm.at[at, :], out_sems.at[len(copies)])
        )
        copies[-1].start()

    get.wait()
    coupled(plan, coup_ref, loc_ref, locb_ref, store)
    for copy in copies:
        copy.wait()


def scatter(plan, place_ref, came_ref, grid_ref, cell_ref):
    depth, tiles, tall = plan.depth, plan.tiles, plan.tall
    sub = lax.broadcasted_iota(jnp.int32, (SUBS, LANES), 0)
    fill = [jnp.zeros((tall - depth, LANES), F32)] if tall > depth else []

    @pl.loop(0, plan.shares)
    def _(s):
        blocks = [
            came_ref[pl.ds(s * plan.block + j, depth, stride=tiles), :] for j in range(tiles)
        ]
        turned = [jnp.concatenate([block] + fill, axis=0).T for block in blocks]
        for j in range(tiles):
            cell_ref[j * LANES : (j + 1) * LANES, 0:tall] = turned[j]

        @pl.loop(0, tiles)
        def _(j):
            first = s * plan.rows + j * LANES
            for g in range(LANES // SUBS):
                at = pl.ds(pl.multiple_of(j * LANES + g * SUBS, SUBS), SUBS)
                values = cell_ref[at, :]
                for t in range(SUBS):
                    spot = place_ref[first + g * SUBS + t]
                    pltpu.store(grid_ref.at[pl.ds(spot, SUBS), :], values, mask=sub == t)


def gather(plan, place_ref, out_ref, grid_ref, cell_ref):
    depth, tiles, tall = plan.depth, plan.tiles, plan.tall
    sub = lax.broadcasted_iota(jnp.int32, (SUBS, LANES), 0)

    @pl.loop(0, plan.shares)
    def _(s):
        @pl.loop(0, tiles)
        def _(j):
            first = s * plan.rows + j * LANES
            for g in range(LANES // SUBS):
                values = grid_ref[pl.ds(place_ref[first + g * SUBS], SUBS), :]
                for t in range(1, SUBS):
                    shifted = grid_ref[pl.ds(place_ref[first + g * SUBS + t], SUBS), :]
                    values = jnp.where(sub == t, shifted, values)
                cell_ref[pl.ds(pl.multiple_of(j * LANES + g * SUBS, SUBS), SUBS), :] = values

        turned = [cell_ref[j * LANES : (j + 1) * LANES, 0:tall].T for j in range(tiles)]
        for j in range(tiles):
            out_ref[pl.ds(s * plan.data + j, depth, stride=tiles), :] = turned[j][0:depth, :]


def spread_drift(plan, came_ref, held, turned, drift_ref):
    held[...] = jnp.zeros((LANES, LANES), F32)
    for s in range(plan.shares):
        first = s * plan.block + plan.data + plan.tiles
        held[s * plan.force : (s + 1) * plan.force, :] = came_ref[first : first + plan.force, :]
    turned[...] = (courant_scale * held[...]).T
    groups = plan.vregs // COARSE
    ordered = jnp.concatenate(
        [
            turned[pl.ds(a * groups * SUBS + m, SUBS, stride=groups), :]
            for a in range(LANES // (groups * SUBS))
            for m in range(groups)
        ],
        axis=0,
    )
    for q in range(plan.shares * plan.force):
        drift_ref[q * LANES : (q + 1) * LANES, :] = jnp.broadcast_to(
            ordered[:, q : q + 1], (LANES, LANES)
        )


def sweep(plan, drift_ref, speed_ref, one_ref, two_ref):
    cols, last = plan.cols, plan.coarse_rows - 1
    groups = plan.vregs // COARSE
    sub = lax.broadcasted_iota(jnp.int32, (SUBS, LANES), 0)
    speeds = [jnp.broadcast_to(speed_ref[d : d + 1, :], (SUBS, LANES)) for d in range(2)]

    for m in range(groups):

        def courant(which, r4):
            at = pl.multiple_of(((which * plan.coarse_rows + r4) * groups + m) * SUBS, SUBS)
            value = speeds[which] + drift_ref[pl.ds(at, SUBS), :]
            return value > 0.0, jnp.abs(value)

        def at(row, q):
            return pl.ds(pl.multiple_of((row + 1) * cols + q * SUBS, SUBS), SUBS)

        def along(row, speed):
            ahead, size = speed
            base = pl.multiple_of((row + 1) * cols, SUBS)
            first, count = m * COARSE, COARSE
            line = [one_ref[at(row, q), :] for q in range(first, first + count)]
            if first:
                before = one_ref[at(row, first - 1), :]
            else:
                before = one_ref[pl.ds(base + cols - SUBS - 1, SUBS), :]
                before = jnp.where(sub == 0, DRY, before)
            if first + count < plan.vregs:
                after = one_ref[at(row, first + count), :]
            else:
                after = jnp.where(sub == SUBS - 1, DRY, one_ref[pl.ds(base + 1, SUBS), :])
            line = [before] + line + [after]
            swept = []
            for q in range(1, count + 1):
                pick = jnp.where(ahead, line[q - 1], line[q + 1])
                pick = jnp.where(pick < DRY, pick, 0.0)
                moved = line[q] + size * (pick - line[q])
                swept.append(jnp.where(line[q] < DRY, moved, 0.0))
            return swept

        def coarse(r4, held):
            above, here = held
            east = courant(0, r4)
            ahead, size = courant(1, r4)
            later = courant(0, jnp.minimum(r4 + 1, last))
            for dr in range(COARSE):
                row = r4 * COARSE + dr
                below = along(row + 1, east if dr < COARSE - 1 else later)
                for q in range(COARSE):
                    pick = jnp.where(ahead, above[q], below[q])
                    two_ref[at(row, m * COARSE + q), :] = here[q] + size * (pick - here[q])
                above, here = here, below
            return above, here

        zero = [jnp.zeros((SUBS, LANES), F32)] * COARSE
        lax.fori_loop(0, plan.coarse_rows, coarse, (zero, along(0, courant(0, 0))), unroll=2)


def middle_kernel(
    plan,
    place_ref, speed_ref, came_ref, out_ref, one_ref, two_ref, drift_ref, cell_ref,
):
    @pl.loop(0, plan.size // LANES)
    def _(i):
        at = pl.ds(pl.multiple_of(i * LANES, LANES), LANES)
        one_ref[at, :] = jnp.full((LANES, LANES), DRY, F32)

    scatter(plan, place_ref, came_ref, one_ref, cell_ref)
    spread_drift(plan, came_ref, cell_ref.at[0:LANES], cell_ref.at[LANES : 2 * LANES], drift_ref)
    me = lax.axis_index("space")
    sweep(plan, drift_ref, speed_ref.at[me], one_ref, two_ref)
    gather(plan, place_ref, out_ref, two_ref, cell_ref)


VMEM = pl.BlockSpec(memory_space=pltpu.VMEM)
SMEM = pl.BlockSpec(memory_space=pltpu.SMEM)
ANY = pl.BlockSpec(memory_space=pl.ANY)


def on_spectrum(
    plan,
    spectra,
    wind_files,
    current_files,
    reader_turn,
    cell_point,
    coupling,
    send_list,
    send_count,
    recv_list,
):
    shares, rows, spec, points = plan.shares, plan.rows, plan.spec, plan.points
    tiles, depth, size, data_rows = plan.tiles, plan.depth, plan.size, plan.shares * plan.data
    source, east_speed, north_speed = wave_tables()
    table = jnp.asarray(source)
    speed = np.zeros((shares, SUBS, LANES), np.float32)
    speed[:, 0, :depth] = east_speed.reshape(shares, depth)
    speed[:, 1, :depth] = north_speed.reshape(shares, depth)

    def kernel(body, *, flops, traffic, vmem=WHOLE_VMEM, **options):
        return pl.pallas_call(
            body,
            compiler_params=pltpu.CompilerParams(vmem_limit_bytes=vmem),
            cost_estimate=pl.CostEstimate(flops=flops, bytes_accessed=traffic, transcendentals=0),
            **options,
        )

    width = points + max(LANES, plan.force * LANES)
    parcel = kernel(
        functools.partial(pack_kernel, plan),
        flops=0, traffic=4 * shares * 2 * width,
        out_shape=jax.ShapeDtypeStruct((shares, 2, width), F32),
        in_specs=[SMEM, VMEM, VMEM, VMEM],
        out_specs=VMEM,
        name="pack",
    )(reader_turn, wind_files, current_files, recv_list)
    parcel = lax.all_to_all(parcel, "space", 0, 0, tiled=True)

    cp = cell_point.reshape(1, rows)
    h_cost = dict(flops=2 * rows * spec * spec, traffic=12 * rows * spec)
    whole = pltpu.VMEM((spec, rows), F32)
    rounded = pltpu.VMEM((spec, rows), BF16)
    square = pltpu.VMEM((spec, spec), BF16)
    unit = pltpu.VMEM((PERIOD, rows), F32)
    dma = pltpu.SemaphoreType.DMA
    unit_loss_held, coup = kernel(
        functools.partial(ready_kernel, plan),
        flops=0, traffic=12 * rows * spec,
        out_shape=[
            jax.ShapeDtypeStruct((PERIOD, rows), F32), jax.ShapeDtypeStruct((spec, spec), BF16)
        ],
        in_specs=[VMEM, ANY, ANY],
        out_specs=[VMEM, ANY],
        scratch_shapes=[square, square, whole, dma((plan.thirds,)), dma, dma((8,))],
        name="ready",
    )(table, coupling, spectra.T)
    winds, sent = kernel(
        functools.partial(first_kernel, plan),
        **h_cost,
        out_shape=[
            jax.ShapeDtypeStruct((SUBS, rows), F32),
            jax.ShapeDtypeStruct((shares * plan.block, LANES), F32),
        ],
        in_specs=[SMEM] + [VMEM] * 5 + [ANY] * 2,
        out_specs=[VMEM, ANY],
        scratch_shapes=[
            pltpu.VMEM((shares * plan.block, LANES), F32),
            pltpu.VMEM((data_rows, LANES), F32),
            whole, square, rounded, dma((plan.thirds,)), dma, dma((plan.thirds,)),
        ],
        name="first_half",
    )(send_count, cp, parcel, send_list, table, unit_loss_held, spectra.T, coup)
    came = lax.all_to_all(
        sent.reshape(shares, plan.block, 1, LANES), "space", 0, 0, tiled=True
    )
    place = came[:, plan.data : plan.data + tiles].astype(jnp.int32).reshape(-1)
    swept = kernel(
        functools.partial(middle_kernel, plan),
        flops=24 * size * LANES, traffic=8 * rows * spec, vmem=32 * MIB,
        out_shape=jax.ShapeDtypeStruct((data_rows, LANES), F32),
        in_specs=[SMEM, VMEM, VMEM],
        out_specs=VMEM,
        scratch_shapes=[
            pltpu.VMEM((size, LANES), F32),
            pltpu.VMEM((size, LANES), F32),
            pltpu.VMEM((2 * points, LANES), F32),
            pltpu.VMEM((rows, LANES), F32),
        ],
        name="sweeps",
    )(place, jnp.asarray(speed), came.reshape(-1, LANES))
    back = lax.all_to_all(
        swept.reshape(shares, depth, tiles, LANES), "space", 0, 0, tiled=True
    )
    result = kernel(
        functools.partial(last_kernel, plan),
        vmem=24 * MIB, **h_cost,
        out_shape=jax.ShapeDtypeStruct((spec, rows), F32),
        in_specs=[VMEM] * 2 + [ANY] * 2,
        out_specs=ANY,
        scratch_shapes=[
            pltpu.VMEM((data_rows, LANES), F32),
            square, whole, rounded, unit, dma((plan.thirds,)), dma, dma((plan.thirds,)),
        ],
        name="last_half",
    )(winds, table, back.reshape(data_rows, LANES), coup)
    return result.T


def on_device(*args):
    spectra, wind_files, send_list, wet_mask = args[0], args[1], args[6], args[9]
    plan = Plan(
        lax.axis_size("space"), *spectra.shape, send_list.shape[2], *wet_mask.shape, wind_files.shape[2]
    )
    if plan.fits():
        return on_spectrum(plan, *args[:9])
    return on_strips(*args)


def solution(mesh):
    placed = (
        P(("members", "space"), None),
        P(("members", "space"), None, None),
        P(("members", "space"), None, None),
        P(),
        P("space"),
        P(),
        P("space", None, None),
        P("space", None),
        P("space", None, None),
        P("space", None),
    )
    return jax.shard_map(
        on_device,
        mesh=mesh,
        in_specs=placed,
        out_specs=P(("members", "space"), None),
        check_vma=False,
    )
```

```python
import functools
import math

import jax
import jax.numpy as jnp
import numpy as np
from jax import lax
from jax.experimental import pallas as pl
from jax.experimental.pallas import tpu as pltpu
from jax.sharding import PartitionSpec as P

DIRS = 36
FREQS = 36
COARSE = 4


gravity = 9.81
base_freq = 0.0418
freq_ratio = 1.1
freq_span = 35.0
input_coef = 0.0001
wind_gain = 1.12
dissip_coef = 0.0005
half_length = 300.0
courant_scale = 0.05


def from_root(array, axis, root):
    mine = lax.axis_index(axis) == root
    return lax.psum(jnp.where(mine, array, jnp.zeros_like(array)), axis)


def extended(array, sides, width):
    for axis, dim in sides:
        size, length = (lax.axis_size(axis), array.shape[dim])
        up = [(i, (i + 1) % size) for i in range(size - 1)]
        down = [(j, i) for i, j in up]
        last = lax.slice_in_dim(array, length - width, length, axis=dim)
        first = lax.slice_in_dim(array, 0, width, axis=dim)
        before = lax.ppermute(last, axis, up)
        after = lax.ppermute(first, axis, down)
        array = jnp.concatenate([before, array, after], axis=dim)
    return array


def spectral_tables():
    direction = 2.0 * math.pi / DIRS * jnp.arange(DIRS, dtype=jnp.float32)
    exponent = jnp.arange(FREQS, dtype=jnp.float32) * (freq_span / (FREQS - 1))
    frequency = base_freq * freq_ratio**exponent
    angular = 2.0 * math.pi * frequency
    phase_speed = gravity / angular
    return (jnp.cos(direction), jnp.sin(direction), angular, phase_speed, 0.5 * phase_speed)


def source_half(energy, wind_east, wind_north, coupling):
    cos_dir, sine_dir, angular, phase_speed, group_speed = spectral_tables()
    along_wind = wind_east[:, None] * cos_dir[None, :] + wind_north[:, None] * sine_dir[None, :]
    growth = (
        input_coef
        * angular[None, None, :]
        * jnp.maximum(wind_gain * along_wind[:, :, None] / phase_speed[None, None, :] - 1.0, 0.0)
    )
    growth = growth.reshape(energy.shape[0], -1)
    mean_square = jnp.mean(energy * energy, axis=1, keepdims=True)
    decay_rate = dissip_coef * jnp.tile(angular, DIRS)[None, :] * mean_square
    local_part = energy * (1.0 + half_length * growth) / (1.0 + half_length * decay_rate)
    return local_part + jnp.dot(
        local_part.astype(jnp.bfloat16), coupling, preferred_element_type=jnp.float32
    )


def advect(center, upwind_lo, upwind_hi, courant):
    ahead_part = jnp.maximum(courant, 0.0)
    behind = jnp.minimum(courant, 0.0)
    return center - ahead_part * (center - upwind_lo) - behind * (upwind_hi - center)


def sweep_cols(energy_grid, drift_east, wet_field):
    cos_dir, sine_dir, angular, phase_speed, group_speed = spectral_tables()
    wave_speed = (cos_dir[:, None] * group_speed[None, :]).reshape(-1)
    courant = (wave_speed[None, None, :] + drift_east[:, :, None]) * courant_scale
    zero_edge = jnp.zeros_like(energy_grid[:, :1])
    upwind_lo = jnp.concatenate([zero_edge, energy_grid[:, :-1]], axis=1)
    upwind_hi = jnp.concatenate([energy_grid[:, 1:], zero_edge], axis=1)
    return advect(energy_grid, upwind_lo, upwind_hi, courant) * wet_field[:, :, None]


def sweep_rows(energy_grid, row_above, row_below, drift_north, wet_field):
    cos_dir, sine_dir, angular, phase_speed, group_speed = spectral_tables()
    wave_speed = (sine_dir[:, None] * group_speed[None, :]).reshape(-1)
    courant = (wave_speed[None, None, :] + drift_north[:, :, None]) * courant_scale
    return advect(energy_grid, row_above, row_below, courant) * wet_field[:, :, None]


def forcing_points(row_start, row_count, col_count):
    rows_idx = row_start + jnp.arange(row_count, dtype=jnp.int32)
    cols_idx = jnp.arange(col_count, dtype=jnp.int32)
    return rows_idx[:, None] // COARSE * (col_count // COARSE) + cols_idx[None, :] // COARSE


def on_strips(
    spectra,
    wind_files,
    current_files,
    reader_turn,
    cell_point,
    coupling,
    send_list,
    send_count,
    recv_list,
    wet_mask,
):
    levels = []
    for time_level in range(2):
        levels.append(
            (
                from_root(wind_files[0], "space", reader_turn[time_level]),
                from_root(current_files[0], "space", reader_turn[time_level]),
            )
        )
    wind_mean = 0.5 * (levels[0][0] + levels[1][0])
    current_mean = 0.5 * (levels[0][1] + levels[1][1])
    cell_wind = jnp.take(wind_mean, cell_point, axis=1)
    first_half = source_half(spectra, cell_wind[0], cell_wind[1], coupling)
    send_rows = send_list[0]
    counts = send_count[0]
    places = recv_list[0]
    slot_count = send_rows.shape[1]
    spec_width = spectra.shape[1]
    live_slots = (jnp.arange(slot_count, dtype=jnp.int32)[None, :] < counts[:, None]).astype(
        jnp.float32
    )
    packed = first_half[send_rows] * live_slots[:, :, None]
    arrived = lax.all_to_all(packed, "space", split_axis=0, concat_axis=0, tiled=True)
    row_count = wet_mask.shape[0]
    col_count = wet_mask.shape[1]
    energy_grid = (
        jnp.zeros((row_count * col_count, spec_width), jnp.float32)
        .at[places.reshape(-1)]
        .add(arrived.reshape(-1, spec_width))
    )
    energy_grid = energy_grid.reshape(row_count, col_count, spec_width)
    points = forcing_points(lax.axis_index("space") * row_count, row_count, col_count)
    drift = jnp.take(current_mean, points, axis=1)
    wet_field = wet_mask.astype(jnp.float32)
    swept_cols = sweep_cols(energy_grid, drift[0], wet_field)
    padded = extended(swept_cols, (("space", 0),), 1)
    swept = sweep_rows(swept_cols, padded[:-2], padded[2:], drift[1], wet_field).reshape(
        -1, spec_width
    )
    outgoing = swept[places]
    flat_rows = send_rows.reshape(-1)
    empty_rows = jnp.zeros((spectra.shape[0], spec_width), jnp.float32)
    returned = lax.all_to_all(outgoing, "space", split_axis=0, concat_axis=0, tiled=True)
    back_rows = empty_rows.at[flat_rows].add(
        (returned * live_slots[:, :, None]).reshape(-1, spec_width)
    )
    result = source_half(back_rows, cell_wind[0], cell_wind[1], coupling)
    return result


LANES = 128
SUBS = 8
F32 = jnp.float32
BF16 = jnp.bfloat16
MIB = 1024 * 1024
WHOLE_VMEM = 60 * MIB
DRY = 1e30
PERIOD = 4 * FREQS


def wave_tables():
    direction = 2.0 * np.pi / DIRS * np.arange(DIRS)
    frequency = base_freq * freq_ratio ** (np.arange(FREQS) * (freq_span / (FREQS - 1)))
    angular = 2.0 * np.pi * frequency
    phase = gravity / angular
    group = 0.5 * phase
    cos_dir, sin_dir = np.cos(direction)[:, None], np.sin(direction)[:, None]
    flat = lambda t: np.broadcast_to(t, (DIRS, FREQS)).reshape(-1)
    growth = half_length * input_coef * angular
    source = np.zeros((DIRS * FREQS, 8), np.float32)
    source[:, 0] = flat(growth * wind_gain * cos_dir / phase)
    source[:, 1] = flat(growth * wind_gain * sin_dir / phase)
    source[:, 2] = flat(1.0 - growth)
    source[:, 3] = flat(half_length * dissip_coef * angular)
    east = flat(courant_scale * cos_dir * group).astype(np.float32)
    north = flat(courant_scale * sin_dir * group).astype(np.float32)
    return source, east, north


def ceil_to(value, step):
    return -(-value // step) * step


def largest_step(size, step, most):
    return max(s for s in range(step, most + 1, step) if size % s == 0)


class Plan:
    def __init__(self, shares, rows, spec, cap, strip_rows, cols, points):
        self.shares, self.rows, self.spec, self.cap = shares, rows, spec, cap
        self.cols, self.points = cols, points
        self.depth = spec // shares
        self.tiles = rows // LANES
        self.data = self.depth * self.tiles
        self.force = 2 * points // (LANES * shares)
        self.block = self.data + self.tiles + self.force
        self.tall = ceil_to(self.depth, SUBS)
        self.strip = strip_rows * cols
        self.grid_rows = strip_rows * shares
        self.coarse_rows = self.grid_rows // COARSE
        self.vregs = cols // SUBS
        self.size = (self.grid_rows + 2) * cols
        self.tall_step = largest_step(spec, PERIOD, 512)
        self.thirds = spec // self.tall_step

    def fits(self):
        if self.spec % self.shares or self.depth > LANES or self.rows % (2 * LANES):
            return False
        if 2 * self.points % (LANES * self.shares) or self.points % LANES or self.cap > LANES:
            return False
        if self.shares * self.block % SUBS or self.shares * self.data % SUBS:
            return False
        if 2 * self.points // LANES > LANES or self.cols != LANES:
            return False
        held = 2 * self.size + 2 * self.points + self.shares * (self.block + self.data)
        return 4 * LANES * held + 4 * MIB < 32 * MIB


def pack_kernel(plan, turn_ref, wind_ref, current_ref, recv_ref, out_ref):
    me = lax.axis_index("space")
    half = lambda at: jnp.where(turn_ref[at] == me, 0.5, 0.0)
    mine = half(0) + half(1)
    wind = mine * wind_ref[0]
    points, width, cap = plan.points, plan.force * LANES, plan.cap
    for s in range(plan.shares):
        out_ref[s, :, 0:points] = wind
        out_ref[s, :, points:] = jnp.zeros((2, out_ref.shape[2] - points), F32)
        out_ref[s, 0:1, points : points + cap] = recv_ref[0, s : s + 1, :].astype(F32)
        which, first = divmod(s * width, points)
        out_ref[s, 1:2, points : points + width] = (
            mine * current_ref[0, which : which + 1, first : first + width]
        )


def cell_winds(wind, cp):
    points, rows = wind.shape[1], cp.shape[1]
    high = wind.astype(BF16).astype(F32)
    middle = (wind - high).astype(BF16).astype(F32)
    low = wind - high - middle
    parts = jnp.concatenate([high, middle, low, jnp.zeros((10, points), F32)], axis=0)
    point = lax.broadcasted_iota(jnp.int32, (points, rows), 0)
    hit = jnp.where(point == cp, 1.0, 0.0).astype(BF16)
    picked = jnp.dot(parts.astype(BF16), hit, preferred_element_type=F32)
    both = picked[0:2] + picked[2:4] + picked[4:6]
    return both[0:1], both[1:2]


def fetch(source, target, sems, parts):
    size = target.shape[0] // parts
    copies = [
        pltpu.make_async_copy(
            source.at[pl.ds(q * size, size), :], target.at[pl.ds(q * size, size), :], sems.at[q]
        )
        for q in range(parts)
    ]
    for copy in copies:
        copy.start()
    return copies


def unit_loss(plan, load, arrive, table_ref, unit_ref):
    parts = max(len(arrive), 1)
    tall = plan.spec // parts

    def squares(i, total):
        piece = load(pl.multiple_of(i * 48, 48), 48)
        return total + jnp.sum((piece * piece).reshape(48 // SUBS, SUBS, plan.rows), axis=0)

    total = jnp.zeros((SUBS, plan.rows), F32)
    for q in range(parts):
        if arrive:
            arrive[q].wait()
        total = lax.fori_loop(q * tall // 48, (q + 1) * tall // 48, squares, total)
    mean_square = jnp.sum(total, axis=0, keepdims=True) * (1.0 / plan.spec)
    unit_ref[...] = 1.0 / (1.0 + table_ref[0:PERIOD, 3:4] * mean_square)


def growth_step(first, east, north, table_ref):
    table = table_ref[pl.ds(first, PERIOD), :]
    return jnp.maximum(east * table[:, 0:1] + north * table[:, 1:2] + table[:, 2:3], 1.0)


def coupled(plan, coup_ref, loc_ref, locb_ref, store):
    for q in range(plan.thirds):
        at = slice(q * plan.tall_step, (q + 1) * plan.tall_step)
        store(
            q * plan.tall_step,
            loc_ref[at, :]
            + jnp.dot(coup_ref[at, :], locb_ref[...], preferred_element_type=F32),
        )


def ready_kernel(
    plan, table_ref, coup_hbm, energy_hbm, unit_ref, turned_hbm,
    coup_ref, turned_ref, energy_ref, sems, coup_sem, out_sems,
):
    spec = plan.spec
    arrive = fetch(energy_hbm, energy_ref, sems, plan.thirds)
    get = pltpu.make_async_copy(coup_hbm, coup_ref, coup_sem)
    get.start()
    unit_loss(plan, lambda first, count: energy_ref[pl.ds(first, count), :], arrive, table_ref, unit_ref)
    get.wait()
    copies, wide = [], 3 * LANES
    for first in range(0, spec, LANES):
        at = slice(first, min(first + LANES, spec))
        turned_ref[at, :] = coup_ref[:, at].T
        if at.stop % wide == 0 or at.stop == spec:
            done = slice((at.stop - 1) // wide * wide, at.stop)
            copies.append(
                pltpu.make_async_copy(
                    turned_ref.at[done, :], turned_hbm.at[done, :], out_sems.at[len(copies)]
                )
            )
            copies[-1].start()
    for copy in copies:
        copy.wait()


def own_places(plan, parcel_ref, send_ref, count_ref):
    points, cols, vregs, cap = plan.points, plan.cols, plan.vregs, plan.cap
    landing = jnp.concatenate(
        [parcel_ref[b, 0:1, points : points + cap] for b in range(plan.shares)], axis=0
    ).astype(jnp.int32)
    cell = landing + plan.strip * lax.broadcasted_iota(jnp.int32, (plan.shares, cap), 0)
    column = lax.rem(cell, cols)
    place = cell - column + cols + lax.rem(column, vregs) * SUBS + lax.div(column, vregs)
    place = place.astype(F32)
    slot = lax.broadcasted_iota(jnp.int32, (1, cap), 1)
    names = [
        jnp.where(slot < count_ref[0, b], send_ref[0, b : b + 1, :], -1) for b in range(plan.shares)
    ]
    rows = []
    for j in range(plan.tiles):
        own = lax.broadcasted_iota(jnp.int32, (LANES, cap), 0) + j * LANES
        found = jnp.zeros((LANES, cap), F32)
        for b in range(plan.shares):
            found += jnp.where(names[b] == own, place[b : b + 1, :], 0.0)
        found = jnp.broadcast_to(jnp.sum(found, axis=1, keepdims=True), (LANES, LANES)).T
        shift = lax.rem(lax.broadcasted_iota(jnp.int32, (1, LANES), 1), SUBS).astype(F32)
        rows.append(found[0:1, :] - shift)
    return rows


def first_kernel(
    plan,
    count_ref, cp_ref, parcel_ref, send_ref, table_ref, unit_ref, energy_hbm, coup_hbm, winds_ref, out_hbm,
    out_ref, buf_ref, loc_ref, coup_ref, locb_ref, sems, coup_sem, out_sems,
):
    tiles, shares, points, block, data = plan.tiles, plan.shares, plan.points, plan.block, plan.data
    arrive = fetch(energy_hbm, loc_ref, sems, plan.thirds)
    get = pltpu.make_async_copy(coup_hbm, coup_ref, coup_sem)
    get.start()
    width = plan.force * LANES
    current = jnp.sum(parcel_ref[:, :, points : points + width], axis=0)
    spare = own_places(plan, parcel_ref, send_ref, count_ref)
    spare += [current[1:2, f * LANES : (f + 1) * LANES] for f in range(plan.force)]
    for d in range(shares):
        out_ref[d * block + data : (d + 1) * block, :] = jnp.concatenate(spare, axis=0)
    east, north = cell_winds(jnp.sum(parcel_ref[:, :, 0:points], axis=0), cp_ref[...])
    winds_ref[0:1, :] = east
    winds_ref[1:2, :] = north
    per = plan.tall_step // PERIOD
    for q in range(plan.thirds):
        arrive[q].wait()

        @pl.loop(q * per, (q + 1) * per)
        def _(i):
            first = pl.multiple_of(i * PERIOD, PERIOD)
            at = pl.ds(first, PERIOD)
            local = loc_ref[at, :] * unit_ref[...] * growth_step(first, east, north, table_ref)
            loc_ref[at, :] = local
            locb_ref[at, :] = local.astype(BF16)

    get.wait()
    sent, copies = [0], []

    def store(first, values):
        for j in range(tiles):
            buf_ref[pl.ds(first * tiles + j, values.shape[0], stride=tiles), :] = values[
                :, j * LANES : (j + 1) * LANES
            ]
        upto = (first + values.shape[0]) // plan.depth
        for d in range(sent[0], upto):
            out_ref[d * block : d * block + data, :] = buf_ref[d * data : (d + 1) * data, :]
        at = slice(sent[0] * block // SUBS * SUBS, upto * block // SUBS * SUBS)
        copies.append(
            pltpu.make_async_copy(out_ref.at[at, :], out_hbm.at[at, :], out_sems.at[len(copies)])
        )
        copies[-1].start()
        sent[0] = upto

    coupled(plan, coup_ref, loc_ref, locb_ref, store)
    for copy in copies:
        copy.wait()


def last_kernel(
    plan,
    winds_ref, table_ref, came_ref, coup_ref, out_hbm, loc_ref, locb_ref, unit_ref, out_sems,
):
    tiles = plan.tiles
    copies = []

    def load(first, count):
        start = pl.multiple_of(first * tiles, SUBS)
        return jnp.concatenate(
            [came_ref[pl.ds(start + j, count, stride=tiles), :] for j in range(tiles)], axis=1
        )

    unit_loss(plan, load, [], table_ref, unit_ref)
    east, north = winds_ref[0:1, :], winds_ref[1:2, :]

    @pl.loop(0, plan.spec // PERIOD)
    def _(i):
        first = pl.multiple_of(i * PERIOD, PERIOD)
        at = pl.ds(first, PERIOD)
        local = load(first, PERIOD) * unit_ref[...] * growth_step(first, east, north, table_ref)
        loc_ref[at, :] = local
        locb_ref[at, :] = local.astype(BF16)

    def store(first, values):
        at = slice(first, first + values.shape[0])
        loc_ref[at, :] = values
        copies.append(
            pltpu.make_async_copy(loc_ref.at[at, :], out_hbm.at[at, :], out_sems.at[len(copies)])
        )
        copies[-1].start()

    coupled(plan, coup_ref, loc_ref, locb_ref, store)
    for copy in copies:
        copy.wait()


def scatter(plan, place_ref, came_ref, grid_ref, cell_ref):
    depth, tiles, tall = plan.depth, plan.tiles, plan.tall
    sub = lax.broadcasted_iota(jnp.int32, (SUBS, LANES), 0)
    fill = [jnp.zeros((tall - depth, LANES), F32)] if tall > depth else []

    @pl.loop(0, plan.shares)
    def _(s):
        blocks = [
            came_ref[pl.ds(s * plan.block + j, depth, stride=tiles), :] for j in range(tiles)
        ]
        turned = [jnp.concatenate([block] + fill, axis=0).T for block in blocks]
        for j in range(tiles):
            cell_ref[j * LANES : (j + 1) * LANES, 0:tall] = turned[j]

        @pl.loop(0, tiles)
        def _(j):
            first = s * plan.rows + j * LANES
            for g in range(LANES // SUBS):
                at = pl.ds(pl.multiple_of(j * LANES + g * SUBS, SUBS), SUBS)
                values = cell_ref[at, :]
                for t in range(SUBS):
                    spot = place_ref[first + g * SUBS + t]
                    pltpu.store(grid_ref.at[pl.ds(spot, SUBS), :], values, mask=sub == t)


def gather(plan, place_ref, out_ref, grid_ref, cell_ref):
    depth, tiles, tall = plan.depth, plan.tiles, plan.tall
    sub = lax.broadcasted_iota(jnp.int32, (SUBS, LANES), 0)

    @pl.loop(0, plan.shares)
    def _(s):
        @pl.loop(0, tiles)
        def _(j):
            first = s * plan.rows + j * LANES
            for g in range(LANES // SUBS):
                values = grid_ref[pl.ds(place_ref[first + g * SUBS], SUBS), :]
                for t in range(1, SUBS):
                    shifted = grid_ref[pl.ds(place_ref[first + g * SUBS + t], SUBS), :]
                    values = jnp.where(sub == t, shifted, values)
                cell_ref[pl.ds(pl.multiple_of(j * LANES + g * SUBS, SUBS), SUBS), :] = values

        turned = [cell_ref[j * LANES : (j + 1) * LANES, 0:tall].T for j in range(tiles)]
        for j in range(tiles):
            out_ref[pl.ds(s * plan.data + j, depth, stride=tiles), :] = turned[j][0:depth, :]


def spread_drift(plan, came_ref, held, turned, drift_ref):
    held[...] = jnp.zeros((LANES, LANES), F32)
    for s in range(plan.shares):
        first = s * plan.block + plan.data + plan.tiles
        held[s * plan.force : (s + 1) * plan.force, :] = came_ref[first : first + plan.force, :]
    turned[...] = (courant_scale * held[...]).T
    groups = plan.vregs // COARSE
    ordered = jnp.concatenate(
        [
            turned[pl.ds(a * groups * SUBS + m, SUBS, stride=groups), :]
            for a in range(LANES // (groups * SUBS))
            for m in range(groups)
        ],
        axis=0,
    )
    for q in range(plan.shares * plan.force):
        drift_ref[q * LANES : (q + 1) * LANES, :] = jnp.broadcast_to(
            ordered[:, q : q + 1], (LANES, LANES)
        )


def sweep(plan, drift_ref, speed_ref, one_ref, two_ref):
    cols, last = plan.cols, plan.coarse_rows - 1
    groups = plan.vregs // COARSE
    sub = lax.broadcasted_iota(jnp.int32, (SUBS, LANES), 0)
    speeds = [jnp.broadcast_to(speed_ref[d : d + 1, :], (SUBS, LANES)) for d in range(2)]

    for m in range(groups):

        def courant(which, r4):
            at = pl.multiple_of(((which * plan.coarse_rows + r4) * groups + m) * SUBS, SUBS)
            value = speeds[which] + drift_ref[pl.ds(at, SUBS), :]
            return value > 0.0, jnp.abs(value)

        def at(row, q):
            return pl.ds(pl.multiple_of((row + 1) * cols + q * SUBS, SUBS), SUBS)

        def along(row, speed):
            ahead, size = speed
            base = pl.multiple_of((row + 1) * cols, SUBS)
            first, count = m * COARSE, COARSE
            line = [one_ref[at(row, q), :] for q in range(first, first + count)]
            if first:
                before = one_ref[at(row, first - 1), :]
            else:
                before = one_ref[pl.ds(base + cols - SUBS - 1, SUBS), :]
                before = jnp.where(sub == 0, DRY, before)
            if first + count < plan.vregs:
                after = one_ref[at(row, first + count), :]
            else:
                after = jnp.where(sub == SUBS - 1, DRY, one_ref[pl.ds(base + 1, SUBS), :])
            line = [before] + line + [after]
            swept = []
            for q in range(1, count + 1):
                pick = jnp.where(ahead, line[q - 1], line[q + 1])
                pick = jnp.where(pick < DRY, pick, 0.0)
                moved = line[q] + size * (pick - line[q])
                swept.append(jnp.where(line[q] < DRY, moved, 0.0))
            return swept

        def coarse(r4, held):
            above, here = held
            east = courant(0, r4)
            ahead, size = courant(1, r4)
            later = courant(0, jnp.minimum(r4 + 1, last))
            for dr in range(COARSE):
                row = r4 * COARSE + dr
                below = along(row + 1, east if dr < COARSE - 1 else later)
                for q in range(COARSE):
                    pick = jnp.where(ahead, above[q], below[q])
                    two_ref[at(row, m * COARSE + q), :] = here[q] + size * (pick - here[q])
                above, here = here, below
            return above, here

        zero = [jnp.zeros((SUBS, LANES), F32)] * COARSE
        lax.fori_loop(0, plan.coarse_rows, coarse, (zero, along(0, courant(0, 0))), unroll=2)


def middle_kernel(
    plan,
    place_ref, speed_ref, came_ref, out_ref, one_ref, two_ref, drift_ref, cell_ref,
):
    @pl.loop(0, plan.size // LANES)
    def _(i):
        at = pl.ds(pl.multiple_of(i * LANES, LANES), LANES)
        one_ref[at, :] = jnp.full((LANES, LANES), DRY, F32)

    scatter(plan, place_ref, came_ref, one_ref, cell_ref)
    spread_drift(plan, came_ref, cell_ref.at[0:LANES], cell_ref.at[LANES : 2 * LANES], drift_ref)
    me = lax.axis_index("space")
    sweep(plan, drift_ref, speed_ref.at[me], one_ref, two_ref)
    gather(plan, place_ref, out_ref, two_ref, cell_ref)


VMEM = pl.BlockSpec(memory_space=pltpu.VMEM)
SMEM = pl.BlockSpec(memory_space=pltpu.SMEM)
ANY = pl.BlockSpec(memory_space=pl.ANY)


def on_spectrum(
    plan,
    spectra,
    wind_files,
    current_files,
    reader_turn,
    cell_point,
    coupling,
    send_list,
    send_count,
    recv_list,
):
    shares, rows, spec, points = plan.shares, plan.rows, plan.spec, plan.points
    tiles, depth, size, data_rows = plan.tiles, plan.depth, plan.size, plan.shares * plan.data
    source, east_speed, north_speed = wave_tables()
    table = jnp.asarray(source)
    speed = np.zeros((shares, SUBS, LANES), np.float32)
    speed[:, 0, :depth] = east_speed.reshape(shares, depth)
    speed[:, 1, :depth] = north_speed.reshape(shares, depth)

    def kernel(body, *, flops, traffic, vmem=WHOLE_VMEM, **options):
        return pl.pallas_call(
            body,
            compiler_params=pltpu.CompilerParams(vmem_limit_bytes=vmem),
            cost_estimate=pl.CostEstimate(flops=flops, bytes_accessed=traffic, transcendentals=0),
            **options,
        )

    width = points + max(LANES, plan.force * LANES)
    parcel = kernel(
        functools.partial(pack_kernel, plan),
        flops=0, traffic=4 * shares * 2 * width,
        out_shape=jax.ShapeDtypeStruct((shares, 2, width), F32),
        in_specs=[SMEM, VMEM, VMEM, VMEM],
        out_specs=VMEM,
        name="pack",
    )(reader_turn, wind_files, current_files, recv_list)
    parcel = lax.all_to_all(parcel, "space", 0, 0, tiled=True)

    cp = cell_point.reshape(1, rows)
    h_cost = dict(flops=2 * rows * spec * spec, traffic=12 * rows * spec)
    whole = pltpu.VMEM((spec, rows), F32)
    rounded = pltpu.VMEM((spec, rows), BF16)
    square = pltpu.VMEM((spec, spec), BF16)
    unit = pltpu.VMEM((PERIOD, rows), F32)
    dma = pltpu.SemaphoreType.DMA
    unit_loss_held, coup = kernel(
        functools.partial(ready_kernel, plan),
        flops=0, traffic=12 * rows * spec,
        out_shape=[
            jax.ShapeDtypeStruct((PERIOD, rows), F32), jax.ShapeDtypeStruct((spec, spec), BF16)
        ],
        in_specs=[VMEM, ANY, ANY],
        out_specs=[VMEM, ANY],
        scratch_shapes=[square, square, whole, dma((plan.thirds,)), dma, dma((8,))],
        name="ready",
    )(table, coupling, spectra.T)
    winds, sent = kernel(
        functools.partial(first_kernel, plan),
        **h_cost,
        out_shape=[
            jax.ShapeDtypeStruct((SUBS, rows), F32),
            jax.ShapeDtypeStruct((shares * plan.block, LANES), F32),
        ],
        in_specs=[SMEM] + [VMEM] * 5 + [ANY] * 2,
        out_specs=[VMEM, ANY],
        scratch_shapes=[
            pltpu.VMEM((shares * plan.block, LANES), F32),
            pltpu.VMEM((data_rows, LANES), F32),
            whole, square, rounded, dma((plan.thirds,)), dma, dma((plan.thirds,)),
        ],
        name="first_half",
    )(send_count, cp, parcel, send_list, table, unit_loss_held, spectra.T, coup)
    came = lax.all_to_all(
        sent.reshape(shares, plan.block, 1, LANES), "space", 0, 0, tiled=True
    )
    place = came[:, plan.data : plan.data + tiles].astype(jnp.int32).reshape(-1)
    swept = kernel(
        functools.partial(middle_kernel, plan),
        flops=24 * size * LANES, traffic=8 * rows * spec, vmem=32 * MIB,
        out_shape=jax.ShapeDtypeStruct((data_rows, LANES), F32),
        in_specs=[SMEM, VMEM, VMEM],
        out_specs=VMEM,
        scratch_shapes=[
            pltpu.VMEM((size, LANES), F32),
            pltpu.VMEM((size, LANES), F32),
            pltpu.VMEM((2 * points, LANES), F32),
            pltpu.VMEM((rows, LANES), F32),
        ],
        name="sweeps",
    )(place, jnp.asarray(speed), came.reshape(-1, LANES))
    back = lax.all_to_all(
        swept.reshape(shares, depth, tiles, LANES), "space", 0, 0, tiled=True
    )
    result = kernel(
        functools.partial(last_kernel, plan),
        vmem=24 * MIB, **h_cost,
        out_shape=jax.ShapeDtypeStruct((spec, rows), F32),
        in_specs=[VMEM] * 4,
        out_specs=ANY,
        scratch_shapes=[whole, rounded, unit, dma((plan.thirds,))],
        name="last_half",
    )(winds, table, back.reshape(data_rows, LANES), coup)
    return result.T


def on_device(*args):
    spectra, wind_files, send_list, wet_mask = args[0], args[1], args[6], args[9]
    plan = Plan(
        lax.axis_size("space"), *spectra.shape, send_list.shape[2], *wet_mask.shape, wind_files.shape[2]
    )
    if plan.fits():
        return on_spectrum(plan, *args[:9])
    return on_strips(*args)


def solution(mesh):
    placed = (
        P(("members", "space"), None),
        P(("members", "space"), None, None),
        P(("members", "space"), None, None),
        P(),
        P("space"),
        P(),
        P("space", None, None),
        P("space", None),
        P("space", None, None),
        P("space", None),
    )
    return jax.shard_map(
        on_device,
        mesh=mesh,
        in_specs=placed,
        out_specs=P(("members", "space"), None),
        check_vma=False,
    )
```

```python
import functools
import math

import jax
import jax.numpy as jnp
import numpy as np
from jax import lax
from jax.experimental import pallas as pl
from jax.experimental.pallas import tpu as pltpu
from jax.sharding import PartitionSpec as P

DIRS = 36
FREQS = 36
COARSE = 4


gravity = 9.81
base_freq = 0.0418
freq_ratio = 1.1
freq_span = 35.0
input_coef = 0.0001
wind_gain = 1.12
dissip_coef = 0.0005
half_length = 300.0
courant_scale = 0.05


def from_root(array, axis, root):
    mine = lax.axis_index(axis) == root
    return lax.psum(jnp.where(mine, array, jnp.zeros_like(array)), axis)


def extended(array, sides, width):
    for axis, dim in sides:
        size, length = (lax.axis_size(axis), array.shape[dim])
        up = [(i, (i + 1) % size) for i in range(size - 1)]
        down = [(j, i) for i, j in up]
        last = lax.slice_in_dim(array, length - width, length, axis=dim)
        first = lax.slice_in_dim(array, 0, width, axis=dim)
        before = lax.ppermute(last, axis, up)
        after = lax.ppermute(first, axis, down)
        array = jnp.concatenate([before, array, after], axis=dim)
    return array


def spectral_tables():
    direction = 2.0 * math.pi / DIRS * jnp.arange(DIRS, dtype=jnp.float32)
    exponent = jnp.arange(FREQS, dtype=jnp.float32) * (freq_span / (FREQS - 1))
    frequency = base_freq * freq_ratio**exponent
    angular = 2.0 * math.pi * frequency
    phase_speed = gravity / angular
    return (jnp.cos(direction), jnp.sin(direction), angular, phase_speed, 0.5 * phase_speed)


def source_half(energy, wind_east, wind_north, coupling):
    cos_dir, sine_dir, angular, phase_speed, group_speed = spectral_tables()
    along_wind = wind_east[:, None] * cos_dir[None, :] + wind_north[:, None] * sine_dir[None, :]
    growth = (
        input_coef
        * angular[None, None, :]
        * jnp.maximum(wind_gain * along_wind[:, :, None] / phase_speed[None, None, :] - 1.0, 0.0)
    )
    growth = growth.reshape(energy.shape[0], -1)
    mean_square = jnp.mean(energy * energy, axis=1, keepdims=True)
    decay_rate = dissip_coef * jnp.tile(angular, DIRS)[None, :] * mean_square
    local_part = energy * (1.0 + half_length * growth) / (1.0 + half_length * decay_rate)
    return local_part + jnp.dot(
        local_part.astype(jnp.bfloat16), coupling, preferred_element_type=jnp.float32
    )


def advect(center, upwind_lo, upwind_hi, courant):
    ahead_part = jnp.maximum(courant, 0.0)
    behind = jnp.minimum(courant, 0.0)
    return center - ahead_part * (center - upwind_lo) - behind * (upwind_hi - center)


def sweep_cols(energy_grid, drift_east, wet_field):
    cos_dir, sine_dir, angular, phase_speed, group_speed = spectral_tables()
    wave_speed = (cos_dir[:, None] * group_speed[None, :]).reshape(-1)
    courant = (wave_speed[None, None, :] + drift_east[:, :, None]) * courant_scale
    zero_edge = jnp.zeros_like(energy_grid[:, :1])
    upwind_lo = jnp.concatenate([zero_edge, energy_grid[:, :-1]], axis=1)
    upwind_hi = jnp.concatenate([energy_grid[:, 1:], zero_edge], axis=1)
    return advect(energy_grid, upwind_lo, upwind_hi, courant) * wet_field[:, :, None]


def sweep_rows(energy_grid, row_above, row_below, drift_north, wet_field):
    cos_dir, sine_dir, angular, phase_speed, group_speed = spectral_tables()
    wave_speed = (sine_dir[:, None] * group_speed[None, :]).reshape(-1)
    courant = (wave_speed[None, None, :] + drift_north[:, :, None]) * courant_scale
    return advect(energy_grid, row_above, row_below, courant) * wet_field[:, :, None]


def forcing_points(row_start, row_count, col_count):
    rows_idx = row_start + jnp.arange(row_count, dtype=jnp.int32)
    cols_idx = jnp.arange(col_count, dtype=jnp.int32)
    return rows_idx[:, None] // COARSE * (col_count // COARSE) + cols_idx[None, :] // COARSE


def on_strips(
    spectra,
    wind_files,
    current_files,
    reader_turn,
    cell_point,
    coupling,
    send_list,
    send_count,
    recv_list,
    wet_mask,
):
    levels = []
    for time_level in range(2):
        levels.append(
            (
                from_root(wind_files[0], "space", reader_turn[time_level]),
                from_root(current_files[0], "space", reader_turn[time_level]),
            )
        )
    wind_mean = 0.5 * (levels[0][0] + levels[1][0])
    current_mean = 0.5 * (levels[0][1] + levels[1][1])
    cell_wind = jnp.take(wind_mean, cell_point, axis=1)
    first_half = source_half(spectra, cell_wind[0], cell_wind[1], coupling)
    send_rows = send_list[0]
    counts = send_count[0]
    places = recv_list[0]
    slot_count = send_rows.shape[1]
    spec_width = spectra.shape[1]
    live_slots = (jnp.arange(slot_count, dtype=jnp.int32)[None, :] < counts[:, None]).astype(
        jnp.float32
    )
    packed = first_half[send_rows] * live_slots[:, :, None]
    arrived = lax.all_to_all(packed, "space", split_axis=0, concat_axis=0, tiled=True)
    row_count = wet_mask.shape[0]
    col_count = wet_mask.shape[1]
    energy_grid = (
        jnp.zeros((row_count * col_count, spec_width), jnp.float32)
        .at[places.reshape(-1)]
        .add(arrived.reshape(-1, spec_width))
    )
    energy_grid = energy_grid.reshape(row_count, col_count, spec_width)
    points = forcing_points(lax.axis_index("space") * row_count, row_count, col_count)
    drift = jnp.take(current_mean, points, axis=1)
    wet_field = wet_mask.astype(jnp.float32)
    swept_cols = sweep_cols(energy_grid, drift[0], wet_field)
    padded = extended(swept_cols, (("space", 0),), 1)
    swept = sweep_rows(swept_cols, padded[:-2], padded[2:], drift[1], wet_field).reshape(
        -1, spec_width
    )
    outgoing = swept[places]
    flat_rows = send_rows.reshape(-1)
    empty_rows = jnp.zeros((spectra.shape[0], spec_width), jnp.float32)
    returned = lax.all_to_all(outgoing, "space", split_axis=0, concat_axis=0, tiled=True)
    back_rows = empty_rows.at[flat_rows].add(
        (returned * live_slots[:, :, None]).reshape(-1, spec_width)
    )
    result = source_half(back_rows, cell_wind[0], cell_wind[1], coupling)
    return result


LANES = 128
SUBS = 8
F32 = jnp.float32
BF16 = jnp.bfloat16
MIB = 1024 * 1024
WHOLE_VMEM = 60 * MIB
DRY = 1e30
PERIOD = 4 * FREQS


def wave_tables():
    direction = 2.0 * np.pi / DIRS * np.arange(DIRS)
    frequency = base_freq * freq_ratio ** (np.arange(FREQS) * (freq_span / (FREQS - 1)))
    angular = 2.0 * np.pi * frequency
    phase = gravity / angular
    group = 0.5 * phase
    cos_dir, sin_dir = np.cos(direction)[:, None], np.sin(direction)[:, None]
    flat = lambda t: np.broadcast_to(t, (DIRS, FREQS)).reshape(-1)
    growth = half_length * input_coef * angular
    source = np.zeros((DIRS * FREQS, 8), np.float32)
    source[:, 0] = flat(growth * wind_gain * cos_dir / phase)
    source[:, 1] = flat(growth * wind_gain * sin_dir / phase)
    source[:, 2] = flat(1.0 - growth)
    source[:, 3] = flat(half_length * dissip_coef * angular)
    east = flat(courant_scale * cos_dir * group).astype(np.float32)
    north = flat(courant_scale * sin_dir * group).astype(np.float32)
    return source, east, north


def ceil_to(value, step):
    return -(-value // step) * step


def largest_step(size, step, most):
    return max(s for s in range(step, most + 1, step) if size % s == 0)


class Plan:
    def __init__(self, shares, rows, spec, cap, strip_rows, cols, points):
        self.shares, self.rows, self.spec, self.cap = shares, rows, spec, cap
        self.cols, self.points = cols, points
        self.depth = spec // shares
        self.tiles = rows // LANES
        self.data = self.depth * self.tiles
        self.force = 2 * points // (LANES * shares)
        self.block = self.data + self.tiles + self.force
        self.tall = ceil_to(self.depth, SUBS)
        self.strip = strip_rows * cols
        self.grid_rows = strip_rows * shares
        self.coarse_rows = self.grid_rows // COARSE
        self.vregs = cols // SUBS
        self.size = (self.grid_rows + 2) * cols
        self.tall_step = largest_step(spec, PERIOD, 512)
        self.thirds = spec // self.tall_step

    def fits(self):
        if self.spec % self.shares or self.depth > LANES or self.rows % (2 * LANES):
            return False
        if 2 * self.points % (LANES * self.shares) or self.points % LANES or self.cap > LANES:
            return False
        if self.shares * self.block % SUBS or self.shares * self.data % SUBS:
            return False
        if 2 * self.points // LANES > LANES or self.cols != LANES:
            return False
        held = 2 * self.size + 2 * self.points + self.shares * (self.block + self.data)
        return 4 * LANES * held + 4 * MIB < 32 * MIB


def pack_kernel(plan, turn_ref, wind_ref, current_ref, recv_ref, out_ref):
    me = lax.axis_index("space")
    half = lambda at: jnp.where(turn_ref[at] == me, 0.5, 0.0)
    mine = half(0) + half(1)
    wind = mine * wind_ref[0]
    points, width, cap = plan.points, plan.force * LANES, plan.cap
    for s in range(plan.shares):
        out_ref[s, :, 0:points] = wind
        out_ref[s, :, points:] = jnp.zeros((2, out_ref.shape[2] - points), F32)
        out_ref[s, 0:1, points : points + cap] = recv_ref[0, s : s + 1, :].astype(F32)
        which, first = divmod(s * width, points)
        out_ref[s, 1:2, points : points + width] = (
            mine * current_ref[0, which : which + 1, first : first + width]
        )


def cell_winds(wind, cp):
    points, rows = wind.shape[1], cp.shape[1]
    high = wind.astype(BF16).astype(F32)
    middle = (wind - high).astype(BF16).astype(F32)
    low = wind - high - middle
    parts = jnp.concatenate([high, middle, low, jnp.zeros((10, points), F32)], axis=0)
    point = lax.broadcasted_iota(jnp.int32, (points, rows), 0)
    hit = jnp.where(point == cp, 1.0, 0.0).astype(BF16)
    picked = jnp.dot(parts.astype(BF16), hit, preferred_element_type=F32)
    both = picked[0:2] + picked[2:4] + picked[4:6]
    return both[0:1], both[1:2]


def fetch(source, target, sems, parts):
    size = target.shape[0] // parts
    copies = [
        pltpu.make_async_copy(
            source.at[pl.ds(q * size, size), :], target.at[pl.ds(q * size, size), :], sems.at[q]
        )
        for q in range(parts)
    ]
    for copy in copies:
        copy.start()
    return copies


def unit_loss(plan, load, arrive, table_ref, unit_ref):
    parts = max(len(arrive), 1)
    tall = plan.spec // parts

    def squares(i, total):
        piece = load(pl.multiple_of(i * 48, 48), 48)
        return total + jnp.sum((piece * piece).reshape(48 // SUBS, SUBS, plan.rows), axis=0)

    total = jnp.zeros((SUBS, plan.rows), F32)
    for q in range(parts):
        if arrive:
            arrive[q].wait()
        total = lax.fori_loop(q * tall // 48, (q + 1) * tall // 48, squares, total)
    mean_square = jnp.sum(total, axis=0, keepdims=True) * (1.0 / plan.spec)
    unit_ref[...] = 1.0 / (1.0 + table_ref[0:PERIOD, 3:4] * mean_square)


def growth_step(first, east, north, table_ref):
    table = table_ref[pl.ds(first, PERIOD), :]
    return jnp.maximum(east * table[:, 0:1] + north * table[:, 1:2] + table[:, 2:3], 1.0)


def coupled(plan, coup_ref, loc_ref, locb_ref, store):
    for q in range(plan.thirds):
        at = slice(q * plan.tall_step, (q + 1) * plan.tall_step)
        store(
            q * plan.tall_step,
            loc_ref[at, :]
            + jnp.dot(coup_ref[at, :], locb_ref[...], preferred_element_type=F32),
        )


def ready_kernel(
    plan, table_ref, coup_hbm, energy_hbm, unit_ref, turned_hbm,
    coup_ref, turned_ref, energy_ref, sems, coup_sem, out_sems,
):
    spec = plan.spec
    arrive = fetch(energy_hbm, energy_ref, sems, plan.thirds)
    get = pltpu.make_async_copy(coup_hbm, coup_ref, coup_sem)
    get.start()
    unit_loss(plan, lambda first, count: energy_ref[pl.ds(first, count), :], arrive, table_ref, unit_ref)
    get.wait()
    copies, wide = [], 3 * LANES
    for first in range(0, spec, LANES):
        at = slice(first, min(first + LANES, spec))
        turned_ref[at, :] = coup_ref[:, at].T
        if at.stop % wide == 0 or at.stop == spec:
            done = slice((at.stop - 1) // wide * wide, at.stop)
            copies.append(
                pltpu.make_async_copy(
                    turned_ref.at[done, :], turned_hbm.at[done, :], out_sems.at[len(copies)]
                )
            )
            copies[-1].start()
    for copy in copies:
        copy.wait()


def own_places(plan, parcel_ref, send_ref, count_ref):
    points, cols, vregs, cap = plan.points, plan.cols, plan.vregs, plan.cap
    landing = jnp.concatenate(
        [parcel_ref[b, 0:1, points : points + cap] for b in range(plan.shares)], axis=0
    ).astype(jnp.int32)
    cell = landing + plan.strip * lax.broadcasted_iota(jnp.int32, (plan.shares, cap), 0)
    column = lax.rem(cell, cols)
    place = cell - column + cols + lax.rem(column, vregs) * SUBS + lax.div(column, vregs)
    place = place.astype(F32)
    slot = lax.broadcasted_iota(jnp.int32, (1, cap), 1)
    names = [
        jnp.where(slot < count_ref[0, b], send_ref[0, b : b + 1, :], -1) for b in range(plan.shares)
    ]
    rows = []
    for j in range(plan.tiles):
        own = lax.broadcasted_iota(jnp.int32, (LANES, cap), 0) + j * LANES
        found = jnp.zeros((LANES, cap), F32)
        for b in range(plan.shares):
            found += jnp.where(names[b] == own, place[b : b + 1, :], 0.0)
        found = jnp.broadcast_to(jnp.sum(found, axis=1, keepdims=True), (LANES, LANES)).T
        shift = lax.rem(lax.broadcasted_iota(jnp.int32, (1, LANES), 1), SUBS).astype(F32)
        rows.append(found[0:1, :] - shift)
    return rows


def first_kernel(
    plan,
    count_ref, cp_ref, parcel_ref, send_ref, table_ref, unit_ref, energy_hbm, coup_hbm, winds_ref, out_hbm,
    out_ref, buf_ref, loc_ref, coup_ref, locb_ref, sems, coup_sem, out_sems,
):
    tiles, shares, points, block, data = plan.tiles, plan.shares, plan.points, plan.block, plan.data
    arrive = fetch(energy_hbm, loc_ref, sems, plan.thirds)
    get = pltpu.make_async_copy(coup_hbm, coup_ref, coup_sem)
    get.start()
    width = plan.force * LANES
    current = jnp.sum(parcel_ref[:, :, points : points + width], axis=0)
    spare = own_places(plan, parcel_ref, send_ref, count_ref)
    spare += [current[1:2, f * LANES : (f + 1) * LANES] for f in range(plan.force)]
    for d in range(shares):
        out_ref[d * block + data : (d + 1) * block, :] = jnp.concatenate(spare, axis=0)
    east, north = cell_winds(jnp.sum(parcel_ref[:, :, 0:points], axis=0), cp_ref[...])
    winds_ref[0:1, :] = east
    winds_ref[1:2, :] = north
    per = plan.tall_step // PERIOD
    for q in range(plan.thirds):
        arrive[q].wait()

        @pl.loop(q * per, (q + 1) * per)
        def _(i):
            first = pl.multiple_of(i * PERIOD, PERIOD)
            at = pl.ds(first, PERIOD)
            local = loc_ref[at, :] * unit_ref[...] * growth_step(first, east, north, table_ref)
            loc_ref[at, :] = local
            locb_ref[at, :] = local.astype(BF16)

    get.wait()
    sent, copies = [0], []

    def store(first, values):
        for j in range(tiles):
            buf_ref[pl.ds(first * tiles + j, values.shape[0], stride=tiles), :] = values[
                :, j * LANES : (j + 1) * LANES
            ]
        upto = (first + values.shape[0]) // plan.depth
        for d in range(sent[0], upto):
            out_ref[d * block : d * block + data, :] = buf_ref[d * data : (d + 1) * data, :]
        at = slice(sent[0] * block // SUBS * SUBS, upto * block // SUBS * SUBS)
        copies.append(
            pltpu.make_async_copy(out_ref.at[at, :], out_hbm.at[at, :], out_sems.at[len(copies)])
        )
        copies[-1].start()
        sent[0] = upto

    coupled(plan, coup_ref, loc_ref, locb_ref, store)
    for copy in copies:
        copy.wait()


def last_kernel(
    plan,
    winds_ref, table_ref, came_ref, coup_ref, out_hbm, loc_ref, locb_ref, unit_ref, out_sems,
):
    tiles = plan.tiles
    copies = []

    def load(first, count):
        start = pl.multiple_of(first * tiles, SUBS)
        return jnp.concatenate(
            [came_ref[pl.ds(start + j, count, stride=tiles), :] for j in range(tiles)], axis=1
        )

    unit_loss(plan, load, [], table_ref, unit_ref)
    east, north = winds_ref[0:1, :], winds_ref[1:2, :]

    @pl.loop(0, plan.spec // PERIOD)
    def _(i):
        first = pl.multiple_of(i * PERIOD, PERIOD)
        at = pl.ds(first, PERIOD)
        local = load(first, PERIOD) * unit_ref[...] * growth_step(first, east, north, table_ref)
        loc_ref[at, :] = local
        locb_ref[at, :] = local.astype(BF16)

    def store(first, values):
        at = slice(first, first + values.shape[0])
        loc_ref[at, :] = values
        copies.append(
            pltpu.make_async_copy(loc_ref.at[at, :], out_hbm.at[at, :], out_sems.at[len(copies)])
        )
        copies[-1].start()

    coupled(plan, coup_ref, loc_ref, locb_ref, store)
    for copy in copies:
        copy.wait()


def scatter(plan, place_ref, came_ref, grid_ref, cell_ref):
    depth, tiles, tall = plan.depth, plan.tiles, plan.tall
    sub = lax.broadcasted_iota(jnp.int32, (SUBS, LANES), 0)
    fill = [jnp.zeros((tall - depth, LANES), F32)] if tall > depth else []

    @pl.loop(0, plan.shares)
    def _(s):
        blocks = [
            came_ref[pl.ds(s * plan.block + j, depth, stride=tiles), :] for j in range(tiles)
        ]
        turned = [jnp.concatenate([block] + fill, axis=0).T for block in blocks]
        for j in range(tiles):
            cell_ref[j * LANES : (j + 1) * LANES, 0:tall] = turned[j]

        @pl.loop(0, tiles, unroll=2)
        def _(j):
            first = s * plan.rows + j * LANES
            for g in range(LANES // SUBS):
                at = pl.ds(pl.multiple_of(j * LANES + g * SUBS, SUBS), SUBS)
                values = cell_ref[at, :]
                for t in range(SUBS):
                    spot = place_ref[first + g * SUBS + t]
                    pltpu.store(grid_ref.at[pl.ds(spot, SUBS), :], values, mask=sub == t)


def gather(plan, place_ref, out_ref, grid_ref, cell_ref):
    depth, tiles, tall = plan.depth, plan.tiles, plan.tall
    sub = lax.broadcasted_iota(jnp.int32, (SUBS, LANES), 0)

    @pl.loop(0, plan.shares)
    def _(s):
        @pl.loop(0, tiles, unroll=2)
        def _(j):
            first = s * plan.rows + j * LANES
            for g in range(LANES // SUBS):
                values = grid_ref[pl.ds(place_ref[first + g * SUBS], SUBS), :]
                for t in range(1, SUBS):
                    shifted = grid_ref[pl.ds(place_ref[first + g * SUBS + t], SUBS), :]
                    values = jnp.where(sub == t, shifted, values)
                cell_ref[pl.ds(pl.multiple_of(j * LANES + g * SUBS, SUBS), SUBS), :] = values

        turned = [cell_ref[j * LANES : (j + 1) * LANES, 0:tall].T for j in range(tiles)]
        for j in range(tiles):
            out_ref[pl.ds(s * plan.data + j, depth, stride=tiles), :] = turned[j][0:depth, :]


def spread_drift(plan, came_ref, held, turned, drift_ref):
    held[...] = jnp.zeros((LANES, LANES), F32)
    for s in range(plan.shares):
        first = s * plan.block + plan.data + plan.tiles
        held[s * plan.force : (s + 1) * plan.force, :] = came_ref[first : first + plan.force, :]
    turned[...] = (courant_scale * held[...]).T
    groups = plan.vregs // COARSE
    ordered = jnp.concatenate(
        [
            turned[pl.ds(a * groups * SUBS + m, SUBS, stride=groups), :]
            for a in range(LANES // (groups * SUBS))
            for m in range(groups)
        ],
        axis=0,
    )
    for q in range(plan.shares * plan.force):
        drift_ref[q * LANES : (q + 1) * LANES, :] = jnp.broadcast_to(
            ordered[:, q : q + 1], (LANES, LANES)
        )


def sweep(plan, drift_ref, speed_ref, one_ref, two_ref):
    cols, last = plan.cols, plan.coarse_rows - 1
    groups = plan.vregs // COARSE
    sub = lax.broadcasted_iota(jnp.int32, (SUBS, LANES), 0)
    speeds = [jnp.broadcast_to(speed_ref[d : d + 1, :], (SUBS, LANES)) for d in range(2)]

    for m in range(groups):

        def courant(which, r4):
            at = pl.multiple_of(((which * plan.coarse_rows + r4) * groups + m) * SUBS, SUBS)
            value = speeds[which] + drift_ref[pl.ds(at, SUBS), :]
            return value > 0.0, jnp.abs(value)

        def at(row, q):
            return pl.ds(pl.multiple_of((row + 1) * cols + q * SUBS, SUBS), SUBS)

        def along(row, speed):
            ahead, size = speed
            base = pl.multiple_of((row + 1) * cols, SUBS)
            first, count = m * COARSE, COARSE
            line = [one_ref[at(row, q), :] for q in range(first, first + count)]
            if first:
                before = one_ref[at(row, first - 1), :]
            else:
                before = one_ref[pl.ds(base + cols - SUBS - 1, SUBS), :]
                before = jnp.where(sub == 0, DRY, before)
            if first + count < plan.vregs:
                after = one_ref[at(row, first + count), :]
            else:
                after = jnp.where(sub == SUBS - 1, DRY, one_ref[pl.ds(base + 1, SUBS), :])
            line = [before] + line + [after]
            swept = []
            for q in range(1, count + 1):
                pick = jnp.where(ahead, line[q - 1], line[q + 1])
                pick = jnp.where(pick < DRY, pick, 0.0)
                moved = line[q] + size * (pick - line[q])
                swept.append(jnp.where(line[q] < DRY, moved, 0.0))
            return swept

        def coarse(r4, held):
            above, here = held
            east = courant(0, r4)
            ahead, size = courant(1, r4)
            later = courant(0, jnp.minimum(r4 + 1, last))
            for dr in range(COARSE):
                row = r4 * COARSE + dr
                below = along(row + 1, east if dr < COARSE - 1 else later)
                for q in range(COARSE):
                    pick = jnp.where(ahead, above[q], below[q])
                    two_ref[at(row, m * COARSE + q), :] = here[q] + size * (pick - here[q])
                above, here = here, below
            return above, here

        zero = [jnp.zeros((SUBS, LANES), F32)] * COARSE
        lax.fori_loop(0, plan.coarse_rows, coarse, (zero, along(0, courant(0, 0))), unroll=2)


def middle_kernel(
    plan,
    place_ref, speed_ref, came_ref, out_ref, one_ref, two_ref, drift_ref, cell_ref,
):
    @pl.loop(0, plan.size // LANES)
    def _(i):
        at = pl.ds(pl.multiple_of(i * LANES, LANES), LANES)
        one_ref[at, :] = jnp.full((LANES, LANES), DRY, F32)

    scatter(plan, place_ref, came_ref, one_ref, cell_ref)
    spread_drift(plan, came_ref, cell_ref.at[0:LANES], cell_ref.at[LANES : 2 * LANES], drift_ref)
    me = lax.axis_index("space")
    sweep(plan, drift_ref, speed_ref.at[me], one_ref, two_ref)
    gather(plan, place_ref, out_ref, two_ref, cell_ref)


VMEM = pl.BlockSpec(memory_space=pltpu.VMEM)
SMEM = pl.BlockSpec(memory_space=pltpu.SMEM)
ANY = pl.BlockSpec(memory_space=pl.ANY)


def on_spectrum(
    plan,
    spectra,
    wind_files,
    current_files,
    reader_turn,
    cell_point,
    coupling,
    send_list,
    send_count,
    recv_list,
):
    shares, rows, spec, points = plan.shares, plan.rows, plan.spec, plan.points
    tiles, depth, size, data_rows = plan.tiles, plan.depth, plan.size, plan.shares * plan.data
    source, east_speed, north_speed = wave_tables()
    table = jnp.asarray(source)
    speed = np.zeros((shares, SUBS, LANES), np.float32)
    speed[:, 0, :depth] = east_speed.reshape(shares, depth)
    speed[:, 1, :depth] = north_speed.reshape(shares, depth)

    def kernel(body, *, flops, traffic, vmem=WHOLE_VMEM, **options):
        return pl.pallas_call(
            body,
            compiler_params=pltpu.CompilerParams(vmem_limit_bytes=vmem),
            cost_estimate=pl.CostEstimate(flops=flops, bytes_accessed=traffic, transcendentals=0),
            **options,
        )

    width = points + max(LANES, plan.force * LANES)
    parcel = kernel(
        functools.partial(pack_kernel, plan),
        flops=0, traffic=4 * shares * 2 * width,
        out_shape=jax.ShapeDtypeStruct((shares, 2, width), F32),
        in_specs=[SMEM, VMEM, VMEM, VMEM],
        out_specs=VMEM,
        name="pack",
    )(reader_turn, wind_files, current_files, recv_list)
    parcel = lax.all_to_all(parcel, "space", 0, 0, tiled=True)

    cp = cell_point.reshape(1, rows)
    h_cost = dict(flops=2 * rows * spec * spec, traffic=12 * rows * spec)
    whole = pltpu.VMEM((spec, rows), F32)
    rounded = pltpu.VMEM((spec, rows), BF16)
    square = pltpu.VMEM((spec, spec), BF16)
    unit = pltpu.VMEM((PERIOD, rows), F32)
    dma = pltpu.SemaphoreType.DMA
    unit_loss_held, coup = kernel(
        functools.partial(ready_kernel, plan),
        flops=0, traffic=12 * rows * spec,
        out_shape=[
            jax.ShapeDtypeStruct((PERIOD, rows), F32), jax.ShapeDtypeStruct((spec, spec), BF16)
        ],
        in_specs=[VMEM, ANY, ANY],
        out_specs=[VMEM, ANY],
        scratch_shapes=[square, square, whole, dma((plan.thirds,)), dma, dma((8,))],
        name="ready",
    )(table, coupling, spectra.T)
    winds, sent = kernel(
        functools.partial(first_kernel, plan),
        **h_cost,
        out_shape=[
            jax.ShapeDtypeStruct((SUBS, rows), F32),
            jax.ShapeDtypeStruct((shares * plan.block, LANES), F32),
        ],
        in_specs=[SMEM] + [VMEM] * 5 + [ANY] * 2,
        out_specs=[VMEM, ANY],
        scratch_shapes=[
            pltpu.VMEM((shares * plan.block, LANES), F32),
            pltpu.VMEM((data_rows, LANES), F32),
            whole, square, rounded, dma((plan.thirds,)), dma, dma((plan.thirds,)),
        ],
        name="first_half",
    )(send_count, cp, parcel, send_list, table, unit_loss_held, spectra.T, coup)
    came = lax.all_to_all(
        sent.reshape(shares, plan.block, 1, LANES), "space", 0, 0, tiled=True
    )
    place = came[:, plan.data : plan.data + tiles].astype(jnp.int32).reshape(-1)
    swept = kernel(
        functools.partial(middle_kernel, plan),
        flops=24 * size * LANES, traffic=8 * rows * spec, vmem=32 * MIB,
        out_shape=jax.ShapeDtypeStruct((data_rows, LANES), F32),
        in_specs=[SMEM, VMEM, VMEM],
        out_specs=VMEM,
        scratch_shapes=[
            pltpu.VMEM((size, LANES), F32),
            pltpu.VMEM((size, LANES), F32),
            pltpu.VMEM((2 * points, LANES), F32),
            pltpu.VMEM((rows, LANES), F32),
        ],
        name="sweeps",
    )(place, jnp.asarray(speed), came.reshape(-1, LANES))
    back = lax.all_to_all(
        swept.reshape(shares, depth, tiles, LANES), "space", 0, 0, tiled=True
    )
    result = kernel(
        functools.partial(last_kernel, plan),
        vmem=24 * MIB, **h_cost,
        out_shape=jax.ShapeDtypeStruct((spec, rows), F32),
        in_specs=[VMEM] * 4,
        out_specs=ANY,
        scratch_shapes=[whole, rounded, unit, dma((plan.thirds,))],
        name="last_half",
    )(winds, table, back.reshape(data_rows, LANES), coup)
    return result.T


def on_device(*args):
    spectra, wind_files, send_list, wet_mask = args[0], args[1], args[6], args[9]
    plan = Plan(
        lax.axis_size("space"), *spectra.shape, send_list.shape[2], *wet_mask.shape, wind_files.shape[2]
    )
    if plan.fits():
        return on_spectrum(plan, *args[:9])
    return on_strips(*args)


def solution(mesh):
    placed = (
        P(("members", "space"), None),
        P(("members", "space"), None, None),
        P(("members", "space"), None, None),
        P(),
        P("space"),
        P(),
        P("space", None, None),
        P("space", None),
        P("space", None, None),
        P("space", None),
    )
    return jax.shard_map(
        on_device,
        mesh=mesh,
        in_specs=placed,
        out_specs=P(("members", "space"), None),
        check_vma=False,
    )
```
